32 devices in a mesh: section: 2 (over x), dp: 16 (over z, y, core).
Axes of the slice: x: 2, y: 2, z: 4, core: 2. Of those that a mesh axis runs over, the one named last changes fastest.
Arguments:
- tokens: bfloat16 [16384, 768], P('dp'), may hold values from -6 to 6
- segments: int32 [32, 512], P('dp'), may hold values from 0 to 7, never falling along the last dimension, each value on 1 to 256 neighbouring positions
- lengths: int32 [32], P('dp'), may hold values from 256 to 512
- cotangent: bfloat16 [16384, 768], P('dp'), may hold values from -6 to 6
- qkv_weight: bfloat16 [2, 768, 2304], P('section'), may hold values from -0.21875 to 0.21875
- qv_bias: float32 [2, 2, 768], P('section'), may hold values from -2 to 2
- out_weight: bfloat16 [2, 768, 768], P('section'), may hold values from -0.875 to 0.875
- out_biases: float32 [2, 2, 768], P('section'), may hold values from -2 to 2
- norm_gains: float32 [2, 2, 768], P('section'), may hold values from 0.5 to 1.5
- norm_shifts: float32 [2, 2, 768], P('section'), may hold values from -2 to 2
- up_weight: bfloat16 [2, 768, 3072], P('section'), may hold values from -0.21875 to 0.21875
- up_bias: float32 [2, 3072], P('section'), may hold values from -2 to 2
- down_weight: bfloat16 [2, 3072, 768], P('section'), may hold values from -0.109375 to 0.109375
Outputs:
- activations: bfloat16 [2, 16384, 768], P('section', 'dp')
- input_grads: bfloat16 [2, 16384, 768], P('section', 'dp')
- grad_qkv_weight: float32 [2, 768, 2304], P('section')
- grad_qv_bias: float32 [2, 2, 768], P('section')
- grad_out_weight: float32 [2, 768, 768], P('section')
- grad_out_biases: float32 [2, 2, 768], P('section')
- grad_norm_gains: float32 [2, 2, 768], P('section')
- grad_norm_shifts: float32 [2, 2, 768], P('section')
- grad_up_weight: float32 [2, 768, 3072], P('section')
- grad_up_bias: float32 [2, 3072], P('section')
- grad_down_weight: float32 [2, 3072, 768], P('section')
The draws below stay inside these ranges and needn't reach their ends.
Inputs may be any that keep to these rules, and one draw needn't show every extreme that they name: `segments`: segment numbers never fall along a sequence. Positions at or beyond a sequence's lengths entry are padding, seen as keys only by themselves.
All inputs are finite; a program needn't handle non-finite values.
Results may differ from the reference program's by a relative error of at most 0.018.
Values may be sent and summed in bfloat16 or wider, within the bound.
A program may use at most 256 MiB of HBM per device.

```python
import math
import jax
import jax.numpy as jnp
import numpy as np
from jax import lax

D = 768
H = 12
HD = 64
FF = 3072
SEQ = 512
SEQS = 32
TOKENS = 16384


def plant(values, key, smallest, top_value):
    shape = values.shape
    place = [jax.random.randint(jax.random.fold_in(key, axis), (), 0, shape[axis]) for axis in range(len(shape))]
    values = values.at[tuple(place)].set(smallest)
    longest = shape.index(max(shape))
    place[longest] = (place[longest] + 1) % shape[longest]
    return values.at[tuple(place)].set(top_value)


def block_scale(key, dims, split, smallest, high):
    level, own = 1.0, jax.random.fold_in(key, 6)
    for dim, shards_of in split:
        heights = jnp.exp(jax.random.uniform(jax.random.fold_in(own, dim), (shards_of,), jnp.float32, smallest / len(split), high / len(split)))
        level = level * jnp.repeat(heights, dims[dim] // shards_of).reshape([-1 if axis == dim else 1 for axis in range(len(dims))])
    return level


def profile(amount, total, reach, slope):
    portions = [(1 << 20) // math.isqrt(standing ** slope) + 1 for standing in range(2, amount + 1)]
    spare, counts = total - reach - (amount - 1), [1] * (amount - 1)
    while spare > 0:
        candidates = [i for i in range(amount - 1) if counts[i] < reach]
        pool, remaining = sum([portions[i] for i in candidates]), spare
        for i in candidates:
            more = min(reach - counts[i], max(1, remaining * portions[i] // pool), spare)
            counts[i] = counts[i] + more
            spare = spare - more
    return np.array([reach] + counts)


def ragged(stream_key, count, total, bound, slope):
    if count == 2:
        one = jax.random.randint(stream_key, (), max(1, total - bound), min(bound, total - 1) + 1)
        return jnp.stack([one, total - one])
    tallies = jnp.asarray(profile(count, total, bound, slope), jnp.int32)
    pairs = (count - 1) // 2
    source_of, receiver = tallies[1:1 + 2 * pairs:2], tallies[2:2 + 2 * pairs:2]
    slack = jnp.minimum(source_of - 1, bound - receiver)
    moved = jax.random.randint(jax.random.fold_in(stream_key, 1), (pairs,), 0, 1 << 20) % (slack + 1)
    tallies = tallies.at[1:1 + 2 * pairs:2].set(source_of - moved).at[2:2 + 2 * pairs:2].set(receiver + moved)
    return tallies[jax.random.permutation(jax.random.fold_in(stream_key, 2), count)]


def bell_draw(stream_key, dims, spread, reach, shards=(), dtype=jnp.bfloat16):
    drawn = jax.random.normal(stream_key, dims, jnp.float32) * spread
    if len(shards) > 0:
        drawn = block_scale(stream_key, dims, shards, -0.22, 0.18) * drawn
    return jnp.clip(drawn, min=-reach, max=reach).astype(dtype)


def setup_inputs(seed: int = 0) -> dict:
    keys = jax.random.split(jax.random.key(seed), 14)
    tokens = bell_draw(keys[0], (TOKENS, D), 1.0, 6.0, ((0, 16),))
    segments = jax.vmap(lambda own: jnp.searchsorted(jnp.cumsum(ragged(own, 8, SEQ, SEQ // 2, 2)), jnp.arange(SEQ), side="right"))(jax.random.split(keys[1], SEQS)).reshape((SEQS, SEQ)).astype(jnp.int32)
    lengths = plant(jax.random.randint(keys[2], (SEQS,), SEQ // 2, SEQ + 1), jax.random.fold_in(keys[2], 1), SEQ // 2, SEQ).astype(jnp.int32)
    cotangent = bell_draw(keys[3], (TOKENS, D), 1.0, 6.0, ((0, 16),))
    qkv_weight = bell_draw(keys[4], (2, D, 3 * D), D ** -0.5, 0.21875, ((0, 2),))
    qv_bias = bell_draw(keys[5], (2, 2, D), 0.3, 2.0, ((0, 2),), jnp.float32)
    out_weight = bell_draw(keys[6], (2, D, D), (D // 16) ** -0.5, 0.875, ((0, 2),))
    out_biases = bell_draw(keys[7], (2, 2, D), 0.3, 2.0, ((0, 2),), jnp.float32)
    norm_gains = jnp.clip(1.0 + 0.1 * jax.random.normal(keys[8], (2, 2, D), jnp.float32), 0.5, 1.5)
    norm_shifts = bell_draw(keys[9], (2, 2, D), 0.3, 2.0, ((0, 2),), jnp.float32)
    up_weight = bell_draw(keys[10], (2, D, FF), D ** -0.5, 0.21875, ((0, 2),))
    up_bias = bell_draw(keys[11], (2, FF), 0.3, 2.0, ((0, 2),), jnp.float32)
    down_weight = bell_draw(keys[12], (2, FF, D), FF ** -0.5, 0.109375, ((0, 2),))
    return {"tokens": tokens, "segments": segments, "lengths": lengths, "cotangent": cotangent, "qkv_weight": qkv_weight, "qv_bias": qv_bias, "out_weight": out_weight, "out_biases": out_biases, "norm_gains": norm_gains, "norm_shifts": norm_shifts, "up_weight": up_weight, "up_bias": up_bias, "down_weight": down_weight}


@jax.custom_vjp
def low(v):
    return lax.optimization_barrier(v.astype(jnp.bfloat16)).astype(jnp.float32)

@jax.custom_vjp
def low_back(v):
    return v

def low_keep(v):
    return (low(v), None)

def low_pass(kept, grad):
    return (grad,)

def back_keep(v):
    return (v, None)

def back_low(kept, grad):
    return (low(grad),)
low.defvjp(low_keep, low_pass)
low_back.defvjp(back_keep, back_low)
EPSILON = 1e-05
SCORE_SCALE = 0.125
PRECISE = lax.Precision.HIGHEST

def matmul(left, right):
    return jnp.dot(left, right, preferred_element_type=jnp.float32, precision=PRECISE)

def layer_norm(resid, gain, shift):
    average = lax.optimization_barrier(jnp.mean(resid, axis=-1, keepdims=True))
    centred = resid - average
    variance = lax.optimization_barrier(jnp.mean(centred * centred, axis=-1, keepdims=True))
    return centred * lax.rsqrt(variance + EPSILON) * gain + shift

def attend(qkv_proj, seg_rows, len_rows):
    group_size, seq_len, _ = qkv_proj.shape
    split_heads = qkv_proj.reshape(group_size, seq_len, 3, H, HD)
    queries = split_heads[:, :, 0]
    keys_head = split_heads[:, :, 1]
    values = split_heads[:, :, 2]
    position = jnp.arange(seq_len)
    key_valid = position[None, :] < len_rows[:, None]
    same_doc = seg_rows[:, :, None] == seg_rows[:, None, :]
    diagonal = position[:, None] == position[None, :]
    allowed = same_doc & (key_valid[:, None, :] | diagonal[None])
    scores = low_back(jnp.einsum('gqhd,gkhd->ghqk', queries, keys_head, precision=PRECISE) * SCORE_SCALE)
    scores = jnp.where(allowed[:, None], scores, -1e+30)
    probs = jax.nn.softmax(scores, axis=-1)
    context = jnp.einsum('ghqk,gkhd->gqhd', low(probs), values, precision=PRECISE)
    return context.reshape(group_size * seq_len, D)

def layer(hidden, seg_rows, len_rows, weights):
    qkv_weight, qv_bias, out_weight, out_biases, gain_rows, shift_rows, up_weight, up_bias, down_weight = weights
    group_size, seq_len, _ = hidden.shape
    flat_rows = hidden.reshape(group_size * seq_len, D)
    bias_full = jnp.concatenate([qv_bias[0], jnp.zeros((D,), jnp.float32), qv_bias[1]])
    qkv_proj = low_back(low(matmul(flat_rows, qkv_weight) + bias_full))
    context = low_back(low(attend(qkv_proj.reshape(group_size, seq_len, 3 * D), seg_rows, len_rows)))
    attn_out = low_back(matmul(context, out_weight) + out_biases[0])
    normed = layer_norm(flat_rows + attn_out, gain_rows[0], shift_rows[0])
    up_pre = low_back(matmul(low(normed), up_weight) + up_bias)
    gelu_low = low(jax.nn.gelu(up_pre, approximate=False))
    down_out = low_back(matmul(gelu_low, down_weight) + out_biases[1])
    result = layer_norm(normed + down_out, gain_rows[1], shift_rows[1])
    return result.reshape(group_size, seq_len, D)

def two_layers(params, inputs, offset, seg_rows, len_rows):
    first_out = layer(inputs, seg_rows, len_rows, [weight[0] for weight in params])
    middle = low(first_out)
    second_in = low_back(middle + offset)
    return (middle, layer(second_in, seg_rows, len_rows, [weight[1] for weight in params]))

def reference(tokens, segments, lengths, cotangent, qkv_weight, qv_bias, out_weight, out_biases, norm_gains, norm_shifts, up_weight, up_bias, down_weight):
    seq_count = segments.shape[0]
    group_size = math.gcd(seq_count, max(1, 4096 // SEQ))
    blocks = seq_count // group_size
    params = tuple((weight.astype(jnp.float32) for weight in (qkv_weight, qv_bias, out_weight, out_biases, norm_gains, norm_shifts, up_weight, up_bias, down_weight)))
    inputs = tokens.astype(jnp.float32).reshape(blocks, group_size, SEQ, D)
    seg_blocks = segments.reshape(blocks, group_size, SEQ)
    len_blocks = lengths.reshape(blocks, group_size)
    offset = jnp.zeros_like(inputs)

    def whole(params, inputs, offset):

        def one_group(pieces):
            return two_layers(params, pieces[0], pieces[1], pieces[2], pieces[3])
        return lax.map(jax.checkpoint(one_group), (inputs, offset, seg_blocks, len_blocks))
    (middle, final_out), pullback = jax.vjp(whole, params, inputs, offset)
    upstream = cotangent.astype(jnp.float32).reshape(final_out.shape)
    grad_params, grad_inputs, grad_offset = pullback((jnp.zeros_like(middle), upstream))
    activations = jnp.stack([middle.reshape(-1, D), final_out.reshape(-1, D)]).astype(jnp.bfloat16)
    input_grads = jnp.stack([grad_inputs.reshape(-1, D), grad_offset.reshape(-1, D)]).astype(jnp.bfloat16)
    return (activations, input_grads, grad_params[0], grad_params[1], grad_params[2], grad_params[3], grad_params[4], grad_params[5], grad_params[6], grad_params[7], grad_params[8])
```

```python
import functools
import math

import jax
import jax.numpy as jnp
from jax import lax
from jax.experimental import pallas as pl
from jax.experimental.pallas import tpu as pltpu
from jax.sharding import PartitionSpec as P

D = 768
H = 12
HD = 64
FF = 3072
SEQ = 512
MICRO = 2
PAIRS = H // 2
PAIR = 2 * HD

EPSILON = 1e-05
SCORE_SCALE = 0.125
NEG_FILL = -1e30
F32 = jnp.float32
BF16 = jnp.bfloat16
VMEM_LIMIT = 60 << 20

ANY = pl.BlockSpec(memory_space=pl.ANY)
VMEM = pl.BlockSpec(memory_space=pltpu.VMEM)
SMEM = pl.BlockSpec(memory_space=pltpu.SMEM)


def dot_nn(left, right):
    return lax.dot_general(left, right, (((1,), (0,)), ((), ())), preferred_element_type=F32)


def dot_nt(left, right):
    return lax.dot_general(left, right, (((1,), (1,)), ((), ())), preferred_element_type=F32)


def dot_tn(left, right):
    return lax.dot_general(left, right, (((0,), (0,)), ((), ())), preferred_element_type=F32)


def begin(source, target, sem):
    copy = pltpu.make_async_copy(source, target, sem)
    copy.start()
    return copy


def gelu_and_slope(u):
    size = jnp.abs(u)
    bell = jnp.exp(-0.5 * (u * u))
    t = 1.0 / (1.0 + (0.3275911 / math.sqrt(2.0)) * size)
    poly = t * (
        0.5 * 0.254829592
        + t * (-0.5 * 0.284496736 + t * (0.5 * 1.421413741 + t * (-0.5 * 1.453152027 + t * (0.5 * 1.061405429))))
    )
    tail = poly * bell
    cdf = jnp.where(u < 0.0, tail, 1.0 - tail)
    return u * cdf, cdf + u * bell * (1.0 / math.sqrt(2.0 * math.pi))


def normalize(resid):
    average = jnp.mean(resid, axis=-1, keepdims=True)
    centred = resid - average
    variance = jnp.mean(centred * centred, axis=-1, keepdims=True)
    inverse = lax.rsqrt(variance + EPSILON)
    return centred * inverse, inverse


def norm_back(grad_out, scaled, inverse, gain):
    weighted = grad_out * gain
    first_mean = jnp.mean(weighted, axis=-1, keepdims=True)
    second_mean = jnp.mean(weighted * scaled, axis=-1, keepdims=True)
    return inverse * (weighted - first_mean - scaled * second_mean)


def half_mask(which):
    lane = lax.broadcasted_iota(jnp.int32, (1, PAIR), 1)
    return ((lane // HD) == which).astype(F32).astype(BF16)


SAVED = (
    ("act", D, BF16),
    ("qkv", 3 * D, BF16),
    ("ctx", D, BF16),
    ("xh1", D, BF16),
    ("inv1", 128, F32),
    ("low", D, BF16),
    ("gelu", FF, BF16),
    ("slope", FF, BF16),
    ("xh2", D, BF16),
    ("inv2", 128, F32),
)


def forward_kernel(step, n_alias, *refs):
    (tok, rec, wqkv, wo, wu, wd, segs, lens, qv_bias, out_biases, gains, shifts, up_bias) = refs[:13]
    outs = refs[13 + n_alias : 13 + n_alias + 13]
    y_hop, hid_out, prob_out = outs[:3]
    saved_out = dict(zip([name for name, _, _ in SAVED], outs[3:]))
    (
        h_v, wqkv_v, wo_v, wu_v, wd_v, bias_v, p_v, acc_v,
        act_v, qkv_v, ctx_v, xh1_v, inv1_v, low_v, gelu_v, slope_v, xh2_v, inv2_v,
        in_sem, w_sem, p_sem, out_sem,
    ) = refs[13 + n_alias + 13 :]
    section = lax.axis_index("section")
    mb = step - section

    @pl.when((mb >= 0) & (mb < MICRO))
    def _():
        rows = pl.ds(pl.multiple_of(mb * SEQ, SEQ), SEQ)

        @pl.when(section == 0)
        def _():
            begin(tok.at[rows], h_v, in_sem.at[0])

        @pl.when(section != 0)
        def _():
            begin(rec, h_v, in_sem.at[0])

        w_copies = [
            begin(wqkv.at[0], wqkv_v, w_sem.at[0]),
            begin(wo.at[0], wo_v, w_sem.at[1]),
            begin(wu.at[0], wu_v, w_sem.at[2]),
            begin(wd.at[0], wd_v, w_sem.at[3]),
        ]
        seg_row = segs[pl.ds(mb, 1), :]
        seg_col = jnp.transpose(jnp.broadcast_to(seg_row.astype(F32), (128, SEQ)))
        length = lens[mb]
        query = lax.broadcasted_iota(jnp.int32, (SEQ, 128), 0)
        for tile in range(SEQ // 128):
            key = lax.broadcasted_iota(jnp.int32, (SEQ, 128), 1) + tile * 128
            same = seg_col == seg_row[:, tile * 128 : (tile + 1) * 128].astype(F32)
            allowed = same & ((key < length) | (key == query))
            bias_v[:, tile * 128 : (tile + 1) * 128] = jnp.where(allowed, 0.0, NEG_FILL)

        pending = []

        def save(name, value_ref):
            pending.append(begin(value_ref, saved_out[name].at[rows], out_sem.at[len(pending)]))

        pltpu.make_async_copy(rec, h_v, in_sem.at[0]).wait()
        pending.append(begin(h_v, hid_out.at[rows], out_sem.at[0]))
        w_copies[0].wait()
        for block in range(3):
            cols = slice(block * D, (block + 1) * D)
            proj = dot_nn(h_v[...], wqkv_v[:, cols])
            if block != 1:
                proj = proj + qv_bias[0, block // 2 : block // 2 + 1, :]
            qkv_v[:, cols] = proj.astype(BF16)
        save("qkv", qkv_v)

        def pair_step(pair, carry):
            slot = lax.rem(pair, 2)

            @pl.when(pair >= 2)
            def _():
                pltpu.make_async_copy(p_v.at[slot], prob_out.at[mb, pl.ds(0, 2)], p_sem.at[slot]).wait()

            at = pl.multiple_of(pair * PAIR, PAIR)
            q2 = qkv_v[:, pl.ds(at, PAIR)] * SCORE_SCALE
            k2 = qkv_v[:, pl.ds(at + D, PAIR)]
            v2 = qkv_v[:, pl.ds(at + 2 * D, PAIR)]
            total = None
            for head in range(2):
                mask = half_mask(head)
                scores = dot_nt(q2, k2 * mask) + bias_v[...]
                exp_vals = jnp.exp(scores - jnp.max(scores, axis=-1, keepdims=True))
                inverse_total = 1.0 / jnp.sum(exp_vals, axis=-1, keepdims=True)
                prob = (exp_vals * inverse_total).astype(BF16)
                p_v[slot, head] = prob
                part = dot_nn(prob, v2 * mask)
                total = part if total is None else total + part
            ctx_v[:, pl.ds(at, PAIR)] = total.astype(BF16)
            begin(p_v.at[slot], prob_out.at[mb, pl.ds(pair * 2, 2)], p_sem.at[slot])
            return carry

        lax.fori_loop(0, PAIRS, pair_step, 0)
        save("ctx", ctx_v)

        w_copies[1].wait()
        resid = h_v[...].astype(F32) + (dot_nn(ctx_v[...], wo_v[...]) + out_biases[0, 0:1, :])
        scaled, inverse = normalize(resid)
        xh1_v[...] = scaled.astype(BF16)
        inv1_v[...] = jnp.broadcast_to(inverse, (SEQ, 128))
        normed = scaled * gains[0, 0:1, :] + shifts[0, 0:1, :]
        low_v[...] = normed.astype(BF16)
        acc_v[...] = normed + out_biases[0, 1:2, :]
        save("xh1", xh1_v)
        save("inv1", inv1_v)
        save("low", low_v)
        w_copies[2].wait()
        w_copies[3].wait()
        width = 512
        for chunk in range(FF // width):
            cols = slice(chunk * width, (chunk + 1) * width)
            up = dot_nn(low_v[...], wu_v[:, cols]) + up_bias[0:1, cols]
            gelu, slope = gelu_and_slope(up)
            gelu = gelu.astype(BF16)
            gelu_v[:, cols] = gelu
            slope_v[:, cols] = slope.astype(BF16)
            acc_v[...] += dot_nn(gelu, wd_v[cols, :])
        save("gelu", gelu_v)
        save("slope", slope_v)
        scaled, inverse = normalize(acc_v[...])
        xh2_v[...] = scaled.astype(BF16)
        inv2_v[...] = jnp.broadcast_to(inverse, (SEQ, 128))
        act_v[...] = (scaled * gains[0, 1:2, :] + shifts[0, 1:2, :]).astype(BF16)
        pending.append(begin(act_v, y_hop, out_sem.at[len(pending)]))
        save("act", act_v)
        save("xh2", xh2_v)
        save("inv2", inv2_v)
        for slot in range(2):
            pltpu.make_async_copy(p_v.at[slot], prob_out.at[mb, pl.ds(0, 2)], p_sem.at[slot]).wait()
        for copy in pending:
            copy.wait()


def forward(step, tokens, received, weights, segments, lengths, params, saved):
    total = MICRO * SEQ
    shapes = [
        jax.ShapeDtypeStruct((SEQ, D), BF16),
        jax.ShapeDtypeStruct((total, D), BF16),
        jax.ShapeDtypeStruct((MICRO, H, SEQ, SEQ), BF16),
    ] + [jax.ShapeDtypeStruct((total, width), dtype) for _, width, dtype in SAVED]
    n_alias = len(saved)
    ins = [tokens, received, *weights, segments, lengths, *params, *saved]
    result = pl.pallas_call(
        functools.partial(forward_kernel, step, n_alias),
        out_shape=shapes,
        in_specs=[ANY] * 6 + [VMEM, SMEM] + [VMEM] * 5 + [ANY] * n_alias,
        out_specs=[ANY] * len(shapes),
        input_output_aliases={13 + i: 1 + i for i in range(n_alias)},
        scratch_shapes=[
            pltpu.VMEM((SEQ, D), BF16),
            pltpu.VMEM((D, 3 * D), BF16),
            pltpu.VMEM((D, D), BF16),
            pltpu.VMEM((D, FF), BF16),
            pltpu.VMEM((FF, D), BF16),
            pltpu.VMEM((SEQ, SEQ), F32),
            pltpu.VMEM((2, 2, SEQ, SEQ), BF16),
            pltpu.VMEM((SEQ, D), F32),
        ]
        + [pltpu.VMEM((SEQ, width), dtype) for _, width, dtype in SAVED]
        + [
            pltpu.SemaphoreType.DMA((1,)),
            pltpu.SemaphoreType.DMA((4,)),
            pltpu.SemaphoreType.DMA((2,)),
            pltpu.SemaphoreType.DMA((16,)),
        ],
        compiler_params=pltpu.CompilerParams(vmem_limit_bytes=VMEM_LIMIT),
        name="forward",
    )(*ins)
    return result[0], list(result[1:])


GRADS = (("d_down", D, BF16), ("d_up", FF, BF16), ("d_attn", D, BF16), ("d_qkv", 3 * D, BF16), ("d_hid", D, BF16))
SMALL_ROWS = 16


def backward_kernel(step, n_alias, *refs):
    (cot, rec, wqkv, wo, wu, wd, gains, prob_in) = refs[:8]
    saved_in = dict(zip([name for name, _, _ in SAVED], refs[8:18]))
    outs = refs[18 + n_alias : 18 + n_alias + 7]
    d_hop, small_out = outs[:2]
    grads_out = dict(zip([name for name, _, _ in GRADS], outs[2:]))
    (
        g_v, wqkv_v, wo_v, wu_v, wd_v, p_v, acc_v, acc2_v, small_v,
        qkv_v, ctx_v, xh1_v, inv1_v, slope_v, xh2_v, inv2_v, d_ctx_v,
        d_down_v, d_up_v, d_attn_v, d_qkv_v, d_hid_v,
        in_sem, w_sem, p_sem, out_sem,
    ) = refs[18 + n_alias + 7 :]
    section = lax.axis_index("section")
    mb = step - (1 - section)

    @pl.when((mb >= 0) & (mb < MICRO))
    def _():
        rows = pl.ds(pl.multiple_of(mb * SEQ, SEQ), SEQ)

        @pl.when(section == 0)
        def _():
            begin(rec, g_v, in_sem.at[0])

        @pl.when(section != 0)
        def _():
            begin(cot.at[rows], g_v, in_sem.at[0])

        def fetch(name, target, index):
            return begin(saved_in[name].at[rows], target, in_sem.at[index])

        get_xh2 = fetch("xh2", xh2_v, 1)
        get_inv2 = fetch("inv2", inv2_v, 2)
        get_wd = begin(wd.at[0], wd_v, w_sem.at[3])
        get_slope = fetch("slope", slope_v, 3)
        get_wu = begin(wu.at[0], wu_v, w_sem.at[2])
        get_xh1 = fetch("xh1", xh1_v, 4)
        get_inv1 = fetch("inv1", inv1_v, 5)
        get_wo = begin(wo.at[0], wo_v, w_sem.at[1])
        get_qkv = fetch("qkv", qkv_v, 6)
        get_ctx = fetch("ctx", ctx_v, 7)
        begin(prob_in.at[mb, pl.ds(0, 2)], p_v.at[0], p_sem.at[0])
        get_wqkv = begin(wqkv.at[0], wqkv_v, w_sem.at[0])

        pending = []

        def save(name, value_ref):
            pending.append(begin(value_ref, grads_out[name].at[rows], out_sem.at[len(pending)]))

        def column_sum(value):
            return jnp.sum(value, axis=0, keepdims=True)

        small_v[...] = jnp.zeros_like(small_v)
        pltpu.make_async_copy(rec, g_v, in_sem.at[0]).wait()
        get_xh2.wait()
        get_inv2.wait()
        grad = g_v[...].astype(F32)
        scaled = xh2_v[...].astype(F32)
        small_v[5:6, :] = column_sum(grad * scaled)
        small_v[7:8, :] = column_sum(grad)
        d_r2 = norm_back(grad, scaled, inv2_v[:, 0:1], gains[0, 1:2, :])
        d_down = d_r2.astype(BF16)
        d_down_v[...] = d_down
        small_v[3:4, :] = column_sum(d_down.astype(F32))
        acc_v[...] = d_r2
        save("d_down", d_down_v)
        get_wd.wait()
        get_slope.wait()
        get_wu.wait()
        width = 512
        for chunk in range(FF // width):
            cols = slice(chunk * width, (chunk + 1) * width)
            d_up = (dot_nt(d_down_v[...], wd_v[cols, :]) * slope_v[:, cols].astype(F32)).astype(BF16)
            d_up_v[:, cols] = d_up
            at = chunk * width
            sums = column_sum(d_up.astype(F32))
            while at < (chunk + 1) * width:
                row = at // D
                stop = min((row + 1) * D, (chunk + 1) * width)
                small_v[8 + row : 9 + row, at - row * D : stop - row * D] = sums[
                    :, at - chunk * width : stop - chunk * width
                ]
                at = stop
            acc_v[...] += dot_nt(d_up, wu_v[:, cols])
        save("d_up", d_up_v)
        get_xh1.wait()
        get_inv1.wait()
        d_normed = acc_v[...]
        scaled = xh1_v[...].astype(F32)
        small_v[4:5, :] = column_sum(d_normed * scaled)
        small_v[6:7, :] = column_sum(d_normed)
        d_r1 = norm_back(d_normed, scaled, inv1_v[:, 0:1], gains[0, 0:1, :])
        d_attn = d_r1.astype(BF16)
        d_attn_v[...] = d_attn
        small_v[2:3, :] = column_sum(d_attn.astype(F32))
        acc_v[...] = d_r1
        save("d_attn", d_attn_v)
        get_wo.wait()
        d_ctx_v[...] = dot_nt(d_attn, wo_v[...]).astype(BF16)
        get_qkv.wait()
        get_ctx.wait()

        def pair_step(pair, carry):
            slot = lax.rem(pair, 2)

            @pl.when(pair + 1 < PAIRS)
            def _():
                begin(prob_in.at[mb, pl.ds((pair + 1) * 2, 2)], p_v.at[1 - slot], p_sem.at[1 - slot])

            pltpu.make_async_copy(prob_in.at[mb, pl.ds(0, 2)], p_v.at[slot], p_sem.at[slot]).wait()
            at = pl.multiple_of(pair * PAIR, PAIR)
            q2 = qkv_v[:, pl.ds(at, PAIR)] * SCORE_SCALE
            k2 = qkv_v[:, pl.ds(at + D, PAIR)]
            v2 = qkv_v[:, pl.ds(at + 2 * D, PAIR)]
            dc2 = d_ctx_v[:, pl.ds(at, PAIR)]
            inner = dc2.astype(F32) * ctx_v[:, pl.ds(at, PAIR)].astype(F32)
            d_q, d_k, d_v = None, None, None
            for head in range(2):
                mask = half_mask(head)
                k_own, q_own, dc_own = k2 * mask, q2 * mask, dc2 * mask
                prob = p_v[slot, head]
                row_inner = jnp.sum(inner * mask.astype(F32), axis=-1, keepdims=True)
                d_prob = dot_nt(dc_own, v2)
                d_score = (prob.astype(F32) * (d_prob - row_inner)).astype(BF16)
                part_v = dot_tn(dc_own, prob)
                part_q = dot_nn(d_score, k_own)
                part_k = dot_tn(q_own, d_score)
                d_v = part_v if d_v is None else d_v + part_v
                d_q = part_q if d_q is None else d_q + part_q
                d_k = part_k if d_k is None else d_k + part_k
            d_qkv_v[:, pl.ds(at, PAIR)] = (d_q * SCORE_SCALE).astype(BF16)
            d_qkv_v[:, pl.ds(at + D, PAIR)] = jnp.transpose(d_k).astype(BF16)
            d_qkv_v[:, pl.ds(at + 2 * D, PAIR)] = jnp.transpose(d_v).astype(BF16)
            return carry

        lax.fori_loop(0, PAIRS, pair_step, 0)
        save("d_qkv", d_qkv_v)
        get_wqkv.wait()
        small_v[0:1, :] = column_sum(d_qkv_v[:, 0:D].astype(F32))
        small_v[1:2, :] = column_sum(d_qkv_v[:, 2 * D : 3 * D].astype(F32))
        d_hid_v[...] = (acc_v[...] + dot_nt(d_qkv_v[...], wqkv_v[...])).astype(BF16)
        pending.append(begin(d_hid_v, d_hop, out_sem.at[len(pending)]))
        save("d_hid", d_hid_v)
        pending.append(begin(small_v, small_out.at[mb], out_sem.at[len(pending)]))
        for copy in pending:
            copy.wait()


def backward(step, cotangent, received, weights, gains, prob, saved, grads):
    total = MICRO * SEQ
    shapes = [
        jax.ShapeDtypeStruct((SEQ, D), BF16),
        jax.ShapeDtypeStruct((MICRO, SMALL_ROWS, D), F32),
    ] + [jax.ShapeDtypeStruct((total, width), dtype) for _, width, dtype in GRADS]
    n_alias = len(grads)
    ins = [cotangent, received, *weights, gains, prob, *saved, *grads]
    widths = {name: (width, dtype) for name, width, dtype in SAVED}
    kept = ("qkv", "ctx", "xh1", "inv1", "slope", "xh2", "inv2")
    result = pl.pallas_call(
        functools.partial(backward_kernel, step, n_alias),
        out_shape=shapes,
        in_specs=[ANY] * 6 + [VMEM] + [ANY] * (11 + n_alias),
        out_specs=[ANY] * len(shapes),
        input_output_aliases={18 + i: 1 + i for i in range(n_alias)},
        scratch_shapes=[
            pltpu.VMEM((SEQ, D), BF16),
            pltpu.VMEM((D, 3 * D), BF16),
            pltpu.VMEM((D, D), BF16),
            pltpu.VMEM((D, FF), BF16),
            pltpu.VMEM((FF, D), BF16),
            pltpu.VMEM((2, 2, SEQ, SEQ), BF16),
            pltpu.VMEM((SEQ, D), F32),
            pltpu.VMEM((8, 128), F32),
            pltpu.VMEM((SMALL_ROWS, D), F32),
        ]
        + [pltpu.VMEM((SEQ, widths[name][0]), widths[name][1]) for name in kept]
        + [pltpu.VMEM((SEQ, D), BF16)]
        + [pltpu.VMEM((SEQ, width), dtype) for _, width, dtype in GRADS]
        + [
            pltpu.SemaphoreType.DMA((8,)),
            pltpu.SemaphoreType.DMA((4,)),
            pltpu.SemaphoreType.DMA((2,)),
            pltpu.SemaphoreType.DMA((8,)),
        ],
        compiler_params=pltpu.CompilerParams(vmem_limit_bytes=VMEM_LIMIT),
        name="backward",
    )(*ins)
    return result[0], list(result[1:])


def reduced(value, dim):
    share = lax.psum_scatter(value.astype(BF16), "dp", scatter_dimension=dim, tiled=True)
    return lax.all_gather(share, "dp", axis=dim, tiled=True).astype(F32)[None]


def shards(
    tokens, segments, lengths, cotangent, qkv_weight, qv_bias, out_weight, out_biases,
    norm_gains, norm_shifts, up_weight, up_bias, down_weight,
):
    weights = (qkv_weight, out_weight, up_weight, down_weight)
    params = (qv_bias, out_biases, norm_gains, norm_shifts, up_bias)
    onward = [(0, 1)]
    back = [(1, 0)]
    received = tokens[:SEQ]
    state = []
    for step in range(MICRO + 1):
        hop, state = forward(step, tokens, received, weights, segments, lengths, params, state)
        if step < MICRO:
            received = lax.ppermute(hop, "section", onward)
    hid, prob = state[:2]
    saved = state[2:]
    act = saved[0]
    received = cotangent[:SEQ]
    grads = []
    for step in range(MICRO + 1):
        hop, grads = backward(step, cotangent, received, weights, norm_gains, prob, saved, grads)
        if step < MICRO:
            received = lax.ppermute(hop, "section", back)
    small = jnp.sum(grads[0], axis=0)
    d_down, d_up, d_attn, d_qkv, d_hid = grads[1:]
    names = {name: index for index, (name, _, _) in enumerate(SAVED)}
    g_down = reduced(dot_tn(saved[names["gelu"]], d_down), 0)
    g_up = reduced(dot_tn(saved[names["low"]], d_up), 0)
    g_out = reduced(dot_tn(saved[names["ctx"]], d_attn), 0)
    g_qkv = reduced(dot_tn(hid, d_qkv), 0)
    small = lax.psum(small, "dp")[None]
    return (
        act[None], d_hid[None], g_qkv, small[:, 0:2], g_out, small[:, 2:4], small[:, 4:6], small[:, 6:8],
        g_up, small[:, 8:12].reshape(1, FF), g_down,
    )


def solution(mesh):
    return jax.shard_map(
        shards,
        mesh=mesh,
        in_specs=(
            P("dp", None), P("dp", None), P("dp"), P("dp", None),
            P("section", None, None), P("section", None, None), P("section", None, None), P("section", None, None),
            P("section", None, None), P("section", None, None), P("section", None, None), P("section", None),
            P("section", None, None),
        ),
        out_specs=(
            P("section", "dp", None), P("section", "dp", None),
            P("section", None, None), P("section", None, None), P("section", None, None), P("section", None, None),
            P("section", None, None), P("section", None, None), P("section", None, None), P("section", None),
            P("section", None, None),
        ),
        check_vma=False,
    )
```

```python
import functools
import math

import jax
import jax.numpy as jnp
from jax import lax
from jax.experimental import pallas as pl
from jax.experimental.pallas import tpu as pltpu
from jax.sharding import PartitionSpec as P

D = 768
H = 12
HD = 64
FF = 3072
SEQ = 512
MICRO = 2
PAIRS = H // 2
PAIR = 2 * HD

EPSILON = 1e-05
SCORE_SCALE = 0.125
NEG_FILL = -1e30
F32 = jnp.float32
BF16 = jnp.bfloat16
VMEM_LIMIT = 60 << 20

ANY = pl.BlockSpec(memory_space=pl.ANY)
VMEM = pl.BlockSpec(memory_space=pltpu.VMEM)
SMEM = pl.BlockSpec(memory_space=pltpu.SMEM)


def dot_nn(left, right):
    return lax.dot_general(left, right, (((1,), (0,)), ((), ())), preferred_element_type=F32)


def dot_nt(left, right):
    return lax.dot_general(left, right, (((1,), (1,)), ((), ())), preferred_element_type=F32)


def dot_tn(left, right):
    return lax.dot_general(left, right, (((0,), (0,)), ((), ())), preferred_element_type=F32)


def begin(source, target, sem):
    copy = pltpu.make_async_copy(source, target, sem)
    copy.start()
    return copy


def gelu_and_slope(u):
    size = jnp.abs(u)
    bell = jnp.exp(-0.5 * (u * u))
    t = 1.0 / (1.0 + (0.3275911 / math.sqrt(2.0)) * size)
    poly = t * (
        0.5 * 0.254829592
        + t * (-0.5 * 0.284496736 + t * (0.5 * 1.421413741 + t * (-0.5 * 1.453152027 + t * (0.5 * 1.061405429))))
    )
    tail = poly * bell
    cdf = jnp.where(u < 0.0, tail, 1.0 - tail)
    return u * cdf, cdf + u * bell * (1.0 / math.sqrt(2.0 * math.pi))


def normalize(resid):
    average = jnp.mean(resid, axis=-1, keepdims=True)
    centred = resid - average
    variance = jnp.mean(centred * centred, axis=-1, keepdims=True)
    inverse = lax.rsqrt(variance + EPSILON)
    return centred * inverse, inverse


def norm_back(grad_out, scaled, inverse, gain):
    weighted = grad_out * gain
    first_mean = jnp.mean(weighted, axis=-1, keepdims=True)
    second_mean = jnp.mean(weighted * scaled, axis=-1, keepdims=True)
    return inverse * (weighted - first_mean - scaled * second_mean)


def half_mask(which):
    lane = lax.broadcasted_iota(jnp.int32, (1, PAIR), 1)
    return ((lane // HD) == which).astype(F32).astype(BF16)


SAVED = (
    ("act", D, BF16),
    ("qkv", 3 * D, BF16),
    ("ctx", D, BF16),
    ("xh1", D, BF16),
    ("inv1", 128, F32),
    ("low", D, BF16),
    ("gelu", FF, BF16),
    ("slope", FF, BF16),
    ("xh2", D, BF16),
    ("inv2", 128, F32),
)


def forward_kernel(step, n_alias, *refs):
    (tok, rec, wqkv, wo, wu, wd, segs, lens, qv_bias, out_biases, gains, shifts, up_bias) = refs[:13]
    outs = refs[13 + n_alias : 13 + n_alias + 13]
    y_hop, hid_out, prob_out = outs[:3]
    saved_out = dict(zip([name for name, _, _ in SAVED], outs[3:]))
    (
        h_v, wqkv_v, wo_v, wu_v, wd_v, bias_v, p_v, acc_v,
        act_v, qkv_v, ctx_v, xh1_v, inv1_v, low_v, gelu_v, slope_v, xh2_v, inv2_v,
        in_sem, w_sem, p_sem, out_sem,
    ) = refs[13 + n_alias + 13 :]
    section = lax.axis_index("section")
    mb = step - section

    @pl.when((mb >= 0) & (mb < MICRO))
    def _():
        rows = pl.ds(pl.multiple_of(mb * SEQ, SEQ), SEQ)

        @pl.when(section == 0)
        def _():
            begin(tok.at[rows], h_v, in_sem.at[0])

        @pl.when(section != 0)
        def _():
            begin(rec, h_v, in_sem.at[0])

        w_copies = [
            begin(wqkv.at[0], wqkv_v, w_sem.at[0]),
            begin(wo.at[0], wo_v, w_sem.at[1]),
            begin(wu.at[0], wu_v, w_sem.at[2]),
            begin(wd.at[0], wd_v, w_sem.at[3]),
        ]
        seg_row = segs[pl.ds(mb, 1), :]
        seg_col = jnp.transpose(jnp.broadcast_to(seg_row.astype(F32), (128, SEQ)))
        length = lens[mb]
        query = lax.broadcasted_iota(jnp.int32, (SEQ, 128), 0)
        for tile in range(SEQ // 128):
            key = lax.broadcasted_iota(jnp.int32, (SEQ, 128), 1) + tile * 128
            same = seg_col == seg_row[:, tile * 128 : (tile + 1) * 128].astype(F32)
            allowed = same & ((key < length) | (key == query))
            bias_v[:, tile * 128 : (tile + 1) * 128] = jnp.where(allowed, 0.0, NEG_FILL)

        pending = []

        def save(name, value_ref):
            pending.append(begin(value_ref, saved_out[name].at[rows], out_sem.at[len(pending)]))

        pltpu.make_async_copy(rec, h_v, in_sem.at[0]).wait()
        pending.append(begin(h_v, hid_out.at[rows], out_sem.at[0]))
        w_copies[0].wait()
        for block in range(3):
            cols = slice(block * D, (block + 1) * D)
            proj = dot_nn(h_v[...], wqkv_v[:, cols])
            if block != 1:
                proj = proj + qv_bias[0, block // 2 : block // 2 + 1, :]
            qkv_v[:, cols] = proj.astype(BF16)
        save("qkv", qkv_v)

        def pair_step(pair, carry):
            slot = lax.rem(pair, 2)

            @pl.when(pair >= 2)
            def _():
                pltpu.make_async_copy(p_v.at[slot], prob_out.at[mb, pl.ds(0, 2)], p_sem.at[slot]).wait()

            at = pl.multiple_of(pair * PAIR, PAIR)
            q2 = qkv_v[:, pl.ds(at, PAIR)] * SCORE_SCALE
            k2 = qkv_v[:, pl.ds(at + D, PAIR)]
            v2 = qkv_v[:, pl.ds(at + 2 * D, PAIR)]
            total = None
            for head in range(2):
                mask = half_mask(head)
                scores = dot_nt(q2, k2 * mask) + bias_v[...]
                exp_vals = jnp.exp(scores - jnp.max(scores, axis=-1, keepdims=True))
                inverse_total = 1.0 / jnp.sum(exp_vals, axis=-1, keepdims=True)
                prob = (exp_vals * inverse_total).astype(BF16)
                p_v[slot, head] = prob
                part = dot_nn(prob, v2 * mask)
                total = part if total is None else total + part
            ctx_v[:, pl.ds(at, PAIR)] = total.astype(BF16)
            begin(p_v.at[slot], prob_out.at[mb, pl.ds(pair * 2, 2)], p_sem.at[slot])
            return carry

        lax.fori_loop(0, PAIRS, pair_step, 0)
        save("ctx", ctx_v)

        w_copies[1].wait()
        resid = h_v[...].astype(F32) + (dot_nn(ctx_v[...], wo_v[...]) + out_biases[0, 0:1, :])
        scaled, inverse = normalize(resid)
        xh1_v[...] = scaled.astype(BF16)
        inv1_v[...] = jnp.broadcast_to(inverse, (SEQ, 128))
        normed = scaled * gains[0, 0:1, :] + shifts[0, 0:1, :]
        low_v[...] = normed.astype(BF16)
        acc_v[...] = normed + out_biases[0, 1:2, :]
        save("xh1", xh1_v)
        save("inv1", inv1_v)
        save("low", low_v)
        w_copies[2].wait()
        w_copies[3].wait()
        width = 512
        for chunk in range(FF // width):
            cols = slice(chunk * width, (chunk + 1) * width)
            up = dot_nn(low_v[...], wu_v[:, cols]) + up_bias[0:1, cols]
            gelu, slope = gelu_and_slope(up)
            gelu = gelu.astype(BF16)
            gelu_v[:, cols] = gelu
            slope_v[:, cols] = slope.astype(BF16)
            acc_v[...] += dot_nn(gelu, wd_v[cols, :])
        save("gelu", gelu_v)
        save("slope", slope_v)
        scaled, inverse = normalize(acc_v[...])
        xh2_v[...] = scaled.astype(BF16)
        inv2_v[...] = jnp.broadcast_to(inverse, (SEQ, 128))
        act_v[...] = (scaled * gains[0, 1:2, :] + shifts[0, 1:2, :]).astype(BF16)
        pending.append(begin(act_v, y_hop, out_sem.at[len(pending)]))
        save("act", act_v)
        save("xh2", xh2_v)
        save("inv2", inv2_v)
        for slot in range(2):
            pltpu.make_async_copy(p_v.at[slot], prob_out.at[mb, pl.ds(0, 2)], p_sem.at[slot]).wait()
        for copy in pending:
            copy.wait()


def forward(step, tokens, received, weights, segments, lengths, params, saved):
    total = MICRO * SEQ
    shapes = [
        jax.ShapeDtypeStruct((SEQ, D), BF16),
        jax.ShapeDtypeStruct((total, D), BF16),
        jax.ShapeDtypeStruct((MICRO, H, SEQ, SEQ), BF16),
    ] + [jax.ShapeDtypeStruct((total, width), dtype) for _, width, dtype in SAVED]
    n_alias = len(saved)
    ins = [tokens, received, *weights, segments, lengths, *params, *saved]
    result = pl.pallas_call(
        functools.partial(forward_kernel, step, n_alias),
        out_shape=shapes,
        in_specs=[ANY] * 6 + [VMEM, SMEM] + [VMEM] * 5 + [ANY] * n_alias,
        out_specs=[ANY] * len(shapes),
        input_output_aliases={13 + i: 1 + i for i in range(n_alias)},
        scratch_shapes=[
            pltpu.VMEM((SEQ, D), BF16),
            pltpu.VMEM((D, 3 * D), BF16),
            pltpu.VMEM((D, D), BF16),
            pltpu.VMEM((D, FF), BF16),
            pltpu.VMEM((FF, D), BF16),
            pltpu.VMEM((SEQ, SEQ), F32),
            pltpu.VMEM((2, 2, SEQ, SEQ), BF16),
            pltpu.VMEM((SEQ, D), F32),
        ]
        + [pltpu.VMEM((SEQ, width), dtype) for _, width, dtype in SAVED]
        + [
            pltpu.SemaphoreType.DMA((1,)),
            pltpu.SemaphoreType.DMA((4,)),
            pltpu.SemaphoreType.DMA((2,)),
            pltpu.SemaphoreType.DMA((16,)),
        ],
        compiler_params=pltpu.CompilerParams(vmem_limit_bytes=VMEM_LIMIT),
        name="forward",
    )(*ins)
    return result[0], list(result[1:])


GRADS = (("d_down", D, BF16), ("d_up", FF, BF16), ("d_attn", D, BF16), ("d_qkv", 3 * D, BF16), ("d_hid", D, BF16))
SMALL_ROWS = 16


def backward_kernel(step, n_alias, *refs):
    (cot, rec, wqkv, wo, wu, wd, gains, prob_in) = refs[:8]
    saved_in = dict(zip([name for name, _, _ in SAVED], refs[8:18]))
    outs = refs[18 + n_alias : 18 + n_alias + 7]
    d_hop, small_out = outs[:2]
    grads_out = dict(zip([name for name, _, _ in GRADS], outs[2:]))
    (
        g_v, wqkv_v, wo_v, wu_v, wd_v, p_v, acc_v, acc2_v, small_v,
        qkv_v, ctx_v, xh1_v, inv1_v, slope_v, xh2_v, inv2_v, d_ctx_v,
        d_down_v, d_up_v, d_attn_v, d_qkv_v, d_hid_v,
        in_sem, w_sem, p_sem, out_sem,
    ) = refs[18 + n_alias + 7 :]
    section = lax.axis_index("section")
    mb = step - (1 - section)

    @pl.when((mb >= 0) & (mb < MICRO))
    def _():
        rows = pl.ds(pl.multiple_of(mb * SEQ, SEQ), SEQ)

        @pl.when(section == 0)
        def _():
            begin(rec, g_v, in_sem.at[0])

        @pl.when(section != 0)
        def _():
            begin(cot.at[rows], g_v, in_sem.at[0])

        def fetch(name, target, index):
            return begin(saved_in[name].at[rows], target, in_sem.at[index])

        get_xh2 = fetch("xh2", xh2_v, 1)
        get_inv2 = fetch("inv2", inv2_v, 2)
        get_wd = begin(wd.at[0], wd_v, w_sem.at[3])
        get_slope = fetch("slope", slope_v, 3)
        get_wu = begin(wu.at[0], wu_v, w_sem.at[2])
        get_xh1 = fetch("xh1", xh1_v, 4)
        get_inv1 = fetch("inv1", inv1_v, 5)
        get_wo = begin(wo.at[0], wo_v, w_sem.at[1])
        get_qkv = fetch("qkv", qkv_v, 6)
        get_ctx = fetch("ctx", ctx_v, 7)
        begin(prob_in.at[mb, pl.ds(0, 2)], p_v.at[0], p_sem.at[0])
        get_wqkv = begin(wqkv.at[0], wqkv_v, w_sem.at[0])

        pending = []

        def save(name, value_ref):
            pending.append(begin(value_ref, grads_out[name].at[rows], out_sem.at[len(pending)]))

        def column_sum(value):
            return jnp.sum(value, axis=0, keepdims=True)

        small_v[...] = jnp.zeros_like(small_v)
        pltpu.make_async_copy(rec, g_v, in_sem.at[0]).wait()
        get_xh2.wait()
        get_inv2.wait()
        grad = g_v[...].astype(F32)
        scaled = xh2_v[...].astype(F32)
        small_v[5:6, :] = column_sum(grad * scaled)
        small_v[7:8, :] = column_sum(grad)
        d_r2 = norm_back(grad, scaled, inv2_v[:, 0:1], gains[0, 1:2, :])
        d_down = d_r2.astype(BF16)
        d_down_v[...] = d_down
        small_v[3:4, :] = column_sum(d_down.astype(F32))
        acc_v[...] = d_r2
        save("d_down", d_down_v)
        get_wd.wait()
        get_slope.wait()
        get_wu.wait()
        width = 512
        for chunk in range(FF // width):
            cols = slice(chunk * width, (chunk + 1) * width)
            d_up = (dot_nt(d_down_v[...], wd_v[cols, :]) * slope_v[:, cols].astype(F32)).astype(BF16)
            d_up_v[:, cols] = d_up
            at = chunk * width
            sums = column_sum(d_up.astype(F32))
            while at < (chunk + 1) * width:
                row = at // D
                stop = min((row + 1) * D, (chunk + 1) * width)
                small_v[8 + row : 9 + row, at - row * D : stop - row * D] = sums[
                    :, at - chunk * width : stop - chunk * width
                ]
                at = stop
            acc_v[...] += dot_nt(d_up, wu_v[:, cols])
        save("d_up", d_up_v)
        get_xh1.wait()
        get_inv1.wait()
        d_normed = acc_v[...]
        scaled = xh1_v[...].astype(F32)
        small_v[4:5, :] = column_sum(d_normed * scaled)
        small_v[6:7, :] = column_sum(d_normed)
        d_r1 = norm_back(d_normed, scaled, inv1_v[:, 0:1], gains[0, 0:1, :])
        d_attn = d_r1.astype(BF16)
        d_attn_v[...] = d_attn
        small_v[2:3, :] = column_sum(d_attn.astype(F32))
        acc_v[...] = d_r1
        save("d_attn", d_attn_v)
        get_wo.wait()
        d_ctx_v[...] = dot_nt(d_attn, wo_v[...]).astype(BF16)
        get_qkv.wait()
        get_ctx.wait()

        def pair_step(pair, carry):
            slot = lax.rem(pair, 2)

            @pl.when(pair + 1 < PAIRS)
            def _():
                begin(prob_in.at[mb, pl.ds((pair + 1) * 2, 2)], p_v.at[1 - slot], p_sem.at[1 - slot])

            pltpu.make_async_copy(prob_in.at[mb, pl.ds(0, 2)], p_v.at[slot], p_sem.at[slot]).wait()
            at = pl.multiple_of(pair * PAIR, PAIR)
            q2 = qkv_v[:, pl.ds(at, PAIR)] * SCORE_SCALE
            k2 = qkv_v[:, pl.ds(at + D, PAIR)]
            v2 = qkv_v[:, pl.ds(at + 2 * D, PAIR)]
            dc2 = d_ctx_v[:, pl.ds(at, PAIR)]
            inner = dc2.astype(F32) * ctx_v[:, pl.ds(at, PAIR)].astype(F32)
            d_q, d_k, d_v = None, None, None
            for head in range(2):
                mask = half_mask(head)
                k_own, q_own, dc_own = k2 * mask, q2 * mask, dc2 * mask
                prob = p_v[slot, head]
                row_inner = jnp.sum(inner * mask.astype(F32), axis=-1, keepdims=True)
                d_prob = dot_nt(dc_own, v2)
                d_score = (prob.astype(F32) * (d_prob - row_inner)).astype(BF16)
                part_v = dot_tn(dc_own, prob)
                part_q = dot_nn(d_score, k_own)
                part_k = dot_tn(q_own, d_score)
                d_v = part_v if d_v is None else d_v + part_v
                d_q = part_q if d_q is None else d_q + part_q
                d_k = part_k if d_k is None else d_k + part_k
            d_qkv_v[:, pl.ds(at, PAIR)] = (d_q * SCORE_SCALE).astype(BF16)
            d_qkv_v[:, pl.ds(at + D, PAIR)] = jnp.transpose(d_k).astype(BF16)
            d_qkv_v[:, pl.ds(at + 2 * D, PAIR)] = jnp.transpose(d_v).astype(BF16)
            return carry

        lax.fori_loop(0, PAIRS, pair_step, 0)
        save("d_qkv", d_qkv_v)
        get_wqkv.wait()
        small_v[0:1, :] = column_sum(d_qkv_v[:, 0:D].astype(F32))
        small_v[1:2, :] = column_sum(d_qkv_v[:, 2 * D : 3 * D].astype(F32))
        d_hid_v[...] = (acc_v[...] + dot_nt(d_qkv_v[...], wqkv_v[...])).astype(BF16)
        pending.append(begin(d_hid_v, d_hop, out_sem.at[len(pending)]))
        save("d_hid", d_hid_v)
        pending.append(begin(small_v, small_out.at[mb], out_sem.at[len(pending)]))
        for copy in pending:
            copy.wait()


def backward(step, cotangent, received, weights, gains, prob, saved, grads):
    total = MICRO * SEQ
    shapes = [
        jax.ShapeDtypeStruct((SEQ, D), BF16),
        jax.ShapeDtypeStruct((MICRO, SMALL_ROWS, D), F32),
    ] + [jax.ShapeDtypeStruct((total, width), dtype) for _, width, dtype in GRADS]
    n_alias = len(grads)
    ins = [cotangent, received, *weights, gains, prob, *saved, *grads]
    widths = {name: (width, dtype) for name, width, dtype in SAVED}
    kept = ("qkv", "ctx", "xh1", "inv1", "slope", "xh2", "inv2")
    result = pl.pallas_call(
        functools.partial(backward_kernel, step, n_alias),
        out_shape=shapes,
        in_specs=[ANY] * 6 + [VMEM] + [ANY] * (11 + n_alias),
        out_specs=[ANY] * len(shapes),
        input_output_aliases={18 + i: 1 + i for i in range(n_alias)},
        scratch_shapes=[
            pltpu.VMEM((SEQ, D), BF16),
            pltpu.VMEM((D, 3 * D), BF16),
            pltpu.VMEM((D, D), BF16),
            pltpu.VMEM((D, FF), BF16),
            pltpu.VMEM((FF, D), BF16),
            pltpu.VMEM((2, 2, SEQ, SEQ), BF16),
            pltpu.VMEM((SEQ, D), F32),
            pltpu.VMEM((8, 128), F32),
            pltpu.VMEM((SMALL_ROWS, D), F32),
        ]
        + [pltpu.VMEM((SEQ, widths[name][0]), widths[name][1]) for name in kept]
        + [pltpu.VMEM((SEQ, D), BF16)]
        + [pltpu.VMEM((SEQ, width), dtype) for _, width, dtype in GRADS]
        + [
            pltpu.SemaphoreType.DMA((8,)),
            pltpu.SemaphoreType.DMA((4,)),
            pltpu.SemaphoreType.DMA((2,)),
            pltpu.SemaphoreType.DMA((8,)),
        ],
        compiler_params=pltpu.CompilerParams(vmem_limit_bytes=VMEM_LIMIT),
        name="backward",
    )(*ins)
    return result[0], list(result[1:])


UNIT = 16
RAIL = 4 * UNIT
ROOTS = 4
HALF = 2 * RAIL + ROOTS * UNIT
SLAB = 2 * HALF
MESH = pl.DeviceIdType.MESH


def reduce_kernel(depth, *refs):
    (gelu, d_down, low, d_up, ctx, d_attn, hid, d_qkv, small) = refs[:9]
    (o_down, o_up, o_out, o_qkv, o_small) = refs[9:14]
    (
        left_v, right_v, p_v, s_v, y_v, rl_v, rr_v, o_v, sm_v, sm_in_v, sm_o_v,
        load_sem, send_sem, recv_sem, out_sem, sm_send, sm_recv,
    ) = refs[14:]
    columns = d_down.shape[1]
    plan = (
        ("down", FF // SLAB, gelu, d_down, o_down),
        ("up", 2 * (FF // D), low, d_up, o_up),
        ("out", 2, ctx, d_attn, o_out),
        ("qkv", 6, hid, d_qkv, o_qkv),
    )
    count = sum(entry[1] for entry in plan)
    section = lax.axis_index("section")
    me = lax.axis_index("dp")
    core = lax.rem(me, 2)
    y = lax.rem(lax.div(me, 2), 2)
    z = lax.div(me, 4)
    sibling = (section, me + 1 - 2 * core)
    partner = (section, me + 2 - 4 * y)
    left = (section, me - 4)
    right = (section, me + 4)

    barrier = pltpu.get_barrier_semaphore()
    pl.semaphore_signal(barrier, inc=1, device_id=sibling, device_id_type=MESH)
    pl.semaphore_signal(barrier, inc=1, device_id=partner, device_id_type=MESH)

    @pl.when(z > 0)
    def _():
        pl.semaphore_signal(barrier, inc=1, device_id=left, device_id_type=MESH)

    @pl.when(z < depth - 1)
    def _():
        pl.semaphore_signal(barrier, inc=1, device_id=right, device_id_type=MESH)

    def at(value, size):
        return pl.ds(pl.multiple_of(value, UNIT), size)

    def load(step, start):
        slot = lax.rem(step, 2)
        if not start:
            pltpu.make_async_copy(gelu.at[:, pl.ds(0, SLAB)], left_v.at[slot], load_sem.at[0, slot]).wait()
            pltpu.make_async_copy(d_down, right_v.at[slot], load_sem.at[1, slot]).wait()
            return
        first = 0
        for name, steps, factor, grad, _ in plan:

            def issue(first=first, name=name, factor=factor, grad=grad):
                index = step - first
                if name == "down":
                    row, column = index, 0
                else:
                    row, column = lax.rem(index, 2), lax.div(index, 2)
                rows = pl.ds(pl.multiple_of(row * SLAB, 128), SLAB)
                cols = pl.ds(pl.multiple_of(column * columns, 128), columns)
                pltpu.make_async_copy(factor.at[:, rows], left_v.at[slot], load_sem.at[0, slot]).start()
                pltpu.make_async_copy(grad.at[:, cols], right_v.at[slot], load_sem.at[1, slot]).start()

            pl.when((step >= first) & (step < first + steps))(issue)
            first += steps

    def out_copy(step, start):
        slot = lax.rem(step, 2)
        if not start:
            pltpu.make_async_copy(o_v.at[0], o_down.at[pl.ds(0, SLAB)], out_sem.at[slot]).wait()
            return
        first = 0
        for name, steps, _, _, result in plan:

            def issue(first=first, name=name, result=result):
                index = step - first
                if name == "down":
                    row, column = index, 0
                else:
                    row, column = lax.rem(index, 2), lax.div(index, 2)
                cols = pl.ds(pl.multiple_of(column * columns, 128), columns)
                pltpu.make_async_copy(o_v.at[step], result.at[at(row * SLAB, SLAB), cols], out_sem.at[slot]).start()

            pl.when((step >= first) & (step < first + steps))(issue)
            first += steps

    def send(kind, step, source, target, arrival, device, compute=None):
        parity = lax.rem(step, 2)
        copy = pltpu.make_async_remote_copy(
            source, target, send_sem.at[kind, parity], arrival, device_id=device, device_id_type=MESH
        )

        @pl.when(step >= 2)
        def _():
            copy.wait_send()

        if compute is not None:
            compute()
        copy.start()

    def finish_send(kind, view):
        for parity in range(2):
            pltpu.make_async_remote_copy(
                view, view, send_sem.at[kind, parity], recv_sem.at[kind, 0], device_id=sibling, device_id_type=MESH
            ).wait_send()

    def arrived(kind, step, view):
        pltpu.make_async_remote_copy(
            view, view, send_sem.at[kind, 0], recv_sem.at[kind, step], device_id=sibling, device_id_type=MESH
        ).wait_recv()

    own = core * HALF
    theirs = HALF - own
    CX, UP, DOWN, SIB_OTHER, YX = range(5)

    def add_into(target, term):
        target[...] = (target[...].astype(F32) + term[...].astype(F32)).astype(target.dtype)

    class Tree:
        def __init__(self, kinds, base, root, reach, size, offset, land, rail):
            self.kinds, self.base, self.root, self.reach = kinds, base, root, reach
            self.size, self.offset, self.land, self.rail = size, offset, land, rail
            self.distance = jnp.abs(z - root)
            self.from_left = (z > 0) & (z <= root)
            self.from_right = (z < depth - 1) & (z >= root)

        def part(self, step):
            return s_v.at[step, at(self.offset, self.size)]

        def total(self, step):
            return o_v.at[step, at(own + self.offset, self.size)]

        def landing(self, buffer, step):
            return buffer.at[step, pl.ds(self.land, self.size)]

        def towards(self, now):
            inward, out_left, out_right, sib = self.kinds
            step = now - self.base - self.reach + self.distance

            @pl.when((step >= 0) & (step < count))
            def _():
                @pl.when(self.from_left)
                def _():
                    arrived(out_left, step, self.landing(rl_v, step))
                    add_into(self.part(step), self.landing(rl_v, step))

                @pl.when(self.from_right)
                def _():
                    arrived(out_right, step, self.landing(rr_v, step))
                    add_into(self.part(step), self.landing(rr_v, step))

                @pl.when(z < self.root)
                def _():
                    send(inward, step, self.part(step), self.landing(rl_v, step), recv_sem.at[out_left, step], right)

                @pl.when(z > self.root)
                def _():
                    send(inward, step, self.part(step), self.landing(rr_v, step), recv_sem.at[out_right, step], left)

                @pl.when(z == self.root)
                def _():
                    if self.rail:
                        self.total(step)[...] = self.part(step)[...]
                    else:
                        view = y_v.at[step, pl.ds(RAIL, UNIT)]
                        send(YX, step, self.part(step), view, recv_sem.at[YX, step], partner)

            if not self.rail:
                late = now - self.base - self.reach - 1

                @pl.when((z == self.root) & (late >= 0) & (late < count))
                def _():
                    view = y_v.at[late, pl.ds(RAIL, UNIT)]
                    arrived(YX, late, view)
                    self.total(late)[...] = (self.part(late)[...].astype(F32) + view[...].astype(F32)).astype(BF16)

        def away(self, now):
            inward, out_left, out_right, sib = self.kinds
            lag = self.base + self.reach + (0 if self.rail else 1)
            step = now - lag - self.distance

            @pl.when((step >= 0) & (step < count))
            def _():
                view = self.total(step)

                @pl.when(z != self.root)
                def _():
                    arrived(inward, step, view)

                @pl.when(self.from_left)
                def _():
                    send(out_left, step, view, view, recv_sem.at[inward, step], left)

                @pl.when(self.from_right)
                def _():
                    send(out_right, step, view, view, recv_sem.at[inward, step], right)

                if self.rail:
                    send(DOWN, step, view, view, recv_sem.at[DOWN, step], partner)
                send(sib, step, view, view, recv_sem.at[sib, step], sibling)

            done = step - 1

            @pl.when((done >= 0) & (done < count))
            def _():
                arrived(sib, done, o_v.at[done, at(theirs + self.offset, self.size)])

        def finish(self):
            inward, out_left, out_right, sib = self.kinds
            view = self.part(0)

            @pl.when(z != self.root)
            def _():
                finish_send(inward, view)

            @pl.when(self.from_left)
            def _():
                finish_send(out_left, view)

            @pl.when(self.from_right)
            def _():
                finish_send(out_right, view)

            finish_send(sib, view)
            if not self.rail:

                @pl.when(z == self.root)
                def _():
                    finish_send(YX, view)

    half_depth = depth // 2
    rail_root = half_depth - 1 + y
    rail = Tree((5, 6, 7, 8), 2, rail_root, half_depth, RAIL, y * RAIL, 0, True)
    line = []
    for index in range(ROOTS):
        root = (2 * index + 1) * depth // (2 * ROOTS)
        kinds = tuple(9 + 4 * index + offset for offset in range(4))
        reach = max(root, depth - 1 - root)
        line.append(Tree(kinds, 1, root, reach, UNIT, 2 * RAIL + index * UNIT, RAIL + index * UNIT, False))
    other_distance = jnp.abs(z - (half_depth - y))
    other = (1 - y) * RAIL

    sm_root = half_depth
    sm_reach = max(sm_root, depth - 1 - sm_root)
    sm_distance = jnp.abs(z - sm_root)

    def sm_copy(kind, source, target, arrival, device):
        return pltpu.make_async_remote_copy(
            source, target, sm_send.at[kind], sm_recv.at[arrival], device_id=device, device_id_type=MESH
        )

    def small_round(now):
        @pl.when(now == 0)
        def _():
            sm_v[...] = small[0] + small[1]
            sm_copy(0, sm_v, sm_in_v.at[0], 0, sibling).start()

        @pl.when(now == 1)
        def _():
            sm_copy(0, sm_v, sm_in_v.at[0], 0, sibling).wait()
            sm_v[...] = sm_v[...] + sm_in_v[0]

        @pl.when(now == 1 + sm_reach - sm_distance)
        def _():
            @pl.when((z > 0) & (z <= sm_root))
            def _():
                sm_copy(1, sm_v, sm_in_v.at[1], 1, sibling).wait_recv()
                sm_v[...] = sm_v[...] + sm_in_v[1]

            @pl.when((z < depth - 1) & (z >= sm_root))
            def _():
                sm_copy(1, sm_v, sm_in_v.at[2], 2, sibling).wait_recv()
                sm_v[...] = sm_v[...] + sm_in_v[2]

            @pl.when(z < sm_root)
            def _():
                sm_copy(1, sm_v, sm_in_v.at[1], 1, right).start()

            @pl.when(z > sm_root)
            def _():
                sm_copy(1, sm_v, sm_in_v.at[2], 2, left).start()

            @pl.when(z == sm_root)
            def _():
                sm_copy(1, sm_v, sm_in_v.at[3], 3, partner).start()

        @pl.when((now == 2 + sm_reach) & (z == sm_root))
        def _():
            sm_copy(1, sm_v, sm_in_v.at[3], 3, partner).wait_recv()
            sm_o_v[...] = sm_v[...] + sm_in_v[3]

        @pl.when(now == 2 + sm_reach + sm_distance)
        def _():
            @pl.when(z != sm_root)
            def _():
                sm_copy(2, sm_o_v, sm_o_v, 4, sibling).wait_recv()

            @pl.when((z > 0) & (z <= sm_root))
            def _():
                sm_copy(2, sm_o_v, sm_o_v, 4, left).start()

            @pl.when((z < depth - 1) & (z >= sm_root))
            def _():
                sm_copy(3, sm_o_v, sm_o_v, 4, right).start()

    def small_finish():
        sm_copy(1, sm_v, sm_in_v.at[1], 1, sibling).wait_send()

        @pl.when((z > 0) & (z <= sm_root))
        def _():
            sm_copy(2, sm_o_v, sm_o_v, 4, left).wait_send()

        @pl.when((z < depth - 1) & (z >= sm_root))
        def _():
            sm_copy(3, sm_o_v, sm_o_v, 4, right).wait_send()

        o_small[...] = sm_o_v[...]

    load(jnp.int32(0), True)
    neighbours = 2 + (z > 0).astype(jnp.int32) + (z < depth - 1).astype(jnp.int32)
    pl.semaphore_wait(barrier, neighbours)

    out_lag = max(
        [2 + half_depth + half_depth + 2] + [2 + tree.reach + max(tree.root, depth - 1 - tree.root) + 1 for tree in line]
    )

    def one_round(now, carry):
        slot = lax.rem(now, 2)

        @pl.when(now < count)
        def _():
            load(now, False)

            @pl.when(now + 1 < count)
            def _():
                load(now + 1, True)

            def form():
                p_v[slot] = dot_tn(left_v[slot], right_v[slot]).astype(BF16)

            view = p_v.at[slot, at(theirs, HALF)]
            send(CX, now, view, s_v.at[now], recv_sem.at[CX, now], sibling, form)

        step = now - 1

        @pl.when((step >= 0) & (step < count))
        def _():
            arrived(CX, step, s_v.at[step])
            add_into(s_v.at[step], p_v.at[1 - slot, at(own, HALF)])
            view = s_v.at[step, at(other, RAIL)]
            send(UP, step, view, y_v.at[step, pl.ds(0, RAIL)], recv_sem.at[UP, step], partner)

        for tree in line:
            tree.towards(now)

        step_up = now - 2

        @pl.when((step_up >= 0) & (step_up < count))
        def _():
            view = y_v.at[step_up, pl.ds(0, RAIL)]
            arrived(UP, step_up, view)
            add_into(rail.part(step_up), view)

        rail.towards(now)
        rail.away(now)
        for tree in line:
            tree.away(now)

        step_down = now - 2 - half_depth - other_distance - 1

        @pl.when((step_down >= 0) & (step_down < count))
        def _():
            view = o_v.at[step_down, at(own + other, RAIL)]
            arrived(DOWN, step_down, view)
            send(SIB_OTHER, step_down, view, view, recv_sem.at[SIB_OTHER, step_down], sibling)

        step_sib = step_down - 1

        @pl.when((step_sib >= 0) & (step_sib < count))
        def _():
            arrived(SIB_OTHER, step_sib, o_v.at[step_sib, at(theirs + other, RAIL)])

        small_round(now)

        step_out = now - out_lag

        @pl.when(step_out >= 0)
        def _():
            @pl.when(step_out >= 2)
            def _():
                out_copy(step_out, False)

            out_copy(step_out, True)

        return carry

    lax.fori_loop(0, count + out_lag, one_round, 0)
    out_copy(jnp.int32(0), False)
    out_copy(jnp.int32(1), False)
    finish_send(CX, s_v.at[0])
    finish_send(UP, rail.part(0))
    finish_send(DOWN, rail.part(0))
    finish_send(SIB_OTHER, rail.part(0))
    rail.finish()
    for tree in line:
        tree.finish()
    small_finish()


def reduce_gradients(depth, gelu, d_down, low, d_up, ctx, d_attn, hid, d_qkv, small):
    rows, columns = d_down.shape
    count = FF // SLAB + 2 * (FF // D) + 8
    kinds = 9 + 4 * ROOTS
    return pl.pallas_call(
        functools.partial(reduce_kernel, depth),
        out_shape=[
            jax.ShapeDtypeStruct((FF, columns), BF16),
            jax.ShapeDtypeStruct((D, 4 * columns), BF16),
            jax.ShapeDtypeStruct((D, columns), BF16),
            jax.ShapeDtypeStruct((D, 3 * columns), BF16),
            jax.ShapeDtypeStruct((SMALL_ROWS, small.shape[-1]), F32),
        ],
        in_specs=[ANY] * 8 + [VMEM],
        out_specs=[ANY] * 4 + [VMEM],
        scratch_shapes=[
            pltpu.VMEM((2, rows, SLAB), BF16),
            pltpu.VMEM((2, rows, columns), BF16),
            pltpu.VMEM((2, SLAB, columns), BF16),
            pltpu.VMEM((count, HALF, columns), BF16),
            pltpu.VMEM((count, RAIL + UNIT, columns), BF16),
            pltpu.VMEM((count, RAIL + ROOTS * UNIT, columns), BF16),
            pltpu.VMEM((count, RAIL + ROOTS * UNIT, columns), BF16),
            pltpu.VMEM((count, SLAB, columns), BF16),
            pltpu.VMEM((SMALL_ROWS, small.shape[-1]), F32),
            pltpu.VMEM((4, SMALL_ROWS, small.shape[-1]), F32),
            pltpu.VMEM((SMALL_ROWS, small.shape[-1]), F32),
            pltpu.SemaphoreType.DMA((2, 2)),
            pltpu.SemaphoreType.DMA((kinds, 2)),
            pltpu.SemaphoreType.DMA((kinds, count)),
            pltpu.SemaphoreType.DMA((2,)),
            pltpu.SemaphoreType.DMA((4,)),
            pltpu.SemaphoreType.DMA((5,)),
        ],
        compiler_params=pltpu.CompilerParams(
            collective_id=0, has_side_effects=True, vmem_limit_bytes=VMEM_LIMIT
        ),
        name="reduce_gradients",
    )(gelu, d_down, low, d_up, ctx, d_attn, hid, d_qkv, small)


def shards(
    tokens, segments, lengths, cotangent, qkv_weight, qv_bias, out_weight, out_biases,
    norm_gains, norm_shifts, up_weight, up_bias, down_weight,
):
    weights = (qkv_weight, out_weight, up_weight, down_weight)
    params = (qv_bias, out_biases, norm_gains, norm_shifts, up_bias)
    onward = [(0, 1)]
    back = [(1, 0)]
    received = tokens[:SEQ]
    state = []
    for step in range(MICRO + 1):
        hop, state = forward(step, tokens, received, weights, segments, lengths, params, state)
        if step < MICRO:
            received = lax.ppermute(hop, "section", onward)
    hid, prob = state[:2]
    saved = state[2:]
    act = saved[0]
    received = cotangent[:SEQ]
    grads = []
    for step in range(MICRO + 1):
        hop, grads = backward(step, cotangent, received, weights, norm_gains, prob, saved, grads)
        if step < MICRO:
            received = lax.ppermute(hop, "section", back)
    d_down, d_up, d_attn, d_qkv, d_hid = grads[1:]
    kept = dict(zip([name for name, _, _ in SAVED], saved))
    *large, small = reduce_gradients(
        lax.axis_size("dp") // 4, kept["gelu"], d_down, kept["low"], d_up, kept["ctx"], d_attn, hid, d_qkv, grads[0]
    )
    g_down, g_up, g_out, g_qkv = [value.astype(F32)[None] for value in large]
    small = small[None]
    return (
        act[None], d_hid[None], g_qkv, small[:, 0:2], g_out, small[:, 2:4], small[:, 4:6], small[:, 6:8],
        g_up, small[:, 8:12].reshape(1, FF), g_down,
    )


def solution(mesh):
    return jax.shard_map(
        shards,
        mesh=mesh,
        in_specs=(
            P("dp", None), P("dp", None), P("dp"), P("dp", None),
            P("section", None, None), P("section", None, None), P("section", None, None), P("section", None, None),
            P("section", None, None), P("section", None, None), P("section", None, None), P("section", None),
            P("section", None, None),
        ),
        out_specs=(
            P("section", "dp", None), P("section", "dp", None),
            P("section", None, None), P("section", None, None), P("section", None, None), P("section", None, None),
            P("section", None, None), P("section", None, None), P("section", None, None), P("section", None),
            P("section", None, None),
        ),
        check_vma=False,
    )
```

```python
import functools
import math

import jax
import jax.numpy as jnp
from jax import lax
from jax.experimental import pallas as pl
from jax.experimental.pallas import tpu as pltpu
from jax.sharding import PartitionSpec as P

D = 768
H = 12
HD = 64
FF = 3072
SEQ = 512
MICRO = 2
PAIRS = H // 2
PAIR = 2 * HD

EPSILON = 1e-05
SCORE_SCALE = 0.125
NEG_FILL = -1e30
F32 = jnp.float32
BF16 = jnp.bfloat16
VMEM_LIMIT = 60 << 20
MESH = pl.DeviceIdType.MESH

ANY = pl.BlockSpec(memory_space=pl.ANY)
VMEM = pl.BlockSpec(memory_space=pltpu.VMEM)
SMEM = pl.BlockSpec(memory_space=pltpu.SMEM)


def dot_nn(left, right):
    return lax.dot_general(left, right, (((1,), (0,)), ((), ())), preferred_element_type=F32)


def dot_nt(left, right):
    return lax.dot_general(left, right, (((1,), (1,)), ((), ())), preferred_element_type=F32)


def dot_tn(left, right):
    return lax.dot_general(left, right, (((0,), (0,)), ((), ())), preferred_element_type=F32)


def begin(source, target, sem):
    copy = pltpu.make_async_copy(source, target, sem)
    copy.start()
    return copy


def gelu_and_slope(u):
    normal_cdf = 0.5 + 0.5 * lax.erf(u * (1.0 / math.sqrt(2.0)))
    bell = jnp.exp((-0.5 * u) * u)
    return u * normal_cdf, normal_cdf + (u * (1.0 / math.sqrt(2.0 * math.pi))) * bell


def normalize(resid):
    average = jnp.mean(resid, axis=-1, keepdims=True)
    centred = resid - average
    variance = jnp.mean(centred * centred, axis=-1, keepdims=True)
    inverse = lax.rsqrt(variance + EPSILON)
    return centred * inverse, inverse


def norm_back(grad_out, scaled, inverse, gain):
    weighted = grad_out * gain
    first_mean = jnp.mean(weighted, axis=-1, keepdims=True)
    second_mean = jnp.mean(weighted * scaled, axis=-1, keepdims=True)
    return inverse * (weighted - first_mean - scaled * second_mean)


def half_mask(which):
    lane = lax.broadcasted_iota(jnp.int32, (1, PAIR), 1)
    return ((lane // HD) == which).astype(F32).astype(BF16)


ROWS = SEQ // 2
SAVED = (
    ("hid", D, BF16),
    ("q", D, BF16),
    ("linv", D, F32),
    ("ctx", D, BF16),
    ("xh1", D, BF16),
    ("inv1", 128, F32),
    ("low", D, BF16),
    ("gelu", FF, BF16),
    ("slope", FF, BF16),
    ("xh2", D, BF16),
    ("inv2", 128, F32),
)
GRADS = (("d_down", D, BF16), ("d_up", FF, BF16), ("d_attn", D, BF16), ("d_qkv", 3 * D, BF16))
SMALL_ROWS = 16


class Place:
    def __init__(self):
        self.section = lax.axis_index("section")
        self.me = lax.axis_index("dp")
        self.core = lax.rem(self.me, 2)
        self.sibling = (self.section, self.me + 1 - 2 * self.core)
        self.other_layer = (1 - self.section, self.me)
        self.own = pl.ds(pl.multiple_of(self.core * ROWS, ROWS), ROWS)
        self.theirs = pl.ds(pl.multiple_of(ROWS - self.core * ROWS, ROWS), ROWS)

    def greet(self):
        barrier = pltpu.get_barrier_semaphore()
        for device in (self.sibling, self.other_layer):
            pl.semaphore_signal(barrier, inc=1, device_id=device, device_id_type=MESH)
        pl.semaphore_wait(barrier, 2)

    def is_mine(self, step, sequences):
        return lax.div(step, sequences) == self.core


def remote(source, target, send_sem, recv_sem, device):
    return pltpu.make_async_remote_copy(source, target, send_sem, recv_sem, device_id=device, device_id_type=MESH)


class Rows:
    def __init__(self, place, sequences, array, steps, local, sent, arrived):
        self.place, self.sequences, self.array, self.steps = place, sequences, array, steps
        self.local, self.sent, self.arrived = local, sent, arrived

    def part(self, sequence, core):
        return self.array.at[pl.ds(pl.multiple_of(sequence * SEQ + core * ROWS, ROWS), ROWS)]

    def spread(self):
        place = self.place
        for sequence in range(self.sequences):
            step = place.core * self.sequences + sequence
            target = self.steps.at[step]
            pltpu.make_async_copy(self.part(sequence, place.core), target, self.local.at[sequence]).start()
            remote(
                self.part(sequence, 1 - place.core), target, self.sent.at[sequence], self.arrived.at[step], place.sibling
            ).start()

    def spread_done(self):
        for sequence in range(self.sequences):
            view = self.steps.at[0]
            remote(view, view, self.sent.at[sequence], self.arrived.at[0], self.place.sibling).wait_send()

    def await_step(self, step, spread):
        mine = spread & self.place.is_mine(step, self.sequences)
        view = self.steps.at[step]

        @pl.when(mine)
        def _():
            pltpu.make_async_copy(view, view, self.local.at[lax.rem(step, self.sequences)]).wait()

        @pl.when(jnp.logical_not(mine))
        def _():
            remote(view, view, self.sent.at[0], self.arrived.at[step], self.place.sibling).wait_recv()

    def collect(self, step):
        sequence = lax.rem(step, self.sequences)
        target = self.part(sequence, self.place.core)
        mine = self.place.is_mine(step, self.sequences)

        @pl.when(mine)
        def _():
            pltpu.make_async_copy(self.steps.at[step], target, self.local.at[sequence]).start()

        @pl.when(jnp.logical_not(mine))
        def _():
            remote(
                self.steps.at[step], target, self.sent.at[sequence], self.arrived.at[sequence], self.place.sibling
            ).start()

    def collect_done(self):
        for sequence in range(self.sequences):
            view = self.steps.at[0]
            pltpu.make_async_copy(view, view, self.local.at[sequence]).wait()
            remote(view, view, self.sent.at[sequence], self.arrived.at[sequence], self.place.sibling).wait()


def forward_kernel(sequences, *refs):
    (tok, wqkv, wo, wu, wd, segs, lens, qv_bias, out_biases, gains, shifts, up_bias) = refs[:12]
    act_out, kv_out, prob_out = refs[12:15]
    count = len(SAVED)
    outs = dict(zip([name for name, _, _ in SAVED], refs[15 : 15 + count]))
    (
        h_v, act_v, kv_v, p_v, wqkv_v, wo_v, wu_v, wd_v, bias_v, acc_v, seg_own, seg_their,
        q_v, linv_v, ctx_v, xh1_v, inv1_v, low_v, gelu_v, slope_v, xh2_v, inv2_v,
        w_sem, save_sem, p_sem, in_local, in_sent, in_arrived, out_local, out_sent, out_arrived,
        kv_sent, kv_arrived, kv_save, seg_sem, hop_sent, hid_save,
    ) = refs[15 + count :]
    place = Place()
    section = place.section
    steps = 2 * sequences
    names = [name for name, _, _ in SAVED]
    inputs = Rows(place, sequences, tok, h_v, in_local, in_sent, in_arrived)
    outputs = Rows(place, sequences, act_out, act_v, out_local, out_sent, out_arrived)

    position = lax.broadcasted_iota(jnp.int32, (1, SEQ), 1)
    for sequence in range(sequences):
        seg_own[sequence, 0:1, :] = segs[sequence : sequence + 1, :].astype(F32)
        seg_own[sequence, 1:2, :] = (position < lens[sequence]).astype(F32)
        seg_own[sequence, 2:8, :] = jnp.zeros((6, SEQ), F32)
    w_first = [begin(wqkv.at[0, :, pl.ds(block * D, D)], wqkv_v.at[:, pl.ds(block * D, D)], w_sem.at[block]) for block in (1, 2, 0)]
    place.greet()
    seg_copy = remote(seg_own, seg_their, seg_sem.at[0], seg_sem.at[1], place.sibling)
    seg_copy.start()

    @pl.when(section == 0)
    def _():
        inputs.spread()

    w_rest = [begin(wo.at[0], wo_v, w_sem.at[3]), begin(wu.at[0], wu_v, w_sem.at[4]), begin(wd.at[0], wd_v, w_sem.at[5])]
    seg_copy.wait()

    def save(name, buffer, step):
        target = outs[name].at[pl.ds(pl.multiple_of(step * ROWS, ROWS), ROWS)]
        pltpu.make_async_copy(buffer, target, save_sem.at[names.index(name)]).start()

    def free(name, buffer):
        pltpu.make_async_copy(buffer, buffer, save_sem.at[names.index(name)]).wait()

    reused = (
        ("q", q_v), ("linv", linv_v), ("ctx", ctx_v), ("xh1", xh1_v), ("inv1", inv1_v), ("low", low_v),
        ("gelu", gelu_v), ("slope", slope_v), ("xh2", xh2_v), ("inv2", inv2_v),
    )

    def one_step(step, carry):
        sequence = lax.rem(step, sequences)
        mine = jnp.where(place.is_mine(step, sequences), 1.0, 0.0)
        key_rows = mine * seg_own[sequence] + (1.0 - mine) * seg_their[sequence]
        query_row = mine * seg_own[sequence, 0:1, place.own] + (1.0 - mine) * seg_their[sequence, 0:1, place.own]
        query_seg = jnp.transpose(jnp.broadcast_to(query_row, (128, ROWS)))
        query = lax.broadcasted_iota(jnp.int32, (ROWS, 128), 0) + place.core * ROWS
        key = lax.broadcasted_iota(jnp.int32, (ROWS, 128), 1)
        for tile in range(SEQ // 128):
            cols = slice(tile * 128, (tile + 1) * 128)
            visible = (key_rows[1:2, cols] > 0.5) | (key + tile * 128 == query)
            bias_v[:, cols] = jnp.where((query_seg == key_rows[0:1, cols]) & visible, 0.0, NEG_FILL)

        inputs.await_step(step, section == 0)
        target = outs["hid"].at[pl.ds(pl.multiple_of(step * ROWS, ROWS), ROWS)]
        pltpu.make_async_copy(h_v.at[step], target, hid_save.at[step]).start()
        hidden = h_v[step]
        for block in (1, 2):

            @pl.when(step == 0)
            def _():
                w_first[block - 1].wait()

            proj = dot_nn(hidden, wqkv_v[:, block * D : (block + 1) * D])
            if block == 2:
                proj = proj + qv_bias[0, 1:2, :]
            cols = pl.ds((block - 1) * D, D)
            kv_v[step, place.own, cols] = proj.astype(BF16)
            view = kv_v.at[step, place.own, cols]
            remote(view, view, kv_sent.at[step, block - 1], kv_arrived.at[step, block - 1], place.sibling).start()

        @pl.when(step == 0)
        def _():
            w_first[2].wait()

        @pl.when(step > 0)
        def _():
            for name, buffer in reused:
                free(name, buffer)
            for pair in range(PAIRS):
                pltpu.make_async_copy(p_v.at[pair], p_v.at[pair], p_sem.at[pair]).wait()

        q_v[...] = (dot_nn(hidden, wqkv_v[:, 0:D]) + qv_bias[0, 0:1, :]).astype(BF16)
        save("q", q_v, step)
        for block in range(2):
            view = kv_v.at[step, place.theirs, pl.ds(block * D, D)]
            remote(view, view, kv_sent.at[step, block], kv_arrived.at[step, block], place.sibling).wait_recv()
        pltpu.make_async_copy(kv_v.at[step], kv_out.at[step], kv_save.at[step]).start()

        def pair_step(pair, carry):
            at = pl.multiple_of(pair * PAIR, PAIR)
            q2 = q_v[:, pl.ds(at, PAIR)] * SCORE_SCALE
            k2 = kv_v[step, :, pl.ds(at, PAIR)]
            v2 = kv_v[step, :, pl.ds(at + D, PAIR)]
            total, inverses = None, []
            for head in range(2):
                mask = half_mask(head)
                scores = dot_nt(q2, k2 * mask) + bias_v[...]
                exp_vals = jnp.exp(scores - jnp.max(scores, axis=-1, keepdims=True))
                inverses.append(1.0 / jnp.sum(exp_vals, axis=-1, keepdims=True))
                weight = exp_vals.astype(BF16)
                p_v[pair, head] = weight
                part = dot_nn(weight, v2 * mask)
                total = part if total is None else total + part
            lane = lax.broadcasted_iota(jnp.int32, (1, PAIR), 1)
            inverse = jnp.where(lane < HD, inverses[0], inverses[1])
            linv_v[:, pl.ds(at, PAIR)] = inverse
            ctx_v[:, pl.ds(at, PAIR)] = (total * inverse).astype(BF16)
            pltpu.make_async_copy(p_v.at[pair], prob_out.at[step, pl.ds(pair * 2, 2)], p_sem.at[pair]).start()
            return carry

        lax.fori_loop(0, PAIRS, pair_step, 0, unroll=3)
        save("linv", linv_v, step)
        save("ctx", ctx_v, step)

        @pl.when(step == 0)
        def _():
            w_rest[0].wait()

        resid = hidden.astype(F32) + (dot_nn(ctx_v[...], wo_v[...]) + out_biases[0, 0:1, :])
        scaled, inverse = normalize(resid)
        xh1_v[...] = scaled.astype(BF16)
        inv1_v[...] = jnp.broadcast_to(inverse, (ROWS, 128))
        normed = scaled * gains[0, 0:1, :] + shifts[0, 0:1, :]
        low_v[...] = normed.astype(BF16)
        acc_v[...] = normed + out_biases[0, 1:2, :]
        save("xh1", xh1_v, step)
        save("inv1", inv1_v, step)
        save("low", low_v, step)

        @pl.when(step == 0)
        def _():
            w_rest[1].wait()
            w_rest[2].wait()

        width = 1024
        for chunk in range(FF // width):
            cols = slice(chunk * width, (chunk + 1) * width)
            up = dot_nn(low_v[...], wu_v[:, cols]) + up_bias[0:1, cols]
            gelu, slope = gelu_and_slope(up)
            gelu = gelu.astype(BF16)
            gelu_v[:, cols] = gelu
            slope_v[:, cols] = slope.astype(BF16)
            acc_v[...] += dot_nn(gelu, wd_v[cols, :])
        save("gelu", gelu_v, step)
        save("slope", slope_v, step)
        scaled, inverse = normalize(acc_v[...])
        act_v[step] = (scaled * gains[0, 1:2, :] + shifts[0, 1:2, :]).astype(BF16)

        @pl.when(section == 0)
        def _():
            remote(act_v.at[step], h_v.at[step], hop_sent.at[step], in_arrived.at[step], place.other_layer).start()

        outputs.collect(step)
        xh2_v[...] = scaled.astype(BF16)
        inv2_v[...] = jnp.broadcast_to(inverse, (ROWS, 128))
        save("xh2", xh2_v, step)
        save("inv2", inv2_v, step)
        return carry

    lax.fori_loop(0, steps, one_step, 0)
    for name, buffer in reused:
        free(name, buffer)
    for step in range(steps):
        pltpu.make_async_copy(h_v.at[step], h_v.at[step], hid_save.at[step]).wait()
        pltpu.make_async_copy(kv_v.at[step], kv_out.at[step], kv_save.at[step]).wait()
        for block in range(2):
            view = kv_v.at[step, place.own, pl.ds(block * D, D)]
            remote(view, view, kv_sent.at[step, block], kv_arrived.at[step, block], place.sibling).wait_send()
    for pair in range(PAIRS):
        pltpu.make_async_copy(p_v.at[pair], p_v.at[pair], p_sem.at[pair]).wait()

    @pl.when(section == 0)
    def _():
        inputs.spread_done()
        for step in range(steps):
            remote(act_v.at[step], h_v.at[step], hop_sent.at[step], in_arrived.at[step], place.other_layer).wait_send()

    outputs.collect_done()


def forward(tokens, weights, segments, lengths, params):
    total = tokens.shape[0]
    sequences = total // SEQ
    steps = 2 * sequences
    shapes = [
        jax.ShapeDtypeStruct((total, D), BF16),
        jax.ShapeDtypeStruct((steps, SEQ, 2 * D), BF16),
        jax.ShapeDtypeStruct((steps, H, ROWS, SEQ), BF16),
    ] + [jax.ShapeDtypeStruct((total, width), dtype) for _, width, dtype in SAVED]
    dma = pltpu.SemaphoreType.DMA
    act, kv, prob, *saved = pl.pallas_call(
        functools.partial(forward_kernel, sequences),
        out_shape=shapes,
        in_specs=[ANY] * 5 + [VMEM, SMEM] + [VMEM] * 5,
        out_specs=[ANY] * len(shapes),
        scratch_shapes=[
            pltpu.VMEM((steps, ROWS, D), BF16),
            pltpu.VMEM((steps, ROWS, D), BF16),
            pltpu.VMEM((steps, SEQ, 2 * D), BF16),
            pltpu.VMEM((PAIRS, 2, ROWS, SEQ), BF16),
            pltpu.VMEM((D, 3 * D), BF16),
            pltpu.VMEM((D, D), BF16),
            pltpu.VMEM((D, FF), BF16),
            pltpu.VMEM((FF, D), BF16),
            pltpu.VMEM((ROWS, SEQ), F32),
            pltpu.VMEM((ROWS, D), F32),
            pltpu.VMEM((sequences, 8, SEQ), F32),
            pltpu.VMEM((sequences, 8, SEQ), F32),
        ]
        + [pltpu.VMEM((ROWS, width), dtype) for name, width, dtype in SAVED if name != "hid"]
        + [
            dma((6,)),
            dma((len(SAVED),)),
            dma((PAIRS,)),
            dma((sequences,)),
            dma((sequences,)),
            dma((steps,)),
            dma((sequences,)),
            dma((sequences,)),
            dma((sequences,)),
            dma((steps, 2)),
            dma((steps, 2)),
            dma((steps,)),
            dma((2,)),
            dma((steps,)),
            dma((steps,)),
        ],
        compiler_params=pltpu.CompilerParams(
            collective_id=1, has_side_effects=True, vmem_limit_bytes=VMEM_LIMIT
        ),
        name="forward",
    )(tokens, *weights, segments, lengths, *params)
    return act, kv, prob, dict(zip([name for name, _, _ in SAVED], saved))


KEPT = ("q", "linv", "ctx", "xh1", "inv1", "slope", "xh2", "inv2")


def backward_kernel(sequences, *refs):
    (cot, wqkv, wo, wu, wd, gains, kv_in, prob_in) = refs[:8]
    ins = dict(zip(KEPT, refs[8:16]))
    d_hid_out, small_out = refs[16:18]
    outs = dict(zip([name for name, _, _ in GRADS], refs[18:22]))
    (
        g_v, d_hid_v, kv_v, p_v, wqkv_v, wo_v, wu_v, wd_v, acc_v, d_ctx_v, part_v, their_v,
        q_v, linv_v, ctx_v, xh1_v, inv1_v, slope_v, xh2_v, inv2_v,
        d_down_v, d_up_v, d_attn_v, d_qkv_v,
        w_sem, load_sem, save_sem, in_local, in_sent, in_arrived, out_local, out_sent, out_arrived,
        part_sent, part_arrived, hop_sent,
    ) = refs[22:]
    place = Place()
    section = place.section
    steps = 2 * sequences
    grad_names = [name for name, _, _ in GRADS]
    inputs = Rows(place, sequences, cot, g_v, in_local, in_sent, in_arrived)
    outputs = Rows(place, sequences, d_hid_out, d_hid_v, out_local, out_sent, out_arrived)
    buffers = dict(zip(KEPT, (q_v, linv_v, ctx_v, xh1_v, inv1_v, slope_v, xh2_v, inv2_v)))

    def at_step(array, step):
        return array.at[pl.ds(pl.multiple_of(step * ROWS, ROWS), ROWS)]

    def fetch(names, step):
        for name in names:
            if name == "kv":
                pltpu.make_async_copy(kv_in.at[step], kv_v, load_sem.at[len(KEPT)]).start()
            elif name == "prob":
                pltpu.make_async_copy(prob_in.at[step], p_v, load_sem.at[len(KEPT) + 1]).start()
            else:
                source = at_step(ins[name], step)
                pltpu.make_async_copy(source, buffers[name], load_sem.at[KEPT.index(name)]).start()

    def fetched(*names):
        for name in names:
            if name == "kv":
                pltpu.make_async_copy(kv_v, kv_v, load_sem.at[len(KEPT)]).wait()
            elif name == "prob":
                pltpu.make_async_copy(p_v, p_v, load_sem.at[len(KEPT) + 1]).wait()
            else:
                pltpu.make_async_copy(buffers[name], buffers[name], load_sem.at[KEPT.index(name)]).wait()

    def fetch_next(names, step):
        @pl.when(step + 1 < steps)
        def _():
            fetch(names, step + 1)

    def save(name, buffer, step):
        pltpu.make_async_copy(buffer, at_step(outs[name], step), save_sem.at[grad_names.index(name)]).start()

    def free(name, buffer):
        pltpu.make_async_copy(buffer, buffer, save_sem.at[grad_names.index(name)]).wait()

    def free_before(name, buffer, step):
        @pl.when(step > 0)
        def _():
            free(name, buffer)

    def when_first(step, copies):
        @pl.when(step == 0)
        def _():
            for copy in copies:
                copy.wait()

    place.greet()

    @pl.when(section == 1)
    def _():
        inputs.spread()

    first = jnp.int32(0)
    fetch(("xh2", "inv2"), first)
    get_wd = begin(wd.at[0], wd_v, w_sem.at[0])
    fetch(("slope",), first)
    get_wu = begin(wu.at[0], wu_v, w_sem.at[1])
    fetch(("xh1", "inv1"), first)
    get_wo = begin(wo.at[0], wo_v, w_sem.at[2])
    fetch(("q", "linv", "ctx", "kv", "prob"), first)
    get_wqkv = begin(wqkv.at[0], wqkv_v, w_sem.at[3])
    small_out[...] = jnp.zeros_like(small_out)

    def column_sum(value):
        return jnp.sum(value, axis=0, keepdims=True)

    def one_step(step, carry):
        inputs.await_step(step, section == 1)
        fetched("xh2", "inv2")
        grad = g_v[step].astype(F32)
        scaled = xh2_v[...].astype(F32)
        small_out[5:6, :] += column_sum(grad * scaled)
        small_out[7:8, :] += column_sum(grad)
        d_r2 = norm_back(grad, scaled, inv2_v[:, 0:1], gains[0, 1:2, :])
        d_down = d_r2.astype(BF16)
        free_before("d_down", d_down_v, step)
        d_down_v[...] = d_down
        small_out[3:4, :] += column_sum(d_down.astype(F32))
        acc_v[...] = d_r2
        save("d_down", d_down_v, step)
        fetch_next(("xh2", "inv2"), step)
        fetched("slope")
        when_first(step, (get_wd, get_wu))
        free_before("d_up", d_up_v, step)
        for chunk in range(FF // D):
            cols = slice(chunk * D, (chunk + 1) * D)
            d_up = (dot_nt(d_down_v[...], wd_v[cols, :]) * slope_v[:, cols].astype(F32)).astype(BF16)
            d_up_v[:, cols] = d_up
            small_out[8 + chunk : 9 + chunk, :] += column_sum(d_up.astype(F32))
            acc_v[...] += dot_nt(d_up, wu_v[:, cols])
        save("d_up", d_up_v, step)
        fetch_next(("slope",), step)
        fetched("xh1", "inv1")
        d_normed = acc_v[...]
        scaled = xh1_v[...].astype(F32)
        small_out[4:5, :] += column_sum(d_normed * scaled)
        small_out[6:7, :] += column_sum(d_normed)
        d_r1 = norm_back(d_normed, scaled, inv1_v[:, 0:1], gains[0, 0:1, :])
        d_attn = d_r1.astype(BF16)
        free_before("d_attn", d_attn_v, step)
        d_attn_v[...] = d_attn
        small_out[2:3, :] += column_sum(d_attn.astype(F32))
        acc_v[...] = d_r1
        save("d_attn", d_attn_v, step)
        fetch_next(("xh1", "inv1"), step)
        when_first(step, (get_wo,))
        fetched("q", "linv", "ctx", "kv", "prob")
        d_ctx_v[...] = (dot_nt(d_attn_v[...], wo_v[...]) * linv_v[...]).astype(BF16)
        free_before("d_qkv", d_qkv_v, step)

        @pl.when(step > 0)
        def _():
            for pair in range(PAIRS):
                view = part_v.at[pair, place.theirs]
                remote(view, view, part_sent.at[pair], part_arrived.at[0, 0], place.sibling).wait_send()

        def pair_step(pair, carry):
            at = pl.multiple_of(pair * PAIR, PAIR)
            q2 = q_v[:, pl.ds(at, PAIR)] * SCORE_SCALE
            k2 = kv_v[:, pl.ds(at, PAIR)]
            v2 = kv_v[:, pl.ds(at + D, PAIR)]
            dc2 = d_ctx_v[:, pl.ds(at, PAIR)]
            inner = dc2.astype(F32) * ctx_v[:, pl.ds(at, PAIR)].astype(F32)
            d_q, d_k, d_v = None, None, None
            for head in range(2):
                mask = half_mask(head)
                dc_own = dc2 * mask
                weight = p_v[pair * 2 + head]
                row_inner = jnp.sum(inner * mask.astype(F32), axis=-1, keepdims=True)
                d_prob = dot_nt(dc_own, v2)
                d_score = (weight.astype(F32) * (d_prob - row_inner)).astype(BF16)
                one_v = dot_tn(dc_own, weight)
                one_k = dot_tn(q2 * mask, d_score)
                one_q = dot_nn(d_score, k2 * mask)
                d_v = one_v if d_v is None else d_v + one_v
                d_k = one_k if d_k is None else d_k + one_k
                d_q = one_q if d_q is None else d_q + one_q
            d_qkv_v[:, pl.ds(at, PAIR)] = (d_q * SCORE_SCALE).astype(BF16)
            part_v[pair, :, 0:PAIR] = jnp.transpose(d_k).astype(BF16)
            part_v[pair, :, PAIR : 2 * PAIR] = jnp.transpose(d_v).astype(BF16)
            remote(
                part_v.at[pair, place.theirs], their_v.at[step, pair], part_sent.at[pair],
                part_arrived.at[step, pair], place.sibling,
            ).start()
            return carry

        lax.fori_loop(0, PAIRS, pair_step, 0, unroll=3)
        fetch_next(("q", "linv", "ctx", "kv", "prob"), step)
        when_first(step, (get_wqkv,))
        d_query = d_qkv_v[:, 0:D]
        acc_v[...] += dot_nt(d_query, wqkv_v[:, 0:D])
        small_out[0:1, :] += column_sum(d_query.astype(F32))
        for pair in range(PAIRS):
            view = their_v.at[step, pair]
            remote(view, view, part_sent.at[pair], part_arrived.at[step, pair], place.sibling).wait_recv()
            total = part_v[pair, place.own, :].astype(F32) + their_v[step, pair].astype(F32)
            at = pair * PAIR
            d_qkv_v[:, D + at : D + at + PAIR] = total[:, 0:PAIR].astype(BF16)
            d_qkv_v[:, 2 * D + at : 2 * D + at + PAIR] = total[:, PAIR : 2 * PAIR].astype(BF16)
        d_hid_v[step] = (acc_v[...] + dot_nt(d_qkv_v[:, D : 3 * D], wqkv_v[:, D : 3 * D])).astype(BF16)

        @pl.when(section == 1)
        def _():
            remote(d_hid_v.at[step], g_v.at[step], hop_sent.at[step], in_arrived.at[step], place.other_layer).start()

        outputs.collect(step)
        small_out[1:2, :] += column_sum(d_qkv_v[:, 2 * D : 3 * D].astype(F32))
        save("d_qkv", d_qkv_v, step)
        return carry

    lax.fori_loop(0, steps, one_step, 0)
    for name, buffer in zip(grad_names, (d_down_v, d_up_v, d_attn_v, d_qkv_v)):
        free(name, buffer)
    for pair in range(PAIRS):
        view = part_v.at[pair, place.theirs]
        remote(view, view, part_sent.at[pair], part_arrived.at[0, 0], place.sibling).wait_send()

    @pl.when(section == 1)
    def _():
        inputs.spread_done()
        for step in range(steps):
            remote(d_hid_v.at[step], g_v.at[step], hop_sent.at[step], in_arrived.at[step], place.other_layer).wait_send()

    outputs.collect_done()


def backward(cotangent, weights, gains, kv, prob, saved):
    total = cotangent.shape[0]
    sequences = total // SEQ
    steps = 2 * sequences
    shapes = [
        jax.ShapeDtypeStruct((total, D), BF16),
        jax.ShapeDtypeStruct((SMALL_ROWS, D), F32),
    ] + [jax.ShapeDtypeStruct((total, width), dtype) for _, width, dtype in GRADS]
    widths = {name: (width, dtype) for name, width, dtype in SAVED}
    dma = pltpu.SemaphoreType.DMA
    d_hid, small, *grads = pl.pallas_call(
        functools.partial(backward_kernel, sequences),
        out_shape=shapes,
        in_specs=[ANY] * 5 + [VMEM] + [ANY] * (2 + len(KEPT)),
        out_specs=[ANY, VMEM] + [ANY] * len(GRADS),
        scratch_shapes=[
            pltpu.VMEM((steps, ROWS, D), BF16),
            pltpu.VMEM((steps, ROWS, D), BF16),
            pltpu.VMEM((SEQ, 2 * D), BF16),
            pltpu.VMEM((H, ROWS, SEQ), BF16),
            pltpu.VMEM((D, 3 * D), BF16),
            pltpu.VMEM((D, D), BF16),
            pltpu.VMEM((D, FF), BF16),
            pltpu.VMEM((FF, D), BF16),
            pltpu.VMEM((ROWS, D), F32),
            pltpu.VMEM((ROWS, D), BF16),
            pltpu.VMEM((PAIRS, SEQ, 2 * PAIR), BF16),
            pltpu.VMEM((steps, PAIRS, ROWS, 2 * PAIR), BF16),
        ]
        + [pltpu.VMEM((ROWS, widths[name][0]), widths[name][1]) for name in KEPT]
        + [pltpu.VMEM((ROWS, width), dtype) for _, width, dtype in GRADS]
        + [
            dma((4,)),
            dma((len(KEPT) + 2,)),
            dma((len(GRADS),)),
            dma((sequences,)),
            dma((sequences,)),
            dma((steps,)),
            dma((sequences,)),
            dma((sequences,)),
            dma((sequences,)),
            dma((PAIRS,)),
            dma((steps, PAIRS)),
            dma((steps,)),
        ],
        compiler_params=pltpu.CompilerParams(
            collective_id=2, has_side_effects=True, vmem_limit_bytes=VMEM_LIMIT
        ),
        name="backward",
    )(cotangent, *weights, gains, kv, prob, *[saved[name] for name in KEPT])
    return d_hid, small, dict(zip([name for name, _, _ in GRADS], grads))


UNIT = 16
RAIL = 4 * UNIT
ROOTS = 4
HALF = 2 * RAIL + ROOTS * UNIT
SLAB = 2 * HALF


def reduce_kernel(depth, *refs):
    (gelu, d_down, low, d_up, ctx, d_attn, hid, d_qkv, small) = refs[:9]
    (o_down, o_up, o_out, o_qkv, o_small) = refs[9:14]
    (
        left_v, right_v, p_v, s_v, y_v, rl_v, rr_v, o_v, sm_v, sm_in_v, sm_o_v,
        load_sem, send_sem, recv_sem, out_sem, sm_send, sm_recv,
    ) = refs[14:]
    columns = d_down.shape[1]
    plan = (
        ("down", FF // SLAB, gelu, d_down, o_down),
        ("up", 2 * (FF // D), low, d_up, o_up),
        ("out", 2, ctx, d_attn, o_out),
        ("qkv", 6, hid, d_qkv, o_qkv),
    )
    count = sum(entry[1] for entry in plan)
    section = lax.axis_index("section")
    me = lax.axis_index("dp")
    core = lax.rem(me, 2)
    y = lax.rem(lax.div(me, 2), 2)
    z = lax.div(me, 4)
    sibling = (section, me + 1 - 2 * core)
    partner = (section, me + 2 - 4 * y)
    left = (section, me - 4)
    right = (section, me + 4)

    barrier = pltpu.get_barrier_semaphore()
    pl.semaphore_signal(barrier, inc=1, device_id=sibling, device_id_type=MESH)
    pl.semaphore_signal(barrier, inc=1, device_id=partner, device_id_type=MESH)

    @pl.when(z > 0)
    def _():
        pl.semaphore_signal(barrier, inc=1, device_id=left, device_id_type=MESH)

    @pl.when(z < depth - 1)
    def _():
        pl.semaphore_signal(barrier, inc=1, device_id=right, device_id_type=MESH)

    def at(value, size):
        return pl.ds(pl.multiple_of(value, UNIT), size)

    def load(step, start):
        slot = lax.rem(step, 2)
        if not start:
            pltpu.make_async_copy(gelu.at[:, pl.ds(0, SLAB)], left_v.at[slot], load_sem.at[0, slot]).wait()
            pltpu.make_async_copy(d_down, right_v.at[slot], load_sem.at[1, slot]).wait()
            return
        first = 0
        for name, steps, factor, grad, _ in plan:

            def issue(first=first, name=name, factor=factor, grad=grad):
                index = step - first
                if name == "down":
                    row, column = index, 0
                else:
                    row, column = lax.rem(index, 2), lax.div(index, 2)
                rows = pl.ds(pl.multiple_of(row * SLAB, 128), SLAB)
                cols = pl.ds(pl.multiple_of(column * columns, 128), columns)
                pltpu.make_async_copy(factor.at[:, rows], left_v.at[slot], load_sem.at[0, slot]).start()
                pltpu.make_async_copy(grad.at[:, cols], right_v.at[slot], load_sem.at[1, slot]).start()

            pl.when((step >= first) & (step < first + steps))(issue)
            first += steps

    def out_copy(step, start):
        slot = lax.rem(step, 2)
        if not start:
            pltpu.make_async_copy(o_v.at[0], o_down.at[pl.ds(0, SLAB)], out_sem.at[slot]).wait()
            return
        first = 0
        for name, steps, _, _, result in plan:

            def issue(first=first, name=name, result=result):
                index = step - first
                if name == "down":
                    row, column = index, 0
                else:
                    row, column = lax.rem(index, 2), lax.div(index, 2)
                cols = pl.ds(pl.multiple_of(column * columns, 128), columns)
                pltpu.make_async_copy(o_v.at[step], result.at[at(row * SLAB, SLAB), cols], out_sem.at[slot]).start()

            pl.when((step >= first) & (step < first + steps))(issue)
            first += steps

    def send(kind, step, source, target, arrival, device, compute=None):
        parity = lax.rem(step, 2)
        copy = pltpu.make_async_remote_copy(
            source, target, send_sem.at[kind, parity], arrival, device_id=device, device_id_type=MESH
        )

        @pl.when(step >= 2)
        def _():
            copy.wait_send()

        if compute is not None:
            compute()
        copy.start()

    def finish_send(kind, view):
        for parity in range(2):
            pltpu.make_async_remote_copy(
                view, view, send_sem.at[kind, parity], recv_sem.at[kind, 0], device_id=sibling, device_id_type=MESH
            ).wait_send()

    def arrived(kind, step, view):
        pltpu.make_async_remote_copy(
            view, view, send_sem.at[kind, 0], recv_sem.at[kind, step], device_id=sibling, device_id_type=MESH
        ).wait_recv()

    own = core * HALF
    theirs = HALF - own
    CX, UP, DOWN, SIB_OTHER, YX = range(5)

    def add_into(target, term):
        target[...] = (target[...].astype(F32) + term[...].astype(F32)).astype(target.dtype)

    class Tree:
        def __init__(self, kinds, base, root, reach, size, offset, land, rail):
            self.kinds, self.base, self.root, self.reach = kinds, base, root, reach
            self.size, self.offset, self.land, self.rail = size, offset, land, rail
            self.distance = jnp.abs(z - root)
            self.from_left = (z > 0) & (z <= root)
            self.from_right = (z < depth - 1) & (z >= root)

        def part(self, step):
            return s_v.at[step, at(self.offset, self.size)]

        def total(self, step):
            return o_v.at[step, at(own + self.offset, self.size)]

        def landing(self, buffer, step):
            return buffer.at[step, pl.ds(self.land, self.size)]

        def towards(self, now):
            inward, out_left, out_right, sib = self.kinds
            step = now - self.base - self.reach + self.distance

            @pl.when((step >= 0) & (step < count))
            def _():
                @pl.when(self.from_left)
                def _():
                    arrived(out_left, step, self.landing(rl_v, step))
                    add_into(self.part(step), self.landing(rl_v, step))

                @pl.when(self.from_right)
                def _():
                    arrived(out_right, step, self.landing(rr_v, step))
                    add_into(self.part(step), self.landing(rr_v, step))

                @pl.when(z < self.root)
                def _():
                    send(inward, step, self.part(step), self.landing(rl_v, step), recv_sem.at[out_left, step], right)

                @pl.when(z > self.root)
                def _():
                    send(inward, step, self.part(step), self.landing(rr_v, step), recv_sem.at[out_right, step], left)

                @pl.when(z == self.root)
                def _():
                    if self.rail:
                        self.total(step)[...] = self.part(step)[...]
                    else:
                        view = y_v.at[step, pl.ds(RAIL, UNIT)]
                        send(YX, step, self.part(step), view, recv_sem.at[YX, step], partner)

            if not self.rail:
                late = now - self.base - self.reach - 1

                @pl.when((z == self.root) & (late >= 0) & (late < count))
                def _():
                    view = y_v.at[late, pl.ds(RAIL, UNIT)]
                    arrived(YX, late, view)
                    self.total(late)[...] = (self.part(late)[...].astype(F32) + view[...].astype(F32)).astype(BF16)

        def away(self, now):
            inward, out_left, out_right, sib = self.kinds
            lag = self.base + self.reach + (0 if self.rail else 1)
            step = now - lag - self.distance

            @pl.when((step >= 0) & (step < count))
            def _():
                view = self.total(step)

                @pl.when(z != self.root)
                def _():
                    arrived(inward, step, view)

                @pl.when(self.from_left)
                def _():
                    send(out_left, step, view, view, recv_sem.at[inward, step], left)

                @pl.when(self.from_right)
                def _():
                    send(out_right, step, view, view, recv_sem.at[inward, step], right)

                if self.rail:
                    send(DOWN, step, view, view, recv_sem.at[DOWN, step], partner)
                send(sib, step, view, view, recv_sem.at[sib, step], sibling)

            done = step - 1

            @pl.when((done >= 0) & (done < count))
            def _():
                arrived(sib, done, o_v.at[done, at(theirs + self.offset, self.size)])

        def finish(self):
            inward, out_left, out_right, sib = self.kinds
            view = self.part(0)

            @pl.when(z != self.root)
            def _():
                finish_send(inward, view)

            @pl.when(self.from_left)
            def _():
                finish_send(out_left, view)

            @pl.when(self.from_right)
            def _():
                finish_send(out_right, view)

            finish_send(sib, view)
            if not self.rail:

                @pl.when(z == self.root)
                def _():
                    finish_send(YX, view)

    half_depth = depth // 2
    rail_root = half_depth - 1 + y
    rail = Tree((5, 6, 7, 8), 2, rail_root, half_depth, RAIL, y * RAIL, 0, True)
    line = []
    for index in range(ROOTS):
        root = (2 * index + 1) * depth // (2 * ROOTS)
        kinds = tuple(9 + 4 * index + offset for offset in range(4))
        reach = max(root, depth - 1 - root)
        line.append(Tree(kinds, 1, root, reach, UNIT, 2 * RAIL + index * UNIT, RAIL + index * UNIT, False))
    other_distance = jnp.abs(z - (half_depth - y))
    other = (1 - y) * RAIL

    sm_root = half_depth
    sm_reach = max(sm_root, depth - 1 - sm_root)
    sm_distance = jnp.abs(z - sm_root)

    def sm_copy(kind, source, target, arrival, device):
        return pltpu.make_async_remote_copy(
            source, target, sm_send.at[kind], sm_recv.at[arrival], device_id=device, device_id_type=MESH
        )

    def small_round(now):
        @pl.when(now == 0)
        def _():
            sm_v[...] = small[...]
            sm_copy(0, sm_v, sm_in_v.at[0], 0, sibling).start()

        @pl.when(now == 1)
        def _():
            sm_copy(0, sm_v, sm_in_v.at[0], 0, sibling).wait()
            sm_v[...] = sm_v[...] + sm_in_v[0]

        @pl.when(now == 1 + sm_reach - sm_distance)
        def _():
            @pl.when((z > 0) & (z <= sm_root))
            def _():
                sm_copy(1, sm_v, sm_in_v.at[1], 1, sibling).wait_recv()
                sm_v[...] = sm_v[...] + sm_in_v[1]

            @pl.when((z < depth - 1) & (z >= sm_root))
            def _():
                sm_copy(1, sm_v, sm_in_v.at[2], 2, sibling).wait_recv()
                sm_v[...] = sm_v[...] + sm_in_v[2]

            @pl.when(z < sm_root)
            def _():
                sm_copy(1, sm_v, sm_in_v.at[1], 1, right).start()

            @pl.when(z > sm_root)
            def _():
                sm_copy(1, sm_v, sm_in_v.at[2], 2, left).start()

            @pl.when(z == sm_root)
            def _():
                sm_copy(1, sm_v, sm_in_v.at[3], 3, partner).start()

        @pl.when((now == 2 + sm_reach) & (z == sm_root))
        def _():
            sm_copy(1, sm_v, sm_in_v.at[3], 3, partner).wait_recv()
            sm_o_v[...] = sm_v[...] + sm_in_v[3]

        @pl.when(now == 2 + sm_reach + sm_distance)
        def _():
            @pl.when(z != sm_root)
            def _():
                sm_copy(2, sm_o_v, sm_o_v, 4, sibling).wait_recv()

            @pl.when((z > 0) & (z <= sm_root))
            def _():
                sm_copy(2, sm_o_v, sm_o_v, 4, left).start()

            @pl.when((z < depth - 1) & (z >= sm_root))
            def _():
                sm_copy(3, sm_o_v, sm_o_v, 4, right).start()

    def small_finish():
        sm_copy(1, sm_v, sm_in_v.at[1], 1, sibling).wait_send()

        @pl.when((z > 0) & (z <= sm_root))
        def _():
            sm_copy(2, sm_o_v, sm_o_v, 4, left).wait_send()

        @pl.when((z < depth - 1) & (z >= sm_root))
        def _():
            sm_copy(3, sm_o_v, sm_o_v, 4, right).wait_send()

        o_small[...] = sm_o_v[...]

    load(jnp.int32(0), True)
    neighbours = 2 + (z > 0).astype(jnp.int32) + (z < depth - 1).astype(jnp.int32)
    pl.semaphore_wait(barrier, neighbours)

    out_lag = max(
        [2 + half_depth + half_depth + 2] + [2 + tree.reach + max(tree.root, depth - 1 - tree.root) + 1 for tree in line]
    )

    def one_round(now, carry):
        slot = lax.rem(now, 2)

        @pl.when(now < count)
        def _():
            load(now, False)

            @pl.when(now + 1 < count)
            def _():
                load(now + 1, True)

            def form():
                p_v[slot] = dot_tn(left_v[slot], right_v[slot]).astype(BF16)

            view = p_v.at[slot, at(theirs, HALF)]
            send(CX, now, view, s_v.at[now], recv_sem.at[CX, now], sibling, form)

        step = now - 1

        @pl.when((step >= 0) & (step < count))
        def _():
            arrived(CX, step, s_v.at[step])
            add_into(s_v.at[step], p_v.at[1 - slot, at(own, HALF)])
            view = s_v.at[step, at(other, RAIL)]
            send(UP, step, view, y_v.at[step, pl.ds(0, RAIL)], recv_sem.at[UP, step], partner)

        for tree in line:
            tree.towards(now)

        step_up = now - 2

        @pl.when((step_up >= 0) & (step_up < count))
        def _():
            view = y_v.at[step_up, pl.ds(0, RAIL)]
            arrived(UP, step_up, view)
            add_into(rail.part(step_up), view)

        rail.towards(now)
        rail.away(now)
        for tree in line:
            tree.away(now)

        step_down = now - 2 - half_depth - other_distance - 1

        @pl.when((step_down >= 0) & (step_down < count))
        def _():
            view = o_v.at[step_down, at(own + other, RAIL)]
            arrived(DOWN, step_down, view)
            send(SIB_OTHER, step_down, view, view, recv_sem.at[SIB_OTHER, step_down], sibling)

        step_sib = step_down - 1

        @pl.when((step_sib >= 0) & (step_sib < count))
        def _():
            arrived(SIB_OTHER, step_sib, o_v.at[step_sib, at(theirs + other, RAIL)])

        small_round(now)

        step_out = now - out_lag

        @pl.when(step_out >= 0)
        def _():
            @pl.when(step_out >= 2)
            def _():
                out_copy(step_out, False)

            out_copy(step_out, True)

        return carry

    lax.fori_loop(0, count + out_lag, one_round, 0)
    out_copy(jnp.int32(0), False)
    out_copy(jnp.int32(1), False)
    finish_send(CX, s_v.at[0])
    finish_send(UP, rail.part(0))
    finish_send(DOWN, rail.part(0))
    finish_send(SIB_OTHER, rail.part(0))
    rail.finish()
    for tree in line:
        tree.finish()
    small_finish()


def reduce_gradients(depth, gelu, d_down, low, d_up, ctx, d_attn, hid, d_qkv, small):
    rows, columns = d_down.shape
    count = FF // SLAB + 2 * (FF // D) + 8
    kinds = 9 + 4 * ROOTS
    return pl.pallas_call(
        functools.partial(reduce_kernel, depth),
        out_shape=[
            jax.ShapeDtypeStruct((FF, columns), BF16),
            jax.ShapeDtypeStruct((D, 4 * columns), BF16),
            jax.ShapeDtypeStruct((D, columns), BF16),
            jax.ShapeDtypeStruct((D, 3 * columns), BF16),
            jax.ShapeDtypeStruct((SMALL_ROWS, small.shape[-1]), F32),
        ],
        in_specs=[ANY] * 8 + [VMEM],
        out_specs=[ANY] * 4 + [VMEM],
        scratch_shapes=[
            pltpu.VMEM((2, rows, SLAB), BF16),
            pltpu.VMEM((2, rows, columns), BF16),
            pltpu.VMEM((2, SLAB, columns), BF16),
            pltpu.VMEM((count, HALF, columns), BF16),
            pltpu.VMEM((count, RAIL + UNIT, columns), BF16),
            pltpu.VMEM((count, RAIL + ROOTS * UNIT, columns), BF16),
            pltpu.VMEM((count, RAIL + ROOTS * UNIT, columns), BF16),
            pltpu.VMEM((count, SLAB, columns), BF16),
            pltpu.VMEM((SMALL_ROWS, small.shape[-1]), F32),
            pltpu.VMEM((4, SMALL_ROWS, small.shape[-1]), F32),
            pltpu.VMEM((SMALL_ROWS, small.shape[-1]), F32),
            pltpu.SemaphoreType.DMA((2, 2)),
            pltpu.SemaphoreType.DMA((kinds, 2)),
            pltpu.SemaphoreType.DMA((kinds, count)),
            pltpu.SemaphoreType.DMA((2,)),
            pltpu.SemaphoreType.DMA((4,)),
            pltpu.SemaphoreType.DMA((5,)),
        ],
        compiler_params=pltpu.CompilerParams(
            collective_id=0, has_side_effects=True, vmem_limit_bytes=VMEM_LIMIT
        ),
        name="reduce_gradients",
    )(gelu, d_down, low, d_up, ctx, d_attn, hid, d_qkv, small)


def shards(
    tokens, segments, lengths, cotangent, qkv_weight, qv_bias, out_weight, out_biases,
    norm_gains, norm_shifts, up_weight, up_bias, down_weight,
):
    weights = (qkv_weight, out_weight, up_weight, down_weight)
    params = (qv_bias, out_biases, norm_gains, norm_shifts, up_bias)
    act, kv, prob, saved = forward(tokens, weights, segments, lengths, params)
    d_hid, small, grads = backward(cotangent, weights, norm_gains, kv, prob, saved)
    *large, small = reduce_gradients(
        lax.axis_size("dp") // 4, saved["gelu"], grads["d_down"], saved["low"], grads["d_up"],
        saved["ctx"], grads["d_attn"], saved["hid"], grads["d_qkv"], small,
    )
    g_down, g_up, g_out, g_qkv = [value.astype(F32)[None] for value in large]
    small = small[None]
    return (
        act[None], d_hid[None], g_qkv, small[:, 0:2], g_out, small[:, 2:4], small[:, 4:6], small[:, 6:8],
        g_up, small[:, 8:12].reshape(1, FF), g_down,
    )


def solution(mesh):
    return jax.shard_map(
        shards,
        mesh=mesh,
        in_specs=(
            P("dp", None), P("dp", None), P("dp"), P("dp", None),
            P("section", None, None), P("section", None, None), P("section", None, None), P("section", None, None),
            P("section", None, None), P("section", None, None), P("section", None, None), P("section", None),
            P("section", None, None),
        ),
        out_specs=(
            P("section", "dp", None), P("section", "dp", None),
            P("section", None, None), P("section", None, None), P("section", None, None), P("section", None, None),
            P("section", None, None), P("section", None, None), P("section", None, None), P("section", None),
            P("section", None, None),
        ),
        check_vma=False,
    )
```

```python
import functools
import math

import jax
import jax.numpy as jnp
from jax import lax
from jax.experimental import pallas as pl
from jax.experimental.pallas import tpu as pltpu
from jax.sharding import PartitionSpec as P

D = 768
H = 12
HD = 64
FF = 3072
SEQ = 512
MICRO = 2
PAIRS = H // 2
PAIR = 2 * HD
GROUP = PAIRS // 2

EPSILON = 1e-05
SCORE_SCALE = 0.125
NEG_FILL = -1e30
F32 = jnp.float32
BF16 = jnp.bfloat16
VMEM_LIMIT = 60 << 20
REDUCE_LIMIT = 44 << 20
MESH = pl.DeviceIdType.MESH

ANY = pl.BlockSpec(memory_space=pl.ANY)
VMEM = pl.BlockSpec(memory_space=pltpu.VMEM)
SMEM = pl.BlockSpec(memory_space=pltpu.SMEM)


def dot_nn(left, right):
    return lax.dot_general(left, right, (((1,), (0,)), ((), ())), preferred_element_type=F32)


def dot_nt(left, right):
    return lax.dot_general(left, right, (((1,), (1,)), ((), ())), preferred_element_type=F32)


def dot_tn(left, right):
    return lax.dot_general(left, right, (((0,), (0,)), ((), ())), preferred_element_type=F32)


def begin(source, target, sem):
    copy = pltpu.make_async_copy(source, target, sem)
    copy.start()
    return copy


def gelu_and_slope(u):
    normal_cdf = 0.5 + 0.5 * lax.erf(u * (1.0 / math.sqrt(2.0)))
    bell = jnp.exp((-0.5 * u) * u)
    return u * normal_cdf, normal_cdf + (u * (1.0 / math.sqrt(2.0 * math.pi))) * bell


def normalize(resid):
    average = jnp.mean(resid, axis=-1, keepdims=True)
    centred = resid - average
    variance = jnp.mean(centred * centred, axis=-1, keepdims=True)
    inverse = lax.rsqrt(variance + EPSILON)
    return centred * inverse, inverse


def norm_back(grad_out, scaled, inverse, gain):
    weighted = grad_out * gain
    first_mean = jnp.mean(weighted, axis=-1, keepdims=True)
    second_mean = jnp.mean(weighted * scaled, axis=-1, keepdims=True)
    return inverse * (weighted - first_mean - scaled * second_mean)


def half_mask(which):
    lane = lax.broadcasted_iota(jnp.int32, (1, PAIR), 1)
    return ((lane // HD) == which).astype(F32).astype(BF16)


ROWS = SEQ // 2
SAVED = (
    ("hid", D, BF16),
    ("q", D, BF16),
    ("linv", D, F32),
    ("ctx", D, BF16),
    ("xh1", D, BF16),
    ("inv1", 128, F32),
    ("low", D, BF16),
    ("gelu", FF, BF16),
    ("slope", FF, BF16),
    ("xh2", D, BF16),
    ("inv2", 128, F32),
)
GRADS = (("d_down", D, BF16), ("d_up", FF, BF16), ("d_attn", D, BF16), ("d_qkv", 3 * D, BF16))
SMALL_ROWS = 16


class Place:
    def __init__(self):
        self.section = lax.axis_index("section")
        self.me = lax.axis_index("dp")
        self.core = lax.rem(self.me, 2)
        self.sibling = (self.section, self.me + 1 - 2 * self.core)
        self.other_layer = (1 - self.section, self.me)
        self.own = pl.ds(pl.multiple_of(self.core * ROWS, ROWS), ROWS)
        self.theirs = pl.ds(pl.multiple_of(ROWS - self.core * ROWS, ROWS), ROWS)

    def greet(self):
        barrier = pltpu.get_barrier_semaphore()
        for device in (self.sibling, self.other_layer):
            pl.semaphore_signal(barrier, inc=1, device_id=device, device_id_type=MESH)
        pl.semaphore_wait(barrier, 2)

    def is_mine(self, step, sequences):
        return lax.div(step, sequences) == self.core


def remote(source, target, send_sem, recv_sem, device):
    return pltpu.make_async_remote_copy(source, target, send_sem, recv_sem, device_id=device, device_id_type=MESH)


class Rows:
    def __init__(self, place, sequences, array, steps, local, sent, arrived):
        self.place, self.sequences, self.array, self.steps = place, sequences, array, steps
        self.local, self.sent, self.arrived = local, sent, arrived

    def part(self, sequence, core):
        return self.array.at[pl.ds(pl.multiple_of(sequence * SEQ + core * ROWS, ROWS), ROWS)]

    def spread(self):
        place = self.place
        for sequence in range(self.sequences):
            step = place.core * self.sequences + sequence
            target = self.steps.at[step]
            pltpu.make_async_copy(self.part(sequence, place.core), target, self.local.at[sequence]).start()
            remote(
                self.part(sequence, 1 - place.core), target, self.sent.at[sequence], self.arrived.at[step], place.sibling
            ).start()

    def spread_done(self):
        for sequence in range(self.sequences):
            view = self.steps.at[0]
            remote(view, view, self.sent.at[sequence], self.arrived.at[0], self.place.sibling).wait_send()

    def await_step(self, step, spread):
        mine = spread & self.place.is_mine(step, self.sequences)
        view = self.steps.at[step]

        @pl.when(mine)
        def _():
            pltpu.make_async_copy(view, view, self.local.at[lax.rem(step, self.sequences)]).wait()

        @pl.when(jnp.logical_not(mine))
        def _():
            remote(view, view, self.sent.at[0], self.arrived.at[step], self.place.sibling).wait_recv()

    def collect(self, step):
        sequence = lax.rem(step, self.sequences)
        target = self.part(sequence, self.place.core)
        mine = self.place.is_mine(step, self.sequences)

        @pl.when(mine)
        def _():
            pltpu.make_async_copy(self.steps.at[step], target, self.local.at[sequence]).start()

        @pl.when(jnp.logical_not(mine))
        def _():
            remote(
                self.steps.at[step], target, self.sent.at[sequence], self.arrived.at[sequence], self.place.sibling
            ).start()

    def collect_done(self):
        for sequence in range(self.sequences):
            view = self.steps.at[0]
            pltpu.make_async_copy(view, view, self.local.at[sequence]).wait()
            remote(view, view, self.sent.at[sequence], self.arrived.at[sequence], self.place.sibling).wait()


def forward_kernel(sequences, *refs):
    (tok, wqkv, wo, wu, wd, segs, lens, qv_bias, out_biases, gains, shifts, up_bias) = refs[:12]
    act_out, kv_out, prob_out = refs[12:15]
    count = len(SAVED)
    outs = dict(zip([name for name, _, _ in SAVED], refs[15 : 15 + count]))
    (
        h_v, act_v, kv_v, p_v, wqkv_v, wo_v, wu_v, wd_v, bias_v, acc_v, seg_own, seg_their,
        q_v, linv_v, ctx_v, xh1_v, inv1_v, low_v, gelu_v, slope_v, xh2_v, inv2_v,
        w_sem, save_sem, p_sem, in_local, in_sent, in_arrived, out_local, out_sent, out_arrived,
        kv_sent, kv_arrived, kv_save, seg_sem, hop_sent, hid_save,
    ) = refs[15 + count :]
    place = Place()
    section = place.section
    steps = 2 * sequences
    names = [name for name, _, _ in SAVED]
    inputs = Rows(place, sequences, tok, h_v, in_local, in_sent, in_arrived)
    outputs = Rows(place, sequences, act_out, act_v, out_local, out_sent, out_arrived)

    position = lax.broadcasted_iota(jnp.int32, (1, SEQ), 1)
    for sequence in range(sequences):
        seg_own[sequence, 0:1, :] = segs[sequence : sequence + 1, :].astype(F32)
        seg_own[sequence, 1:2, :] = (position < lens[sequence]).astype(F32)
        seg_own[sequence, 2:8, :] = jnp.zeros((6, SEQ), F32)
    w_first = [begin(wqkv.at[0, :, pl.ds(block * D, D)], wqkv_v.at[:, pl.ds(block * D, D)], w_sem.at[block]) for block in (1, 2, 0)]
    place.greet()
    seg_copy = remote(seg_own, seg_their, seg_sem.at[0], seg_sem.at[1], place.sibling)
    seg_copy.start()

    @pl.when(section == 0)
    def _():
        inputs.spread()

    w_rest = [begin(wo.at[0], wo_v, w_sem.at[3]), begin(wu.at[0], wu_v, w_sem.at[4]), begin(wd.at[0], wd_v, w_sem.at[5])]

    def save(name, buffer, step):
        target = outs[name].at[pl.ds(pl.multiple_of(step * ROWS, ROWS), ROWS)]
        pltpu.make_async_copy(buffer, target, save_sem.at[names.index(name)]).start()

    def free(name, buffer):
        pltpu.make_async_copy(buffer, buffer, save_sem.at[names.index(name)]).wait()

    def free_prob():
        for group in range(2):
            view = p_v.at[pl.ds(group * 2 * GROUP, 2 * GROUP)]
            pltpu.make_async_copy(view, view, p_sem.at[group]).wait()

    reused = (
        ("q", q_v), ("linv", linv_v), ("ctx", ctx_v), ("xh1", xh1_v), ("inv1", inv1_v), ("low", low_v),
        ("gelu", gelu_v), ("slope", slope_v), ("xh2", xh2_v), ("inv2", inv2_v),
    )

    def one_step(step, carry):
        inputs.await_step(step, section == 0)
        target = outs["hid"].at[pl.ds(pl.multiple_of(step * ROWS, ROWS), ROWS)]
        pltpu.make_async_copy(h_v.at[step], target, hid_save.at[step]).start()
        hidden = h_v[step]
        for block in (1, 2):

            @pl.when(step == 0)
            def _():
                w_first[block - 1].wait()

            proj = dot_nn(hidden, wqkv_v[:, block * D : (block + 1) * D])
            if block == 2:
                proj = proj + qv_bias[0, 1:2, :]
            cols = pl.ds((block - 1) * D, D)
            kv_v[step, place.own, cols] = proj.astype(BF16)
            view = kv_v.at[step, place.own, cols]
            remote(view, view, kv_sent.at[step, block - 1], kv_arrived.at[step, block - 1], place.sibling).start()

        @pl.when(step == 0)
        def _():
            w_first[2].wait()

        @pl.when(step > 0)
        def _():
            for name, buffer in reused:
                free(name, buffer)
            free_prob()

        q_v[...] = (dot_nn(hidden, wqkv_v[:, 0:D]) + qv_bias[0, 0:1, :]).astype(BF16)
        save("q", q_v, step)

        @pl.when(step == 0)
        def _():
            seg_copy.wait()

        sequence = lax.rem(step, sequences)
        mine = jnp.where(place.is_mine(step, sequences), 1.0, 0.0)
        key_rows = mine * seg_own[sequence] + (1.0 - mine) * seg_their[sequence]
        query_row = mine * seg_own[sequence, 0:1, place.own] + (1.0 - mine) * seg_their[sequence, 0:1, place.own]
        query_seg = jnp.transpose(jnp.broadcast_to(query_row, (128, ROWS)))
        query = lax.broadcasted_iota(jnp.int32, (ROWS, 128), 0) + place.core * ROWS
        key = lax.broadcasted_iota(jnp.int32, (ROWS, 128), 1)
        for tile in range(SEQ // 128):
            cols = slice(tile * 128, (tile + 1) * 128)
            visible = (key_rows[1:2, cols] > 0.5) | (key + tile * 128 == query)
            bias_v[:, cols] = jnp.where((query_seg == key_rows[0:1, cols]) & visible, 0.0, NEG_FILL)

        for block in range(2):
            view = kv_v.at[step, place.theirs, pl.ds(block * D, D)]
            remote(view, view, kv_sent.at[step, block], kv_arrived.at[step, block], place.sibling).wait_recv()
        pltpu.make_async_copy(kv_v.at[step], kv_out.at[step], kv_save.at[step]).start()

        def pair_step(pair):
            at = pl.multiple_of(pair * PAIR, PAIR)
            q2 = q_v[:, pl.ds(at, PAIR)] * SCORE_SCALE
            k2 = kv_v[step, :, pl.ds(at, PAIR)]
            v2 = kv_v[step, :, pl.ds(at + D, PAIR)]
            total, inverses = None, []
            for head in range(2):
                mask = half_mask(head)
                scores = dot_nt(q2, k2 * mask) + bias_v[...]
                exp_vals = jnp.exp(scores - jnp.max(scores, axis=-1, keepdims=True))
                inverses.append(1.0 / jnp.sum(exp_vals, axis=-1, keepdims=True))
                weight = exp_vals.astype(BF16)
                p_v[pair * 2 + head] = weight
                part = dot_nn(weight, v2 * mask)
                total = part if total is None else total + part
            lane = lax.broadcasted_iota(jnp.int32, (1, PAIR), 1)
            inverse = jnp.where(lane < HD, inverses[0], inverses[1])
            linv_v[:, pl.ds(at, PAIR)] = inverse
            ctx_v[:, pl.ds(at, PAIR)] = (total * inverse).astype(BF16)

        def group_step(group, carry):
            for index in range(GROUP):
                pair_step(group * GROUP + index)
            target = prob_out.at[step, pl.ds(group * 2 * GROUP, 2 * GROUP)]
            pltpu.make_async_copy(p_v.at[pl.ds(group * 2 * GROUP, 2 * GROUP)], target, p_sem.at[group]).start()
            return carry

        lax.fori_loop(0, 2, group_step, 0)
        save("linv", linv_v, step)
        save("ctx", ctx_v, step)

        @pl.when(step == 0)
        def _():
            w_rest[0].wait()

        resid = hidden.astype(F32) + (dot_nn(ctx_v[...], wo_v[...]) + out_biases[0, 0:1, :])
        scaled, inverse = normalize(resid)
        xh1_v[...] = scaled.astype(BF16)
        inv1_v[...] = jnp.broadcast_to(inverse, (ROWS, 128))
        normed = scaled * gains[0, 0:1, :] + shifts[0, 0:1, :]
        low_v[...] = normed.astype(BF16)
        acc_v[...] = normed + out_biases[0, 1:2, :]
        save("xh1", xh1_v, step)
        save("inv1", inv1_v, step)
        save("low", low_v, step)

        @pl.when(step == 0)
        def _():
            w_rest[1].wait()
            w_rest[2].wait()

        width = 1024
        for chunk in range(FF // width):
            cols = slice(chunk * width, (chunk + 1) * width)
            up = dot_nn(low_v[...], wu_v[:, cols]) + up_bias[0:1, cols]
            gelu, slope = gelu_and_slope(up)
            gelu = gelu.astype(BF16)
            gelu_v[:, cols] = gelu
            slope_v[:, cols] = slope.astype(BF16)
            acc_v[...] += dot_nn(gelu, wd_v[cols, :])
        save("gelu", gelu_v, step)
        save("slope", slope_v, step)
        scaled, inverse = normalize(acc_v[...])
        act_v[step] = (scaled * gains[0, 1:2, :] + shifts[0, 1:2, :]).astype(BF16)

        @pl.when(section == 0)
        def _():
            remote(act_v.at[step], h_v.at[step], hop_sent.at[step], in_arrived.at[step], place.other_layer).start()

        outputs.collect(step)
        xh2_v[...] = scaled.astype(BF16)
        inv2_v[...] = jnp.broadcast_to(inverse, (ROWS, 128))
        save("xh2", xh2_v, step)
        save("inv2", inv2_v, step)
        return carry

    lax.fori_loop(0, steps, one_step, 0)
    for name, buffer in reused:
        free(name, buffer)
    for step in range(steps):
        pltpu.make_async_copy(h_v.at[step], h_v.at[step], hid_save.at[step]).wait()
        pltpu.make_async_copy(kv_v.at[step], kv_out.at[step], kv_save.at[step]).wait()
        for block in range(2):
            view = kv_v.at[step, place.own, pl.ds(block * D, D)]
            remote(view, view, kv_sent.at[step, block], kv_arrived.at[step, block], place.sibling).wait_send()
    free_prob()

    @pl.when(section == 0)
    def _():
        inputs.spread_done()
        for step in range(steps):
            remote(act_v.at[step], h_v.at[step], hop_sent.at[step], in_arrived.at[step], place.other_layer).wait_send()

    outputs.collect_done()


def forward(tokens, weights, segments, lengths, params):
    total = tokens.shape[0]
    sequences = total // SEQ
    steps = 2 * sequences
    shapes = [
        jax.ShapeDtypeStruct((total, D), BF16),
        jax.ShapeDtypeStruct((steps, SEQ, 2 * D), BF16),
        jax.ShapeDtypeStruct((steps, H, ROWS, SEQ), BF16),
    ] + [jax.ShapeDtypeStruct((total, width), dtype) for _, width, dtype in SAVED]
    dma = pltpu.SemaphoreType.DMA
    act, kv, prob, *saved = pl.pallas_call(
        functools.partial(forward_kernel, sequences),
        out_shape=shapes,
        in_specs=[ANY] * 5 + [VMEM, SMEM] + [VMEM] * 5,
        out_specs=[ANY] * len(shapes),
        scratch_shapes=[
            pltpu.VMEM((steps, ROWS, D), BF16),
            pltpu.VMEM((steps, ROWS, D), BF16),
            pltpu.VMEM((steps, SEQ, 2 * D), BF16),
            pltpu.VMEM((H, ROWS, SEQ), BF16),
            pltpu.VMEM((D, 3 * D), BF16),
            pltpu.VMEM((D, D), BF16),
            pltpu.VMEM((D, FF), BF16),
            pltpu.VMEM((FF, D), BF16),
            pltpu.VMEM((ROWS, SEQ), F32),
            pltpu.VMEM((ROWS, D), F32),
            pltpu.VMEM((sequences, 8, SEQ), F32),
            pltpu.VMEM((sequences, 8, SEQ), F32),
        ]
        + [pltpu.VMEM((ROWS, width), dtype) for name, width, dtype in SAVED if name != "hid"]
        + [
            dma((6,)),
            dma((len(SAVED),)),
            dma((2,)),
            dma((sequences,)),
            dma((sequences,)),
            dma((steps,)),
            dma((sequences,)),
            dma((sequences,)),
            dma((sequences,)),
            dma((steps, 2)),
            dma((steps, 2)),
            dma((steps,)),
            dma((2,)),
            dma((steps,)),
            dma((steps,)),
        ],
        compiler_params=pltpu.CompilerParams(
            collective_id=1, has_side_effects=True, vmem_limit_bytes=VMEM_LIMIT
        ),
        name="forward",
    )(tokens, *weights, segments, lengths, *params)
    return act, kv, prob, dict(zip([name for name, _, _ in SAVED], saved))


KEPT = ("q", "linv", "ctx", "xh1", "inv1", "slope", "xh2", "inv2")


def backward_kernel(sequences, *refs):
    (cot, wqkv, wo, wu, wd, gains, kv_in, prob_in) = refs[:8]
    ins = dict(zip(KEPT, refs[8:16]))
    d_hid_out, small_out = refs[16:18]
    outs = dict(zip([name for name, _, _ in GRADS], refs[18:22]))
    (
        g_v, d_hid_v, kv_v, p_v, wqkv_v, wo_v, wu_v, wd_v, acc_v, d_ctx_v, part_v, their_v,
        q_v, linv_v, ctx_v, xh1_v, inv1_v, slope_v, xh2_v, inv2_v,
        d_down_v, d_up_v, d_attn_v, d_qkv_v,
        w_sem, load_sem, save_sem, in_local, in_sent, in_arrived, out_local, out_sent, out_arrived,
        part_sent, part_arrived, hop_sent,
    ) = refs[22:]
    place = Place()
    section = place.section
    steps = 2 * sequences
    grad_names = [name for name, _, _ in GRADS]
    inputs = Rows(place, sequences, cot, g_v, in_local, in_sent, in_arrived)
    outputs = Rows(place, sequences, d_hid_out, d_hid_v, out_local, out_sent, out_arrived)
    buffers = dict(zip(KEPT, (q_v, linv_v, ctx_v, xh1_v, inv1_v, slope_v, xh2_v, inv2_v)))

    def at_step(array, step):
        return array.at[pl.ds(pl.multiple_of(step * ROWS, ROWS), ROWS)]

    def fetch(names, step):
        for name in names:
            if name == "kv":
                pltpu.make_async_copy(kv_in.at[step], kv_v, load_sem.at[len(KEPT)]).start()
            elif name == "prob":
                pltpu.make_async_copy(prob_in.at[step], p_v, load_sem.at[len(KEPT) + 1]).start()
            else:
                source = at_step(ins[name], step)
                pltpu.make_async_copy(source, buffers[name], load_sem.at[KEPT.index(name)]).start()

    def fetched(*names):
        for name in names:
            if name == "kv":
                pltpu.make_async_copy(kv_v, kv_v, load_sem.at[len(KEPT)]).wait()
            elif name == "prob":
                pltpu.make_async_copy(p_v, p_v, load_sem.at[len(KEPT) + 1]).wait()
            else:
                pltpu.make_async_copy(buffers[name], buffers[name], load_sem.at[KEPT.index(name)]).wait()

    def fetch_next(names, step):
        @pl.when(step + 1 < steps)
        def _():
            fetch(names, step + 1)

    def save(name, buffer, step):
        pltpu.make_async_copy(buffer, at_step(outs[name], step), save_sem.at[grad_names.index(name)]).start()

    def free(name, buffer):
        pltpu.make_async_copy(buffer, buffer, save_sem.at[grad_names.index(name)]).wait()

    def free_before(name, buffer, step):
        @pl.when(step > 0)
        def _():
            free(name, buffer)

    def when_first(step, copies):
        @pl.when(step == 0)
        def _():
            for copy in copies:
                copy.wait()

    def free_parts():
        for group in range(2):
            view = part_v.at[pl.ds(group * GROUP, GROUP), place.theirs]
            remote(view, view, part_sent.at[group], part_arrived.at[0, 0], place.sibling).wait_send()

    place.greet()

    @pl.when(section == 1)
    def _():
        inputs.spread()

    first = jnp.int32(0)
    fetch(("xh2", "inv2"), first)
    get_wd = begin(wd.at[0], wd_v, w_sem.at[0])
    fetch(("slope",), first)
    get_wu = begin(wu.at[0], wu_v, w_sem.at[1])
    fetch(("xh1", "inv1"), first)
    get_wo = begin(wo.at[0], wo_v, w_sem.at[2])
    fetch(("q", "linv", "ctx", "kv", "prob"), first)
    get_wqkv = begin(wqkv.at[0], wqkv_v, w_sem.at[3])
    small_out[...] = jnp.zeros_like(small_out)

    def column_sum(value):
        return jnp.sum(value, axis=0, keepdims=True)

    def one_step(step, carry):
        inputs.await_step(step, section == 1)
        fetched("xh2", "inv2")
        grad = g_v[step].astype(F32)
        scaled = xh2_v[...].astype(F32)
        small_out[5:6, :] += column_sum(grad * scaled)
        small_out[7:8, :] += column_sum(grad)
        d_r2 = norm_back(grad, scaled, inv2_v[:, 0:1], gains[0, 1:2, :])
        d_down = d_r2.astype(BF16)
        free_before("d_down", d_down_v, step)
        d_down_v[...] = d_down
        small_out[3:4, :] += column_sum(d_down.astype(F32))
        acc_v[...] = d_r2
        save("d_down", d_down_v, step)
        fetch_next(("xh2", "inv2"), step)
        fetched("slope")
        when_first(step, (get_wd, get_wu))
        free_before("d_up", d_up_v, step)
        for chunk in range(FF // D):
            cols = slice(chunk * D, (chunk + 1) * D)
            d_up = (dot_nt(d_down_v[...], wd_v[cols, :]) * slope_v[:, cols].astype(F32)).astype(BF16)
            d_up_v[:, cols] = d_up
            small_out[8 + chunk : 9 + chunk, :] += column_sum(d_up.astype(F32))
            acc_v[...] += dot_nt(d_up, wu_v[:, cols])
        save("d_up", d_up_v, step)
        fetch_next(("slope",), step)
        fetched("xh1", "inv1")
        d_normed = acc_v[...]
        scaled = xh1_v[...].astype(F32)
        small_out[4:5, :] += column_sum(d_normed * scaled)
        small_out[6:7, :] += column_sum(d_normed)
        d_r1 = norm_back(d_normed, scaled, inv1_v[:, 0:1], gains[0, 0:1, :])
        d_attn = d_r1.astype(BF16)
        free_before("d_attn", d_attn_v, step)
        d_attn_v[...] = d_attn
        small_out[2:3, :] += column_sum(d_attn.astype(F32))
        acc_v[...] = d_r1
        save("d_attn", d_attn_v, step)
        fetch_next(("xh1", "inv1"), step)
        when_first(step, (get_wo,))
        fetched("q", "linv", "ctx", "kv", "prob")
        d_ctx_v[...] = (dot_nt(d_attn_v[...], wo_v[...]) * linv_v[...]).astype(BF16)
        free_before("d_qkv", d_qkv_v, step)

        @pl.when(step > 0)
        def _():
            free_parts()

        def pair_step(pair):
            at = pl.multiple_of(pair * PAIR, PAIR)
            q2 = q_v[:, pl.ds(at, PAIR)] * SCORE_SCALE
            k2 = kv_v[:, pl.ds(at, PAIR)]
            v2 = kv_v[:, pl.ds(at + D, PAIR)]
            dc2 = d_ctx_v[:, pl.ds(at, PAIR)]
            inner = dc2.astype(F32) * ctx_v[:, pl.ds(at, PAIR)].astype(F32)
            d_q, d_k, d_v = None, None, None
            for head in range(2):
                mask = half_mask(head)
                dc_own = dc2 * mask
                weight = p_v[pair * 2 + head]
                row_inner = jnp.sum(inner * mask.astype(F32), axis=-1, keepdims=True)
                d_prob = dot_nt(dc_own, v2)
                d_score = (weight.astype(F32) * (d_prob - row_inner)).astype(BF16)
                one_v = dot_tn(dc_own, weight)
                one_k = dot_tn(q2 * mask, d_score)
                one_q = dot_nn(d_score, k2 * mask)
                d_v = one_v if d_v is None else d_v + one_v
                d_k = one_k if d_k is None else d_k + one_k
                d_q = one_q if d_q is None else d_q + one_q
            d_qkv_v[:, pl.ds(at, PAIR)] = (d_q * SCORE_SCALE).astype(BF16)
            part_v[pair, :, 0:PAIR] = jnp.transpose(d_k).astype(BF16)
            part_v[pair, :, PAIR : 2 * PAIR] = jnp.transpose(d_v).astype(BF16)

        def group_step(group, carry):
            for index in range(GROUP):
                pair_step(group * GROUP + index)
            pairs = pl.ds(group * GROUP, GROUP)
            remote(
                part_v.at[pairs, place.theirs], their_v.at[step, pairs], part_sent.at[group],
                part_arrived.at[step, group], place.sibling,
            ).start()
            return carry

        lax.fori_loop(0, 2, group_step, 0)
        fetch_next(("q", "linv", "ctx", "kv", "prob"), step)
        when_first(step, (get_wqkv,))
        d_query = d_qkv_v[:, 0:D]
        acc_v[...] += dot_nt(d_query, wqkv_v[:, 0:D])
        small_out[0:1, :] += column_sum(d_query.astype(F32))
        for group in range(2):
            start = group * GROUP
            view = their_v.at[step, pl.ds(start, GROUP)]
            remote(view, view, part_sent.at[group], part_arrived.at[step, group], place.sibling).wait_recv()
            for pair in range(start, start + GROUP):
                total = part_v[pair, place.own, :].astype(F32) + their_v[step, pair].astype(F32)
                at = pair * PAIR
                d_qkv_v[:, D + at : D + at + PAIR] = total[:, 0:PAIR].astype(BF16)
                d_qkv_v[:, 2 * D + at : 2 * D + at + PAIR] = total[:, PAIR : 2 * PAIR].astype(BF16)
            keys = slice(D + start * PAIR, D + (start + GROUP) * PAIR)
            values = slice(2 * D + start * PAIR, 2 * D + (start + GROUP) * PAIR)
            d_hid = acc_v[...] + dot_nt(d_qkv_v[:, keys], wqkv_v[:, keys]) + dot_nt(d_qkv_v[:, values], wqkv_v[:, values])
            if start == 0:
                acc_v[...] = d_hid
            else:
                d_hid_v[step] = d_hid.astype(BF16)

        @pl.when(section == 1)
        def _():
            remote(d_hid_v.at[step], g_v.at[step], hop_sent.at[step], in_arrived.at[step], place.other_layer).start()

        outputs.collect(step)
        small_out[1:2, :] += column_sum(d_qkv_v[:, 2 * D : 3 * D].astype(F32))
        save("d_qkv", d_qkv_v, step)
        return carry

    lax.fori_loop(0, steps, one_step, 0)
    for name, buffer in zip(grad_names, (d_down_v, d_up_v, d_attn_v, d_qkv_v)):
        free(name, buffer)
    free_parts()

    @pl.when(section == 1)
    def _():
        inputs.spread_done()
        for step in range(steps):
            remote(d_hid_v.at[step], g_v.at[step], hop_sent.at[step], in_arrived.at[step], place.other_layer).wait_send()

    outputs.collect_done()


def backward(cotangent, weights, gains, kv, prob, saved):
    total = cotangent.shape[0]
    sequences = total // SEQ
    steps = 2 * sequences
    shapes = [
        jax.ShapeDtypeStruct((total, D), BF16),
        jax.ShapeDtypeStruct((SMALL_ROWS, D), F32),
    ] + [jax.ShapeDtypeStruct((total, width), dtype) for _, width, dtype in GRADS]
    widths = {name: (width, dtype) for name, width, dtype in SAVED}
    dma = pltpu.SemaphoreType.DMA
    d_hid, small, *grads = pl.pallas_call(
        functools.partial(backward_kernel, sequences),
        out_shape=shapes,
        in_specs=[ANY] * 5 + [VMEM] + [ANY] * (2 + len(KEPT)),
        out_specs=[ANY, VMEM] + [ANY] * len(GRADS),
        scratch_shapes=[
            pltpu.VMEM((steps, ROWS, D), BF16),
            pltpu.VMEM((steps, ROWS, D), BF16),
            pltpu.VMEM((SEQ, 2 * D), BF16),
            pltpu.VMEM((H, ROWS, SEQ), BF16),
            pltpu.VMEM((D, 3 * D), BF16),
            pltpu.VMEM((D, D), BF16),
            pltpu.VMEM((D, FF), BF16),
            pltpu.VMEM((FF, D), BF16),
            pltpu.VMEM((ROWS, D), F32),
            pltpu.VMEM((ROWS, D), BF16),
            pltpu.VMEM((PAIRS, SEQ, 2 * PAIR), BF16),
            pltpu.VMEM((steps, PAIRS, ROWS, 2 * PAIR), BF16),
        ]
        + [pltpu.VMEM((ROWS, widths[name][0]), widths[name][1]) for name in KEPT]
        + [pltpu.VMEM((ROWS, width), dtype) for _, width, dtype in GRADS]
        + [
            dma((4,)),
            dma((len(KEPT) + 2,)),
            dma((len(GRADS),)),
            dma((sequences,)),
            dma((sequences,)),
            dma((steps,)),
            dma((sequences,)),
            dma((sequences,)),
            dma((sequences,)),
            dma((2,)),
            dma((steps, 2)),
            dma((steps,)),
        ],
        compiler_params=pltpu.CompilerParams(
            collective_id=2, has_side_effects=True, vmem_limit_bytes=VMEM_LIMIT
        ),
        name="backward",
    )(cotangent, *weights, gains, kv, prob, *[saved[name] for name in KEPT])
    return d_hid, small, dict(zip([name for name, _, _ in GRADS], grads))


UNIT = 16
SLAB = D
WIDTH = D // 2
HALF = SLAB // 2
RAIL = 7 * UNIT
LINES = (3 * UNIT, 2 * UNIT, 2 * UNIT, 3 * UNIT)
SLABS = 2 * FF // D + FF // WIDTH + D // WIDTH + 3 * D // WIDTH


def reduce_kernel(depth, *refs):
    (gelu, d_down, low, d_up, ctx, d_attn, hid, d_qkv, small) = refs[:9]
    (o_v, o_small) = refs[9:11]
    (
        left_v, right_v, p_v, s_v, y_v, rl_v, rr_v, sm_v, sm_in_v, sm_o_v,
        load_sem, send_sem, recv_sem, sm_send, sm_recv,
    ) = refs[11:]
    plan = (
        (2 * FF // D, gelu, d_down),
        (FF // WIDTH, low, d_up),
        (D // WIDTH, ctx, d_attn),
        (3 * D // WIDTH, hid, d_qkv),
    )
    count = SLABS
    section = lax.axis_index("section")
    me = lax.axis_index("dp")
    core = lax.rem(me, 2)
    y = lax.rem(lax.div(me, 2), 2)
    z = lax.div(me, 4)
    sibling = (section, me + 1 - 2 * core)
    partner = (section, me + 2 - 4 * y)
    left = (section, me - 4)
    right = (section, me + 4)

    barrier = pltpu.get_barrier_semaphore()
    pl.semaphore_signal(barrier, inc=1, device_id=sibling, device_id_type=MESH)
    pl.semaphore_signal(barrier, inc=1, device_id=partner, device_id_type=MESH)

    @pl.when(z > 0)
    def _():
        pl.semaphore_signal(barrier, inc=1, device_id=left, device_id_type=MESH)

    @pl.when(z < depth - 1)
    def _():
        pl.semaphore_signal(barrier, inc=1, device_id=right, device_id_type=MESH)

    def at(value, size):
        return pl.ds(pl.multiple_of(value, UNIT), size)

    def load(step, start):
        slot = lax.rem(step, 2)
        if not start:
            pltpu.make_async_copy(low, left_v.at[slot], load_sem.at[0, slot]).wait()
            pltpu.make_async_copy(d_down.at[:, pl.ds(0, WIDTH)], right_v.at[slot], load_sem.at[1, slot]).wait()
            return
        first = 0
        for steps, factor, grad in plan:

            def issue(first=first, factor=factor, grad=grad):
                index = step - first
                halves = grad.shape[1] // WIDTH
                rows = pl.ds(pl.multiple_of(lax.div(index, halves) * SLAB, 128), SLAB)
                cols = pl.ds(pl.multiple_of(lax.rem(index, halves) * WIDTH, 128), WIDTH)
                pltpu.make_async_copy(factor.at[:, rows], left_v.at[slot], load_sem.at[0, slot]).start()
                pltpu.make_async_copy(grad.at[:, cols], right_v.at[slot], load_sem.at[1, slot]).start()

            pl.when((step >= first) & (step < first + steps))(issue)
            first += steps

    def send(kind, step, source, target, arrival, device, compute=None):
        parity = lax.rem(step, 2)
        copy = pltpu.make_async_remote_copy(
            source, target, send_sem.at[kind, parity], arrival, device_id=device, device_id_type=MESH
        )

        @pl.when(step >= 2)
        def _():
            copy.wait_send()

        if compute is not None:
            compute()
        copy.start()

    def finish_send(kind, view):
        for parity in range(2):
            pltpu.make_async_remote_copy(
                view, view, send_sem.at[kind, parity], recv_sem.at[kind, 0], device_id=sibling, device_id_type=MESH
            ).wait_send()

    def arrived(kind, step, view):
        pltpu.make_async_remote_copy(
            view, view, send_sem.at[kind, 0], recv_sem.at[kind, step], device_id=sibling, device_id_type=MESH
        ).wait_recv()

    own = core * HALF
    theirs = HALF - own
    CX, UP, DOWN, SIB_OTHER, YX = range(5)

    def add_into(target, term):
        target[...] = (target[...].astype(F32) + term[...].astype(F32)).astype(target.dtype)

    class Tree:
        def __init__(self, kinds, base, root, reach, size, offset, land, rail):
            self.kinds, self.base, self.root, self.reach = kinds, base, root, reach
            self.size, self.offset, self.land, self.rail = size, offset, land, rail
            self.distance = jnp.abs(z - root)
            self.from_left = (z > 0) & (z <= root)
            self.from_right = (z < depth - 1) & (z >= root)

        def part(self, step):
            return s_v.at[step, at(self.offset, self.size)]

        def total(self, step):
            return o_v.at[step, at(own + self.offset, self.size)]

        def landing(self, buffer, step):
            return buffer.at[step, pl.ds(self.land, self.size)]

        def towards(self, now):
            inward, out_left, out_right, sib = self.kinds
            step = now - self.base - self.reach + self.distance

            @pl.when((step >= 0) & (step < count))
            def _():
                @pl.when(self.from_left)
                def _():
                    arrived(out_left, step, self.landing(rl_v, step))
                    add_into(self.part(step), self.landing(rl_v, step))

                @pl.when(self.from_right)
                def _():
                    arrived(out_right, step, self.landing(rr_v, step))
                    add_into(self.part(step), self.landing(rr_v, step))

                @pl.when(z < self.root)
                def _():
                    send(inward, step, self.part(step), self.landing(rl_v, step), recv_sem.at[out_left, step], right)

                @pl.when(z > self.root)
                def _():
                    send(inward, step, self.part(step), self.landing(rr_v, step), recv_sem.at[out_right, step], left)

                @pl.when(z == self.root)
                def _():
                    if self.rail:
                        self.total(step)[...] = self.part(step)[...]
                    else:
                        view = y_v.at[step, pl.ds(RAIL, self.size)]
                        send(YX, step, self.part(step), view, recv_sem.at[YX, step], partner)

            if not self.rail:
                late = now - self.base - self.reach - 1

                @pl.when((z == self.root) & (late >= 0) & (late < count))
                def _():
                    view = y_v.at[late, pl.ds(RAIL, self.size)]
                    arrived(YX, late, view)
                    self.total(late)[...] = (self.part(late)[...].astype(F32) + view[...].astype(F32)).astype(BF16)

        def away(self, now):
            inward, out_left, out_right, sib = self.kinds
            lag = self.base + self.reach + (0 if self.rail else 1)
            step = now - lag - self.distance

            @pl.when((step >= 0) & (step < count))
            def _():
                view = self.total(step)

                @pl.when(z != self.root)
                def _():
                    arrived(inward, step, view)

                @pl.when(self.from_left)
                def _():
                    send(out_left, step, view, view, recv_sem.at[inward, step], left)

                @pl.when(self.from_right)
                def _():
                    send(out_right, step, view, view, recv_sem.at[inward, step], right)

                if self.rail:
                    send(DOWN, step, view, view, recv_sem.at[DOWN, step], partner)
                send(sib, step, view, view, recv_sem.at[sib, step], sibling)

            done = step - 1

            @pl.when((done >= 0) & (done < count))
            def _():
                arrived(sib, done, o_v.at[done, at(theirs + self.offset, self.size)])

        def finish(self):
            inward, out_left, out_right, sib = self.kinds
            view = self.part(0)

            @pl.when(z != self.root)
            def _():
                finish_send(inward, view)

            @pl.when(self.from_left)
            def _():
                finish_send(out_left, view)

            @pl.when(self.from_right)
            def _():
                finish_send(out_right, view)

            finish_send(sib, view)
            if not self.rail:

                @pl.when(z == self.root)
                def _():
                    finish_send(YX, view)

    half_depth = depth // 2
    rail_root = half_depth - 1 + y
    rail = Tree((5, 6, 7, 8), 2, rail_root, half_depth, RAIL, y * RAIL, 0, True)
    line = []
    offset = 0
    for index, size in enumerate(LINES):
        root = (2 * index + 1) * depth // (2 * len(LINES))
        kinds = tuple(9 + 4 * index + kind for kind in range(4))
        reach = max(root, depth - 1 - root)
        line.append(Tree(kinds, 1, root, reach, size, 2 * RAIL + offset, RAIL + offset, False))
        offset += size
    other_distance = jnp.abs(z - (half_depth - y))
    other = (1 - y) * RAIL

    sm_root = half_depth
    sm_reach = max(sm_root, depth - 1 - sm_root)
    sm_distance = jnp.abs(z - sm_root)

    def sm_copy(kind, source, target, arrival, device):
        return pltpu.make_async_remote_copy(
            source, target, sm_send.at[kind], sm_recv.at[arrival], device_id=device, device_id_type=MESH
        )

    def small_round(now):
        @pl.when(now == 0)
        def _():
            sm_v[...] = small[...]
            sm_copy(0, sm_v, sm_in_v.at[0], 0, sibling).start()

        @pl.when(now == 1)
        def _():
            sm_copy(0, sm_v, sm_in_v.at[0], 0, sibling).wait()
            sm_v[...] = sm_v[...] + sm_in_v[0]

        @pl.when(now == 1 + sm_reach - sm_distance)
        def _():
            @pl.when((z > 0) & (z <= sm_root))
            def _():
                sm_copy(1, sm_v, sm_in_v.at[1], 1, sibling).wait_recv()
                sm_v[...] = sm_v[...] + sm_in_v[1]

            @pl.when((z < depth - 1) & (z >= sm_root))
            def _():
                sm_copy(1, sm_v, sm_in_v.at[2], 2, sibling).wait_recv()
                sm_v[...] = sm_v[...] + sm_in_v[2]

            @pl.when(z < sm_root)
            def _():
                sm_copy(1, sm_v, sm_in_v.at[1], 1, right).start()

            @pl.when(z > sm_root)
            def _():
                sm_copy(1, sm_v, sm_in_v.at[2], 2, left).start()

            @pl.when(z == sm_root)
            def _():
                sm_copy(1, sm_v, sm_in_v.at[3], 3, partner).start()

        @pl.when((now == 2 + sm_reach) & (z == sm_root))
        def _():
            sm_copy(1, sm_v, sm_in_v.at[3], 3, partner).wait_recv()
            sm_o_v[...] = sm_v[...] + sm_in_v[3]

        @pl.when(now == 2 + sm_reach + sm_distance)
        def _():
            @pl.when(z != sm_root)
            def _():
                sm_copy(2, sm_o_v, sm_o_v, 4, sibling).wait_recv()

            @pl.when((z > 0) & (z <= sm_root))
            def _():
                sm_copy(2, sm_o_v, sm_o_v, 4, left).start()

            @pl.when((z < depth - 1) & (z >= sm_root))
            def _():
                sm_copy(3, sm_o_v, sm_o_v, 4, right).start()

    def small_finish():
        sm_copy(1, sm_v, sm_in_v.at[1], 1, sibling).wait_send()

        @pl.when((z > 0) & (z <= sm_root))
        def _():
            sm_copy(2, sm_o_v, sm_o_v, 4, left).wait_send()

        @pl.when((z < depth - 1) & (z >= sm_root))
        def _():
            sm_copy(3, sm_o_v, sm_o_v, 4, right).wait_send()

        o_small[...] = sm_o_v[...]

    load(jnp.int32(0), True)
    neighbours = 2 + (z > 0).astype(jnp.int32) + (z < depth - 1).astype(jnp.int32)
    pl.semaphore_wait(barrier, neighbours)

    last = max(
        [2 + half_depth + half_depth + 2] + [2 + tree.reach + max(tree.root, depth - 1 - tree.root) + 1 for tree in line]
    )

    def one_round(now, carry):
        slot = lax.rem(now, 2)

        @pl.when(now < count)
        def _():
            load(now, False)

            @pl.when(now + 1 < count)
            def _():
                load(now + 1, True)

            def form():
                p_v[slot] = dot_tn(left_v[slot], right_v[slot]).astype(BF16)

            view = p_v.at[slot, at(theirs, HALF)]
            send(CX, now, view, s_v.at[now], recv_sem.at[CX, now], sibling, form)

        step = now - 1

        @pl.when((step >= 0) & (step < count))
        def _():
            arrived(CX, step, s_v.at[step])
            add_into(s_v.at[step], p_v.at[1 - slot, at(own, HALF)])
            view = s_v.at[step, at(other, RAIL)]
            send(UP, step, view, y_v.at[step, pl.ds(0, RAIL)], recv_sem.at[UP, step], partner)

        for tree in line:
            tree.towards(now)

        step_up = now - 2

        @pl.when((step_up >= 0) & (step_up < count))
        def _():
            view = y_v.at[step_up, pl.ds(0, RAIL)]
            arrived(UP, step_up, view)
            add_into(rail.part(step_up), view)

        rail.towards(now)
        rail.away(now)
        for tree in line:
            tree.away(now)

        step_down = now - 2 - half_depth - other_distance - 1

        @pl.when((step_down >= 0) & (step_down < count))
        def _():
            view = o_v.at[step_down, at(own + other, RAIL)]
            arrived(DOWN, step_down, view)
            send(SIB_OTHER, step_down, view, view, recv_sem.at[SIB_OTHER, step_down], sibling)

        step_sib = step_down - 1

        @pl.when((step_sib >= 0) & (step_sib < count))
        def _():
            arrived(SIB_OTHER, step_sib, o_v.at[step_sib, at(theirs + other, RAIL)])

        small_round(now)

        return carry

    lax.fori_loop(0, count + last, one_round, 0)
    finish_send(CX, s_v.at[0])
    finish_send(UP, rail.part(0))
    finish_send(DOWN, rail.part(0))
    finish_send(SIB_OTHER, rail.part(0))
    rail.finish()
    for tree in line:
        tree.finish()
    small_finish()


def reduce_gradients(depth, gelu, d_down, low, d_up, ctx, d_attn, hid, d_qkv, small):
    rows = d_down.shape[0]
    columns = WIDTH
    count = SLABS
    kinds = 9 + 4 * len(LINES)
    return pl.pallas_call(
        functools.partial(reduce_kernel, depth),
        out_shape=[
            pltpu.VMEM((count, SLAB, columns), BF16),
            jax.ShapeDtypeStruct((SMALL_ROWS, small.shape[-1]), F32),
        ],
        in_specs=[ANY] * 8 + [VMEM],
        out_specs=[VMEM] * 2,
        scratch_shapes=[
            pltpu.VMEM((2, rows, SLAB), BF16),
            pltpu.VMEM((2, rows, columns), BF16),
            pltpu.VMEM((2, SLAB, columns), BF16),
            pltpu.VMEM((count, HALF, columns), BF16),
            pltpu.VMEM((count, RAIL + max(LINES), columns), BF16),
            pltpu.VMEM((count, RAIL + sum(LINES), columns), BF16),
            pltpu.VMEM((count, RAIL + sum(LINES), columns), BF16),
            pltpu.VMEM((SMALL_ROWS, small.shape[-1]), F32),
            pltpu.VMEM((4, SMALL_ROWS, small.shape[-1]), F32),
            pltpu.VMEM((SMALL_ROWS, small.shape[-1]), F32),
            pltpu.SemaphoreType.DMA((2, 2)),
            pltpu.SemaphoreType.DMA((kinds, 2)),
            pltpu.SemaphoreType.DMA((kinds, count)),
            pltpu.SemaphoreType.DMA((4,)),
            pltpu.SemaphoreType.DMA((5,)),
        ],
        compiler_params=pltpu.CompilerParams(
            collective_id=0, has_side_effects=True, vmem_limit_bytes=REDUCE_LIMIT
        ),
        name="reduce_gradients",
    )(gelu, d_down, low, d_up, ctx, d_attn, hid, d_qkv, small)


def finish_kernel(*refs):
    (totals, small, act, d_hid) = refs[:4]
    (o_act, o_hid, o_down, o_up, o_out, o_qkv, o_qv, o_bias, o_gain, o_shift, o_up_bias) = refs[4:15]
    stage_v, stage_sem, move_sem = refs[15:]
    moves = [begin(act, o_act.at[0], move_sem.at[0]), begin(d_hid, o_hid.at[0], move_sem.at[1])]
    o_qv[0] = small[0:2, :]
    o_bias[0] = small[2:4, :]
    o_gain[0] = small[4:6, :]
    o_shift[0] = small[6:8, :]
    for part in range(FF // D):
        o_up_bias[0:1, part * D : (part + 1) * D] = small[8 + part : 9 + part, :]
    places = []
    for array in (o_down, o_up, o_out, o_qkv):
        _, rows, columns = array.shape
        places += [(array, row, column) for row in range(rows // SLAB) for column in range(columns // WIDTH)]
    slots = stage_v.shape[0]
    copies = []
    for index, (array, row, column) in enumerate(places):
        slot = index % slots
        if index >= slots:
            copies[index - slots].wait()
        stage_v[slot] = totals[index].astype(F32)
        target = array.at[0, pl.ds(row * SLAB, SLAB), pl.ds(column * WIDTH, WIDTH)]
        copies.append(begin(stage_v.at[slot], target, stage_sem.at[slot]))
    for copy in copies[-slots:] + moves:
        copy.wait()


def finish(totals, small, act, d_hid):
    slots = 6
    shapes = [
        jax.ShapeDtypeStruct((1, *act.shape), BF16),
        jax.ShapeDtypeStruct((1, *act.shape), BF16),
        jax.ShapeDtypeStruct((1, FF, D), F32),
        jax.ShapeDtypeStruct((1, D, FF), F32),
        jax.ShapeDtypeStruct((1, D, D), F32),
        jax.ShapeDtypeStruct((1, D, 3 * D), F32),
        jax.ShapeDtypeStruct((1, 2, D), F32),
        jax.ShapeDtypeStruct((1, 2, D), F32),
        jax.ShapeDtypeStruct((1, 2, D), F32),
        jax.ShapeDtypeStruct((1, 2, D), F32),
        jax.ShapeDtypeStruct((1, FF), F32),
    ]
    return pl.pallas_call(
        finish_kernel,
        out_shape=shapes,
        in_specs=[VMEM, VMEM, ANY, ANY],
        out_specs=[ANY] * 6 + [VMEM] * 5,
        scratch_shapes=[
            pltpu.VMEM((slots, SLAB, WIDTH), F32),
            pltpu.SemaphoreType.DMA((slots,)),
            pltpu.SemaphoreType.DMA((2,)),
        ],
        compiler_params=pltpu.CompilerParams(vmem_limit_bytes=16 << 20),
        name="finish",
    )(pltpu.with_memory_space_constraint(totals, pltpu.VMEM), small, act, d_hid)


def shards(
    tokens, segments, lengths, cotangent, qkv_weight, qv_bias, out_weight, out_biases,
    norm_gains, norm_shifts, up_weight, up_bias, down_weight,
):
    weights = (qkv_weight, out_weight, up_weight, down_weight)
    params = (qv_bias, out_biases, norm_gains, norm_shifts, up_bias)
    act, kv, prob, saved = forward(tokens, weights, segments, lengths, params)
    d_hid, small, grads = backward(cotangent, weights, norm_gains, kv, prob, saved)
    totals, small = reduce_gradients(
        lax.axis_size("dp") // 4, saved["gelu"], grads["d_down"], saved["low"], grads["d_up"],
        saved["ctx"], grads["d_attn"], saved["hid"], grads["d_qkv"], small,
    )
    (
        o_act, o_hid, g_down, g_up, g_out, g_qkv, g_qv, g_bias, g_gain, g_shift, g_up_bias
    ) = finish(totals, small, act, d_hid)
    return (o_act, o_hid, g_qkv, g_qv, g_out, g_bias, g_gain, g_shift, g_up, g_up_bias, g_down)


def solution(mesh):
    return jax.shard_map(
        shards,
        mesh=mesh,
        in_specs=(
            P("dp", None), P("dp", None), P("dp"), P("dp", None),
            P("section", None, None), P("section", None, None), P("section", None, None), P("section", None, None),
            P("section", None, None), P("section", None, None), P("section", None, None), P("section", None),
            P("section", None, None),
        ),
        out_specs=(
            P("section", "dp", None), P("section", "dp", None),
            P("section", None, None), P("section", None, None), P("section", None, None), P("section", None, None),
            P("section", None, None), P("section", None, None), P("section", None, None), P("section", None),
            P("section", None, None),
        ),
        check_vma=False,
    )
```

```python
import functools
import math

import jax
import jax.numpy as jnp
from jax import lax
from jax.experimental import pallas as pl
from jax.experimental.pallas import tpu as pltpu
from jax.sharding import PartitionSpec as P

D = 768
H = 12
HD = 64
FF = 3072
SEQ = 512
MICRO = 2
PAIRS = H // 2
PAIR = 2 * HD
GROUP = PAIRS // 2

EPSILON = 1e-05
SCORE_SCALE = 0.125
NEG_FILL = -1e30
F32 = jnp.float32
BF16 = jnp.bfloat16
VMEM_LIMIT = 60 << 20
REDUCE_LIMIT = 44 << 20
MESH = pl.DeviceIdType.MESH

ANY = pl.BlockSpec(memory_space=pl.ANY)
VMEM = pl.BlockSpec(memory_space=pltpu.VMEM)
SMEM = pl.BlockSpec(memory_space=pltpu.SMEM)


def dot_nn(left, right):
    return lax.dot_general(left, right, (((1,), (0,)), ((), ())), preferred_element_type=F32)


def dot_nt(left, right):
    return lax.dot_general(left, right, (((1,), (1,)), ((), ())), preferred_element_type=F32)


def dot_tn(left, right):
    return lax.dot_general(left, right, (((0,), (0,)), ((), ())), preferred_element_type=F32)


def begin(source, target, sem):
    copy = pltpu.make_async_copy(source, target, sem)
    copy.start()
    return copy


def gelu_and_slope(u):
    normal_cdf = 0.5 + 0.5 * lax.erf(u * (1.0 / math.sqrt(2.0)))
    bell = jnp.exp((-0.5 * u) * u)
    return u * normal_cdf, normal_cdf + (u * (1.0 / math.sqrt(2.0 * math.pi))) * bell


def normalize(resid):
    average = jnp.mean(resid, axis=-1, keepdims=True)
    centred = resid - average
    variance = jnp.mean(centred * centred, axis=-1, keepdims=True)
    inverse = lax.rsqrt(variance + EPSILON)
    return centred * inverse, inverse


def norm_back(grad_out, scaled, inverse, gain):
    weighted = grad_out * gain
    first_mean = jnp.mean(weighted, axis=-1, keepdims=True)
    second_mean = jnp.mean(weighted * scaled, axis=-1, keepdims=True)
    return inverse * (weighted - first_mean - scaled * second_mean)


def half_mask(which):
    lane = lax.broadcasted_iota(jnp.int32, (1, PAIR), 1)
    return ((lane // HD) == which).astype(F32).astype(BF16)


ROWS = SEQ // 2
class Place:
    def __init__(self):
        self.section = lax.axis_index("section")
        self.me = lax.axis_index("dp")
        self.core = lax.rem(self.me, 2)
        self.sibling = (self.section, self.me + 1 - 2 * self.core)
        self.other_layer = (1 - self.section, self.me)
        self.own = pl.ds(pl.multiple_of(self.core * ROWS, ROWS), ROWS)
        self.theirs = pl.ds(pl.multiple_of(ROWS - self.core * ROWS, ROWS), ROWS)

    def greet(self):
        barrier = pltpu.get_barrier_semaphore()
        for device in (self.sibling, self.other_layer):
            pl.semaphore_signal(barrier, inc=1, device_id=device, device_id_type=MESH)
        pl.semaphore_wait(barrier, 2)

    def is_mine(self, step, sequences):
        return lax.div(step, sequences) == self.core


def remote(source, target, send_sem, recv_sem, device):
    return pltpu.make_async_remote_copy(source, target, send_sem, recv_sem, device_id=device, device_id_type=MESH)


class Rows:
    def __init__(self, place, sequences, array, steps, local, sent, arrived):
        self.place, self.sequences, self.array, self.steps = place, sequences, array, steps
        self.local, self.sent, self.arrived = local, sent, arrived

    def part(self, sequence, core):
        return self.array.at[pl.ds(pl.multiple_of(sequence * SEQ + core * ROWS, ROWS), ROWS)]

    def spread(self):
        place = self.place
        for sequence in range(self.sequences):
            step = place.core * self.sequences + sequence
            target = self.steps.at[step]
            pltpu.make_async_copy(self.part(sequence, place.core), target, self.local.at[sequence]).start()
            remote(
                self.part(sequence, 1 - place.core), target, self.sent.at[sequence], self.arrived.at[step], place.sibling
            ).start()

    def spread_done(self):
        for sequence in range(self.sequences):
            view = self.steps.at[0]
            remote(view, view, self.sent.at[sequence], self.arrived.at[0], self.place.sibling).wait_send()

    def await_step(self, step, spread):
        mine = spread & self.place.is_mine(step, self.sequences)
        view = self.steps.at[step]

        @pl.when(mine)
        def _():
            pltpu.make_async_copy(view, view, self.local.at[lax.rem(step, self.sequences)]).wait()

        @pl.when(jnp.logical_not(mine))
        def _():
            remote(view, view, self.sent.at[0], self.arrived.at[step], self.place.sibling).wait_recv()

    def collect(self, step):
        sequence = lax.rem(step, self.sequences)
        target = self.part(sequence, self.place.core)
        mine = self.place.is_mine(step, self.sequences)

        @pl.when(mine)
        def _():
            pltpu.make_async_copy(self.steps.at[step], target, self.local.at[sequence]).start()

        @pl.when(jnp.logical_not(mine))
        def _():
            remote(
                self.steps.at[step], target, self.sent.at[sequence], self.arrived.at[sequence], self.place.sibling
            ).start()

    def collect_done(self):
        for sequence in range(self.sequences):
            view = self.steps.at[0]
            pltpu.make_async_copy(view, view, self.local.at[sequence]).wait()
            remote(view, view, self.sent.at[sequence], self.arrived.at[sequence], self.place.sibling).wait()


SAVED = (
    ("hid", D, BF16),
    ("low", D, BF16),
    ("gelu", FF, BF16),
    ("ctx", D, BF16),
    ("q", D, BF16),
    ("linv", D, F32),
    ("xh1", D, BF16),
    ("inv1", 128, F32),
    ("slope", FF, BF16),
    ("xh2", D, BF16),
    ("inv2", 128, F32),
)
GRADS = (("d_down", D, BF16), ("d_up", FF, BF16), ("d_attn", D, BF16), ("d_qkv", 3 * D, BF16))
SMALL_ROWS = 16


def layers_kernel(sequences, *refs):
    (tok, cot, wqkv, wo, wu, wd, segs, lens, qv_bias, out_biases, gains, shifts, up_bias) = refs[:13]
    act_out, d_hid_out, small_out, prob_io = refs[13:17]
    stop = 17 + len(SAVED)
    saved = dict(zip([name for name, _, _ in SAVED], refs[17:stop]))
    grads = dict(zip([name for name, _, _ in GRADS], refs[stop : stop + len(GRADS)]))
    stop += len(GRADS)
    (
        h_v, act_v, g_v, d_hid_v, kv_v, p_v, wqkv_v, wo_v, wu_v, wd_v, bias_v, acc_v, seg_own, seg_their,
        d_ctx_v, part_v, their_v,
    ) = refs[stop : stop + 17]
    stop += 17
    buffers = dict(zip([name for name, _, _ in SAVED if name != "hid"], refs[stop : stop + len(SAVED) - 1]))
    stop += len(SAVED) - 1
    grad_buffers = dict(zip([name for name, _, _ in GRADS], refs[stop : stop + len(GRADS)]))
    stop += len(GRADS)
    (
        w_sem, save_sem, hid_sem, grad_sem, p_sem, seg_sem, kv_sent, kv_arrived, part_sent, part_arrived,
        in_local, in_sent, in_arrived, out_local, out_sent, out_arrived, hop_sent,
        up_local, up_sent, up_arrived, down_local, down_sent, down_arrived, back_sent,
    ) = refs[stop:]
    place = Place()
    section = place.section
    steps = 2 * sequences
    names = [name for name, _, _ in SAVED]
    grad_names = [name for name, _, _ in GRADS]
    inputs = Rows(place, sequences, tok, h_v, in_local, in_sent, in_arrived)
    outputs = Rows(place, sequences, act_out, act_v, out_local, out_sent, out_arrived)
    upstream = Rows(place, sequences, cot, g_v, up_local, up_sent, up_arrived)
    downstream = Rows(place, sequences, d_hid_out, d_hid_v, down_local, down_sent, down_arrived)

    def at_step(array, step):
        return array.at[pl.ds(pl.multiple_of(step * ROWS, ROWS), ROWS)]

    def save(name, step):
        pltpu.make_async_copy(buffers[name], at_step(saved[name], step), save_sem.at[names.index(name)]).start()

    def fetch(name, step):
        pltpu.make_async_copy(at_step(saved[name], step), buffers[name], save_sem.at[names.index(name)]).start()

    def settle(name):
        pltpu.make_async_copy(buffers[name], buffers[name], save_sem.at[names.index(name)]).wait()

    def prob_part(group, step):
        heads = pl.ds(group * 2 * GROUP, 2 * GROUP)
        return p_v.at[heads], prob_io.at[step, heads], p_sem.at[group]

    def settle_prob():
        for group in range(2):
            view, _, sem = prob_part(group, 0)
            pltpu.make_async_copy(view, view, sem).wait()

    def when_first(step, copies):
        @pl.when(step == 0)
        def _():
            for copy in copies:
                copy.wait()

    def column_sum(value):
        return jnp.sum(value, axis=0, keepdims=True)

    get_qkv = [
        begin(wqkv.at[0, :, pl.ds(block * D, D)], wqkv_v.at[:, pl.ds(block * D, D)], w_sem.at[block])
        for block in (1, 2, 0)
    ]
    position = lax.broadcasted_iota(jnp.int32, (1, SEQ), 1)
    for sequence in range(sequences):
        seg_own[sequence, 0:1, :] = segs[sequence : sequence + 1, :].astype(F32)
        seg_own[sequence, 1:2, :] = (position < lens[sequence]).astype(F32)
        seg_own[sequence, 2:8, :] = jnp.zeros((6, SEQ), F32)
    place.greet()
    seg_copy = remote(seg_own, seg_their, seg_sem.at[0], seg_sem.at[1], place.sibling)

    @pl.when(section == 0)
    def _():
        inputs.spread()

    @pl.when(section == 1)
    def _():
        upstream.spread()

    seg_copy.start()
    get_wo = begin(wo.at[0], wo_v, w_sem.at[3])
    get_wu = begin(wu.at[0], wu_v, w_sem.at[4])
    get_wd = begin(wd.at[0], wd_v, w_sem.at[5])
    small_out[...] = jnp.zeros_like(small_out)

    def forward_step(step, carry):
        inputs.await_step(step, section == 0)
        pltpu.make_async_copy(h_v.at[step], at_step(saved["hid"], step), hid_sem.at[step]).start()
        hidden = h_v[step]
        for block in (1, 2):
            when_first(step, (get_qkv[block - 1],))
            proj = dot_nn(hidden, wqkv_v[:, block * D : (block + 1) * D])
            if block == 2:
                proj = proj + qv_bias[0, 1:2, :]
            cols = pl.ds((block - 1) * D, D)
            kv_v[step, place.own, cols] = proj.astype(BF16)
            view = kv_v.at[step, place.own, cols]
            remote(view, view, kv_sent.at[step, block - 1], kv_arrived.at[step, block - 1], place.sibling).start()

        def await_keys_or_values(block):
            view = kv_v.at[step, place.theirs, pl.ds(block * D, D)]
            remote(view, view, kv_sent.at[step, block], kv_arrived.at[step, block], place.sibling).wait_recv()

        when_first(step, (get_qkv[2],))

        @pl.when(step > 0)
        def _():
            for name in buffers:
                settle(name)
            settle_prob()

        buffers["q"][...] = (dot_nn(hidden, wqkv_v[:, 0:D]) + qv_bias[0, 0:1, :]).astype(BF16)
        save("q", step)
        when_first(step, (seg_copy,))

        sequence = lax.rem(step, sequences)
        mine = jnp.where(place.is_mine(step, sequences), 1.0, 0.0)
        key_rows = mine * seg_own[sequence] + (1.0 - mine) * seg_their[sequence]
        query_row = mine * seg_own[sequence, 0:1, place.own] + (1.0 - mine) * seg_their[sequence, 0:1, place.own]
        query_seg = jnp.transpose(jnp.broadcast_to(query_row, (128, ROWS)))
        query = lax.broadcasted_iota(jnp.int32, (ROWS, 128), 0) + place.core * ROWS
        key = lax.broadcasted_iota(jnp.int32, (ROWS, 128), 1)
        for tile in range(SEQ // 128):
            cols = slice(tile * 128, (tile + 1) * 128)
            visible = (key_rows[1:2, cols] > 0.5) | (key + tile * 128 == query)
            bias_v[:, cols] = jnp.where((query_seg == key_rows[0:1, cols]) & visible, 0.0, NEG_FILL)

        await_keys_or_values(0)
        q_v, linv_v, ctx_v = buffers["q"], buffers["linv"], buffers["ctx"]
        for group in range(2):
            for pair in range(group * GROUP, (group + 1) * GROUP):
                at = pair * PAIR
                q2 = q_v[:, at : at + PAIR] * SCORE_SCALE
                k2 = kv_v[step, :, at : at + PAIR]
                weights = []
                for head in range(2):
                    scores = dot_nt(q2, k2 * half_mask(head)) + bias_v[...]
                    weight = jnp.exp(scores - jnp.max(scores, axis=-1, keepdims=True)).astype(BF16)
                    p_v[pair * 2 + head] = weight
                    weights.append(weight)
                if pair == 0:
                    await_keys_or_values(1)
                v2 = kv_v[step, :, D + at : D + at + PAIR]
                total = None
                for head in range(2):
                    mask = half_mask(head)
                    values = jnp.concatenate([v2 * mask, jnp.broadcast_to(mask, (SEQ, PAIR))], axis=1)
                    part = dot_nn(weights[head], values)
                    total = part if total is None else total + part
                inverse = 1.0 / total[:, PAIR : 2 * PAIR]
                linv_v[:, at : at + PAIR] = inverse
                ctx_v[:, at : at + PAIR] = (total[:, 0:PAIR] * inverse).astype(BF16)
            view, target, sem = prob_part(group, step)
            pltpu.make_async_copy(view, target, sem).start()
        save("linv", step)
        save("ctx", step)
        when_first(step, (get_wo,))
        resid = hidden.astype(F32) + (dot_nn(ctx_v[...], wo_v[...]) + out_biases[0, 0:1, :])
        scaled, inverse = normalize(resid)
        buffers["xh1"][...] = scaled.astype(BF16)
        buffers["inv1"][...] = jnp.broadcast_to(inverse, (ROWS, 128))
        normed = scaled * gains[0, 0:1, :] + shifts[0, 0:1, :]
        buffers["low"][...] = normed.astype(BF16)
        acc_v[...] = normed + out_biases[0, 1:2, :]
        for name in ("xh1", "inv1", "low"):
            save(name, step)
        when_first(step, (get_wu, get_wd))
        width = 1024
        for chunk in range(FF // width):
            cols = slice(chunk * width, (chunk + 1) * width)
            up = dot_nn(buffers["low"][...], wu_v[:, cols]) + up_bias[0:1, cols]
            gelu, slope = gelu_and_slope(up)
            gelu = gelu.astype(BF16)
            buffers["gelu"][:, cols] = gelu
            buffers["slope"][:, cols] = slope.astype(BF16)
            acc_v[...] += dot_nn(gelu, wd_v[cols, :])
        scaled, inverse = normalize(acc_v[...])
        act_v[step] = (scaled * gains[0, 1:2, :] + shifts[0, 1:2, :]).astype(BF16)

        @pl.when(section == 0)
        def _():
            remote(act_v.at[step], h_v.at[step], hop_sent.at[step], in_arrived.at[step], place.other_layer).start()

        outputs.collect(step)
        buffers["xh2"][...] = scaled.astype(BF16)
        buffers["inv2"][...] = jnp.broadcast_to(inverse, (ROWS, 128))
        for name in ("gelu", "slope", "xh2", "inv2"):
            save(name, step)
        return carry

    lax.fori_loop(0, steps, forward_step, 0)

    def backward_step(turn, carry):
        step = steps - 1 - turn

        def fetched(*wanted):
            @pl.when(turn > 0)
            def _():
                for name in wanted:
                    settle(name)

        def fetch_next(*wanted):
            @pl.when(turn == 0)
            def _():
                for name in wanted:
                    settle(name)

            @pl.when(turn + 1 < steps)
            def _():
                for name in wanted:
                    fetch(name, step - 1)

        def keep(name):
            pltpu.make_async_copy(
                grad_buffers[name], at_step(grads[name], step), grad_sem.at[grad_names.index(name)]
            ).start()

        def free(name):
            @pl.when(turn > 0)
            def _():
                buffer = grad_buffers[name]
                pltpu.make_async_copy(buffer, buffer, grad_sem.at[grad_names.index(name)]).wait()

        upstream.await_step(step, section == 1)
        fetched("xh2", "inv2")
        grad = g_v[step].astype(F32)
        scaled = buffers["xh2"][...].astype(F32)
        small_out[5:6, :] += column_sum(grad * scaled)
        small_out[7:8, :] += column_sum(grad)
        d_r2 = norm_back(grad, scaled, buffers["inv2"][:, 0:1], gains[0, 1:2, :])
        d_down = d_r2.astype(BF16)
        free("d_down")
        d_down_v, d_up_v, d_attn_v, d_qkv_v = [grad_buffers[name] for name in grad_names]
        d_down_v[...] = d_down
        small_out[3:4, :] += column_sum(d_down.astype(F32))
        acc_v[...] = d_r2
        keep("d_down")
        fetch_next("xh2", "inv2")
        fetched("slope")
        free("d_up")
        for chunk in range(FF // D):
            cols = slice(chunk * D, (chunk + 1) * D)
            d_up = (dot_nt(d_down_v[...], wd_v[cols, :]) * buffers["slope"][:, cols].astype(F32)).astype(BF16)
            d_up_v[:, cols] = d_up
            small_out[8 + chunk : 9 + chunk, :] += column_sum(d_up.astype(F32))
            acc_v[...] += dot_nt(d_up, wu_v[:, cols])
        keep("d_up")
        fetch_next("slope")
        fetched("xh1", "inv1")
        d_normed = acc_v[...]
        scaled = buffers["xh1"][...].astype(F32)
        small_out[4:5, :] += column_sum(d_normed * scaled)
        small_out[6:7, :] += column_sum(d_normed)
        d_r1 = norm_back(d_normed, scaled, buffers["inv1"][:, 0:1], gains[0, 0:1, :])
        d_attn = d_r1.astype(BF16)
        free("d_attn")
        d_attn_v[...] = d_attn
        small_out[2:3, :] += column_sum(d_attn.astype(F32))
        acc_v[...] = d_r1
        keep("d_attn")
        fetch_next("xh1", "inv1")
        fetched("q", "linv", "ctx")

        @pl.when(turn > 0)
        def _():
            settle_prob()

        d_ctx_v[...] = (dot_nt(d_attn_v[...], wo_v[...]) * buffers["linv"][...]).astype(BF16)
        free("d_qkv")

        def part_copy(group):
            pairs = pl.ds(group * GROUP, GROUP)
            return remote(
                part_v.at[pairs, place.theirs], their_v.at[step, pairs], part_sent.at[group],
                part_arrived.at[step, group], place.sibling,
            )

        @pl.when(turn > 0)
        def _():
            for group in range(2):
                part_copy(group).wait_send()

        q_v, ctx_v = buffers["q"], buffers["ctx"]
        for group in range(2):
            for pair in range(group * GROUP, (group + 1) * GROUP):
                at = pair * PAIR
                q2 = q_v[:, at : at + PAIR] * SCORE_SCALE
                k2 = kv_v[step, :, at : at + PAIR]
                v2 = kv_v[step, :, D + at : D + at + PAIR]
                dc2 = d_ctx_v[:, at : at + PAIR]
                inner = dc2.astype(F32) * ctx_v[:, at : at + PAIR].astype(F32)
                d_q, d_k, d_v = None, None, None
                for head in range(2):
                    mask = half_mask(head)
                    dc_own = dc2 * mask
                    weight = p_v[pair * 2 + head]
                    row_inner = jnp.sum(inner * mask.astype(F32), axis=-1, keepdims=True)
                    d_prob = dot_nt(dc_own, v2)
                    d_score = (weight.astype(F32) * (d_prob - row_inner)).astype(BF16)
                    one_v = dot_tn(dc_own, weight)
                    one_k = dot_tn(q2 * mask, d_score)
                    one_q = dot_nn(d_score, k2 * mask)
                    d_v = one_v if d_v is None else d_v + one_v
                    d_k = one_k if d_k is None else d_k + one_k
                    d_q = one_q if d_q is None else d_q + one_q
                d_qkv_v[:, at : at + PAIR] = (d_q * SCORE_SCALE).astype(BF16)
                part_v[pair, :, 0:PAIR] = jnp.transpose(d_k).astype(BF16)
                part_v[pair, :, PAIR : 2 * PAIR] = jnp.transpose(d_v).astype(BF16)
            part_copy(group).start()

        fetch_next("q", "linv", "ctx")

        @pl.when(turn == 0)
        def _():
            settle_prob()

        @pl.when(turn + 1 < steps)
        def _():
            for group in range(2):
                view, source, sem = prob_part(group, step - 1)
                pltpu.make_async_copy(source, view, sem).start()

        d_query = d_qkv_v[:, 0:D]
        acc_v[...] += dot_nt(d_query, wqkv_v[:, 0:D])
        small_out[0:1, :] += column_sum(d_query.astype(F32))
        for group in range(2):
            start = group * GROUP
            part_copy(group).wait_recv()
            for pair in range(start, start + GROUP):
                total = part_v[pair, place.own, :].astype(F32) + their_v[step, pair].astype(F32)
                at = pair * PAIR
                d_qkv_v[:, D + at : D + at + PAIR] = total[:, 0:PAIR].astype(BF16)
                d_qkv_v[:, 2 * D + at : 2 * D + at + PAIR] = total[:, PAIR : 2 * PAIR].astype(BF16)
            keys = slice(D + start * PAIR, D + (start + GROUP) * PAIR)
            values = slice(2 * D + start * PAIR, 2 * D + (start + GROUP) * PAIR)
            d_hid = acc_v[...] + dot_nt(d_qkv_v[:, keys], wqkv_v[:, keys]) + dot_nt(d_qkv_v[:, values], wqkv_v[:, values])
            if group == 0:
                acc_v[...] = d_hid
            else:
                d_hid_v[step] = d_hid.astype(BF16)

        @pl.when(section == 1)
        def _():
            remote(d_hid_v.at[step], g_v.at[step], back_sent.at[step], up_arrived.at[step], place.other_layer).start()

        downstream.collect(step)
        small_out[1:2, :] += column_sum(d_qkv_v[:, 2 * D : 3 * D].astype(F32))
        keep("d_qkv")
        return carry

    lax.fori_loop(0, steps, backward_step, 0)

    for name in ("low", "gelu"):
        settle(name)
    for name in grad_names:
        buffer = grad_buffers[name]
        pltpu.make_async_copy(buffer, buffer, grad_sem.at[grad_names.index(name)]).wait()
    for group in range(2):
        view = part_v.at[pl.ds(group * GROUP, GROUP), place.theirs]
        remote(view, view, part_sent.at[group], part_arrived.at[0, group], place.sibling).wait_send()
    for step in range(steps):
        pltpu.make_async_copy(h_v.at[step], h_v.at[step], hid_sem.at[step]).wait()
        for block in range(2):
            view = kv_v.at[step, place.own, pl.ds(block * D, D)]
            remote(view, view, kv_sent.at[step, block], kv_arrived.at[step, block], place.sibling).wait_send()

    @pl.when(section == 0)
    def _():
        inputs.spread_done()
        for step in range(steps):
            remote(act_v.at[step], h_v.at[step], hop_sent.at[step], in_arrived.at[step], place.other_layer).wait_send()

    @pl.when(section == 1)
    def _():
        upstream.spread_done()
        for step in range(steps):
            remote(d_hid_v.at[step], g_v.at[step], back_sent.at[step], up_arrived.at[step], place.other_layer).wait_send()

    outputs.collect_done()
    downstream.collect_done()


def layers(tokens, cotangent, weights, segments, lengths, params):
    total = tokens.shape[0]
    sequences = total // SEQ
    steps = 2 * sequences
    shapes = [
        jax.ShapeDtypeStruct((total, D), BF16),
        jax.ShapeDtypeStruct((total, D), BF16),
        jax.ShapeDtypeStruct((SMALL_ROWS, D), F32),
        jax.ShapeDtypeStruct((steps, H, ROWS, SEQ), BF16),
    ] + [jax.ShapeDtypeStruct((total, width), dtype) for _, width, dtype in SAVED + GRADS]
    dma = pltpu.SemaphoreType.DMA
    act, d_hid, small, _, *rest = pl.pallas_call(
        functools.partial(layers_kernel, sequences),
        out_shape=shapes,
        in_specs=[ANY] * 6 + [VMEM, SMEM] + [VMEM] * 5,
        out_specs=[ANY, ANY, VMEM] + [ANY] * (len(shapes) - 3),
        scratch_shapes=[pltpu.VMEM((steps, ROWS, D), BF16)] * 4
        + [
            pltpu.VMEM((steps, SEQ, 2 * D), BF16),
            pltpu.VMEM((H, ROWS, SEQ), BF16),
            pltpu.VMEM((D, 3 * D), BF16),
            pltpu.VMEM((D, D), BF16),
            pltpu.VMEM((D, FF), BF16),
            pltpu.VMEM((FF, D), BF16),
            pltpu.VMEM((ROWS, SEQ), F32),
            pltpu.VMEM((ROWS, D), F32),
            pltpu.VMEM((sequences, 8, SEQ), F32),
            pltpu.VMEM((sequences, 8, SEQ), F32),
            pltpu.VMEM((ROWS, D), BF16),
            pltpu.VMEM((PAIRS, SEQ, 2 * PAIR), BF16),
            pltpu.VMEM((steps, PAIRS, ROWS, 2 * PAIR), BF16),
        ]
        + [pltpu.VMEM((ROWS, width), dtype) for name, width, dtype in SAVED + GRADS if name != "hid"]
        + [
            dma((6,)), dma((len(SAVED),)), dma((steps,)), dma((len(GRADS),)), dma((2,)), dma((2,)),
            dma((steps, 2)), dma((steps, 2)), dma((2,)), dma((steps, 2)),
        ]
        + [dma((sequences,)), dma((sequences,)), dma((steps,))]
        + [dma((sequences,)), dma((sequences,)), dma((sequences,)), dma((steps,))]
        + [dma((sequences,)), dma((sequences,)), dma((steps,))]
        + [dma((sequences,)), dma((sequences,)), dma((sequences,)), dma((steps,))],
        compiler_params=pltpu.CompilerParams(
            collective_id=1, has_side_effects=True, vmem_limit_bytes=VMEM_LIMIT
        ),
        name="layers",
    )(tokens, cotangent, *weights, segments, lengths, *params)
    return act, d_hid, small, dict(zip([name for name, _, _ in SAVED + GRADS], rest))


UNIT = 16
SLAB = D
WIDTH = D // 2
HALF = SLAB // 2
RAIL = 7 * UNIT
LINES = (3 * UNIT, 2 * UNIT, 2 * UNIT, 3 * UNIT)
SLABS = 2 * FF // D + FF // WIDTH + D // WIDTH + 3 * D // WIDTH


def reduce_kernel(depth, *refs):
    (gelu, d_down, low, d_up, ctx, d_attn, hid, d_qkv, small) = refs[:9]
    (o_v, o_small) = refs[9:11]
    (
        left_v, right_v, p_v, s_v, y_v, rl_v, rr_v, sm_v, sm_in_v, sm_o_v,
        load_sem, send_sem, recv_sem, sm_send, sm_recv,
    ) = refs[11:]
    plan = (
        (2 * FF // D, gelu, d_down),
        (FF // WIDTH, low, d_up),
        (D // WIDTH, ctx, d_attn),
        (3 * D // WIDTH, hid, d_qkv),
    )
    count = SLABS
    section = lax.axis_index("section")
    me = lax.axis_index("dp")
    core = lax.rem(me, 2)
    y = lax.rem(lax.div(me, 2), 2)
    z = lax.div(me, 4)
    sibling = (section, me + 1 - 2 * core)
    partner = (section, me + 2 - 4 * y)
    left = (section, me - 4)
    right = (section, me + 4)

    barrier = pltpu.get_barrier_semaphore()
    pl.semaphore_signal(barrier, inc=1, device_id=sibling, device_id_type=MESH)
    pl.semaphore_signal(barrier, inc=1, device_id=partner, device_id_type=MESH)

    @pl.when(z > 0)
    def _():
        pl.semaphore_signal(barrier, inc=1, device_id=left, device_id_type=MESH)

    @pl.when(z < depth - 1)
    def _():
        pl.semaphore_signal(barrier, inc=1, device_id=right, device_id_type=MESH)

    def at(value, size):
        return pl.ds(pl.multiple_of(value, UNIT), size)

    def load(step, start):
        slot = lax.rem(step, 2)
        if not start:
            pltpu.make_async_copy(low, left_v.at[slot], load_sem.at[0, slot]).wait()
            pltpu.make_async_copy(d_down.at[:, pl.ds(0, WIDTH)], right_v.at[slot], load_sem.at[1, slot]).wait()
            return
        first = 0
        for steps, factor, grad in plan:

            def issue(first=first, factor=factor, grad=grad):
                index = step - first
                halves = grad.shape[1] // WIDTH
                rows = pl.ds(pl.multiple_of(lax.div(index, halves) * SLAB, 128), SLAB)
                cols = pl.ds(pl.multiple_of(lax.rem(index, halves) * WIDTH, 128), WIDTH)
                pltpu.make_async_copy(factor.at[:, rows], left_v.at[slot], load_sem.at[0, slot]).start()
                pltpu.make_async_copy(grad.at[:, cols], right_v.at[slot], load_sem.at[1, slot]).start()

            pl.when((step >= first) & (step < first + steps))(issue)
            first += steps

    def send(kind, step, source, target, arrival, device, compute=None):
        parity = lax.rem(step, 2)
        copy = pltpu.make_async_remote_copy(
            source, target, send_sem.at[kind, parity], arrival, device_id=device, device_id_type=MESH
        )

        @pl.when(step >= 2)
        def _():
            copy.wait_send()

        if compute is not None:
            compute()
        copy.start()

    def finish_send(kind, view):
        for parity in range(2):
            pltpu.make_async_remote_copy(
                view, view, send_sem.at[kind, parity], recv_sem.at[kind, 0], device_id=sibling, device_id_type=MESH
            ).wait_send()

    def arrived(kind, step, view):
        pltpu.make_async_remote_copy(
            view, view, send_sem.at[kind, 0], recv_sem.at[kind, step], device_id=sibling, device_id_type=MESH
        ).wait_recv()

    own = core * HALF
    theirs = HALF - own
    CX, UP, DOWN, SIB_OTHER, YX = range(5)

    def add_into(target, term):
        target[...] = (target[...].astype(F32) + term[...].astype(F32)).astype(target.dtype)

    class Tree:
        def __init__(self, kinds, base, root, reach, size, offset, land, rail):
            self.kinds, self.base, self.root, self.reach = kinds, base, root, reach
            self.size, self.offset, self.land, self.rail = size, offset, land, rail
            self.distance = jnp.abs(z - root)
            self.from_left = (z > 0) & (z <= root)
            self.from_right = (z < depth - 1) & (z >= root)

        def part(self, step):
            return s_v.at[step, at(self.offset, self.size)]

        def total(self, step):
            return o_v.at[step, at(own + self.offset, self.size)]

        def landing(self, buffer, step):
            return buffer.at[step, pl.ds(self.land, self.size)]

        def towards(self, now):
            inward, out_left, out_right, sib = self.kinds
            step = now - self.base - self.reach + self.distance

            @pl.when((step >= 0) & (step < count))
            def _():
                @pl.when(self.from_left)
                def _():
                    arrived(out_left, step, self.landing(rl_v, step))
                    add_into(self.part(step), self.landing(rl_v, step))

                @pl.when(self.from_right)
                def _():
                    arrived(out_right, step, self.landing(rr_v, step))
                    add_into(self.part(step), self.landing(rr_v, step))

                @pl.when(z < self.root)
                def _():
                    send(inward, step, self.part(step), self.landing(rl_v, step), recv_sem.at[out_left, step], right)

                @pl.when(z > self.root)
                def _():
                    send(inward, step, self.part(step), self.landing(rr_v, step), recv_sem.at[out_right, step], left)

                @pl.when(z == self.root)
                def _():
                    if self.rail:
                        self.total(step)[...] = self.part(step)[...]
                    else:
                        view = y_v.at[step, pl.ds(RAIL, self.size)]
                        send(YX, step, self.part(step), view, recv_sem.at[YX, step], partner)

            if not self.rail:
                late = now - self.base - self.reach - 1

                @pl.when((z == self.root) & (late >= 0) & (late < count))
                def _():
                    view = y_v.at[late, pl.ds(RAIL, self.size)]
                    arrived(YX, late, view)
                    self.total(late)[...] = (self.part(late)[...].astype(F32) + view[...].astype(F32)).astype(BF16)

        def away(self, now):
            inward, out_left, out_right, sib = self.kinds
            lag = self.base + self.reach + (0 if self.rail else 1)
            step = now - lag - self.distance

            @pl.when((step >= 0) & (step < count))
            def _():
                view = self.total(step)

                @pl.when(z != self.root)
                def _():
                    arrived(inward, step, view)

                @pl.when(self.from_left)
                def _():
                    send(out_left, step, view, view, recv_sem.at[inward, step], left)

                @pl.when(self.from_right)
                def _():
                    send(out_right, step, view, view, recv_sem.at[inward, step], right)

                if self.rail:
                    send(DOWN, step, view, view, recv_sem.at[DOWN, step], partner)
                send(sib, step, view, view, recv_sem.at[sib, step], sibling)

            done = step - 1

            @pl.when((done >= 0) & (done < count))
            def _():
                arrived(sib, done, o_v.at[done, at(theirs + self.offset, self.size)])

        def finish(self):
            inward, out_left, out_right, sib = self.kinds
            view = self.part(0)

            @pl.when(z != self.root)
            def _():
                finish_send(inward, view)

            @pl.when(self.from_left)
            def _():
                finish_send(out_left, view)

            @pl.when(self.from_right)
            def _():
                finish_send(out_right, view)

            finish_send(sib, view)
            if not self.rail:

                @pl.when(z == self.root)
                def _():
                    finish_send(YX, view)

    half_depth = depth // 2
    rail_root = half_depth - 1 + y
    rail = Tree((5, 6, 7, 8), 2, rail_root, half_depth, RAIL, y * RAIL, 0, True)
    line = []
    offset = 0
    for index, size in enumerate(LINES):
        root = (2 * index + 1) * depth // (2 * len(LINES))
        kinds = tuple(9 + 4 * index + kind for kind in range(4))
        reach = max(root, depth - 1 - root)
        line.append(Tree(kinds, 1, root, reach, size, 2 * RAIL + offset, RAIL + offset, False))
        offset += size
    other_distance = jnp.abs(z - (half_depth - y))
    other = (1 - y) * RAIL

    sm_root = half_depth
    sm_reach = max(sm_root, depth - 1 - sm_root)
    sm_distance = jnp.abs(z - sm_root)

    def sm_copy(kind, source, target, arrival, device):
        return pltpu.make_async_remote_copy(
            source, target, sm_send.at[kind], sm_recv.at[arrival], device_id=device, device_id_type=MESH
        )

    def small_round(now):
        @pl.when(now == 0)
        def _():
            sm_v[...] = small[...]
            sm_copy(0, sm_v, sm_in_v.at[0], 0, sibling).start()

        @pl.when(now == 1)
        def _():
            sm_copy(0, sm_v, sm_in_v.at[0], 0, sibling).wait()
            sm_v[...] = sm_v[...] + sm_in_v[0]

        @pl.when(now == 1 + sm_reach - sm_distance)
        def _():
            @pl.when((z > 0) & (z <= sm_root))
            def _():
                sm_copy(1, sm_v, sm_in_v.at[1], 1, sibling).wait_recv()
                sm_v[...] = sm_v[...] + sm_in_v[1]

            @pl.when((z < depth - 1) & (z >= sm_root))
            def _():
                sm_copy(1, sm_v, sm_in_v.at[2], 2, sibling).wait_recv()
                sm_v[...] = sm_v[...] + sm_in_v[2]

            @pl.when(z < sm_root)
            def _():
                sm_copy(1, sm_v, sm_in_v.at[1], 1, right).start()

            @pl.when(z > sm_root)
            def _():
                sm_copy(1, sm_v, sm_in_v.at[2], 2, left).start()

            @pl.when(z == sm_root)
            def _():
                sm_copy(1, sm_v, sm_in_v.at[3], 3, partner).start()

        @pl.when((now == 2 + sm_reach) & (z == sm_root))
        def _():
            sm_copy(1, sm_v, sm_in_v.at[3], 3, partner).wait_recv()
            sm_o_v[...] = sm_v[...] + sm_in_v[3]

        @pl.when(now == 2 + sm_reach + sm_distance)
        def _():
            @pl.when(z != sm_root)
            def _():
                sm_copy(2, sm_o_v, sm_o_v, 4, sibling).wait_recv()

            @pl.when((z > 0) & (z <= sm_root))
            def _():
                sm_copy(2, sm_o_v, sm_o_v, 4, left).start()

            @pl.when((z < depth - 1) & (z >= sm_root))
            def _():
                sm_copy(3, sm_o_v, sm_o_v, 4, right).start()

    def small_finish():
        sm_copy(1, sm_v, sm_in_v.at[1], 1, sibling).wait_send()

        @pl.when((z > 0) & (z <= sm_root))
        def _():
            sm_copy(2, sm_o_v, sm_o_v, 4, left).wait_send()

        @pl.when((z < depth - 1) & (z >= sm_root))
        def _():
            sm_copy(3, sm_o_v, sm_o_v, 4, right).wait_send()

        o_small[...] = sm_o_v[...]

    load(jnp.int32(0), True)
    neighbours = 2 + (z > 0).astype(jnp.int32) + (z < depth - 1).astype(jnp.int32)
    pl.semaphore_wait(barrier, neighbours)

    last = max(
        [2 + half_depth + half_depth + 2] + [2 + tree.reach + max(tree.root, depth - 1 - tree.root) + 1 for tree in line]
    )

    def one_round(now, carry):
        slot = lax.rem(now, 2)

        @pl.when(now < count)
        def _():
            load(now, False)

            @pl.when(now + 1 < count)
            def _():
                load(now + 1, True)

            def form():
                p_v[slot] = dot_tn(left_v[slot], right_v[slot]).astype(BF16)

            view = p_v.at[slot, at(theirs, HALF)]
            send(CX, now, view, s_v.at[now], recv_sem.at[CX, now], sibling, form)

        step = now - 1

        @pl.when((step >= 0) & (step < count))
        def _():
            arrived(CX, step, s_v.at[step])
            add_into(s_v.at[step], p_v.at[1 - slot, at(own, HALF)])
            view = s_v.at[step, at(other, RAIL)]
            send(UP, step, view, y_v.at[step, pl.ds(0, RAIL)], recv_sem.at[UP, step], partner)

        for tree in line:
            tree.towards(now)

        step_up = now - 2

        @pl.when((step_up >= 0) & (step_up < count))
        def _():
            view = y_v.at[step_up, pl.ds(0, RAIL)]
            arrived(UP, step_up, view)
            add_into(rail.part(step_up), view)

        rail.towards(now)
        rail.away(now)
        for tree in line:
            tree.away(now)

        step_down = now - 2 - half_depth - other_distance - 1

        @pl.when((step_down >= 0) & (step_down < count))
        def _():
            view = o_v.at[step_down, at(own + other, RAIL)]
            arrived(DOWN, step_down, view)
            send(SIB_OTHER, step_down, view, view, recv_sem.at[SIB_OTHER, step_down], sibling)

        step_sib = step_down - 1

        @pl.when((step_sib >= 0) & (step_sib < count))
        def _():
            arrived(SIB_OTHER, step_sib, o_v.at[step_sib, at(theirs + other, RAIL)])

        small_round(now)

        return carry

    lax.fori_loop(0, count + last, one_round, 0)
    finish_send(CX, s_v.at[0])
    finish_send(UP, rail.part(0))
    finish_send(DOWN, rail.part(0))
    finish_send(SIB_OTHER, rail.part(0))
    rail.finish()
    for tree in line:
        tree.finish()
    small_finish()


def reduce_gradients(depth, gelu, d_down, low, d_up, ctx, d_attn, hid, d_qkv, small):
    rows = d_down.shape[0]
    columns = WIDTH
    count = SLABS
    kinds = 9 + 4 * len(LINES)
    return pl.pallas_call(
        functools.partial(reduce_kernel, depth),
        out_shape=[
            pltpu.VMEM((count, SLAB, columns), BF16),
            jax.ShapeDtypeStruct((SMALL_ROWS, small.shape[-1]), F32),
        ],
        in_specs=[ANY] * 8 + [VMEM],
        out_specs=[VMEM] * 2,
        scratch_shapes=[
            pltpu.VMEM((2, rows, SLAB), BF16),
            pltpu.VMEM((2, rows, columns), BF16),
            pltpu.VMEM((2, SLAB, columns), BF16),
            pltpu.VMEM((count, HALF, columns), BF16),
            pltpu.VMEM((count, RAIL + max(LINES), columns), BF16),
            pltpu.VMEM((count, RAIL + sum(LINES), columns), BF16),
            pltpu.VMEM((count, RAIL + sum(LINES), columns), BF16),
            pltpu.VMEM((SMALL_ROWS, small.shape[-1]), F32),
            pltpu.VMEM((4, SMALL_ROWS, small.shape[-1]), F32),
            pltpu.VMEM((SMALL_ROWS, small.shape[-1]), F32),
            pltpu.SemaphoreType.DMA((2, 2)),
            pltpu.SemaphoreType.DMA((kinds, 2)),
            pltpu.SemaphoreType.DMA((kinds, count)),
            pltpu.SemaphoreType.DMA((4,)),
            pltpu.SemaphoreType.DMA((5,)),
        ],
        compiler_params=pltpu.CompilerParams(
            collective_id=0, has_side_effects=True, vmem_limit_bytes=REDUCE_LIMIT
        ),
        name="reduce_gradients",
    )(gelu, d_down, low, d_up, ctx, d_attn, hid, d_qkv, small)


def finish_kernel(*refs):
    (totals, small, act, d_hid) = refs[:4]
    (o_act, o_hid, o_down, o_up, o_out, o_qkv, o_qv, o_bias, o_gain, o_shift, o_up_bias) = refs[4:15]
    stage_v, stage_sem, move_sem = refs[15:]
    moves = [begin(act, o_act.at[0], move_sem.at[0]), begin(d_hid, o_hid.at[0], move_sem.at[1])]
    o_qv[0] = small[0:2, :]
    o_bias[0] = small[2:4, :]
    o_gain[0] = small[4:6, :]
    o_shift[0] = small[6:8, :]
    for part in range(FF // D):
        o_up_bias[0:1, part * D : (part + 1) * D] = small[8 + part : 9 + part, :]
    places = []
    for array in (o_down, o_up, o_out, o_qkv):
        _, rows, columns = array.shape
        places += [(array, row, column) for row in range(rows // SLAB) for column in range(columns // WIDTH)]
    slots = stage_v.shape[0]
    copies = []
    for index, (array, row, column) in enumerate(places):
        slot = index % slots
        if index >= slots:
            copies[index - slots].wait()
        stage_v[slot] = totals[index].astype(F32)
        target = array.at[0, pl.ds(row * SLAB, SLAB), pl.ds(column * WIDTH, WIDTH)]
        copies.append(begin(stage_v.at[slot], target, stage_sem.at[slot]))
    for copy in copies[-slots:] + moves:
        copy.wait()


def finish(totals, small, act, d_hid):
    slots = 6
    shapes = [
        jax.ShapeDtypeStruct((1, *act.shape), BF16),
        jax.ShapeDtypeStruct((1, *act.shape), BF16),
        jax.ShapeDtypeStruct((1, FF, D), F32),
        jax.ShapeDtypeStruct((1, D, FF), F32),
        jax.ShapeDtypeStruct((1, D, D), F32),
        jax.ShapeDtypeStruct((1, D, 3 * D), F32),
        jax.ShapeDtypeStruct((1, 2, D), F32),
        jax.ShapeDtypeStruct((1, 2, D), F32),
        jax.ShapeDtypeStruct((1, 2, D), F32),
        jax.ShapeDtypeStruct((1, 2, D), F32),
        jax.ShapeDtypeStruct((1, FF), F32),
    ]
    return pl.pallas_call(
        finish_kernel,
        out_shape=shapes,
        in_specs=[VMEM, VMEM, ANY, ANY],
        out_specs=[ANY] * 6 + [VMEM] * 5,
        scratch_shapes=[
            pltpu.VMEM((slots, SLAB, WIDTH), F32),
            pltpu.SemaphoreType.DMA((slots,)),
            pltpu.SemaphoreType.DMA((2,)),
        ],
        compiler_params=pltpu.CompilerParams(vmem_limit_bytes=16 << 20),
        name="finish",
    )(pltpu.with_memory_space_constraint(totals, pltpu.VMEM), small, act, d_hid)


def shards(
    tokens, segments, lengths, cotangent, qkv_weight, qv_bias, out_weight, out_biases,
    norm_gains, norm_shifts, up_weight, up_bias, down_weight,
):
    weights = (qkv_weight, out_weight, up_weight, down_weight)
    params = (qv_bias, out_biases, norm_gains, norm_shifts, up_bias)
    act, d_hid, small, kept = layers(tokens, cotangent, weights, segments, lengths, params)
    totals, small = reduce_gradients(
        lax.axis_size("dp") // 4, kept["gelu"], kept["d_down"], kept["low"], kept["d_up"],
        kept["ctx"], kept["d_attn"], kept["hid"], kept["d_qkv"], small,
    )
    (
        o_act, o_hid, g_down, g_up, g_out, g_qkv, g_qv, g_bias, g_gain, g_shift, g_up_bias
    ) = finish(totals, small, act, d_hid)
    return (o_act, o_hid, g_qkv, g_qv, g_out, g_bias, g_gain, g_shift, g_up, g_up_bias, g_down)


def solution(mesh):
    return jax.shard_map(
        shards,
        mesh=mesh,
        in_specs=(
            P("dp", None), P("dp", None), P("dp"), P("dp", None),
            P("section", None, None), P("section", None, None), P("section", None, None), P("section", None, None),
            P("section", None, None), P("section", None, None), P("section", None, None), P("section", None),
            P("section", None, None),
        ),
        out_specs=(
            P("section", "dp", None), P("section", "dp", None),
            P("section", None, None), P("section", None, None), P("section", None, None), P("section", None, None),
            P("section", None, None), P("section", None, None), P("section", None, None), P("section", None),
            P("section", None, None),
        ),
        check_vma=False,
    )
```

```python
import functools
import math

import jax
import jax.numpy as jnp
from jax import lax
from jax.experimental import pallas as pl
from jax.experimental.pallas import tpu as pltpu
from jax.sharding import PartitionSpec as P

D = 768
H = 12
HD = 64
FF = 3072
SEQ = 512
MICRO = 2
PAIRS = H // 2
PAIR = 2 * HD
GROUP = PAIRS // 2

EPSILON = 1e-05
SCORE_SCALE = 0.125
NEG_FILL = -1e30
F32 = jnp.float32
BF16 = jnp.bfloat16
VMEM_LIMIT = 60 << 20
REDUCE_LIMIT = 44 << 20
MESH = pl.DeviceIdType.MESH

ANY = pl.BlockSpec(memory_space=pl.ANY)
VMEM = pl.BlockSpec(memory_space=pltpu.VMEM)
SMEM = pl.BlockSpec(memory_space=pltpu.SMEM)


def dot_nn(left, right):
    return lax.dot_general(left, right, (((1,), (0,)), ((), ())), preferred_element_type=F32)


def dot_nt(left, right):
    return lax.dot_general(left, right, (((1,), (1,)), ((), ())), preferred_element_type=F32)


def dot_tn(left, right):
    return lax.dot_general(left, right, (((0,), (0,)), ((), ())), preferred_element_type=F32)


def begin(source, target, sem):
    copy = pltpu.make_async_copy(source, target, sem)
    copy.start()
    return copy


def gelu_and_slope(u):
    normal_cdf = 0.5 + 0.5 * lax.erf(u * (1.0 / math.sqrt(2.0)))
    bell = jnp.exp((-0.5 * u) * u)
    return u * normal_cdf, normal_cdf + (u * (1.0 / math.sqrt(2.0 * math.pi))) * bell


def normalize(resid):
    average = jnp.mean(resid, axis=-1, keepdims=True)
    centred = resid - average
    variance = jnp.mean(centred * centred, axis=-1, keepdims=True)
    inverse = lax.rsqrt(variance + EPSILON)
    return centred * inverse, inverse


def norm_back(grad_out, scaled, inverse, gain):
    weighted = grad_out * gain
    first_mean = jnp.mean(weighted, axis=-1, keepdims=True)
    second_mean = jnp.mean(weighted * scaled, axis=-1, keepdims=True)
    return inverse * (weighted - first_mean - scaled * second_mean)


def half_mask(which):
    lane = lax.broadcasted_iota(jnp.int32, (1, PAIR), 1)
    return ((lane // HD) == which).astype(F32).astype(BF16)


ROWS = SEQ // 2
class Place:
    def __init__(self):
        self.section = lax.axis_index("section")
        self.me = lax.axis_index("dp")
        self.core = lax.rem(self.me, 2)
        self.sibling = (self.section, self.me + 1 - 2 * self.core)
        self.other_layer = (1 - self.section, self.me)
        self.own = pl.ds(pl.multiple_of(self.core * ROWS, ROWS), ROWS)
        self.theirs = pl.ds(pl.multiple_of(ROWS - self.core * ROWS, ROWS), ROWS)

    def greet(self):
        barrier = pltpu.get_barrier_semaphore()
        for device in (self.sibling, self.other_layer):
            pl.semaphore_signal(barrier, inc=1, device_id=device, device_id_type=MESH)
        pl.semaphore_wait(barrier, 2)

    def is_mine(self, step, sequences):
        return lax.div(step, sequences) == self.core


def remote(source, target, send_sem, recv_sem, device):
    return pltpu.make_async_remote_copy(source, target, send_sem, recv_sem, device_id=device, device_id_type=MESH)


class Rows:
    def __init__(self, place, sequences, array, steps, local, sent, arrived):
        self.place, self.sequences, self.array, self.steps = place, sequences, array, steps
        self.local, self.sent, self.arrived = local, sent, arrived

    def part(self, sequence, core):
        return self.array.at[pl.ds(pl.multiple_of(sequence * SEQ + core * ROWS, ROWS), ROWS)]

    def spread(self):
        place = self.place
        for sequence in range(self.sequences):
            step = place.core * self.sequences + sequence
            target = self.steps.at[step]
            pltpu.make_async_copy(self.part(sequence, place.core), target, self.local.at[sequence]).start()
            remote(
                self.part(sequence, 1 - place.core), target, self.sent.at[sequence], self.arrived.at[step], place.sibling
            ).start()

    def spread_done(self):
        for sequence in range(self.sequences):
            view = self.steps.at[0]
            remote(view, view, self.sent.at[sequence], self.arrived.at[0], self.place.sibling).wait_send()

    def await_step(self, step, spread):
        mine = spread & self.place.is_mine(step, self.sequences)
        view = self.steps.at[step]

        @pl.when(mine)
        def _():
            pltpu.make_async_copy(view, view, self.local.at[lax.rem(step, self.sequences)]).wait()

        @pl.when(jnp.logical_not(mine))
        def _():
            remote(view, view, self.sent.at[0], self.arrived.at[step], self.place.sibling).wait_recv()

    def collect(self, step):
        sequence = lax.rem(step, self.sequences)
        target = self.part(sequence, self.place.core)
        mine = self.place.is_mine(step, self.sequences)

        @pl.when(mine)
        def _():
            pltpu.make_async_copy(self.steps.at[step], target, self.local.at[sequence]).start()

        @pl.when(jnp.logical_not(mine))
        def _():
            remote(
                self.steps.at[step], target, self.sent.at[sequence], self.arrived.at[sequence], self.place.sibling
            ).start()

    def collect_done(self):
        for sequence in range(self.sequences):
            view = self.steps.at[0]
            pltpu.make_async_copy(view, view, self.local.at[sequence]).wait()
            remote(view, view, self.sent.at[sequence], self.arrived.at[sequence], self.place.sibling).wait()


SAVED = (
    ("hid", D, BF16),
    ("low", D, BF16),
    ("gelu", FF, BF16),
    ("ctx", D, BF16),
    ("q", D, BF16),
    ("linv", D, F32),
    ("xh1", D, BF16),
    ("inv1", 128, F32),
    ("slope", FF, BF16),
    ("xh2", D, BF16),
    ("inv2", 128, F32),
)
GRADS = (("d_down", D, BF16), ("d_up", FF, BF16), ("d_attn", D, BF16), ("d_qkv", 3 * D, BF16))
SMALL_ROWS = 16


def layers_kernel(sequences, *refs):
    (tok, cot, wqkv, wo, wu, wd, segs, lens, qv_bias, out_biases, gains, shifts, up_bias) = refs[:13]
    act_out, d_hid_out, small_out, prob_io = refs[13:17]
    stop = 17 + len(SAVED)
    saved = dict(zip([name for name, _, _ in SAVED], refs[17:stop]))
    grads = dict(zip([name for name, _, _ in GRADS], refs[stop : stop + len(GRADS)]))
    stop += len(GRADS)
    (
        h_v, act_v, g_v, d_hid_v, kv_v, p_v, wqkv_v, wo_v, wu_v, wd_v, bias_v, acc_v, seg_own, seg_their,
        d_ctx_v, part_v, their_v,
    ) = refs[stop : stop + 17]
    stop += 17
    buffers = dict(zip([name for name, _, _ in SAVED if name != "hid"], refs[stop : stop + len(SAVED) - 1]))
    stop += len(SAVED) - 1
    grad_buffers = dict(zip([name for name, _, _ in GRADS], refs[stop : stop + len(GRADS)]))
    stop += len(GRADS)
    (
        w_sem, save_sem, hid_sem, grad_sem, p_sem, seg_sem, kv_sent, kv_arrived, part_sent, part_arrived,
        in_local, in_sent, in_arrived, out_local, out_sent, out_arrived, hop_sent,
        up_local, up_sent, up_arrived, down_local, down_sent, down_arrived, back_sent,
    ) = refs[stop:]
    place = Place()
    section = place.section
    steps = 2 * sequences
    names = [name for name, _, _ in SAVED]
    grad_names = [name for name, _, _ in GRADS]
    inputs = Rows(place, sequences, tok, h_v, in_local, in_sent, in_arrived)
    outputs = Rows(place, sequences, act_out, act_v, out_local, out_sent, out_arrived)
    upstream = Rows(place, sequences, cot, g_v, up_local, up_sent, up_arrived)
    downstream = Rows(place, sequences, d_hid_out, d_hid_v, down_local, down_sent, down_arrived)

    def at_step(array, step):
        return array.at[pl.ds(pl.multiple_of(step * ROWS, ROWS), ROWS)]

    def save(name, step):
        pltpu.make_async_copy(buffers[name], at_step(saved[name], step), save_sem.at[names.index(name)]).start()

    def fetch(name, step):
        pltpu.make_async_copy(at_step(saved[name], step), buffers[name], save_sem.at[names.index(name)]).start()

    def settle(name):
        pltpu.make_async_copy(buffers[name], buffers[name], save_sem.at[names.index(name)]).wait()

    def prob_part(group, step):
        heads = pl.ds(group * 2 * GROUP, 2 * GROUP)
        return p_v.at[heads], prob_io.at[step, heads], p_sem.at[group]

    def settle_prob():
        for group in range(2):
            view, _, sem = prob_part(group, 0)
            pltpu.make_async_copy(view, view, sem).wait()

    def when_first(step, copies):
        @pl.when(step == 0)
        def _():
            for copy in copies:
                copy.wait()

    def column_sum(value):
        return jnp.sum(value, axis=0, keepdims=True)

    get_qkv = [
        begin(wqkv.at[0, :, pl.ds(block * D, D)], wqkv_v.at[:, pl.ds(block * D, D)], w_sem.at[block])
        for block in (1, 2, 0)
    ]
    position = lax.broadcasted_iota(jnp.int32, (1, SEQ), 1)
    for sequence in range(sequences):
        seg_own[sequence, 0:1, :] = segs[sequence : sequence + 1, :].astype(F32)
        seg_own[sequence, 1:2, :] = (position < lens[sequence]).astype(F32)
        seg_own[sequence, 2:8, :] = jnp.zeros((6, SEQ), F32)
    place.greet()
    seg_copy = remote(seg_own, seg_their, seg_sem.at[0], seg_sem.at[1], place.sibling)

    @pl.when(section == 0)
    def _():
        inputs.spread()

    @pl.when(section == 1)
    def _():
        upstream.spread()

    seg_copy.start()
    get_wo = begin(wo.at[0], wo_v, w_sem.at[3])
    get_wu = begin(wu.at[0], wu_v, w_sem.at[4])
    get_wd = begin(wd.at[0], wd_v, w_sem.at[5])
    small_out[...] = jnp.zeros_like(small_out)

    def forward_step(step, carry):
        inputs.await_step(step, section == 0)
        pltpu.make_async_copy(h_v.at[step], at_step(saved["hid"], step), hid_sem.at[step]).start()
        hidden = h_v[step]
        for block in (1, 2):
            when_first(step, (get_qkv[block - 1],))
            proj = dot_nn(hidden, wqkv_v[:, block * D : (block + 1) * D])
            if block == 2:
                proj = proj + qv_bias[0, 1:2, :]
            cols = pl.ds((block - 1) * D, D)
            kv_v[step, place.own, cols] = proj.astype(BF16)
            view = kv_v.at[step, place.own, cols]
            remote(view, view, kv_sent.at[step, block - 1], kv_arrived.at[step, block - 1], place.sibling).start()

        def await_keys_or_values(block):
            view = kv_v.at[step, place.theirs, pl.ds(block * D, D)]
            remote(view, view, kv_sent.at[step, block], kv_arrived.at[step, block], place.sibling).wait_recv()

        @pl.when(step == 0)
        def _():
            get_qkv[2].wait()
            seg_copy.wait()

        @pl.when(step > 0)
        def _():
            settle("q")

        buffers["q"][...] = (dot_nn(hidden, wqkv_v[:, 0:D]) + qv_bias[0, 0:1, :]).astype(BF16)

        sequence = lax.rem(step, sequences)
        mine = jnp.where(place.is_mine(step, sequences), 1.0, 0.0)
        key_rows = mine * seg_own[sequence] + (1.0 - mine) * seg_their[sequence]
        query_row = mine * seg_own[sequence, 0:1, place.own] + (1.0 - mine) * seg_their[sequence, 0:1, place.own]
        query_seg = jnp.transpose(jnp.broadcast_to(query_row, (128, ROWS)))
        query = lax.broadcasted_iota(jnp.int32, (ROWS, 128), 0) + place.core * ROWS
        key = lax.broadcasted_iota(jnp.int32, (ROWS, 128), 1)
        for tile in range(SEQ // 128):
            cols = slice(tile * 128, (tile + 1) * 128)
            visible = (key_rows[1:2, cols] > 0.5) | (key + tile * 128 == query)
            bias_v[:, cols] = jnp.where((query_seg == key_rows[0:1, cols]) & visible, 0.0, NEG_FILL)

        @pl.when(step > 0)
        def _():
            for name in buffers:
                if name != "q":
                    settle(name)
            settle_prob()

        await_keys_or_values(0)
        q_v, linv_v, ctx_v = buffers["q"], buffers["linv"], buffers["ctx"]
        for group in range(2):
            for pair in range(group * GROUP, (group + 1) * GROUP):
                at = pair * PAIR
                q2 = q_v[:, at : at + PAIR] * SCORE_SCALE
                k2 = kv_v[step, :, at : at + PAIR]
                weights = []
                for head in range(2):
                    scores = dot_nt(q2, k2 * half_mask(head)) + bias_v[...]
                    weight = jnp.exp(scores - jnp.max(scores, axis=-1, keepdims=True)).astype(BF16)
                    p_v[pair * 2 + head] = weight
                    weights.append(weight)
                if pair == 0:
                    await_keys_or_values(1)
                    when_first(step, (get_wo, get_wu, get_wd))
                v2 = kv_v[step, :, D + at : D + at + PAIR]
                total = None
                for head in range(2):
                    mask = half_mask(head)
                    values = jnp.concatenate([v2 * mask, jnp.broadcast_to(mask, (SEQ, PAIR))], axis=1)
                    part = dot_nn(weights[head], values)
                    total = part if total is None else total + part
                inverse = 1.0 / total[:, PAIR : 2 * PAIR]
                linv_v[:, at : at + PAIR] = inverse
                ctx_v[:, at : at + PAIR] = (total[:, 0:PAIR] * inverse).astype(BF16)
            view, target, sem = prob_part(group, step)
            pltpu.make_async_copy(view, target, sem).start()
        resid = hidden.astype(F32) + (dot_nn(ctx_v[...], wo_v[...]) + out_biases[0, 0:1, :])
        scaled, inverse = normalize(resid)
        buffers["xh1"][...] = scaled.astype(BF16)
        buffers["inv1"][...] = jnp.broadcast_to(inverse, (ROWS, 128))
        normed = scaled * gains[0, 0:1, :] + shifts[0, 0:1, :]
        buffers["low"][...] = normed.astype(BF16)
        acc_v[...] = normed + out_biases[0, 1:2, :]
        width = 1024
        for half in range(2):
            rows = slice(half * ROWS // 2, (half + 1) * ROWS // 2)
            for chunk in range(FF // width):
                cols = slice(chunk * width, (chunk + 1) * width)
                up = dot_nn(buffers["low"][rows, :], wu_v[:, cols]) + up_bias[0:1, cols]
                gelu, slope = gelu_and_slope(up)
                gelu = gelu.astype(BF16)
                buffers["gelu"][rows, cols] = gelu
                buffers["slope"][rows, cols] = slope.astype(BF16)
                acc_v[rows, :] += dot_nn(gelu, wd_v[cols, :])
            scaled, inverse = normalize(acc_v[rows, :])
            act_v[step, rows, :] = (scaled * gains[0, 1:2, :] + shifts[0, 1:2, :]).astype(BF16)
            buffers["xh2"][rows, :] = scaled.astype(BF16)
            buffers["inv2"][rows, :] = jnp.broadcast_to(inverse, (ROWS // 2, 128))

            @pl.when(section == 0)
            def _():
                source, target = [array.at[step, pl.ds(half * (ROWS // 2), ROWS // 2)] for array in (act_v, h_v)]
                remote(source, target, hop_sent.at[step], in_arrived.at[step], place.other_layer).start()

        outputs.collect(step)
        for name in buffers:
            save(name, step)
        return carry

    lax.fori_loop(0, steps, forward_step, 0)

    def backward_step(turn, carry):
        step = steps - 1 - turn

        early = ("xh2", "inv2", "slope", "xh1", "inv1")
        late = ("q", "linv", "ctx")

        def part_copy(group):
            pairs = pl.ds(group * GROUP, GROUP)
            return remote(
                part_v.at[pairs, place.theirs], their_v.at[step, pairs], part_sent.at[group],
                part_arrived.at[step, group], place.sibling,
            )

        def keep(name):
            pltpu.make_async_copy(
                grad_buffers[name], at_step(grads[name], step), grad_sem.at[grad_names.index(name)]
            ).start()

        def free(name):
            buffer = grad_buffers[name]
            pltpu.make_async_copy(buffer, buffer, grad_sem.at[grad_names.index(name)]).wait()

        upstream.await_step(step, section == 1)

        @pl.when(turn > 0)
        def _():
            for name in early:
                settle(name)
            for name in ("d_down", "d_up", "d_attn"):
                free(name)

        grad = g_v[step].astype(F32)
        scaled = buffers["xh2"][...].astype(F32)
        small_out[5:6, :] += column_sum(grad * scaled)
        small_out[7:8, :] += column_sum(grad)
        d_r2 = norm_back(grad, scaled, buffers["inv2"][:, 0:1], gains[0, 1:2, :])
        d_down = d_r2.astype(BF16)
        d_down_v, d_up_v, d_attn_v, d_qkv_v = [grad_buffers[name] for name in grad_names]
        d_down_v[...] = d_down
        small_out[3:4, :] += column_sum(d_down.astype(F32))
        acc_v[...] = d_r2
        for chunk in range(FF // D):
            cols = slice(chunk * D, (chunk + 1) * D)
            d_up = (dot_nt(d_down_v[...], wd_v[cols, :]) * buffers["slope"][:, cols].astype(F32)).astype(BF16)
            d_up_v[:, cols] = d_up
            small_out[8 + chunk : 9 + chunk, :] += column_sum(d_up.astype(F32))
            acc_v[...] += dot_nt(d_up, wu_v[:, cols])
        d_normed = acc_v[...]
        scaled = buffers["xh1"][...].astype(F32)
        small_out[4:5, :] += column_sum(d_normed * scaled)
        small_out[6:7, :] += column_sum(d_normed)
        d_r1 = norm_back(d_normed, scaled, buffers["inv1"][:, 0:1], gains[0, 0:1, :])
        d_attn = d_r1.astype(BF16)
        d_attn_v[...] = d_attn
        small_out[2:3, :] += column_sum(d_attn.astype(F32))
        acc_v[...] = d_r1

        @pl.when(turn == 0)
        def _():
            for name in early:
                settle(name)

        @pl.when(turn > 0)
        def _():
            for name in late:
                settle(name)
            settle_prob()
            free("d_qkv")
            for group in range(2):
                part_copy(group).wait_send()

        @pl.when(turn + 1 < steps)
        def _():
            for name in early:
                fetch(name, step - 1)

        for name in ("d_down", "d_up", "d_attn"):
            keep(name)
        d_ctx_v[...] = (dot_nt(d_attn_v[...], wo_v[...]) * buffers["linv"][...]).astype(BF16)
        q_v, ctx_v = buffers["q"], buffers["ctx"]
        for group in range(2):
            for pair in range(group * GROUP, (group + 1) * GROUP):
                at = pair * PAIR
                q2 = q_v[:, at : at + PAIR] * SCORE_SCALE
                k2 = kv_v[step, :, at : at + PAIR]
                v2 = kv_v[step, :, D + at : D + at + PAIR]
                dc2 = d_ctx_v[:, at : at + PAIR]
                inner = dc2.astype(F32) * ctx_v[:, at : at + PAIR].astype(F32)
                d_q, d_k, d_v = None, None, None
                for head in range(2):
                    mask = half_mask(head)
                    dc_own = dc2 * mask
                    weight = p_v[pair * 2 + head]
                    row_inner = jnp.sum(inner * mask.astype(F32), axis=-1, keepdims=True)
                    d_prob = dot_nt(dc_own, v2)
                    d_score = (weight.astype(F32) * (d_prob - row_inner)).astype(BF16)
                    one_v = dot_tn(dc_own, weight)
                    one_k = dot_tn(q2 * mask, d_score)
                    one_q = dot_nn(d_score, k2 * mask)
                    d_v = one_v if d_v is None else d_v + one_v
                    d_k = one_k if d_k is None else d_k + one_k
                    d_q = one_q if d_q is None else d_q + one_q
                d_qkv_v[:, at : at + PAIR] = (d_q * SCORE_SCALE).astype(BF16)
                part_v[pair, :, 0:PAIR] = jnp.transpose(d_k).astype(BF16)
                part_v[pair, :, PAIR : 2 * PAIR] = jnp.transpose(d_v).astype(BF16)
            part_copy(group).start()

        @pl.when(turn == 0)
        def _():
            for name in late:
                settle(name)
            settle_prob()

        @pl.when(turn + 1 < steps)
        def _():
            for name in late:
                fetch(name, step - 1)
            for group in range(2):
                view, source, sem = prob_part(group, step - 1)
                pltpu.make_async_copy(source, view, sem).start()

        d_query = d_qkv_v[:, 0:D]
        acc_v[...] += dot_nt(d_query, wqkv_v[:, 0:D])
        small_out[0:1, :] += column_sum(d_query.astype(F32))
        for group in range(2):
            start = group * GROUP
            part_copy(group).wait_recv()
            for pair in range(start, start + GROUP):
                total = part_v[pair, place.own, :].astype(F32) + their_v[step, pair].astype(F32)
                at = pair * PAIR
                d_qkv_v[:, D + at : D + at + PAIR] = total[:, 0:PAIR].astype(BF16)
                d_qkv_v[:, 2 * D + at : 2 * D + at + PAIR] = total[:, PAIR : 2 * PAIR].astype(BF16)
            keys = slice(D + start * PAIR, D + (start + GROUP) * PAIR)
            values = slice(2 * D + start * PAIR, 2 * D + (start + GROUP) * PAIR)
            d_hid = acc_v[...] + dot_nt(d_qkv_v[:, keys], wqkv_v[:, keys]) + dot_nt(d_qkv_v[:, values], wqkv_v[:, values])
            if group == 0:
                acc_v[...] = d_hid
            else:
                d_hid_v[step] = d_hid.astype(BF16)

        @pl.when(section == 1)
        def _():
            remote(d_hid_v.at[step], g_v.at[step], back_sent.at[step], up_arrived.at[step], place.other_layer).start()

        downstream.collect(step)
        small_out[1:2, :] += column_sum(d_qkv_v[:, 2 * D : 3 * D].astype(F32))
        keep("d_qkv")
        return carry

    lax.fori_loop(0, steps, backward_step, 0)

    for name in ("low", "gelu"):
        settle(name)
    for name in grad_names:
        buffer = grad_buffers[name]
        pltpu.make_async_copy(buffer, buffer, grad_sem.at[grad_names.index(name)]).wait()
    for group in range(2):
        view = part_v.at[pl.ds(group * GROUP, GROUP), place.theirs]
        remote(view, view, part_sent.at[group], part_arrived.at[0, group], place.sibling).wait_send()
    for step in range(steps):
        pltpu.make_async_copy(h_v.at[step], h_v.at[step], hid_sem.at[step]).wait()
        for block in range(2):
            view = kv_v.at[step, place.own, pl.ds(block * D, D)]
            remote(view, view, kv_sent.at[step, block], kv_arrived.at[step, block], place.sibling).wait_send()

    @pl.when(section == 0)
    def _():
        inputs.spread_done()
        for step in range(steps):
            remote(act_v.at[step], h_v.at[step], hop_sent.at[step], in_arrived.at[step], place.other_layer).wait_send()

    @pl.when(section == 1)
    def _():
        upstream.spread_done()
        for step in range(steps):
            remote(d_hid_v.at[step], g_v.at[step], back_sent.at[step], up_arrived.at[step], place.other_layer).wait_send()

    outputs.collect_done()
    downstream.collect_done()


def layers(tokens, cotangent, weights, segments, lengths, params):
    total = tokens.shape[0]
    sequences = total // SEQ
    steps = 2 * sequences
    shapes = [
        jax.ShapeDtypeStruct((total, D), BF16),
        jax.ShapeDtypeStruct((total, D), BF16),
        jax.ShapeDtypeStruct((SMALL_ROWS, D), F32),
        jax.ShapeDtypeStruct((steps, H, ROWS, SEQ), BF16),
    ] + [jax.ShapeDtypeStruct((total, width), dtype) for _, width, dtype in SAVED + GRADS]
    dma = pltpu.SemaphoreType.DMA
    act, d_hid, small, _, *rest = pl.pallas_call(
        functools.partial(layers_kernel, sequences),
        out_shape=shapes,
        in_specs=[ANY] * 6 + [VMEM, SMEM] + [VMEM] * 5,
        out_specs=[ANY, ANY, VMEM] + [ANY] * (len(shapes) - 3),
        scratch_shapes=[pltpu.VMEM((steps, ROWS, D), BF16)] * 4
        + [
            pltpu.VMEM((steps, SEQ, 2 * D), BF16),
            pltpu.VMEM((H, ROWS, SEQ), BF16),
            pltpu.VMEM((D, 3 * D), BF16),
            pltpu.VMEM((D, D), BF16),
            pltpu.VMEM((D, FF), BF16),
            pltpu.VMEM((FF, D), BF16),
            pltpu.VMEM((ROWS, SEQ), F32),
            pltpu.VMEM((ROWS, D), F32),
            pltpu.VMEM((sequences, 8, SEQ), F32),
            pltpu.VMEM((sequences, 8, SEQ), F32),
            pltpu.VMEM((ROWS, D), BF16),
            pltpu.VMEM((PAIRS, SEQ, 2 * PAIR), BF16),
            pltpu.VMEM((steps, PAIRS, ROWS, 2 * PAIR), BF16),
        ]
        + [pltpu.VMEM((ROWS, width), dtype) for name, width, dtype in SAVED + GRADS if name != "hid"]
        + [
            dma((6,)), dma((len(SAVED),)), dma((steps,)), dma((len(GRADS),)), dma((2,)), dma((2,)),
            dma((steps, 2)), dma((steps, 2)), dma((2,)), dma((steps, 2)),
        ]
        + [dma((sequences,)), dma((sequences,)), dma((steps,))]
        + [dma((sequences,)), dma((sequences,)), dma((sequences,)), dma((steps,))]
        + [dma((sequences,)), dma((sequences,)), dma((steps,))]
        + [dma((sequences,)), dma((sequences,)), dma((sequences,)), dma((steps,))],
        compiler_params=pltpu.CompilerParams(
            collective_id=1, has_side_effects=True, vmem_limit_bytes=VMEM_LIMIT
        ),
        name="layers",
    )(tokens, cotangent, *weights, segments, lengths, *params)
    return act, d_hid, small, dict(zip([name for name, _, _ in SAVED + GRADS], rest))


UNIT = 16
SLAB = D
WIDTH = D // 2
HALF = SLAB // 2
RAIL = 7 * UNIT
LINES = (3 * UNIT, 2 * UNIT, 2 * UNIT, 3 * UNIT)
SLABS = 2 * FF // D + FF // WIDTH + D // WIDTH + 3 * D // WIDTH


def reduce_kernel(depth, *refs):
    (gelu, d_down, low, d_up, ctx, d_attn, hid, d_qkv, small) = refs[:9]
    (o_v, o_small) = refs[9:11]
    (
        left_v, right_v, p_v, s_v, y_v, rl_v, rr_v, sm_v, sm_in_v, sm_o_v,
        load_sem, send_sem, recv_sem, sm_send, sm_recv,
    ) = refs[11:]
    plan = (
        (2 * FF // D, gelu, d_down),
        (FF // WIDTH, low, d_up),
        (D // WIDTH, ctx, d_attn),
        (3 * D // WIDTH, hid, d_qkv),
    )
    count = SLABS
    section = lax.axis_index("section")
    me = lax.axis_index("dp")
    core = lax.rem(me, 2)
    y = lax.rem(lax.div(me, 2), 2)
    z = lax.div(me, 4)
    sibling = (section, me + 1 - 2 * core)
    partner = (section, me + 2 - 4 * y)
    left = (section, me - 4)
    right = (section, me + 4)

    barrier = pltpu.get_barrier_semaphore()
    pl.semaphore_signal(barrier, inc=1, device_id=sibling, device_id_type=MESH)
    pl.semaphore_signal(barrier, inc=1, device_id=partner, device_id_type=MESH)

    @pl.when(z > 0)
    def _():
        pl.semaphore_signal(barrier, inc=1, device_id=left, device_id_type=MESH)

    @pl.when(z < depth - 1)
    def _():
        pl.semaphore_signal(barrier, inc=1, device_id=right, device_id_type=MESH)

    def at(value, size):
        return pl.ds(pl.multiple_of(value, UNIT), size)

    def load(step, start):
        slot = lax.rem(step, 2)
        if not start:
            pltpu.make_async_copy(low, left_v.at[slot], load_sem.at[0, slot]).wait()
            pltpu.make_async_copy(d_down.at[:, pl.ds(0, WIDTH)], right_v.at[slot], load_sem.at[1, slot]).wait()
            return
        first = 0
        for steps, factor, grad in plan:

            def issue(first=first, factor=factor, grad=grad):
                index = step - first
                halves = grad.shape[1] // WIDTH
                rows = pl.ds(pl.multiple_of(lax.div(index, halves) * SLAB, 128), SLAB)
                cols = pl.ds(pl.multiple_of(lax.rem(index, halves) * WIDTH, 128), WIDTH)
                pltpu.make_async_copy(factor.at[:, rows], left_v.at[slot], load_sem.at[0, slot]).start()
                pltpu.make_async_copy(grad.at[:, cols], right_v.at[slot], load_sem.at[1, slot]).start()

            pl.when((step >= first) & (step < first + steps))(issue)
            first += steps

    def send(kind, step, source, target, arrival, device, compute=None):
        parity = lax.rem(step, 2)
        copy = pltpu.make_async_remote_copy(
            source, target, send_sem.at[kind, parity], arrival, device_id=device, device_id_type=MESH
        )

        @pl.when(step >= 2)
        def _():
            copy.wait_send()

        if compute is not None:
            compute()
        copy.start()

    def finish_send(kind, view):
        for parity in range(2):
            pltpu.make_async_remote_copy(
                view, view, send_sem.at[kind, parity], recv_sem.at[kind, 0], device_id=sibling, device_id_type=MESH
            ).wait_send()

    def arrived(kind, step, view):
        pltpu.make_async_remote_copy(
            view, view, send_sem.at[kind, 0], recv_sem.at[kind, step], device_id=sibling, device_id_type=MESH
        ).wait_recv()

    own = core * HALF
    theirs = HALF - own
    CX, UP, DOWN, SIB_OTHER, YX = range(5)

    def add_into(target, term):
        target[...] = (target[...].astype(F32) + term[...].astype(F32)).astype(target.dtype)

    class Tree:
        def __init__(self, kinds, base, root, reach, size, offset, land, rail):
            self.kinds, self.base, self.root, self.reach = kinds, base, root, reach
            self.size, self.offset, self.land, self.rail = size, offset, land, rail
            self.distance = jnp.abs(z - root)
            self.from_left = (z > 0) & (z <= root)
            self.from_right = (z < depth - 1) & (z >= root)

        def part(self, step):
            return s_v.at[step, at(self.offset, self.size)]

        def total(self, step):
            return o_v.at[step, at(own + self.offset, self.size)]

        def landing(self, buffer, step):
            return buffer.at[step, pl.ds(self.land, self.size)]

        def towards(self, now):
            inward, out_left, out_right, sib = self.kinds
            step = now - self.base - self.reach + self.distance

            @pl.when((step >= 0) & (step < count))
            def _():
                @pl.when(self.from_left)
                def _():
                    arrived(out_left, step, self.landing(rl_v, step))
                    add_into(self.part(step), self.landing(rl_v, step))

                @pl.when(self.from_right)
                def _():
                    arrived(out_right, step, self.landing(rr_v, step))
                    add_into(self.part(step), self.landing(rr_v, step))

                @pl.when(z < self.root)
                def _():
                    send(inward, step, self.part(step), self.landing(rl_v, step), recv_sem.at[out_left, step], right)

                @pl.when(z > self.root)
                def _():
                    send(inward, step, self.part(step), self.landing(rr_v, step), recv_sem.at[out_right, step], left)

                @pl.when(z == self.root)
                def _():
                    if self.rail:
                        self.total(step)[...] = self.part(step)[...]
                    else:
                        view = y_v.at[step, pl.ds(RAIL, self.size)]
                        send(YX, step, self.part(step), view, recv_sem.at[YX, step], partner)

            if not self.rail:
                late = now - self.base - self.reach - 1

                @pl.when((z == self.root) & (late >= 0) & (late < count))
                def _():
                    view = y_v.at[late, pl.ds(RAIL, self.size)]
                    arrived(YX, late, view)
                    self.total(late)[...] = (self.part(late)[...].astype(F32) + view[...].astype(F32)).astype(BF16)

        def away(self, now):
            inward, out_left, out_right, sib = self.kinds
            lag = self.base + self.reach + (0 if self.rail else 1)
            step = now - lag - self.distance

            @pl.when((step >= 0) & (step < count))
            def _():
                view = self.total(step)

                @pl.when(z != self.root)
                def _():
                    arrived(inward, step, view)

                @pl.when(self.from_left)
                def _():
                    send(out_left, step, view, view, recv_sem.at[inward, step], left)

                @pl.when(self.from_right)
                def _():
                    send(out_right, step, view, view, recv_sem.at[inward, step], right)

                if self.rail:
                    send(DOWN, step, view, view, recv_sem.at[DOWN, step], partner)
                send(sib, step, view, view, recv_sem.at[sib, step], sibling)

            done = step - 1

            @pl.when((done >= 0) & (done < count))
            def _():
                arrived(sib, done, o_v.at[done, at(theirs + self.offset, self.size)])

        def finish(self):
            inward, out_left, out_right, sib = self.kinds
            view = self.part(0)

            @pl.when(z != self.root)
            def _():
                finish_send(inward, view)

            @pl.when(self.from_left)
            def _():
                finish_send(out_left, view)

            @pl.when(self.from_right)
            def _():
                finish_send(out_right, view)

            finish_send(sib, view)
            if not self.rail:

                @pl.when(z == self.root)
                def _():
                    finish_send(YX, view)

    half_depth = depth // 2
    rail_root = half_depth - 1 + y
    rail = Tree((5, 6, 7, 8), 2, rail_root, half_depth, RAIL, y * RAIL, 0, True)
    line = []
    offset = 0
    for index, size in enumerate(LINES):
        root = (2 * index + 1) * depth // (2 * len(LINES))
        kinds = tuple(9 + 4 * index + kind for kind in range(4))
        reach = max(root, depth - 1 - root)
        line.append(Tree(kinds, 1, root, reach, size, 2 * RAIL + offset, RAIL + offset, False))
        offset += size
    other_distance = jnp.abs(z - (half_depth - y))
    other = (1 - y) * RAIL

    sm_root = half_depth
    sm_reach = max(sm_root, depth - 1 - sm_root)
    sm_distance = jnp.abs(z - sm_root)

    def sm_copy(kind, source, target, arrival, device):
        return pltpu.make_async_remote_copy(
            source, target, sm_send.at[kind], sm_recv.at[arrival], device_id=device, device_id_type=MESH
        )

    def small_round(now):
        @pl.when(now == 0)
        def _():
            sm_v[...] = small[...]
            sm_copy(0, sm_v, sm_in_v.at[0], 0, sibling).start()

        @pl.when(now == 1)
        def _():
            sm_copy(0, sm_v, sm_in_v.at[0], 0, sibling).wait()
            sm_v[...] = sm_v[...] + sm_in_v[0]

        @pl.when(now == 1 + sm_reach - sm_distance)
        def _():
            @pl.when((z > 0) & (z <= sm_root))
            def _():
                sm_copy(1, sm_v, sm_in_v.at[1], 1, sibling).wait_recv()
                sm_v[...] = sm_v[...] + sm_in_v[1]

            @pl.when((z < depth - 1) & (z >= sm_root))
            def _():
                sm_copy(1, sm_v, sm_in_v.at[2], 2, sibling).wait_recv()
                sm_v[...] = sm_v[...] + sm_in_v[2]

            @pl.when(z < sm_root)
            def _():
                sm_copy(1, sm_v, sm_in_v.at[1], 1, right).start()

            @pl.when(z > sm_root)
            def _():
                sm_copy(1, sm_v, sm_in_v.at[2], 2, left).start()

            @pl.when(z == sm_root)
            def _():
                sm_copy(1, sm_v, sm_in_v.at[3], 3, partner).start()

        @pl.when((now == 2 + sm_reach) & (z == sm_root))
        def _():
            sm_copy(1, sm_v, sm_in_v.at[3], 3, partner).wait_recv()
            sm_o_v[...] = sm_v[...] + sm_in_v[3]

        @pl.when(now == 2 + sm_reach + sm_distance)
        def _():
            @pl.when(z != sm_root)
            def _():
                sm_copy(2, sm_o_v, sm_o_v, 4, sibling).wait_recv()

            @pl.when((z > 0) & (z <= sm_root))
            def _():
                sm_copy(2, sm_o_v, sm_o_v, 4, left).start()

            @pl.when((z < depth - 1) & (z >= sm_root))
            def _():
                sm_copy(3, sm_o_v, sm_o_v, 4, right).start()

    def small_finish():
        sm_copy(1, sm_v, sm_in_v.at[1], 1, sibling).wait_send()

        @pl.when((z > 0) & (z <= sm_root))
        def _():
            sm_copy(2, sm_o_v, sm_o_v, 4, left).wait_send()

        @pl.when((z < depth - 1) & (z >= sm_root))
        def _():
            sm_copy(3, sm_o_v, sm_o_v, 4, right).wait_send()

        o_small[...] = sm_o_v[...]

    load(jnp.int32(0), True)
    neighbours = 2 + (z > 0).astype(jnp.int32) + (z < depth - 1).astype(jnp.int32)
    pl.semaphore_wait(barrier, neighbours)

    last = max(
        [2 + half_depth + half_depth + 2] + [2 + tree.reach + max(tree.root, depth - 1 - tree.root) + 1 for tree in line]
    )

    def one_round(now, carry):
        slot = lax.rem(now, 2)

        @pl.when(now < count)
        def _():
            load(now, False)

            @pl.when(now + 1 < count)
            def _():
                load(now + 1, True)

            def form():
                p_v[slot] = dot_tn(left_v[slot], right_v[slot]).astype(BF16)

            view = p_v.at[slot, at(theirs, HALF)]
            send(CX, now, view, s_v.at[now], recv_sem.at[CX, now], sibling, form)

        step = now - 1

        @pl.when((step >= 0) & (step < count))
        def _():
            arrived(CX, step, s_v.at[step])
            add_into(s_v.at[step], p_v.at[1 - slot, at(own, HALF)])
            view = s_v.at[step, at(other, RAIL)]
            send(UP, step, view, y_v.at[step, pl.ds(0, RAIL)], recv_sem.at[UP, step], partner)

        for tree in line:
            tree.towards(now)

        step_up = now - 2

        @pl.when((step_up >= 0) & (step_up < count))
        def _():
            view = y_v.at[step_up, pl.ds(0, RAIL)]
            arrived(UP, step_up, view)
            add_into(rail.part(step_up), view)

        rail.towards(now)
        rail.away(now)
        for tree in line:
            tree.away(now)

        step_down = now - 2 - half_depth - other_distance - 1

        @pl.when((step_down >= 0) & (step_down < count))
        def _():
            view = o_v.at[step_down, at(own + other, RAIL)]
            arrived(DOWN, step_down, view)
            send(SIB_OTHER, step_down, view, view, recv_sem.at[SIB_OTHER, step_down], sibling)

        step_sib = step_down - 1

        @pl.when((step_sib >= 0) & (step_sib < count))
        def _():
            arrived(SIB_OTHER, step_sib, o_v.at[step_sib, at(theirs + other, RAIL)])

        small_round(now)

        return carry

    lax.fori_loop(0, count + last, one_round, 0)
    finish_send(CX, s_v.at[0])
    finish_send(UP, rail.part(0))
    finish_send(DOWN, rail.part(0))
    finish_send(SIB_OTHER, rail.part(0))
    rail.finish()
    for tree in line:
        tree.finish()
    small_finish()


def reduce_gradients(depth, gelu, d_down, low, d_up, ctx, d_attn, hid, d_qkv, small):
    rows = d_down.shape[0]
    columns = WIDTH
    count = SLABS
    kinds = 9 + 4 * len(LINES)
    return pl.pallas_call(
        functools.partial(reduce_kernel, depth),
        out_shape=[
            pltpu.VMEM((count, SLAB, columns), BF16),
            pltpu.VMEM((SMALL_ROWS, small.shape[-1]), F32),
        ],
        in_specs=[ANY] * 8 + [VMEM],
        out_specs=[VMEM] * 2,
        scratch_shapes=[
            pltpu.VMEM((2, rows, SLAB), BF16),
            pltpu.VMEM((2, rows, columns), BF16),
            pltpu.VMEM((2, SLAB, columns), BF16),
            pltpu.VMEM((count, HALF, columns), BF16),
            pltpu.VMEM((count, RAIL + max(LINES), columns), BF16),
            pltpu.VMEM((count, RAIL + sum(LINES), columns), BF16),
            pltpu.VMEM((count, RAIL + sum(LINES), columns), BF16),
            pltpu.VMEM((SMALL_ROWS, small.shape[-1]), F32),
            pltpu.VMEM((4, SMALL_ROWS, small.shape[-1]), F32),
            pltpu.VMEM((SMALL_ROWS, small.shape[-1]), F32),
            pltpu.SemaphoreType.DMA((2, 2)),
            pltpu.SemaphoreType.DMA((kinds, 2)),
            pltpu.SemaphoreType.DMA((kinds, count)),
            pltpu.SemaphoreType.DMA((4,)),
            pltpu.SemaphoreType.DMA((5,)),
        ],
        compiler_params=pltpu.CompilerParams(
            collective_id=0, has_side_effects=True, vmem_limit_bytes=REDUCE_LIMIT
        ),
        name="reduce_gradients",
    )(gelu, d_down, low, d_up, ctx, d_attn, hid, d_qkv, small)


def finish_kernel(*refs):
    (totals, small, act, d_hid) = refs[:4]
    (o_act, o_hid, o_down, o_up, o_out, o_qkv, o_qv, o_bias, o_gain, o_shift, o_up_bias) = refs[4:15]
    stage_v, stage_sem, move_sem = refs[15:]
    moves = [begin(act, o_act.at[0], move_sem.at[0]), begin(d_hid, o_hid.at[0], move_sem.at[1])]
    o_qv[0] = small[0:2, :]
    o_bias[0] = small[2:4, :]
    o_gain[0] = small[4:6, :]
    o_shift[0] = small[6:8, :]
    for part in range(FF // D):
        o_up_bias[0:1, part * D : (part + 1) * D] = small[8 + part : 9 + part, :]
    places = []
    for array in (o_down, o_up, o_out, o_qkv):
        _, rows, columns = array.shape
        places += [(array, row, column) for row in range(rows // SLAB) for column in range(columns // WIDTH)]
    slots = stage_v.shape[0]
    copies = []
    for index, (array, row, column) in enumerate(places):
        slot = index % slots
        if index >= slots:
            copies[index - slots].wait()
        stage_v[slot] = totals[index].astype(F32)
        target = array.at[0, pl.ds(row * SLAB, SLAB), pl.ds(column * WIDTH, WIDTH)]
        copies.append(begin(stage_v.at[slot], target, stage_sem.at[slot]))
    for copy in copies[-slots:] + moves:
        copy.wait()


def finish(totals, small, act, d_hid):
    slots = 6
    shapes = [
        jax.ShapeDtypeStruct((1, *act.shape), BF16),
        jax.ShapeDtypeStruct((1, *act.shape), BF16),
        jax.ShapeDtypeStruct((1, FF, D), F32),
        jax.ShapeDtypeStruct((1, D, FF), F32),
        jax.ShapeDtypeStruct((1, D, D), F32),
        jax.ShapeDtypeStruct((1, D, 3 * D), F32),
        jax.ShapeDtypeStruct((1, 2, D), F32),
        jax.ShapeDtypeStruct((1, 2, D), F32),
        jax.ShapeDtypeStruct((1, 2, D), F32),
        jax.ShapeDtypeStruct((1, 2, D), F32),
        jax.ShapeDtypeStruct((1, FF), F32),
    ]
    return pl.pallas_call(
        finish_kernel,
        out_shape=shapes,
        in_specs=[VMEM, VMEM, ANY, ANY],
        out_specs=[ANY] * 6 + [VMEM] * 5,
        scratch_shapes=[
            pltpu.VMEM((slots, SLAB, WIDTH), F32),
            pltpu.SemaphoreType.DMA((slots,)),
            pltpu.SemaphoreType.DMA((2,)),
        ],
        compiler_params=pltpu.CompilerParams(vmem_limit_bytes=16 << 20),
        name="finish",
    )(*[pltpu.with_memory_space_constraint(array, pltpu.VMEM) for array in (totals, small)], act, d_hid)


def shards(
    tokens, segments, lengths, cotangent, qkv_weight, qv_bias, out_weight, out_biases,
    norm_gains, norm_shifts, up_weight, up_bias, down_weight,
):
    weights = (qkv_weight, out_weight, up_weight, down_weight)
    params = (qv_bias, out_biases, norm_gains, norm_shifts, up_bias)
    act, d_hid, small, kept = layers(tokens, cotangent, weights, segments, lengths, params)
    totals, small = reduce_gradients(
        lax.axis_size("dp") // 4, kept["gelu"], kept["d_down"], kept["low"], kept["d_up"],
        kept["ctx"], kept["d_attn"], kept["hid"], kept["d_qkv"], small,
    )
    (
        o_act, o_hid, g_down, g_up, g_out, g_qkv, g_qv, g_bias, g_gain, g_shift, g_up_bias
    ) = finish(totals, small, act, d_hid)
    return (o_act, o_hid, g_qkv, g_qv, g_out, g_bias, g_gain, g_shift, g_up, g_up_bias, g_down)


def solution(mesh):
    return jax.shard_map(
        shards,
        mesh=mesh,
        in_specs=(
            P("dp", None), P("dp", None), P("dp"), P("dp", None),
            P("section", None, None), P("section", None, None), P("section", None, None), P("section", None, None),
            P("section", None, None), P("section", None, None), P("section", None, None), P("section", None),
            P("section", None, None),
        ),
        out_specs=(
            P("section", "dp", None), P("section", "dp", None),
            P("section", None, None), P("section", None, None), P("section", None, None), P("section", None, None),
            P("section", None, None), P("section", None, None), P("section", None, None), P("section", None),
            P("section", None, None),
        ),
        check_vma=False,
    )
```

```python
import functools
import math

import jax
import jax.numpy as jnp
from jax import lax
from jax.experimental import pallas as pl
from jax.experimental.pallas import tpu as pltpu
from jax.sharding import PartitionSpec as P

D = 768
H = 12
HD = 64
FF = 3072
SEQ = 512
MICRO = 2
PAIRS = H // 2
PAIR = 2 * HD
GROUP = PAIRS // 2
BACK_GROUPS = ((0, 4), (4, 6))

EPSILON = 1e-05
SCORE_SCALE = 0.125
NEG_FILL = -1e30
F32 = jnp.float32
BF16 = jnp.bfloat16
VMEM_LIMIT = 60 << 20
REDUCE_LIMIT = 44 << 20
MESH = pl.DeviceIdType.MESH

ANY = pl.BlockSpec(memory_space=pl.ANY)
VMEM = pl.BlockSpec(memory_space=pltpu.VMEM)
SMEM = pl.BlockSpec(memory_space=pltpu.SMEM)


def dot_nn(left, right):
    return lax.dot_general(left, right, (((1,), (0,)), ((), ())), preferred_element_type=F32)


def dot_nt(left, right):
    return lax.dot_general(left, right, (((1,), (1,)), ((), ())), preferred_element_type=F32)


def dot_tn(left, right):
    return lax.dot_general(left, right, (((0,), (0,)), ((), ())), preferred_element_type=F32)


def begin(source, target, sem):
    copy = pltpu.make_async_copy(source, target, sem)
    copy.start()
    return copy


def gelu_and_slope(u):
    normal_cdf = 0.5 + 0.5 * lax.erf(u * (1.0 / math.sqrt(2.0)))
    bell = jnp.exp((-0.5 * u) * u)
    return u * normal_cdf, normal_cdf + (u * (1.0 / math.sqrt(2.0 * math.pi))) * bell


def normalize(resid):
    average = jnp.mean(resid, axis=-1, keepdims=True)
    centred = resid - average
    variance = jnp.mean(centred * centred, axis=-1, keepdims=True)
    inverse = lax.rsqrt(variance + EPSILON)
    return centred * inverse, inverse


def norm_back(grad_out, scaled, inverse, gain):
    weighted = grad_out * gain
    first_mean = jnp.mean(weighted, axis=-1, keepdims=True)
    second_mean = jnp.mean(weighted * scaled, axis=-1, keepdims=True)
    return inverse * (weighted - first_mean - scaled * second_mean)


def half_mask(which):
    lane = lax.broadcasted_iota(jnp.int32, (1, PAIR), 1)
    return ((lane // HD) == which).astype(F32).astype(BF16)


ROWS = SEQ // 2
class Place:
    def __init__(self):
        self.section = lax.axis_index("section")
        self.me = lax.axis_index("dp")
        self.core = lax.rem(self.me, 2)
        self.sibling = (self.section, self.me + 1 - 2 * self.core)
        self.other_layer = (1 - self.section, self.me)
        self.own = pl.ds(pl.multiple_of(self.core * ROWS, ROWS), ROWS)
        self.theirs = pl.ds(pl.multiple_of(ROWS - self.core * ROWS, ROWS), ROWS)

    def greet(self):
        barrier = pltpu.get_barrier_semaphore()
        for device in (self.sibling, self.other_layer):
            pl.semaphore_signal(barrier, inc=1, device_id=device, device_id_type=MESH)
        pl.semaphore_wait(barrier, 2)

    def is_mine(self, step, sequences):
        return lax.div(step, sequences) == self.core


def remote(source, target, send_sem, recv_sem, device):
    return pltpu.make_async_remote_copy(source, target, send_sem, recv_sem, device_id=device, device_id_type=MESH)


class Rows:
    def __init__(self, place, sequences, array, steps, local, sent, arrived):
        self.place, self.sequences, self.array, self.steps = place, sequences, array, steps
        self.local, self.sent, self.arrived = local, sent, arrived

    def part(self, sequence, core):
        return self.array.at[pl.ds(pl.multiple_of(sequence * SEQ + core * ROWS, ROWS), ROWS)]

    def spread(self):
        place = self.place
        for sequence in range(self.sequences):
            step = place.core * self.sequences + sequence
            target = self.steps.at[step]
            pltpu.make_async_copy(self.part(sequence, place.core), target, self.local.at[sequence]).start()
            remote(
                self.part(sequence, 1 - place.core), target, self.sent.at[sequence], self.arrived.at[step], place.sibling
            ).start()

    def spread_done(self):
        for sequence in range(self.sequences):
            view = self.steps.at[0]
            remote(view, view, self.sent.at[sequence], self.arrived.at[0], self.place.sibling).wait_send()

    def await_step(self, step, spread):
        mine = spread & self.place.is_mine(step, self.sequences)
        view = self.steps.at[step]

        @pl.when(mine)
        def _():
            pltpu.make_async_copy(view, view, self.local.at[lax.rem(step, self.sequences)]).wait()

        @pl.when(jnp.logical_not(mine))
        def _():
            remote(view, view, self.sent.at[0], self.arrived.at[step], self.place.sibling).wait_recv()

    def collect(self, step):
        sequence = lax.rem(step, self.sequences)
        target = self.part(sequence, self.place.core)
        mine = self.place.is_mine(step, self.sequences)

        @pl.when(mine)
        def _():
            pltpu.make_async_copy(self.steps.at[step], target, self.local.at[sequence]).start()

        @pl.when(jnp.logical_not(mine))
        def _():
            remote(
                self.steps.at[step], target, self.sent.at[sequence], self.arrived.at[sequence], self.place.sibling
            ).start()

    def collect_done(self):
        for sequence in range(self.sequences):
            view = self.steps.at[0]
            pltpu.make_async_copy(view, view, self.local.at[sequence]).wait()
            remote(view, view, self.sent.at[sequence], self.arrived.at[sequence], self.place.sibling).wait()


SAVED = (
    ("hid", D, BF16),
    ("low", D, BF16),
    ("gelu", FF, BF16),
    ("ctx", D, BF16),
    ("q", D, BF16),
    ("linv", D, F32),
    ("xh1", D, BF16),
    ("inv1", 128, F32),
    ("slope", FF, BF16),
    ("xh2", D, BF16),
    ("inv2", 128, F32),
)
GRADS = (("d_down", D, BF16), ("d_up", FF, BF16), ("d_attn", D, BF16), ("d_qkv", 3 * D, BF16))
SMALL_ROWS = 16


def layers_kernel(sequences, *refs):
    (tok, cot, wqkv, wo, wu, wd, segs, lens, qv_bias, out_biases, gains, shifts, up_bias) = refs[:13]
    act_out, d_hid_out, small_out, prob_io = refs[13:17]
    stop = 17 + len(SAVED)
    saved = dict(zip([name for name, _, _ in SAVED], refs[17:stop]))
    grads = dict(zip([name for name, _, _ in GRADS], refs[stop : stop + len(GRADS)]))
    stop += len(GRADS)
    (
        h_v, act_v, g_v, d_hid_v, kv_v, p_v, wqkv_v, wo_v, wu_v, wd_v, bias_v, acc_v, seg_own, seg_their,
        d_ctx_v, part_v, their_v,
    ) = refs[stop : stop + 17]
    stop += 17
    buffers = dict(zip([name for name, _, _ in SAVED if name != "hid"], refs[stop : stop + len(SAVED) - 1]))
    stop += len(SAVED) - 1
    grad_buffers = dict(zip([name for name, _, _ in GRADS], refs[stop : stop + len(GRADS)]))
    stop += len(GRADS)
    (
        w_sem, save_sem, hid_sem, grad_sem, p_sem, seg_sem, kv_sent, kv_arrived, part_sent, part_arrived,
        in_local, in_sent, in_arrived, out_local, out_sent, out_arrived, hop_sent,
        up_local, up_sent, up_arrived, down_local, down_sent, down_arrived, back_sent,
    ) = refs[stop:]
    place = Place()
    section = place.section
    steps = 2 * sequences
    names = [name for name, _, _ in SAVED]
    grad_names = [name for name, _, _ in GRADS]
    inputs = Rows(place, sequences, tok, h_v, in_local, in_sent, in_arrived)
    outputs = Rows(place, sequences, act_out, act_v, out_local, out_sent, out_arrived)
    upstream = Rows(place, sequences, cot, g_v, up_local, up_sent, up_arrived)
    downstream = Rows(place, sequences, d_hid_out, d_hid_v, down_local, down_sent, down_arrived)

    def at_step(array, step):
        return array.at[pl.ds(pl.multiple_of(step * ROWS, ROWS), ROWS)]

    def save(name, step):
        pltpu.make_async_copy(buffers[name], at_step(saved[name], step), save_sem.at[names.index(name)]).start()

    def fetch(name, step):
        pltpu.make_async_copy(at_step(saved[name], step), buffers[name], save_sem.at[names.index(name)]).start()

    def settle(name):
        pltpu.make_async_copy(buffers[name], buffers[name], save_sem.at[names.index(name)]).wait()

    def prob_part(group, step):
        heads = pl.ds(group * 2 * GROUP, 2 * GROUP)
        return p_v.at[heads], prob_io.at[step, heads], p_sem.at[group]

    def settle_prob():
        for group in range(2):
            view, _, sem = prob_part(group, 0)
            pltpu.make_async_copy(view, view, sem).wait()

    def when_first(step, copies):
        @pl.when(step == 0)
        def _():
            for copy in copies:
                copy.wait()

    def column_sum(value):
        return jnp.sum(value, axis=0, keepdims=True)

    get_qkv = [
        begin(wqkv.at[0, :, pl.ds(block * D, D)], wqkv_v.at[:, pl.ds(block * D, D)], w_sem.at[block])
        for block in (1, 2, 0)
    ]
    position = lax.broadcasted_iota(jnp.int32, (1, SEQ), 1)
    for sequence in range(sequences):
        seg_own[sequence, 0:1, :] = segs[sequence : sequence + 1, :].astype(F32)
        seg_own[sequence, 1:2, :] = (position < lens[sequence]).astype(F32)
        seg_own[sequence, 2:8, :] = jnp.zeros((6, SEQ), F32)
    place.greet()
    seg_copy = remote(seg_own, seg_their, seg_sem.at[0], seg_sem.at[1], place.sibling)

    @pl.when(section == 0)
    def _():
        inputs.spread()

    @pl.when(section == 1)
    def _():
        upstream.spread()

    seg_copy.start()
    get_wo = begin(wo.at[0], wo_v, w_sem.at[3])
    get_wu = begin(wu.at[0], wu_v, w_sem.at[4])
    get_wd = begin(wd.at[0], wd_v, w_sem.at[5])
    small_out[...] = jnp.zeros_like(small_out)

    def forward_step(step, carry):
        inputs.await_step(step, section == 0)
        pltpu.make_async_copy(h_v.at[step], at_step(saved["hid"], step), hid_sem.at[step]).start()
        hidden = h_v[step]
        for block in (1, 2):
            when_first(step, (get_qkv[block - 1],))
            proj = dot_nn(hidden, wqkv_v[:, block * D : (block + 1) * D])
            if block == 2:
                proj = proj + qv_bias[0, 1:2, :]
            cols = pl.ds((block - 1) * D, D)
            kv_v[step, place.own, cols] = proj.astype(BF16)
            view = kv_v.at[step, place.own, cols]
            remote(view, view, kv_sent.at[step, block - 1], kv_arrived.at[step, block - 1], place.sibling).start()

        def await_keys_or_values(block):
            view = kv_v.at[step, place.theirs, pl.ds(block * D, D)]
            remote(view, view, kv_sent.at[step, block], kv_arrived.at[step, block], place.sibling).wait_recv()

        @pl.when(step == 0)
        def _():
            get_qkv[2].wait()
            seg_copy.wait()

        @pl.when(step > 0)
        def _():
            settle("q")

        buffers["q"][...] = (dot_nn(hidden, wqkv_v[:, 0:D]) + qv_bias[0, 0:1, :]).astype(BF16)

        sequence = lax.rem(step, sequences)
        mine = jnp.where(place.is_mine(step, sequences), 1.0, 0.0)
        key_rows = mine * seg_own[sequence] + (1.0 - mine) * seg_their[sequence]
        query_row = mine * seg_own[sequence, 0:1, place.own] + (1.0 - mine) * seg_their[sequence, 0:1, place.own]
        query_seg = jnp.transpose(jnp.broadcast_to(query_row, (128, ROWS)))
        query = lax.broadcasted_iota(jnp.int32, (ROWS, 128), 0) + place.core * ROWS
        key = lax.broadcasted_iota(jnp.int32, (ROWS, 128), 1)
        for tile in range(SEQ // 128):
            cols = slice(tile * 128, (tile + 1) * 128)
            visible = (key_rows[1:2, cols] > 0.5) | (key + tile * 128 == query)
            bias_v[:, cols] = jnp.where((query_seg == key_rows[0:1, cols]) & visible, 0.0, NEG_FILL)

        @pl.when(step > 0)
        def _():
            for name in buffers:
                if name != "q":
                    settle(name)
            settle_prob()

        await_keys_or_values(0)
        q_v, linv_v, ctx_v = buffers["q"], buffers["linv"], buffers["ctx"]
        for group in range(2):
            for pair in range(group * GROUP, (group + 1) * GROUP):
                at = pair * PAIR
                q2 = q_v[:, at : at + PAIR] * SCORE_SCALE
                k2 = kv_v[step, :, at : at + PAIR]
                weights = []
                for head in range(2):
                    scores = dot_nt(q2, k2 * half_mask(head)) + bias_v[...]
                    weight = jnp.exp(scores - jnp.max(scores, axis=-1, keepdims=True)).astype(BF16)
                    p_v[pair * 2 + head] = weight
                    weights.append(weight)
                if pair == 0:
                    await_keys_or_values(1)
                    when_first(step, (get_wo, get_wu, get_wd))
                v2 = kv_v[step, :, D + at : D + at + PAIR]
                total = None
                for head in range(2):
                    mask = half_mask(head)
                    values = jnp.concatenate([v2 * mask, jnp.broadcast_to(mask, (SEQ, PAIR))], axis=1)
                    part = dot_nn(weights[head], values)
                    total = part if total is None else total + part
                inverse = 1.0 / total[:, PAIR : 2 * PAIR]
                linv_v[:, at : at + PAIR] = inverse
                ctx_v[:, at : at + PAIR] = (total[:, 0:PAIR] * inverse).astype(BF16)
            view, target, sem = prob_part(group, step)
            pltpu.make_async_copy(view, target, sem).start()
        resid = hidden.astype(F32) + (dot_nn(ctx_v[...], wo_v[...]) + out_biases[0, 0:1, :])
        scaled, inverse = normalize(resid)
        buffers["xh1"][...] = scaled.astype(BF16)
        buffers["inv1"][...] = jnp.broadcast_to(inverse, (ROWS, 128))
        normed = scaled * gains[0, 0:1, :] + shifts[0, 0:1, :]
        buffers["low"][...] = normed.astype(BF16)
        acc_v[...] = normed + out_biases[0, 1:2, :]
        for name in ("q", "linv", "ctx", "xh1", "inv1", "low"):
            save(name, step)
        width = 1024
        for half in range(2):
            rows = slice(half * ROWS // 2, (half + 1) * ROWS // 2)
            for chunk in range(FF // width):
                cols = slice(chunk * width, (chunk + 1) * width)
                up = dot_nn(buffers["low"][rows, :], wu_v[:, cols]) + up_bias[0:1, cols]
                gelu, slope = gelu_and_slope(up)
                gelu = gelu.astype(BF16)
                buffers["gelu"][rows, cols] = gelu
                buffers["slope"][rows, cols] = slope.astype(BF16)
                acc_v[rows, :] += dot_nn(gelu, wd_v[cols, :])
            scaled, inverse = normalize(acc_v[rows, :])
            act_v[step, rows, :] = (scaled * gains[0, 1:2, :] + shifts[0, 1:2, :]).astype(BF16)
            buffers["xh2"][rows, :] = scaled.astype(BF16)
            buffers["inv2"][rows, :] = jnp.broadcast_to(inverse, (ROWS // 2, 128))

            @pl.when(section == 0)
            def _():
                source, target = [array.at[step, pl.ds(half * (ROWS // 2), ROWS // 2)] for array in (act_v, h_v)]
                remote(source, target, hop_sent.at[step], in_arrived.at[step], place.other_layer).start()

        outputs.collect(step)
        for name in ("gelu", "slope", "xh2", "inv2"):
            save(name, step)
        return carry

    lax.fori_loop(0, steps, forward_step, 0)

    def backward_step(turn, carry):
        step = steps - 1 - turn

        early = ("xh2", "inv2", "slope", "xh1", "inv1")
        late = ("q", "linv", "ctx")

        def part_copy(group):
            first, last = BACK_GROUPS[group]
            pairs = pl.ds(first, last - first)
            return remote(
                part_v.at[pairs, place.theirs], their_v.at[step, pairs], part_sent.at[group],
                part_arrived.at[step, group], place.sibling,
            )

        def keep(name):
            pltpu.make_async_copy(
                grad_buffers[name], at_step(grads[name], step), grad_sem.at[grad_names.index(name)]
            ).start()

        def free(name):
            buffer = grad_buffers[name]
            pltpu.make_async_copy(buffer, buffer, grad_sem.at[grad_names.index(name)]).wait()

        upstream.await_step(step, section == 1)

        @pl.when(turn > 0)
        def _():
            for name in early:
                settle(name)
            for name in ("d_down", "d_up", "d_attn"):
                free(name)

        grad = g_v[step].astype(F32)
        scaled = buffers["xh2"][...].astype(F32)
        small_out[5:6, :] += column_sum(grad * scaled)
        small_out[7:8, :] += column_sum(grad)
        d_r2 = norm_back(grad, scaled, buffers["inv2"][:, 0:1], gains[0, 1:2, :])
        d_down = d_r2.astype(BF16)
        d_down_v, d_up_v, d_attn_v, d_qkv_v = [grad_buffers[name] for name in grad_names]
        d_down_v[...] = d_down
        small_out[3:4, :] += column_sum(d_down.astype(F32))
        acc_v[...] = d_r2
        for chunk in range(FF // D):
            cols = slice(chunk * D, (chunk + 1) * D)
            d_up = (dot_nt(d_down_v[...], wd_v[cols, :]) * buffers["slope"][:, cols].astype(F32)).astype(BF16)
            d_up_v[:, cols] = d_up
            small_out[8 + chunk : 9 + chunk, :] += column_sum(d_up.astype(F32))
            acc_v[...] += dot_nt(d_up, wu_v[:, cols])
        d_normed = acc_v[...]
        scaled = buffers["xh1"][...].astype(F32)
        small_out[4:5, :] += column_sum(d_normed * scaled)
        small_out[6:7, :] += column_sum(d_normed)
        d_r1 = norm_back(d_normed, scaled, buffers["inv1"][:, 0:1], gains[0, 0:1, :])
        d_attn = d_r1.astype(BF16)
        d_attn_v[...] = d_attn
        small_out[2:3, :] += column_sum(d_attn.astype(F32))
        acc_v[...] = d_r1

        @pl.when(turn == 0)
        def _():
            for name in early:
                settle(name)

        @pl.when(turn > 0)
        def _():
            for name in late:
                settle(name)
            settle_prob()
            free("d_qkv")
            for group in range(len(BACK_GROUPS)):
                part_copy(group).wait_send()

        @pl.when(turn + 1 < steps)
        def _():
            for name in early:
                fetch(name, step - 1)

        for name in ("d_down", "d_up", "d_attn"):
            keep(name)
        d_ctx_v[...] = (dot_nt(d_attn_v[...], wo_v[...]) * buffers["linv"][...]).astype(BF16)
        q_v, ctx_v = buffers["q"], buffers["ctx"]
        for group, (first, last) in enumerate(BACK_GROUPS):
            for pair in range(first, last):
                at = pair * PAIR
                q2 = q_v[:, at : at + PAIR] * SCORE_SCALE
                k2 = kv_v[step, :, at : at + PAIR]
                v2 = kv_v[step, :, D + at : D + at + PAIR]
                dc2 = d_ctx_v[:, at : at + PAIR]
                inner = dc2.astype(F32) * ctx_v[:, at : at + PAIR].astype(F32)
                d_q, d_k, d_v = None, None, None
                for head in range(2):
                    mask = half_mask(head)
                    dc_own = dc2 * mask
                    weight = p_v[pair * 2 + head]
                    row_inner = jnp.sum(inner * mask.astype(F32), axis=-1, keepdims=True)
                    d_prob = dot_nt(dc_own, v2)
                    d_score = (weight.astype(F32) * (d_prob - row_inner)).astype(BF16)
                    one_v = dot_tn(dc_own, weight)
                    one_k = dot_tn(q2 * mask, d_score)
                    one_q = dot_nn(d_score, k2 * mask)
                    d_v = one_v if d_v is None else d_v + one_v
                    d_k = one_k if d_k is None else d_k + one_k
                    d_q = one_q if d_q is None else d_q + one_q
                d_qkv_v[:, at : at + PAIR] = (d_q * SCORE_SCALE).astype(BF16)
                part_v[pair, :, 0:PAIR] = jnp.transpose(d_k).astype(BF16)
                part_v[pair, :, PAIR : 2 * PAIR] = jnp.transpose(d_v).astype(BF16)
            part_copy(group).start()

        @pl.when(turn == 0)
        def _():
            for name in late:
                settle(name)
            settle_prob()

        @pl.when(turn + 1 < steps)
        def _():
            for name in late:
                fetch(name, step - 1)
            for group in range(2):
                view, source, sem = prob_part(group, step - 1)
                pltpu.make_async_copy(source, view, sem).start()

        d_query = d_qkv_v[:, 0:D]
        acc_v[...] += dot_nt(d_query, wqkv_v[:, 0:D])
        small_out[0:1, :] += column_sum(d_query.astype(F32))
        for group, (first, last) in enumerate(BACK_GROUPS):
            part_copy(group).wait_recv()
            for pair in range(first, last):
                total = part_v[pair, place.own, :].astype(F32) + their_v[step, pair].astype(F32)
                at = pair * PAIR
                d_qkv_v[:, D + at : D + at + PAIR] = total[:, 0:PAIR].astype(BF16)
                d_qkv_v[:, 2 * D + at : 2 * D + at + PAIR] = total[:, PAIR : 2 * PAIR].astype(BF16)
            keys = slice(D + first * PAIR, D + last * PAIR)
            values = slice(2 * D + first * PAIR, 2 * D + last * PAIR)
            d_hid = acc_v[...] + dot_nt(d_qkv_v[:, keys], wqkv_v[:, keys]) + dot_nt(d_qkv_v[:, values], wqkv_v[:, values])
            if last < PAIRS:
                acc_v[...] = d_hid
            else:
                d_hid_v[step] = d_hid.astype(BF16)

        @pl.when(section == 1)
        def _():
            remote(d_hid_v.at[step], g_v.at[step], back_sent.at[step], up_arrived.at[step], place.other_layer).start()

        downstream.collect(step)
        small_out[1:2, :] += column_sum(d_qkv_v[:, 2 * D : 3 * D].astype(F32))
        keep("d_qkv")
        return carry

    lax.fori_loop(0, steps, backward_step, 0)

    for name in ("low", "gelu"):
        settle(name)
    for name in grad_names:
        buffer = grad_buffers[name]
        pltpu.make_async_copy(buffer, buffer, grad_sem.at[grad_names.index(name)]).wait()
    for group, (first, last) in enumerate(BACK_GROUPS):
        view = part_v.at[pl.ds(first, last - first), place.theirs]
        remote(view, view, part_sent.at[group], part_arrived.at[0, group], place.sibling).wait_send()
    for step in range(steps):
        pltpu.make_async_copy(h_v.at[step], h_v.at[step], hid_sem.at[step]).wait()
        for block in range(2):
            view = kv_v.at[step, place.own, pl.ds(block * D, D)]
            remote(view, view, kv_sent.at[step, block], kv_arrived.at[step, block], place.sibling).wait_send()

    @pl.when(section == 0)
    def _():
        inputs.spread_done()
        for step in range(steps):
            remote(act_v.at[step], h_v.at[step], hop_sent.at[step], in_arrived.at[step], place.other_layer).wait_send()

    @pl.when(section == 1)
    def _():
        upstream.spread_done()
        for step in range(steps):
            remote(d_hid_v.at[step], g_v.at[step], back_sent.at[step], up_arrived.at[step], place.other_layer).wait_send()

    outputs.collect_done()
    downstream.collect_done()


def layers(tokens, cotangent, weights, segments, lengths, params):
    total = tokens.shape[0]
    sequences = total // SEQ
    steps = 2 * sequences
    shapes = [
        jax.ShapeDtypeStruct((total, D), BF16),
        jax.ShapeDtypeStruct((total, D), BF16),
        jax.ShapeDtypeStruct((SMALL_ROWS, D), F32),
        jax.ShapeDtypeStruct((steps, H, ROWS, SEQ), BF16),
    ] + [jax.ShapeDtypeStruct((total, width), dtype) for _, width, dtype in SAVED + GRADS]
    dma = pltpu.SemaphoreType.DMA
    act, d_hid, small, _, *rest = pl.pallas_call(
        functools.partial(layers_kernel, sequences),
        out_shape=shapes,
        in_specs=[ANY] * 6 + [VMEM, SMEM] + [VMEM] * 5,
        out_specs=[ANY, ANY, VMEM] + [ANY] * (len(shapes) - 3),
        scratch_shapes=[pltpu.VMEM((steps, ROWS, D), BF16)] * 4
        + [
            pltpu.VMEM((steps, SEQ, 2 * D), BF16),
            pltpu.VMEM((H, ROWS, SEQ), BF16),
            pltpu.VMEM((D, 3 * D), BF16),
            pltpu.VMEM((D, D), BF16),
            pltpu.VMEM((D, FF), BF16),
            pltpu.VMEM((FF, D), BF16),
            pltpu.VMEM((ROWS, SEQ), F32),
            pltpu.VMEM((ROWS, D), F32),
            pltpu.VMEM((sequences, 8, SEQ), F32),
            pltpu.VMEM((sequences, 8, SEQ), F32),
            pltpu.VMEM((ROWS, D), BF16),
            pltpu.VMEM((PAIRS, SEQ, 2 * PAIR), BF16),
            pltpu.VMEM((steps, PAIRS, ROWS, 2 * PAIR), BF16),
        ]
        + [pltpu.VMEM((ROWS, width), dtype) for name, width, dtype in SAVED + GRADS if name != "hid"]
        + [
            dma((6,)), dma((len(SAVED),)), dma((steps,)), dma((len(GRADS),)), dma((2,)), dma((2,)),
            dma((steps, 2)), dma((steps, 2)), dma((len(BACK_GROUPS),)), dma((steps, len(BACK_GROUPS))),
        ]
        + [dma((sequences,)), dma((sequences,)), dma((steps,))]
        + [dma((sequences,)), dma((sequences,)), dma((sequences,)), dma((steps,))]
        + [dma((sequences,)), dma((sequences,)), dma((steps,))]
        + [dma((sequences,)), dma((sequences,)), dma((sequences,)), dma((steps,))],
        compiler_params=pltpu.CompilerParams(
            collective_id=1, has_side_effects=True, vmem_limit_bytes=VMEM_LIMIT
        ),
        name="layers",
    )(tokens, cotangent, *weights, segments, lengths, *params)
    return act, d_hid, small, dict(zip([name for name, _, _ in SAVED + GRADS], rest))


UNIT = 16
SLAB = D
WIDTH = D // 2
HALF = SLAB // 2
RAIL = 7 * UNIT
LINES = (3 * UNIT, 2 * UNIT, 2 * UNIT, 3 * UNIT)
SLABS = 2 * FF // D + FF // WIDTH + D // WIDTH + 3 * D // WIDTH


def reduce_kernel(depth, *refs):
    (gelu, d_down, low, d_up, ctx, d_attn, hid, d_qkv, small) = refs[:9]
    (o_v, o_small) = refs[9:11]
    (
        left_v, right_v, p_v, s_v, y_v, rl_v, rr_v, sm_v, sm_in_v, sm_o_v,
        load_sem, send_sem, recv_sem, sm_send, sm_recv,
    ) = refs[11:]
    plan = (
        (2 * FF // D, gelu, d_down),
        (FF // WIDTH, low, d_up),
        (D // WIDTH, ctx, d_attn),
        (3 * D // WIDTH, hid, d_qkv),
    )
    count = SLABS
    section = lax.axis_index("section")
    me = lax.axis_index("dp")
    core = lax.rem(me, 2)
    y = lax.rem(lax.div(me, 2), 2)
    z = lax.div(me, 4)
    sibling = (section, me + 1 - 2 * core)
    partner = (section, me + 2 - 4 * y)
    left = (section, me - 4)
    right = (section, me + 4)

    barrier = pltpu.get_barrier_semaphore()
    pl.semaphore_signal(barrier, inc=1, device_id=sibling, device_id_type=MESH)
    pl.semaphore_signal(barrier, inc=1, device_id=partner, device_id_type=MESH)

    @pl.when(z > 0)
    def _():
        pl.semaphore_signal(barrier, inc=1, device_id=left, device_id_type=MESH)

    @pl.when(z < depth - 1)
    def _():
        pl.semaphore_signal(barrier, inc=1, device_id=right, device_id_type=MESH)

    def at(value, size):
        return pl.ds(pl.multiple_of(value, UNIT), size)

    def load(step, start):
        slot = lax.rem(step, 2)
        if not start:
            pltpu.make_async_copy(low, left_v.at[slot], load_sem.at[0, slot]).wait()
            pltpu.make_async_copy(d_down.at[:, pl.ds(0, WIDTH)], right_v.at[slot], load_sem.at[1, slot]).wait()
            return
        first = 0
        for steps, factor, grad in plan:

            def issue(first=first, factor=factor, grad=grad):
                index = step - first
                halves = grad.shape[1] // WIDTH
                rows = pl.ds(pl.multiple_of(lax.div(index, halves) * SLAB, 128), SLAB)
                cols = pl.ds(pl.multiple_of(lax.rem(index, halves) * WIDTH, 128), WIDTH)
                pltpu.make_async_copy(factor.at[:, rows], left_v.at[slot], load_sem.at[0, slot]).start()
                pltpu.make_async_copy(grad.at[:, cols], right_v.at[slot], load_sem.at[1, slot]).start()

            pl.when((step >= first) & (step < first + steps))(issue)
            first += steps

    def send(kind, step, source, target, arrival, device, compute=None):
        parity = lax.rem(step, 2)
        copy = pltpu.make_async_remote_copy(
            source, target, send_sem.at[kind, parity], arrival, device_id=device, device_id_type=MESH
        )

        @pl.when(step >= 2)
        def _():
            copy.wait_send()

        if compute is not None:
            compute()
        copy.start()

    def finish_send(kind, view):
        for parity in range(2):
            pltpu.make_async_remote_copy(
                view, view, send_sem.at[kind, parity], recv_sem.at[kind, 0], device_id=sibling, device_id_type=MESH
            ).wait_send()

    def arrived(kind, step, view):
        pltpu.make_async_remote_copy(
            view, view, send_sem.at[kind, 0], recv_sem.at[kind, step], device_id=sibling, device_id_type=MESH
        ).wait_recv()

    own = core * HALF
    theirs = HALF - own
    CX, UP, DOWN, SIB_OTHER, YX = range(5)

    def add_into(target, term):
        target[...] = (target[...].astype(F32) + term[...].astype(F32)).astype(target.dtype)

    class Tree:
        def __init__(self, kinds, base, root, reach, size, offset, land, rail):
            self.kinds, self.base, self.root, self.reach = kinds, base, root, reach
            self.size, self.offset, self.land, self.rail = size, offset, land, rail
            self.distance = jnp.abs(z - root)
            self.from_left = (z > 0) & (z <= root)
            self.from_right = (z < depth - 1) & (z >= root)

        def part(self, step):
            return s_v.at[step, at(self.offset, self.size)]

        def total(self, step):
            return o_v.at[step, at(own + self.offset, self.size)]

        def landing(self, buffer, step):
            return buffer.at[step, pl.ds(self.land, self.size)]

        def towards(self, now):
            inward, out_left, out_right, sib = self.kinds
            step = now - self.base - self.reach + self.distance

            @pl.when((step >= 0) & (step < count))
            def _():
                @pl.when(self.from_left)
                def _():
                    arrived(out_left, step, self.landing(rl_v, step))
                    add_into(self.part(step), self.landing(rl_v, step))

                @pl.when(self.from_right)
                def _():
                    arrived(out_right, step, self.landing(rr_v, step))
                    add_into(self.part(step), self.landing(rr_v, step))

                @pl.when(z < self.root)
                def _():
                    send(inward, step, self.part(step), self.landing(rl_v, step), recv_sem.at[out_left, step], right)

                @pl.when(z > self.root)
                def _():
                    send(inward, step, self.part(step), self.landing(rr_v, step), recv_sem.at[out_right, step], left)

                @pl.when(z == self.root)
                def _():
                    if self.rail:
                        self.total(step)[...] = self.part(step)[...]
                    else:
                        view = y_v.at[step, pl.ds(RAIL, self.size)]
                        send(YX, step, self.part(step), view, recv_sem.at[YX, step], partner)

            if not self.rail:
                late = now - self.base - self.reach - 1

                @pl.when((z == self.root) & (late >= 0) & (late < count))
                def _():
                    view = y_v.at[late, pl.ds(RAIL, self.size)]
                    arrived(YX, late, view)
                    self.total(late)[...] = (self.part(late)[...].astype(F32) + view[...].astype(F32)).astype(BF16)

        def away(self, now):
            inward, out_left, out_right, sib = self.kinds
            lag = self.base + self.reach + (0 if self.rail else 1)
            step = now - lag - self.distance

            @pl.when((step >= 0) & (step < count))
            def _():
                view = self.total(step)

                @pl.when(z != self.root)
                def _():
                    arrived(inward, step, view)

                @pl.when(self.from_left)
                def _():
                    send(out_left, step, view, view, recv_sem.at[inward, step], left)

                @pl.when(self.from_right)
                def _():
                    send(out_right, step, view, view, recv_sem.at[inward, step], right)

                if self.rail:
                    send(DOWN, step, view, view, recv_sem.at[DOWN, step], partner)
                send(sib, step, view, view, recv_sem.at[sib, step], sibling)

            done = step - 1

            @pl.when((done >= 0) & (done < count))
            def _():
                arrived(sib, done, o_v.at[done, at(theirs + self.offset, self.size)])

        def finish(self):
            inward, out_left, out_right, sib = self.kinds
            view = self.part(0)

            @pl.when(z != self.root)
            def _():
                finish_send(inward, view)

            @pl.when(self.from_left)
            def _():
                finish_send(out_left, view)

            @pl.when(self.from_right)
            def _():
                finish_send(out_right, view)

            finish_send(sib, view)
            if not self.rail:

                @pl.when(z == self.root)
                def _():
                    finish_send(YX, view)

    half_depth = depth // 2
    rail_root = half_depth - 1 + y
    rail = Tree((5, 6, 7, 8), 2, rail_root, half_depth, RAIL, y * RAIL, 0, True)
    line = []
    offset = 0
    for index, size in enumerate(LINES):
        root = (2 * index + 1) * depth // (2 * len(LINES))
        kinds = tuple(9 + 4 * index + kind for kind in range(4))
        reach = max(root, depth - 1 - root)
        line.append(Tree(kinds, 1, root, reach, size, 2 * RAIL + offset, RAIL + offset, False))
        offset += size
    other_distance = jnp.abs(z - (half_depth - y))
    other = (1 - y) * RAIL

    sm_root = half_depth
    sm_reach = max(sm_root, depth - 1 - sm_root)
    sm_distance = jnp.abs(z - sm_root)

    def sm_copy(kind, source, target, arrival, device):
        return pltpu.make_async_remote_copy(
            source, target, sm_send.at[kind], sm_recv.at[arrival], device_id=device, device_id_type=MESH
        )

    def small_round(now):
        @pl.when(now == 0)
        def _():
            sm_v[...] = small[...]
            sm_copy(0, sm_v, sm_in_v.at[0], 0, sibling).start()

        @pl.when(now == 1)
        def _():
            sm_copy(0, sm_v, sm_in_v.at[0], 0, sibling).wait()
            sm_v[...] = sm_v[...] + sm_in_v[0]

        @pl.when(now == 1 + sm_reach - sm_distance)
        def _():
            @pl.when((z > 0) & (z <= sm_root))
            def _():
                sm_copy(1, sm_v, sm_in_v.at[1], 1, sibling).wait_recv()
                sm_v[...] = sm_v[...] + sm_in_v[1]

            @pl.when((z < depth - 1) & (z >= sm_root))
            def _():
                sm_copy(1, sm_v, sm_in_v.at[2], 2, sibling).wait_recv()
                sm_v[...] = sm_v[...] + sm_in_v[2]

            @pl.when(z < sm_root)
            def _():
                sm_copy(1, sm_v, sm_in_v.at[1], 1, right).start()

            @pl.when(z > sm_root)
            def _():
                sm_copy(1, sm_v, sm_in_v.at[2], 2, left).start()

            @pl.when(z == sm_root)
            def _():
                sm_copy(1, sm_v, sm_in_v.at[3], 3, partner).start()

        @pl.when((now == 2 + sm_reach) & (z == sm_root))
        def _():
            sm_copy(1, sm_v, sm_in_v.at[3], 3, partner).wait_recv()
            sm_o_v[...] = sm_v[...] + sm_in_v[3]

        @pl.when(now == 2 + sm_reach + sm_distance)
        def _():
            @pl.when(z != sm_root)
            def _():
                sm_copy(2, sm_o_v, sm_o_v, 4, sibling).wait_recv()

            @pl.when((z > 0) & (z <= sm_root))
            def _():
                sm_copy(2, sm_o_v, sm_o_v, 4, left).start()

            @pl.when((z < depth - 1) & (z >= sm_root))
            def _():
                sm_copy(3, sm_o_v, sm_o_v, 4, right).start()

    def small_finish():
        sm_copy(1, sm_v, sm_in_v.at[1], 1, sibling).wait_send()

        @pl.when((z > 0) & (z <= sm_root))
        def _():
            sm_copy(2, sm_o_v, sm_o_v, 4, left).wait_send()

        @pl.when((z < depth - 1) & (z >= sm_root))
        def _():
            sm_copy(3, sm_o_v, sm_o_v, 4, right).wait_send()

        o_small[...] = sm_o_v[...]

    load(jnp.int32(0), True)
    neighbours = 2 + (z > 0).astype(jnp.int32) + (z < depth - 1).astype(jnp.int32)

    last = max(
        [2 + half_depth + half_depth + 2] + [2 + tree.reach + max(tree.root, depth - 1 - tree.root) + 1 for tree in line]
    )

    def one_round(now, carry):
        slot = lax.rem(now, 2)

        @pl.when(now < count)
        def _():
            load(now, False)

            @pl.when(now + 1 < count)
            def _():
                load(now + 1, True)

            def form():
                p_v[slot] = dot_tn(left_v[slot], right_v[slot]).astype(BF16)

                @pl.when(now == 0)
                def _():
                    pl.semaphore_wait(barrier, neighbours)

            view = p_v.at[slot, at(theirs, HALF)]
            send(CX, now, view, s_v.at[now], recv_sem.at[CX, now], sibling, form)

        step = now - 1

        @pl.when((step >= 0) & (step < count))
        def _():
            arrived(CX, step, s_v.at[step])
            add_into(s_v.at[step], p_v.at[1 - slot, at(own, HALF)])
            view = s_v.at[step, at(other, RAIL)]
            send(UP, step, view, y_v.at[step, pl.ds(0, RAIL)], recv_sem.at[UP, step], partner)

        for tree in line:
            tree.towards(now)

        step_up = now - 2

        @pl.when((step_up >= 0) & (step_up < count))
        def _():
            view = y_v.at[step_up, pl.ds(0, RAIL)]
            arrived(UP, step_up, view)
            add_into(rail.part(step_up), view)

        rail.towards(now)
        rail.away(now)
        for tree in line:
            tree.away(now)

        step_down = now - 2 - half_depth - other_distance - 1

        @pl.when((step_down >= 0) & (step_down < count))
        def _():
            view = o_v.at[step_down, at(own + other, RAIL)]
            arrived(DOWN, step_down, view)
            send(SIB_OTHER, step_down, view, view, recv_sem.at[SIB_OTHER, step_down], sibling)

        step_sib = step_down - 1

        @pl.when((step_sib >= 0) & (step_sib < count))
        def _():
            arrived(SIB_OTHER, step_sib, o_v.at[step_sib, at(theirs + other, RAIL)])

        small_round(now)

        return carry

    lax.fori_loop(0, count + last, one_round, 0)
    finish_send(CX, s_v.at[0])
    finish_send(UP, rail.part(0))
    finish_send(DOWN, rail.part(0))
    finish_send(SIB_OTHER, rail.part(0))
    rail.finish()
    for tree in line:
        tree.finish()
    small_finish()


def reduce_gradients(depth, gelu, d_down, low, d_up, ctx, d_attn, hid, d_qkv, small):
    rows = d_down.shape[0]
    columns = WIDTH
    count = SLABS
    kinds = 9 + 4 * len(LINES)
    return pl.pallas_call(
        functools.partial(reduce_kernel, depth),
        out_shape=[
            pltpu.VMEM((count, SLAB, columns), BF16),
            pltpu.VMEM((SMALL_ROWS, small.shape[-1]), F32),
        ],
        in_specs=[ANY] * 8 + [VMEM],
        out_specs=[VMEM] * 2,
        scratch_shapes=[
            pltpu.VMEM((2, rows, SLAB), BF16),
            pltpu.VMEM((2, rows, columns), BF16),
            pltpu.VMEM((2, SLAB, columns), BF16),
            pltpu.VMEM((count, HALF, columns), BF16),
            pltpu.VMEM((count, RAIL + max(LINES), columns), BF16),
            pltpu.VMEM((count, RAIL + sum(LINES), columns), BF16),
            pltpu.VMEM((count, RAIL + sum(LINES), columns), BF16),
            pltpu.VMEM((SMALL_ROWS, small.shape[-1]), F32),
            pltpu.VMEM((4, SMALL_ROWS, small.shape[-1]), F32),
            pltpu.VMEM((SMALL_ROWS, small.shape[-1]), F32),
            pltpu.SemaphoreType.DMA((2, 2)),
            pltpu.SemaphoreType.DMA((kinds, 2)),
            pltpu.SemaphoreType.DMA((kinds, count)),
            pltpu.SemaphoreType.DMA((4,)),
            pltpu.SemaphoreType.DMA((5,)),
        ],
        compiler_params=pltpu.CompilerParams(
            collective_id=0, has_side_effects=True, vmem_limit_bytes=REDUCE_LIMIT
        ),
        name="reduce_gradients",
    )(gelu, d_down, low, d_up, ctx, d_attn, hid, d_qkv, small)


def finish_kernel(*refs):
    (totals, small, act, d_hid) = refs[:4]
    (o_act, o_hid, o_down, o_up, o_out, o_qkv, o_qv, o_bias, o_gain, o_shift, o_up_bias) = refs[4:15]
    stage_v, stage_sem, move_sem = refs[15:]
    moves = [begin(act, o_act.at[0], move_sem.at[0]), begin(d_hid, o_hid.at[0], move_sem.at[1])]
    o_qv[0] = small[0:2, :]
    o_bias[0] = small[2:4, :]
    o_gain[0] = small[4:6, :]
    o_shift[0] = small[6:8, :]
    for part in range(FF // D):
        o_up_bias[0:1, part * D : (part + 1) * D] = small[8 + part : 9 + part, :]
    places = []
    for array in (o_down, o_up, o_out, o_qkv):
        _, rows, columns = array.shape
        places += [(array, row, column) for row in range(rows // SLAB) for column in range(columns // WIDTH)]
    slots = stage_v.shape[0]
    copies = []
    for index, (array, row, column) in enumerate(places):
        slot = index % slots
        if index >= slots:
            copies[index - slots].wait()
        stage_v[slot] = totals[index].astype(F32)
        target = array.at[0, pl.ds(row * SLAB, SLAB), pl.ds(column * WIDTH, WIDTH)]
        copies.append(begin(stage_v.at[slot], target, stage_sem.at[slot]))
    for copy in copies[-slots:] + moves:
        copy.wait()


def finish(totals, small, act, d_hid):
    slots = 6
    shapes = [
        jax.ShapeDtypeStruct((1, *act.shape), BF16),
        jax.ShapeDtypeStruct((1, *act.shape), BF16),
        jax.ShapeDtypeStruct((1, FF, D), F32),
        jax.ShapeDtypeStruct((1, D, FF), F32),
        jax.ShapeDtypeStruct((1, D, D), F32),
        jax.ShapeDtypeStruct((1, D, 3 * D), F32),
        jax.ShapeDtypeStruct((1, 2, D), F32),
        jax.ShapeDtypeStruct((1, 2, D), F32),
        jax.ShapeDtypeStruct((1, 2, D), F32),
        jax.ShapeDtypeStruct((1, 2, D), F32),
        jax.ShapeDtypeStruct((1, FF), F32),
    ]
    return pl.pallas_call(
        finish_kernel,
        out_shape=shapes,
        in_specs=[VMEM, VMEM, ANY, ANY],
        out_specs=[ANY] * 6 + [VMEM] * 5,
        scratch_shapes=[
            pltpu.VMEM((slots, SLAB, WIDTH), F32),
            pltpu.SemaphoreType.DMA((slots,)),
            pltpu.SemaphoreType.DMA((2,)),
        ],
        compiler_params=pltpu.CompilerParams(vmem_limit_bytes=16 << 20),
        name="finish",
    )(*[pltpu.with_memory_space_constraint(array, pltpu.VMEM) for array in (totals, small)], act, d_hid)


def shards(
    tokens, segments, lengths, cotangent, qkv_weight, qv_bias, out_weight, out_biases,
    norm_gains, norm_shifts, up_weight, up_bias, down_weight,
):
    weights = (qkv_weight, out_weight, up_weight, down_weight)
    params = (qv_bias, out_biases, norm_gains, norm_shifts, up_bias)
    act, d_hid, small, kept = layers(tokens, cotangent, weights, segments, lengths, params)
    totals, small = reduce_gradients(
        lax.axis_size("dp") // 4, kept["gelu"], kept["d_down"], kept["low"], kept["d_up"],
        kept["ctx"], kept["d_attn"], kept["hid"], kept["d_qkv"], small,
    )
    (
        o_act, o_hid, g_down, g_up, g_out, g_qkv, g_qv, g_bias, g_gain, g_shift, g_up_bias
    ) = finish(totals, small, act, d_hid)
    return (o_act, o_hid, g_qkv, g_qv, g_out, g_bias, g_gain, g_shift, g_up, g_up_bias, g_down)


def solution(mesh):
    return jax.shard_map(
        shards,
        mesh=mesh,
        in_specs=(
            P("dp", None), P("dp", None), P("dp"), P("dp", None),
            P("section", None, None), P("section", None, None), P("section", None, None), P("section", None, None),
            P("section", None, None), P("section", None, None), P("section", None, None), P("section", None),
            P("section", None, None),
        ),
        out_specs=(
            P("section", "dp", None), P("section", "dp", None),
            P("section", None, None), P("section", None, None), P("section", None, None), P("section", None, None),
            P("section", None, None), P("section", None, None), P("section", None, None), P("section", None),
            P("section", None, None),
        ),
        check_vma=False,
    )
```

```python
import functools
import math

import jax
import jax.numpy as jnp
from jax import lax
from jax.experimental import pallas as pl
from jax.experimental.pallas import tpu as pltpu
from jax.sharding import PartitionSpec as P

D = 768
H = 12
HD = 64
FF = 3072
SEQ = 512
MICRO = 2
PAIRS = H // 2
PAIR = 2 * HD
GROUP = PAIRS // 2
BACK_GROUPS = ((0, 4), (4, 6))

EPSILON = 1e-05
SCORE_SCALE = 0.125
NEG_FILL = -1e30
F32 = jnp.float32
BF16 = jnp.bfloat16
VMEM_LIMIT = 60 << 20
REDUCE_LIMIT = 44 << 20
MESH = pl.DeviceIdType.MESH

ANY = pl.BlockSpec(memory_space=pl.ANY)
VMEM = pl.BlockSpec(memory_space=pltpu.VMEM)
SMEM = pl.BlockSpec(memory_space=pltpu.SMEM)


def dot_nn(left, right):
    return lax.dot_general(left, right, (((1,), (0,)), ((), ())), preferred_element_type=F32)


def dot_nt(left, right):
    return lax.dot_general(left, right, (((1,), (1,)), ((), ())), preferred_element_type=F32)


def dot_tn(left, right):
    return lax.dot_general(left, right, (((0,), (0,)), ((), ())), preferred_element_type=F32)


def begin(source, target, sem):
    copy = pltpu.make_async_copy(source, target, sem)
    copy.start()
    return copy


def gelu_and_slope(u):
    normal_cdf = 0.5 + 0.5 * lax.erf(u * (1.0 / math.sqrt(2.0)))
    bell = jnp.exp((-0.5 * u) * u)
    return u * normal_cdf, normal_cdf + (u * (1.0 / math.sqrt(2.0 * math.pi))) * bell


def normalize(resid):
    average = jnp.mean(resid, axis=-1, keepdims=True)
    centred = resid - average
    variance = jnp.mean(centred * centred, axis=-1, keepdims=True)
    inverse = lax.rsqrt(variance + EPSILON)
    return centred * inverse, inverse


def norm_back(grad_out, scaled, inverse, gain):
    weighted = grad_out * gain
    first_mean = jnp.mean(weighted, axis=-1, keepdims=True)
    second_mean = jnp.mean(weighted * scaled, axis=-1, keepdims=True)
    return inverse * (weighted - first_mean - scaled * second_mean)


def half_mask(which):
    lane = lax.broadcasted_iota(jnp.int32, (1, PAIR), 1)
    return ((lane // HD) == which).astype(F32).astype(BF16)


ROWS = SEQ // 2
class Place:
    def __init__(self):
        self.section = lax.axis_index("section")
        self.me = lax.axis_index("dp")
        self.core = lax.rem(self.me, 2)
        self.sibling = (self.section, self.me + 1 - 2 * self.core)
        self.other_layer = (1 - self.section, self.me)
        self.own = pl.ds(pl.multiple_of(self.core * ROWS, ROWS), ROWS)
        self.theirs = pl.ds(pl.multiple_of(ROWS - self.core * ROWS, ROWS), ROWS)

    def greet(self):
        barrier = pltpu.get_barrier_semaphore()
        for device in (self.sibling, self.other_layer):
            pl.semaphore_signal(barrier, inc=1, device_id=device, device_id_type=MESH)
        pl.semaphore_wait(barrier, 2)

    def is_mine(self, step, sequences):
        return lax.div(step, sequences) == self.core


def remote(source, target, send_sem, recv_sem, device):
    return pltpu.make_async_remote_copy(source, target, send_sem, recv_sem, device_id=device, device_id_type=MESH)


class Rows:
    def __init__(self, place, sequences, array, steps, local, sent, arrived):
        self.place, self.sequences, self.array, self.steps = place, sequences, array, steps
        self.local, self.sent, self.arrived = local, sent, arrived

    def part(self, sequence, core):
        return self.array.at[pl.ds(pl.multiple_of(sequence * SEQ + core * ROWS, ROWS), ROWS)]

    def spread(self):
        place = self.place
        for sequence in range(self.sequences):
            step = place.core * self.sequences + sequence
            target = self.steps.at[step]
            pltpu.make_async_copy(self.part(sequence, place.core), target, self.local.at[sequence]).start()
            remote(
                self.part(sequence, 1 - place.core), target, self.sent.at[sequence], self.arrived.at[step], place.sibling
            ).start()

    def spread_done(self):
        for sequence in range(self.sequences):
            view = self.steps.at[0]
            remote(view, view, self.sent.at[sequence], self.arrived.at[0], self.place.sibling).wait_send()

    def await_step(self, step, spread):
        mine = spread & self.place.is_mine(step, self.sequences)
        view = self.steps.at[step]

        @pl.when(mine)
        def _():
            pltpu.make_async_copy(view, view, self.local.at[lax.rem(step, self.sequences)]).wait()

        @pl.when(jnp.logical_not(mine))
        def _():
            remote(view, view, self.sent.at[0], self.arrived.at[step], self.place.sibling).wait_recv()

    def collect(self, step):
        sequence = lax.rem(step, self.sequences)
        target = self.part(sequence, self.place.core)
        mine = self.place.is_mine(step, self.sequences)

        @pl.when(mine)
        def _():
            pltpu.make_async_copy(self.steps.at[step], target, self.local.at[sequence]).start()

        @pl.when(jnp.logical_not(mine))
        def _():
            remote(
                self.steps.at[step], target, self.sent.at[sequence], self.arrived.at[sequence], self.place.sibling
            ).start()

    def collect_done(self):
        for sequence in range(self.sequences):
            view = self.steps.at[0]
            pltpu.make_async_copy(view, view, self.local.at[sequence]).wait()
            remote(view, view, self.sent.at[sequence], self.arrived.at[sequence], self.place.sibling).wait()


SAVED = (
    ("hid", D, BF16),
    ("low", D, BF16),
    ("gelu", FF, BF16),
    ("ctx", D, BF16),
    ("q", D, BF16),
    ("linv", D, F32),
    ("xh1", D, BF16),
    ("inv1", 128, F32),
    ("slope", FF, BF16),
    ("xh2", D, BF16),
    ("inv2", 128, F32),
)
GRADS = (("d_down", D, BF16), ("d_up", FF, BF16), ("d_attn", D, BF16), ("d_qkv", 3 * D, BF16))
SMALL_ROWS = 16


def layers_kernel(sequences, *refs):
    (tok, cot, wqkv, wo, wu, wd, segs, lens, qv_bias, out_biases, gains, shifts, up_bias) = refs[:13]
    act_out, d_hid_out, small_out, prob_io = refs[13:17]
    stop = 17 + len(SAVED)
    saved = dict(zip([name for name, _, _ in SAVED], refs[17:stop]))
    grads = dict(zip([name for name, _, _ in GRADS], refs[stop : stop + len(GRADS)]))
    stop += len(GRADS)
    (
        h_v, act_v, g_v, d_hid_v, kv_v, p_v, wqkv_v, wo_v, wu_v, wd_v, bias_v, acc_v, seg_own, seg_their,
        d_ctx_v, part_v, their_v,
    ) = refs[stop : stop + 17]
    stop += 17
    buffers = dict(zip([name for name, _, _ in SAVED if name != "hid"], refs[stop : stop + len(SAVED) - 1]))
    stop += len(SAVED) - 1
    grad_buffers = dict(zip([name for name, _, _ in GRADS], refs[stop : stop + len(GRADS)]))
    stop += len(GRADS)
    (
        w_sem, save_sem, hid_sem, grad_sem, p_sem, seg_sem, kv_sent, kv_arrived, part_sent, part_arrived,
        in_local, in_sent, in_arrived, out_local, out_sent, out_arrived, hop_sent,
        up_local, up_sent, up_arrived, down_local, down_sent, down_arrived, back_sent,
    ) = refs[stop:]
    place = Place()
    section = place.section
    steps = 2 * sequences
    names = [name for name, _, _ in SAVED]
    grad_names = [name for name, _, _ in GRADS]
    inputs = Rows(place, sequences, tok, h_v, in_local, in_sent, in_arrived)
    outputs = Rows(place, sequences, act_out, act_v, out_local, out_sent, out_arrived)
    upstream = Rows(place, sequences, cot, g_v, up_local, up_sent, up_arrived)
    downstream = Rows(place, sequences, d_hid_out, d_hid_v, down_local, down_sent, down_arrived)

    def at_step(array, step):
        return array.at[pl.ds(pl.multiple_of(step * ROWS, ROWS), ROWS)]

    def save(name, step):
        pltpu.make_async_copy(buffers[name], at_step(saved[name], step), save_sem.at[names.index(name)]).start()

    def fetch(name, step):
        pltpu.make_async_copy(at_step(saved[name], step), buffers[name], save_sem.at[names.index(name)]).start()

    def settle(name):
        pltpu.make_async_copy(buffers[name], buffers[name], save_sem.at[names.index(name)]).wait()

    def prob_part(group, step):
        heads = pl.ds(group * 2 * GROUP, 2 * GROUP)
        return p_v.at[heads], prob_io.at[step, heads], p_sem.at[group]

    def settle_prob():
        for group in range(2):
            view, _, sem = prob_part(group, 0)
            pltpu.make_async_copy(view, view, sem).wait()

    def when_first(step, copies):
        @pl.when(step == 0)
        def _():
            for copy in copies:
                copy.wait()

    def column_sum(value):
        return jnp.sum(value, axis=0, keepdims=True)

    get_qkv = [
        begin(wqkv.at[0, :, pl.ds(block * D, D)], wqkv_v.at[:, pl.ds(block * D, D)], w_sem.at[block])
        for block in (1, 2, 0)
    ]
    position = lax.broadcasted_iota(jnp.int32, (1, SEQ), 1)
    for sequence in range(sequences):
        seg_own[sequence, 0:1, :] = segs[sequence : sequence + 1, :].astype(F32)
        seg_own[sequence, 1:2, :] = (position < lens[sequence]).astype(F32)
        seg_own[sequence, 2:8, :] = jnp.zeros((6, SEQ), F32)
    place.greet()
    seg_copy = remote(seg_own, seg_their, seg_sem.at[0], seg_sem.at[1], place.sibling)

    @pl.when(section == 0)
    def _():
        inputs.spread()

    @pl.when(section == 1)
    def _():
        upstream.spread()

    seg_copy.start()
    get_wo = begin(wo.at[0], wo_v, w_sem.at[3])
    get_wu = begin(wu.at[0], wu_v, w_sem.at[4])
    get_wd = begin(wd.at[0], wd_v, w_sem.at[5])
    small_out[...] = jnp.zeros_like(small_out)

    def forward_step(step, carry):
        inputs.await_step(step, section == 0)
        pltpu.make_async_copy(h_v.at[step], at_step(saved["hid"], step), hid_sem.at[step]).start()
        hidden = h_v[step]
        for block in (1, 2):
            when_first(step, (get_qkv[block - 1],))
            proj = dot_nn(hidden, wqkv_v[:, block * D : (block + 1) * D])
            if block == 2:
                proj = proj + qv_bias[0, 1:2, :]
            cols = pl.ds((block - 1) * D, D)
            kv_v[step, place.own, cols] = proj.astype(BF16)
            view = kv_v.at[step, place.own, cols]
            remote(view, view, kv_sent.at[step, block - 1], kv_arrived.at[step, block - 1], place.sibling).start()

        def await_keys_or_values(block):
            view = kv_v.at[step, place.theirs, pl.ds(block * D, D)]
            remote(view, view, kv_sent.at[step, block], kv_arrived.at[step, block], place.sibling).wait_recv()

        @pl.when(step == 0)
        def _():
            get_qkv[2].wait()
            seg_copy.wait()

        @pl.when(step > 0)
        def _():
            settle("q")

        buffers["q"][...] = (dot_nn(hidden, wqkv_v[:, 0:D]) + qv_bias[0, 0:1, :]).astype(BF16)

        sequence = lax.rem(step, sequences)
        mine = jnp.where(place.is_mine(step, sequences), 1.0, 0.0)
        key_rows = mine * seg_own[sequence] + (1.0 - mine) * seg_their[sequence]
        query_row = mine * seg_own[sequence, 0:1, place.own] + (1.0 - mine) * seg_their[sequence, 0:1, place.own]
        query_seg = jnp.transpose(jnp.broadcast_to(query_row, (128, ROWS)))
        query = lax.broadcasted_iota(jnp.int32, (ROWS, 128), 0) + place.core * ROWS
        key = lax.broadcasted_iota(jnp.int32, (ROWS, 128), 1)
        for tile in range(SEQ // 128):
            cols = slice(tile * 128, (tile + 1) * 128)
            visible = (key_rows[1:2, cols] > 0.5) | (key + tile * 128 == query)
            bias_v[:, cols] = jnp.where((query_seg == key_rows[0:1, cols]) & visible, 0.0, NEG_FILL)

        @pl.when(step > 0)
        def _():
            for name in buffers:
                if name != "q":
                    settle(name)
            settle_prob()

        await_keys_or_values(0)
        q_v, linv_v, ctx_v = buffers["q"], buffers["linv"], buffers["ctx"]
        for pair in range(PAIRS):
            at = pair * PAIR
            q2 = q_v[:, at : at + PAIR] * SCORE_SCALE
            k2 = kv_v[step, :, at : at + PAIR]
            weights = []
            for head in range(2):
                scores = dot_nt(q2, k2 * half_mask(head)) + bias_v[...]
                weight = jnp.exp(scores - jnp.max(scores, axis=-1, keepdims=True)).astype(BF16)
                p_v[pair * 2 + head] = weight
                weights.append(weight)
            if pair == 0:
                await_keys_or_values(1)
                when_first(step, (get_wo, get_wu, get_wd))
            v2 = kv_v[step, :, D + at : D + at + PAIR]
            total = None
            for head in range(2):
                mask = half_mask(head)
                values = jnp.concatenate([v2 * mask, jnp.broadcast_to(mask, (SEQ, PAIR))], axis=1)
                part = dot_nn(weights[head], values)
                total = part if total is None else total + part
            inverse = 1.0 / total[:, PAIR : 2 * PAIR]
            linv_v[:, at : at + PAIR] = inverse
            ctx_v[:, at : at + PAIR] = (total[:, 0:PAIR] * inverse).astype(BF16)
        for group in range(2):
            view, target, sem = prob_part(group, step)
            pltpu.make_async_copy(view, target, sem).start()
        resid = hidden.astype(F32) + (dot_nn(ctx_v[...], wo_v[...]) + out_biases[0, 0:1, :])
        scaled, inverse = normalize(resid)
        buffers["xh1"][...] = scaled.astype(BF16)
        buffers["inv1"][...] = jnp.broadcast_to(inverse, (ROWS, 128))
        normed = scaled * gains[0, 0:1, :] + shifts[0, 0:1, :]
        buffers["low"][...] = normed.astype(BF16)
        acc_v[...] = normed + out_biases[0, 1:2, :]
        for name in ("q", "linv", "ctx", "xh1", "inv1", "low"):
            save(name, step)
        width = 1536
        for half in range(2):
            rows = slice(half * ROWS // 2, (half + 1) * ROWS // 2)
            for chunk in range(FF // width):
                cols = slice(chunk * width, (chunk + 1) * width)
                up = dot_nn(buffers["low"][rows, :], wu_v[:, cols]) + up_bias[0:1, cols]
                gelu, slope = gelu_and_slope(up)
                gelu = gelu.astype(BF16)
                buffers["gelu"][rows, cols] = gelu
                buffers["slope"][rows, cols] = slope.astype(BF16)
                acc_v[rows, :] += dot_nn(gelu, wd_v[cols, :])
            scaled, inverse = normalize(acc_v[rows, :])
            act_v[step, rows, :] = (scaled * gains[0, 1:2, :] + shifts[0, 1:2, :]).astype(BF16)
            buffers["xh2"][rows, :] = scaled.astype(BF16)
            buffers["inv2"][rows, :] = jnp.broadcast_to(inverse, (ROWS // 2, 128))

            @pl.when(section == 0)
            def _():
                source, target = [array.at[step, pl.ds(half * (ROWS // 2), ROWS // 2)] for array in (act_v, h_v)]
                remote(source, target, hop_sent.at[step], in_arrived.at[step], place.other_layer).start()

        outputs.collect(step)
        for name in ("gelu", "slope", "xh2", "inv2"):
            save(name, step)
        return carry

    lax.fori_loop(0, steps, forward_step, 0)

    def backward_step(turn, carry):
        step = steps - 1 - turn

        early = ("xh2", "inv2", "slope", "xh1", "inv1")
        late = ("q", "linv", "ctx")

        def part_copy(group):
            first, last = BACK_GROUPS[group]
            pairs = pl.ds(first, last - first)
            return remote(
                part_v.at[pairs, place.theirs], their_v.at[step, pairs], part_sent.at[group],
                part_arrived.at[step, group], place.sibling,
            )

        def keep(name):
            pltpu.make_async_copy(
                grad_buffers[name], at_step(grads[name], step), grad_sem.at[grad_names.index(name)]
            ).start()

        def free(name):
            buffer = grad_buffers[name]
            pltpu.make_async_copy(buffer, buffer, grad_sem.at[grad_names.index(name)]).wait()

        upstream.await_step(step, section == 1)

        @pl.when(turn > 0)
        def _():
            for name in early:
                settle(name)
            for name in ("d_down", "d_up", "d_attn"):
                free(name)

        grad = g_v[step].astype(F32)
        scaled = buffers["xh2"][...].astype(F32)
        small_out[5:6, :] += column_sum(grad * scaled)
        small_out[7:8, :] += column_sum(grad)
        d_r2 = norm_back(grad, scaled, buffers["inv2"][:, 0:1], gains[0, 1:2, :])
        d_down = d_r2.astype(BF16)
        d_down_v, d_up_v, d_attn_v, d_qkv_v = [grad_buffers[name] for name in grad_names]
        d_down_v[...] = d_down
        small_out[3:4, :] += column_sum(d_down.astype(F32))
        acc_v[...] = d_r2
        for chunk in range(FF // D):
            cols = slice(chunk * D, (chunk + 1) * D)
            d_up = (dot_nt(d_down_v[...], wd_v[cols, :]) * buffers["slope"][:, cols].astype(F32)).astype(BF16)
            d_up_v[:, cols] = d_up
            small_out[8 + chunk : 9 + chunk, :] += column_sum(d_up.astype(F32))
            acc_v[...] += dot_nt(d_up, wu_v[:, cols])
        d_normed = acc_v[...]
        scaled = buffers["xh1"][...].astype(F32)
        small_out[4:5, :] += column_sum(d_normed * scaled)
        small_out[6:7, :] += column_sum(d_normed)
        d_r1 = norm_back(d_normed, scaled, buffers["inv1"][:, 0:1], gains[0, 0:1, :])
        d_attn = d_r1.astype(BF16)
        d_attn_v[...] = d_attn
        small_out[2:3, :] += column_sum(d_attn.astype(F32))
        acc_v[...] = d_r1

        @pl.when(turn == 0)
        def _():
            for name in early:
                settle(name)

        @pl.when(turn > 0)
        def _():
            for name in late:
                settle(name)
            settle_prob()
            free("d_qkv")
            for group in range(len(BACK_GROUPS)):
                part_copy(group).wait_send()

        @pl.when(turn + 1 < steps)
        def _():
            for name in early:
                fetch(name, step - 1)

        for name in ("d_down", "d_up", "d_attn"):
            keep(name)
        d_ctx_v[...] = (dot_nt(d_attn_v[...], wo_v[...]) * buffers["linv"][...]).astype(BF16)
        q_v, ctx_v = buffers["q"], buffers["ctx"]
        for group, (first, last) in enumerate(BACK_GROUPS):
            for pair in range(first, last):
                at = pair * PAIR
                q2 = q_v[:, at : at + PAIR] * SCORE_SCALE
                k2 = kv_v[step, :, at : at + PAIR]
                v2 = kv_v[step, :, D + at : D + at + PAIR]
                dc2 = d_ctx_v[:, at : at + PAIR]
                inner = dc2.astype(F32) * ctx_v[:, at : at + PAIR].astype(F32)
                d_q, d_k, d_v = None, None, None
                for head in range(2):
                    mask = half_mask(head)
                    dc_own = dc2 * mask
                    weight = p_v[pair * 2 + head]
                    row_inner = jnp.sum(inner * mask.astype(F32), axis=-1, keepdims=True)
                    d_prob = dot_nt(dc_own, v2)
                    d_score = (weight.astype(F32) * (d_prob - row_inner)).astype(BF16)
                    one_v = dot_tn(dc_own, weight)
                    one_k = dot_tn(q2 * mask, d_score)
                    one_q = dot_nn(d_score, k2 * mask)
                    d_v = one_v if d_v is None else d_v + one_v
                    d_k = one_k if d_k is None else d_k + one_k
                    d_q = one_q if d_q is None else d_q + one_q
                d_qkv_v[:, at : at + PAIR] = (d_q * SCORE_SCALE).astype(BF16)
                part_v[pair, :, 0:PAIR] = jnp.transpose(d_k).astype(BF16)
                part_v[pair, :, PAIR : 2 * PAIR] = jnp.transpose(d_v).astype(BF16)
            part_copy(group).start()

        @pl.when(turn == 0)
        def _():
            for name in late:
                settle(name)
            settle_prob()

        @pl.when(turn + 1 < steps)
        def _():
            for name in late:
                fetch(name, step - 1)
            for group in range(2):
                view, source, sem = prob_part(group, step - 1)
                pltpu.make_async_copy(source, view, sem).start()

        d_query = d_qkv_v[:, 0:D]
        acc_v[...] += dot_nt(d_query, wqkv_v[:, 0:D])
        small_out[0:1, :] += column_sum(d_query.astype(F32))
        for group, (first, last) in enumerate(BACK_GROUPS):
            part_copy(group).wait_recv()
            for pair in range(first, last):
                total = part_v[pair, place.own, :].astype(F32) + their_v[step, pair].astype(F32)
                at = pair * PAIR
                d_qkv_v[:, D + at : D + at + PAIR] = total[:, 0:PAIR].astype(BF16)
                d_qkv_v[:, 2 * D + at : 2 * D + at + PAIR] = total[:, PAIR : 2 * PAIR].astype(BF16)
            keys = slice(D + first * PAIR, D + last * PAIR)
            values = slice(2 * D + first * PAIR, 2 * D + last * PAIR)
            d_hid = acc_v[...] + dot_nt(d_qkv_v[:, keys], wqkv_v[:, keys]) + dot_nt(d_qkv_v[:, values], wqkv_v[:, values])
            if last < PAIRS:
                acc_v[...] = d_hid
            else:
                d_hid_v[step] = d_hid.astype(BF16)

        @pl.when(section == 1)
        def _():
            remote(d_hid_v.at[step], g_v.at[step], back_sent.at[step], up_arrived.at[step], place.other_layer).start()

        downstream.collect(step)
        small_out[1:2, :] += column_sum(d_qkv_v[:, 2 * D : 3 * D].astype(F32))
        keep("d_qkv")
        return carry

    lax.fori_loop(0, steps, backward_step, 0)

    for name in ("low", "gelu"):
        settle(name)
    for name in grad_names:
        buffer = grad_buffers[name]
        pltpu.make_async_copy(buffer, buffer, grad_sem.at[grad_names.index(name)]).wait()
    for group, (first, last) in enumerate(BACK_GROUPS):
        view = part_v.at[pl.ds(first, last - first), place.theirs]
        remote(view, view, part_sent.at[group], part_arrived.at[0, group], place.sibling).wait_send()
    for step in range(steps):
        pltpu.make_async_copy(h_v.at[step], h_v.at[step], hid_sem.at[step]).wait()
        for block in range(2):
            view = kv_v.at[step, place.own, pl.ds(block * D, D)]
            remote(view, view, kv_sent.at[step, block], kv_arrived.at[step, block], place.sibling).wait_send()

    @pl.when(section == 0)
    def _():
        inputs.spread_done()
        for step in range(steps):
            remote(act_v.at[step], h_v.at[step], hop_sent.at[step], in_arrived.at[step], place.other_layer).wait_send()

    @pl.when(section == 1)
    def _():
        upstream.spread_done()
        for step in range(steps):
            remote(d_hid_v.at[step], g_v.at[step], back_sent.at[step], up_arrived.at[step], place.other_layer).wait_send()

    outputs.collect_done()
    downstream.collect_done()


def layers(tokens, cotangent, weights, segments, lengths, params):
    total = tokens.shape[0]
    sequences = total // SEQ
    steps = 2 * sequences
    shapes = [
        jax.ShapeDtypeStruct((total, D), BF16),
        jax.ShapeDtypeStruct((total, D), BF16),
        jax.ShapeDtypeStruct((SMALL_ROWS, D), F32),
        jax.ShapeDtypeStruct((steps, H, ROWS, SEQ), BF16),
    ] + [jax.ShapeDtypeStruct((total, width), dtype) for _, width, dtype in SAVED + GRADS]
    dma = pltpu.SemaphoreType.DMA
    act, d_hid, small, _, *rest = pl.pallas_call(
        functools.partial(layers_kernel, sequences),
        out_shape=shapes,
        in_specs=[ANY] * 6 + [VMEM, SMEM] + [VMEM] * 5,
        out_specs=[ANY, ANY, VMEM] + [ANY] * (len(shapes) - 3),
        scratch_shapes=[pltpu.VMEM((steps, ROWS, D), BF16)] * 4
        + [
            pltpu.VMEM((steps, SEQ, 2 * D), BF16),
            pltpu.VMEM((H, ROWS, SEQ), BF16),
            pltpu.VMEM((D, 3 * D), BF16),
            pltpu.VMEM((D, D), BF16),
            pltpu.VMEM((D, FF), BF16),
            pltpu.VMEM((FF, D), BF16),
            pltpu.VMEM((ROWS, SEQ), F32),
            pltpu.VMEM((ROWS, D), F32),
            pltpu.VMEM((sequences, 8, SEQ), F32),
            pltpu.VMEM((sequences, 8, SEQ), F32),
            pltpu.VMEM((ROWS, D), BF16),
            pltpu.VMEM((PAIRS, SEQ, 2 * PAIR), BF16),
            pltpu.VMEM((steps, PAIRS, ROWS, 2 * PAIR), BF16),
        ]
        + [pltpu.VMEM((ROWS, width), dtype) for name, width, dtype in SAVED + GRADS if name != "hid"]
        + [
            dma((6,)), dma((len(SAVED),)), dma((steps,)), dma((len(GRADS),)), dma((2,)), dma((2,)),
            dma((steps, 2)), dma((steps, 2)), dma((len(BACK_GROUPS),)), dma((steps, len(BACK_GROUPS))),
        ]
        + [dma((sequences,)), dma((sequences,)), dma((steps,))]
        + [dma((sequences,)), dma((sequences,)), dma((sequences,)), dma((steps,))]
        + [dma((sequences,)), dma((sequences,)), dma((steps,))]
        + [dma((sequences,)), dma((sequences,)), dma((sequences,)), dma((steps,))],
        compiler_params=pltpu.CompilerParams(
            collective_id=1, has_side_effects=True, vmem_limit_bytes=VMEM_LIMIT
        ),
        name="layers",
    )(tokens, cotangent, *weights, segments, lengths, *params)
    return act, d_hid, small, dict(zip([name for name, _, _ in SAVED + GRADS], rest))


UNIT = 16
SLAB = D
WIDTH = D // 2
HALF = SLAB // 2
RAIL = 7 * UNIT
LINES = (3 * UNIT, 2 * UNIT, 2 * UNIT, 3 * UNIT)
SLABS = 2 * FF // D + FF // WIDTH + D // WIDTH + 3 * D // WIDTH


def reduce_kernel(depth, *refs):
    (gelu, d_down, low, d_up, ctx, d_attn, hid, d_qkv, small) = refs[:9]
    (o_v, o_small) = refs[9:11]
    (
        left_v, right_v, p_v, s_v, y_v, rl_v, rr_v, sm_v, sm_in_v, sm_o_v,
        load_sem, send_sem, recv_sem, sm_send, sm_recv,
    ) = refs[11:]
    plan = (
        (2 * FF // D, gelu, d_down),
        (FF // WIDTH, low, d_up),
        (D // WIDTH, ctx, d_attn),
        (3 * D // WIDTH, hid, d_qkv),
    )
    count = SLABS
    section = lax.axis_index("section")
    me = lax.axis_index("dp")
    core = lax.rem(me, 2)
    y = lax.rem(lax.div(me, 2), 2)
    z = lax.div(me, 4)
    sibling = (section, me + 1 - 2 * core)
    partner = (section, me + 2 - 4 * y)
    left = (section, me - 4)
    right = (section, me + 4)

    barrier = pltpu.get_barrier_semaphore()
    pl.semaphore_signal(barrier, inc=1, device_id=sibling, device_id_type=MESH)
    pl.semaphore_signal(barrier, inc=1, device_id=partner, device_id_type=MESH)

    @pl.when(z > 0)
    def _():
        pl.semaphore_signal(barrier, inc=1, device_id=left, device_id_type=MESH)

    @pl.when(z < depth - 1)
    def _():
        pl.semaphore_signal(barrier, inc=1, device_id=right, device_id_type=MESH)

    def at(value, size):
        return pl.ds(pl.multiple_of(value, UNIT), size)

    def load(step, start):
        slot = lax.rem(step, 2)
        if not start:
            pltpu.make_async_copy(low, left_v.at[slot], load_sem.at[0, slot]).wait()
            pltpu.make_async_copy(d_down.at[:, pl.ds(0, WIDTH)], right_v.at[slot], load_sem.at[1, slot]).wait()
            return
        first = 0
        for steps, factor, grad in plan:

            def issue(first=first, factor=factor, grad=grad):
                index = step - first
                halves = grad.shape[1] // WIDTH
                rows = pl.ds(pl.multiple_of(lax.div(index, halves) * SLAB, 128), SLAB)
                cols = pl.ds(pl.multiple_of(lax.rem(index, halves) * WIDTH, 128), WIDTH)
                pltpu.make_async_copy(factor.at[:, rows], left_v.at[slot], load_sem.at[0, slot]).start()
                pltpu.make_async_copy(grad.at[:, cols], right_v.at[slot], load_sem.at[1, slot]).start()

            pl.when((step >= first) & (step < first + steps))(issue)
            first += steps

    def send(kind, step, source, target, arrival, device, compute=None):
        parity = lax.rem(step, 2)
        copy = pltpu.make_async_remote_copy(
            source, target, send_sem.at[kind, parity], arrival, device_id=device, device_id_type=MESH
        )

        @pl.when(step >= 2)
        def _():
            copy.wait_send()

        if compute is not None:
            compute()
        copy.start()

    def finish_send(kind, view):
        for parity in range(2):
            pltpu.make_async_remote_copy(
                view, view, send_sem.at[kind, parity], recv_sem.at[kind, 0], device_id=sibling, device_id_type=MESH
            ).wait_send()

    def arrived(kind, step, view):
        pltpu.make_async_remote_copy(
            view, view, send_sem.at[kind, 0], recv_sem.at[kind, step], device_id=sibling, device_id_type=MESH
        ).wait_recv()

    own = core * HALF
    theirs = HALF - own
    CX, UP, DOWN, SIB_OTHER, YX = range(5)

    def add_into(target, term):
        target[...] = (target[...].astype(F32) + term[...].astype(F32)).astype(target.dtype)

    class Tree:
        def __init__(self, kinds, base, root, reach, size, offset, land, rail):
            self.kinds, self.base, self.root, self.reach = kinds, base, root, reach
            self.size, self.offset, self.land, self.rail = size, offset, land, rail
            self.distance = jnp.abs(z - root)
            self.from_left = (z > 0) & (z <= root)
            self.from_right = (z < depth - 1) & (z >= root)

        def part(self, step):
            return s_v.at[step, at(self.offset, self.size)]

        def total(self, step):
            return o_v.at[step, at(own + self.offset, self.size)]

        def landing(self, buffer, step):
            return buffer.at[step, pl.ds(self.land, self.size)]

        def towards(self, now):
            inward, out_left, out_right, sib = self.kinds
            step = now - self.base - self.reach + self.distance

            @pl.when((step >= 0) & (step < count))
            def _():
                @pl.when(self.from_left)
                def _():
                    arrived(out_left, step, self.landing(rl_v, step))
                    add_into(self.part(step), self.landing(rl_v, step))

                @pl.when(self.from_right)
                def _():
                    arrived(out_right, step, self.landing(rr_v, step))
                    add_into(self.part(step), self.landing(rr_v, step))

                @pl.when(z < self.root)
                def _():
                    send(inward, step, self.part(step), self.landing(rl_v, step), recv_sem.at[out_left, step], right)

                @pl.when(z > self.root)
                def _():
                    send(inward, step, self.part(step), self.landing(rr_v, step), recv_sem.at[out_right, step], left)

                @pl.when(z == self.root)
                def _():
                    if self.rail:
                        self.total(step)[...] = self.part(step)[...]
                    else:
                        view = y_v.at[step, pl.ds(RAIL, self.size)]
                        send(YX, step, self.part(step), view, recv_sem.at[YX, step], partner)

            if not self.rail:
                late = now - self.base - self.reach - 1

                @pl.when((z == self.root) & (late >= 0) & (late < count))
                def _():
                    view = y_v.at[late, pl.ds(RAIL, self.size)]
                    arrived(YX, late, view)
                    self.total(late)[...] = (self.part(late)[...].astype(F32) + view[...].astype(F32)).astype(BF16)

        def away(self, now):
            inward, out_left, out_right, sib = self.kinds
            lag = self.base + self.reach + (0 if self.rail else 1)
            step = now - lag - self.distance

            @pl.when((step >= 0) & (step < count))
            def _():
                view = self.total(step)

                @pl.when(z != self.root)
                def _():
                    arrived(inward, step, view)

                @pl.when(self.from_left)
                def _():
                    send(out_left, step, view, view, recv_sem.at[inward, step], left)

                @pl.when(self.from_right)
                def _():
                    send(out_right, step, view, view, recv_sem.at[inward, step], right)

                if self.rail:
                    send(DOWN, step, view, view, recv_sem.at[DOWN, step], partner)
                send(sib, step, view, view, recv_sem.at[sib, step], sibling)

            done = step - 1

            @pl.when((done >= 0) & (done < count))
            def _():
                arrived(sib, done, o_v.at[done, at(theirs + self.offset, self.size)])

        def finish(self):
            inward, out_left, out_right, sib = self.kinds
            view = self.part(0)

            @pl.when(z != self.root)
            def _():
                finish_send(inward, view)

            @pl.when(self.from_left)
            def _():
                finish_send(out_left, view)

            @pl.when(self.from_right)
            def _():
                finish_send(out_right, view)

            finish_send(sib, view)
            if not self.rail:

                @pl.when(z == self.root)
                def _():
                    finish_send(YX, view)

    half_depth = depth // 2
    rail_root = half_depth - 1 + y
    rail = Tree((5, 6, 7, 8), 2, rail_root, half_depth, RAIL, y * RAIL, 0, True)
    line = []
    offset = 0
    for index, size in enumerate(LINES):
        root = (2 * index + 1) * depth // (2 * len(LINES))
        kinds = tuple(9 + 4 * index + kind for kind in range(4))
        reach = max(root, depth - 1 - root)
        line.append(Tree(kinds, 1, root, reach, size, 2 * RAIL + offset, RAIL + offset, False))
        offset += size
    other_distance = jnp.abs(z - (half_depth - y))
    other = (1 - y) * RAIL

    sm_root = half_depth
    sm_reach = max(sm_root, depth - 1 - sm_root)
    sm_distance = jnp.abs(z - sm_root)

    def sm_copy(kind, source, target, arrival, device):
        return pltpu.make_async_remote_copy(
            source, target, sm_send.at[kind], sm_recv.at[arrival], device_id=device, device_id_type=MESH
        )

    def small_round(now):
        @pl.when(now == 0)
        def _():
            sm_v[...] = small[...]
            sm_copy(0, sm_v, sm_in_v.at[0], 0, sibling).start()

        @pl.when(now == 1)
        def _():
            sm_copy(0, sm_v, sm_in_v.at[0], 0, sibling).wait()
            sm_v[...] = sm_v[...] + sm_in_v[0]

        @pl.when(now == 1 + sm_reach - sm_distance)
        def _():
            @pl.when((z > 0) & (z <= sm_root))
            def _():
                sm_copy(1, sm_v, sm_in_v.at[1], 1, sibling).wait_recv()
                sm_v[...] = sm_v[...] + sm_in_v[1]

            @pl.when((z < depth - 1) & (z >= sm_root))
            def _():
                sm_copy(1, sm_v, sm_in_v.at[2], 2, sibling).wait_recv()
                sm_v[...] = sm_v[...] + sm_in_v[2]

            @pl.when(z < sm_root)
            def _():
                sm_copy(1, sm_v, sm_in_v.at[1], 1, right).start()

            @pl.when(z > sm_root)
            def _():
                sm_copy(1, sm_v, sm_in_v.at[2], 2, left).start()

            @pl.when(z == sm_root)
            def _():
                sm_copy(1, sm_v, sm_in_v.at[3], 3, partner).start()

        @pl.when((now == 2 + sm_reach) & (z == sm_root))
        def _():
            sm_copy(1, sm_v, sm_in_v.at[3], 3, partner).wait_recv()
            sm_o_v[...] = sm_v[...] + sm_in_v[3]

        @pl.when(now == 2 + sm_reach + sm_distance)
        def _():
            @pl.when(z != sm_root)
            def _():
                sm_copy(2, sm_o_v, sm_o_v, 4, sibling).wait_recv()

            @pl.when((z > 0) & (z <= sm_root))
            def _():
                sm_copy(2, sm_o_v, sm_o_v, 4, left).start()

            @pl.when((z < depth - 1) & (z >= sm_root))
            def _():
                sm_copy(3, sm_o_v, sm_o_v, 4, right).start()

    def small_finish():
        sm_copy(1, sm_v, sm_in_v.at[1], 1, sibling).wait_send()

        @pl.when((z > 0) & (z <= sm_root))
        def _():
            sm_copy(2, sm_o_v, sm_o_v, 4, left).wait_send()

        @pl.when((z < depth - 1) & (z >= sm_root))
        def _():
            sm_copy(3, sm_o_v, sm_o_v, 4, right).wait_send()

        o_small[...] = sm_o_v[...]

    load(jnp.int32(0), True)
    neighbours = 2 + (z > 0).astype(jnp.int32) + (z < depth - 1).astype(jnp.int32)

    last = max(
        [2 + half_depth + half_depth + 2] + [2 + tree.reach + max(tree.root, depth - 1 - tree.root) + 1 for tree in line]
    )

    def one_round(now, carry):
        slot = lax.rem(now, 2)

        @pl.when(now < count)
        def _():
            load(now, False)

            @pl.when(now + 1 < count)
            def _():
                load(now + 1, True)

            def form():
                p_v[slot] = dot_tn(left_v[slot], right_v[slot]).astype(BF16)

                @pl.when(now == 0)
                def _():
                    pl.semaphore_wait(barrier, neighbours)

            view = p_v.at[slot, at(theirs, HALF)]
            send(CX, now, view, s_v.at[now], recv_sem.at[CX, now], sibling, form)

        step = now - 1

        @pl.when((step >= 0) & (step < count))
        def _():
            arrived(CX, step, s_v.at[step])
            add_into(s_v.at[step], p_v.at[1 - slot, at(own, HALF)])
            view = s_v.at[step, at(other, RAIL)]
            send(UP, step, view, y_v.at[step, pl.ds(0, RAIL)], recv_sem.at[UP, step], partner)

        for tree in line[::-1]:
            tree.towards(now)

        step_up = now - 2

        @pl.when((step_up >= 0) & (step_up < count))
        def _():
            view = y_v.at[step_up, pl.ds(0, RAIL)]
            arrived(UP, step_up, view)
            add_into(rail.part(step_up), view)

        rail.towards(now)
        rail.away(now)
        for tree in line[::-1]:
            tree.away(now)

        step_down = now - 2 - half_depth - other_distance - 1

        @pl.when((step_down >= 0) & (step_down < count))
        def _():
            view = o_v.at[step_down, at(own + other, RAIL)]
            arrived(DOWN, step_down, view)
            send(SIB_OTHER, step_down, view, view, recv_sem.at[SIB_OTHER, step_down], sibling)

        step_sib = step_down - 1

        @pl.when((step_sib >= 0) & (step_sib < count))
        def _():
            arrived(SIB_OTHER, step_sib, o_v.at[step_sib, at(theirs + other, RAIL)])

        small_round(now)

        return carry

    lax.fori_loop(0, count + last, one_round, 0)
    finish_send(CX, s_v.at[0])
    finish_send(UP, rail.part(0))
    finish_send(DOWN, rail.part(0))
    finish_send(SIB_OTHER, rail.part(0))
    rail.finish()
    for tree in line:
        tree.finish()
    small_finish()


def reduce_gradients(depth, gelu, d_down, low, d_up, ctx, d_attn, hid, d_qkv, small):
    rows = d_down.shape[0]
    columns = WIDTH
    count = SLABS
    kinds = 9 + 4 * len(LINES)
    return pl.pallas_call(
        functools.partial(reduce_kernel, depth),
        out_shape=[
            pltpu.VMEM((count, SLAB, columns), BF16),
            pltpu.VMEM((SMALL_ROWS, small.shape[-1]), F32),
        ],
        in_specs=[ANY] * 8 + [VMEM],
        out_specs=[VMEM] * 2,
        scratch_shapes=[
            pltpu.VMEM((2, rows, SLAB), BF16),
            pltpu.VMEM((2, rows, columns), BF16),
            pltpu.VMEM((2, SLAB, columns), BF16),
            pltpu.VMEM((count, HALF, columns), BF16),
            pltpu.VMEM((count, RAIL + max(LINES), columns), BF16),
            pltpu.VMEM((count, RAIL + sum(LINES), columns), BF16),
            pltpu.VMEM((count, RAIL + sum(LINES), columns), BF16),
            pltpu.VMEM((SMALL_ROWS, small.shape[-1]), F32),
            pltpu.VMEM((4, SMALL_ROWS, small.shape[-1]), F32),
            pltpu.VMEM((SMALL_ROWS, small.shape[-1]), F32),
            pltpu.SemaphoreType.DMA((2, 2)),
            pltpu.SemaphoreType.DMA((kinds, 2)),
            pltpu.SemaphoreType.DMA((kinds, count)),
            pltpu.SemaphoreType.DMA((4,)),
            pltpu.SemaphoreType.DMA((5,)),
        ],
        compiler_params=pltpu.CompilerParams(
            collective_id=0, has_side_effects=True, vmem_limit_bytes=REDUCE_LIMIT
        ),
        name="reduce_gradients",
    )(gelu, d_down, low, d_up, ctx, d_attn, hid, d_qkv, small)


def finish_kernel(*refs):
    (totals, small, act, d_hid) = refs[:4]
    (o_act, o_hid, o_down, o_up, o_out, o_qkv, o_qv, o_bias, o_gain, o_shift, o_up_bias) = refs[4:15]
    stage_v, stage_sem, move_sem = refs[15:]
    moves = [begin(act, o_act.at[0], move_sem.at[0]), begin(d_hid, o_hid.at[0], move_sem.at[1])]
    o_qv[0] = small[0:2, :]
    o_bias[0] = small[2:4, :]
    o_gain[0] = small[4:6, :]
    o_shift[0] = small[6:8, :]
    for part in range(FF // D):
        o_up_bias[0:1, part * D : (part + 1) * D] = small[8 + part : 9 + part, :]
    places = []
    for array in (o_down, o_up, o_out, o_qkv):
        _, rows, columns = array.shape
        places += [(array, row, column) for row in range(rows // SLAB) for column in range(columns // WIDTH)]
    slots = stage_v.shape[0]
    copies = []
    for index, (array, row, column) in enumerate(places):
        slot = index % slots
        if index >= slots:
            copies[index - slots].wait()
        stage_v[slot] = totals[index].astype(F32)
        target = array.at[0, pl.ds(row * SLAB, SLAB), pl.ds(column * WIDTH, WIDTH)]
        copies.append(begin(stage_v.at[slot], target, stage_sem.at[slot]))
    for copy in copies[-slots:] + moves:
        copy.wait()


def finish(totals, small, act, d_hid):
    slots = 6
    shapes = [
        jax.ShapeDtypeStruct((1, *act.shape), BF16),
        jax.ShapeDtypeStruct((1, *act.shape), BF16),
        jax.ShapeDtypeStruct((1, FF, D), F32),
        jax.ShapeDtypeStruct((1, D, FF), F32),
        jax.ShapeDtypeStruct((1, D, D), F32),
        jax.ShapeDtypeStruct((1, D, 3 * D), F32),
        jax.ShapeDtypeStruct((1, 2, D), F32),
        jax.ShapeDtypeStruct((1, 2, D), F32),
        jax.ShapeDtypeStruct((1, 2, D), F32),
        jax.ShapeDtypeStruct((1, 2, D), F32),
        jax.ShapeDtypeStruct((1, FF), F32),
    ]
    return pl.pallas_call(
        finish_kernel,
        out_shape=shapes,
        in_specs=[VMEM, VMEM, ANY, ANY],
        out_specs=[ANY] * 6 + [VMEM] * 5,
        scratch_shapes=[
            pltpu.VMEM((slots, SLAB, WIDTH), F32),
            pltpu.SemaphoreType.DMA((slots,)),
            pltpu.SemaphoreType.DMA((2,)),
        ],
        compiler_params=pltpu.CompilerParams(vmem_limit_bytes=16 << 20),
        name="finish",
    )(*[pltpu.with_memory_space_constraint(array, pltpu.VMEM) for array in (totals, small)], act, d_hid)


def shards(
    tokens, segments, lengths, cotangent, qkv_weight, qv_bias, out_weight, out_biases,
    norm_gains, norm_shifts, up_weight, up_bias, down_weight,
):
    weights = (qkv_weight, out_weight, up_weight, down_weight)
    params = (qv_bias, out_biases, norm_gains, norm_shifts, up_bias)
    act, d_hid, small, kept = layers(tokens, cotangent, weights, segments, lengths, params)
    totals, small = reduce_gradients(
        lax.axis_size("dp") // 4, kept["gelu"], kept["d_down"], kept["low"], kept["d_up"],
        kept["ctx"], kept["d_attn"], kept["hid"], kept["d_qkv"], small,
    )
    (
        o_act, o_hid, g_down, g_up, g_out, g_qkv, g_qv, g_bias, g_gain, g_shift, g_up_bias
    ) = finish(totals, small, act, d_hid)
    return (o_act, o_hid, g_qkv, g_qv, g_out, g_bias, g_gain, g_shift, g_up, g_up_bias, g_down)


def solution(mesh):
    return jax.shard_map(
        shards,
        mesh=mesh,
        in_specs=(
            P("dp", None), P("dp", None), P("dp"), P("dp", None),
            P("section", None, None), P("section", None, None), P("section", None, None), P("section", None, None),
            P("section", None, None), P("section", None, None), P("section", None, None), P("section", None),
            P("section", None, None),
        ),
        out_specs=(
            P("section", "dp", None), P("section", "dp", None),
            P("section", None, None), P("section", None, None), P("section", None, None), P("section", None, None),
            P("section", None, None), P("section", None, None), P("section", None, None), P("section", None),
            P("section", None, None),
        ),
        check_vma=False,
    )
```

```python
import functools
import math

import jax
import jax.numpy as jnp
from jax import lax
from jax.experimental import pallas as pl
from jax.experimental.pallas import tpu as pltpu
from jax.sharding import PartitionSpec as P

D = 768
H = 12
HD = 64
FF = 3072
SEQ = 512
MICRO = 2
PAIRS = H // 2
PAIR = 2 * HD
GROUP = PAIRS // 2
BACK_GROUPS = ((0, 4), (4, 6))

EPSILON = 1e-05
SCORE_SCALE = 0.125
NEG_FILL = -1e30
F32 = jnp.float32
BF16 = jnp.bfloat16
VMEM_LIMIT = 60 << 20
REDUCE_LIMIT = 44 << 20
MESH = pl.DeviceIdType.MESH

ANY = pl.BlockSpec(memory_space=pl.ANY)
VMEM = pl.BlockSpec(memory_space=pltpu.VMEM)
SMEM = pl.BlockSpec(memory_space=pltpu.SMEM)


def dot_nn(left, right):
    return lax.dot_general(left, right, (((1,), (0,)), ((), ())), preferred_element_type=F32)


def dot_nt(left, right):
    return lax.dot_general(left, right, (((1,), (1,)), ((), ())), preferred_element_type=F32)


def dot_tn(left, right):
    return lax.dot_general(left, right, (((0,), (0,)), ((), ())), preferred_element_type=F32)


def begin(source, target, sem):
    copy = pltpu.make_async_copy(source, target, sem)
    copy.start()
    return copy


def gelu_and_slope(u):
    normal_cdf = 0.5 + 0.5 * lax.erf(u * (1.0 / math.sqrt(2.0)))
    bell = jnp.exp((-0.5 * u) * u)
    return u * normal_cdf, normal_cdf + (u * (1.0 / math.sqrt(2.0 * math.pi))) * bell


def normalize(resid):
    average = jnp.mean(resid, axis=-1, keepdims=True)
    centred = resid - average
    variance = jnp.mean(centred * centred, axis=-1, keepdims=True)
    inverse = lax.rsqrt(variance + EPSILON)
    return centred * inverse, inverse


def norm_back(grad_out, scaled, inverse, gain):
    weighted = grad_out * gain
    first_mean = jnp.mean(weighted, axis=-1, keepdims=True)
    second_mean = jnp.mean(weighted * scaled, axis=-1, keepdims=True)
    return inverse * (weighted - first_mean - scaled * second_mean)


def half_mask(which):
    lane = lax.broadcasted_iota(jnp.int32, (1, PAIR), 1)
    return ((lane // HD) == which).astype(F32).astype(BF16)


ROWS = SEQ // 2
class Place:
    def __init__(self):
        self.section = lax.axis_index("section")
        self.me = lax.axis_index("dp")
        self.core = lax.rem(self.me, 2)
        self.sibling = (self.section, self.me + 1 - 2 * self.core)
        self.other_layer = (1 - self.section, self.me)
        self.own = pl.ds(pl.multiple_of(self.core * ROWS, ROWS), ROWS)
        self.theirs = pl.ds(pl.multiple_of(ROWS - self.core * ROWS, ROWS), ROWS)

    def greet(self):
        barrier = pltpu.get_barrier_semaphore()
        for device in (self.sibling, self.other_layer):
            pl.semaphore_signal(barrier, inc=1, device_id=device, device_id_type=MESH)
        pl.semaphore_wait(barrier, 2)

    def is_mine(self, step, sequences):
        return lax.div(step, sequences) == self.core


def remote(source, target, send_sem, recv_sem, device):
    return pltpu.make_async_remote_copy(source, target, send_sem, recv_sem, device_id=device, device_id_type=MESH)


class Rows:
    def __init__(self, place, sequences, array, steps, local, sent, arrived):
        self.place, self.sequences, self.array, self.steps = place, sequences, array, steps
        self.local, self.sent, self.arrived = local, sent, arrived

    def part(self, sequence, core):
        return self.array.at[pl.ds(pl.multiple_of(sequence * SEQ + core * ROWS, ROWS), ROWS)]

    def spread_own(self):
        place = self.place
        for sequence in range(self.sequences):
            target = self.steps.at[place.core * self.sequences + sequence]
            pltpu.make_async_copy(self.part(sequence, place.core), target, self.local.at[sequence]).start()

    def spread(self):
        place = self.place
        for sequence in range(self.sequences):
            step = place.core * self.sequences + sequence
            remote(
                self.part(sequence, 1 - place.core), self.steps.at[step], self.sent.at[sequence],
                self.arrived.at[step], place.sibling,
            ).start()

    def spread_done(self):
        for sequence in range(self.sequences):
            view = self.steps.at[0]
            remote(view, view, self.sent.at[sequence], self.arrived.at[0], self.place.sibling).wait_send()

    def await_step(self, step, spread):
        mine = spread & self.place.is_mine(step, self.sequences)
        view = self.steps.at[step]

        @pl.when(mine)
        def _():
            pltpu.make_async_copy(view, view, self.local.at[lax.rem(step, self.sequences)]).wait()

        @pl.when(jnp.logical_not(mine))
        def _():
            remote(view, view, self.sent.at[0], self.arrived.at[step], self.place.sibling).wait_recv()

    def collect(self, step):
        sequence = lax.rem(step, self.sequences)
        target = self.part(sequence, self.place.core)
        mine = self.place.is_mine(step, self.sequences)

        @pl.when(mine)
        def _():
            pltpu.make_async_copy(self.steps.at[step], target, self.local.at[sequence]).start()

        @pl.when(jnp.logical_not(mine))
        def _():
            remote(
                self.steps.at[step], target, self.sent.at[sequence], self.arrived.at[sequence], self.place.sibling
            ).start()

    def collect_done(self):
        for sequence in range(self.sequences):
            view = self.steps.at[0]
            pltpu.make_async_copy(view, view, self.local.at[sequence]).wait()
            remote(view, view, self.sent.at[sequence], self.arrived.at[sequence], self.place.sibling).wait()


SAVED = (
    ("hid", D, BF16),
    ("low", D, BF16),
    ("gelu", FF, BF16),
    ("ctx", D, BF16),
    ("q", D, BF16),
    ("linv", D, F32),
    ("xh1", D, BF16),
    ("inv1", 128, F32),
    ("slope", FF, BF16),
    ("xh2", D, BF16),
    ("inv2", 128, F32),
)
GRADS = (("d_down", D, BF16), ("d_up", FF, BF16), ("d_attn", D, BF16), ("d_qkv", 3 * D, BF16))
SMALL_ROWS = 16


def layers_kernel(sequences, *refs):
    (tok, cot, wqkv, wo, wu, wd, segs, lens, qv_bias, out_biases, gains, shifts, up_bias) = refs[:13]
    act_out, d_hid_out, small_out, prob_io = refs[13:17]
    stop = 17 + len(SAVED)
    saved = dict(zip([name for name, _, _ in SAVED], refs[17:stop]))
    grads = dict(zip([name for name, _, _ in GRADS], refs[stop : stop + len(GRADS)]))
    stop += len(GRADS)
    (
        h_v, act_v, g_v, d_hid_v, kv_v, p_v, wqkv_v, wo_v, wu_v, wd_v, bias_v, acc_v, seg_own, seg_their,
        d_ctx_v, part_v, their_v,
    ) = refs[stop : stop + 17]
    stop += 17
    buffers = dict(zip([name for name, _, _ in SAVED if name != "hid"], refs[stop : stop + len(SAVED) - 1]))
    stop += len(SAVED) - 1
    grad_buffers = dict(zip([name for name, _, _ in GRADS], refs[stop : stop + len(GRADS)]))
    stop += len(GRADS)
    (
        w_sem, save_sem, hid_sem, grad_sem, p_sem, seg_sem, kv_sent, kv_arrived, part_sent, part_arrived,
        in_local, in_sent, in_arrived, out_local, out_sent, out_arrived, hop_sent,
        up_local, up_sent, up_arrived, down_local, down_sent, down_arrived, back_sent,
    ) = refs[stop:]
    place = Place()
    section = place.section
    steps = 2 * sequences
    names = [name for name, _, _ in SAVED]
    grad_names = [name for name, _, _ in GRADS]
    inputs = Rows(place, sequences, tok, h_v, in_local, in_sent, in_arrived)
    outputs = Rows(place, sequences, act_out, act_v, out_local, out_sent, out_arrived)
    upstream = Rows(place, sequences, cot, g_v, up_local, up_sent, up_arrived)
    downstream = Rows(place, sequences, d_hid_out, d_hid_v, down_local, down_sent, down_arrived)

    def at_step(array, step):
        return array.at[pl.ds(pl.multiple_of(step * ROWS, ROWS), ROWS)]

    def save(name, step):
        pltpu.make_async_copy(buffers[name], at_step(saved[name], step), save_sem.at[names.index(name)]).start()

    def fetch(name, step):
        pltpu.make_async_copy(at_step(saved[name], step), buffers[name], save_sem.at[names.index(name)]).start()

    def settle(name):
        pltpu.make_async_copy(buffers[name], buffers[name], save_sem.at[names.index(name)]).wait()

    def prob_part(group, step):
        heads = pl.ds(group * 2 * GROUP, 2 * GROUP)
        return p_v.at[heads], prob_io.at[step, heads], p_sem.at[group]

    def settle_prob():
        for group in range(2):
            view, _, sem = prob_part(group, 0)
            pltpu.make_async_copy(view, view, sem).wait()

    def when_first(step, copies):
        @pl.when(step == 0)
        def _():
            for copy in copies:
                copy.wait()

    def column_sum(value):
        return jnp.sum(value, axis=0, keepdims=True)

    get_qkv = [
        begin(wqkv.at[0, :, pl.ds(block * D, D)], wqkv_v.at[:, pl.ds(block * D, D)], w_sem.at[block])
        for block in (1, 2, 0)
    ]

    @pl.when(section == 0)
    def _():
        inputs.spread_own()

    @pl.when(section == 1)
    def _():
        upstream.spread_own()

    get_wo = begin(wo.at[0], wo_v, w_sem.at[3])
    get_wu = begin(wu.at[0], wu_v, w_sem.at[4])
    get_wd = begin(wd.at[0], wd_v, w_sem.at[5])
    position = lax.broadcasted_iota(jnp.int32, (1, SEQ), 1)
    for sequence in range(sequences):
        seg_own[sequence, 0:1, :] = segs[sequence : sequence + 1, :].astype(F32)
        seg_own[sequence, 1:2, :] = (position < lens[sequence]).astype(F32)
        seg_own[sequence, 2:8, :] = jnp.zeros((6, SEQ), F32)
    place.greet()
    seg_copy = remote(seg_own, seg_their, seg_sem.at[0], seg_sem.at[1], place.sibling)

    @pl.when(section == 0)
    def _():
        inputs.spread()

    @pl.when(section == 1)
    def _():
        upstream.spread()

    seg_copy.start()
    small_out[...] = jnp.zeros_like(small_out)

    def forward_step(step, carry):
        inputs.await_step(step, section == 0)
        pltpu.make_async_copy(h_v.at[step], at_step(saved["hid"], step), hid_sem.at[step]).start()
        hidden = h_v[step]
        for block in (1, 2):
            when_first(step, (get_qkv[block - 1],))
            proj = dot_nn(hidden, wqkv_v[:, block * D : (block + 1) * D])
            if block == 2:
                proj = proj + qv_bias[0, 1:2, :]
            cols = pl.ds((block - 1) * D, D)
            kv_v[step, place.own, cols] = proj.astype(BF16)
            view = kv_v.at[step, place.own, cols]
            remote(view, view, kv_sent.at[step, block - 1], kv_arrived.at[step, block - 1], place.sibling).start()

        def await_keys_or_values(block):
            view = kv_v.at[step, place.theirs, pl.ds(block * D, D)]
            remote(view, view, kv_sent.at[step, block], kv_arrived.at[step, block], place.sibling).wait_recv()

        @pl.when(step == 0)
        def _():
            get_qkv[2].wait()
            seg_copy.wait()

        @pl.when(step > 0)
        def _():
            settle("q")

        buffers["q"][...] = (dot_nn(hidden, wqkv_v[:, 0:D]) + qv_bias[0, 0:1, :]).astype(BF16)

        sequence = lax.rem(step, sequences)
        mine = jnp.where(place.is_mine(step, sequences), 1.0, 0.0)
        key_rows = mine * seg_own[sequence] + (1.0 - mine) * seg_their[sequence]
        query_row = mine * seg_own[sequence, 0:1, place.own] + (1.0 - mine) * seg_their[sequence, 0:1, place.own]
        query_seg = jnp.transpose(jnp.broadcast_to(query_row, (128, ROWS)))
        query = lax.broadcasted_iota(jnp.int32, (ROWS, 128), 0) + place.core * ROWS
        key = lax.broadcasted_iota(jnp.int32, (ROWS, 128), 1)
        for tile in range(SEQ // 128):
            cols = slice(tile * 128, (tile + 1) * 128)
            visible = (key_rows[1:2, cols] > 0.5) | (key + tile * 128 == query)
            bias_v[:, cols] = jnp.where((query_seg == key_rows[0:1, cols]) & visible, 0.0, NEG_FILL)

        @pl.when(step > 0)
        def _():
            for name in buffers:
                if name != "q":
                    settle(name)
            settle_prob()

        await_keys_or_values(0)
        q_v, linv_v, ctx_v = buffers["q"], buffers["linv"], buffers["ctx"]
        for pair in range(PAIRS):
            at = pair * PAIR
            q2 = q_v[:, at : at + PAIR] * SCORE_SCALE
            k2 = kv_v[step, :, at : at + PAIR]
            weights = []
            for head in range(2):
                scores = dot_nt(q2, k2 * half_mask(head)) + bias_v[...]
                weight = jnp.exp(scores - jnp.max(scores, axis=-1, keepdims=True)).astype(BF16)
                p_v[pair * 2 + head] = weight
                weights.append(weight)
            if pair == 0:
                await_keys_or_values(1)
                when_first(step, (get_wo, get_wu, get_wd))
            v2 = kv_v[step, :, D + at : D + at + PAIR]
            total = None
            for head in range(2):
                mask = half_mask(head)
                values = jnp.concatenate([v2 * mask, jnp.broadcast_to(mask, (SEQ, PAIR))], axis=1)
                part = dot_nn(weights[head], values)
                total = part if total is None else total + part
            inverse = 1.0 / total[:, PAIR : 2 * PAIR]
            linv_v[:, at : at + PAIR] = inverse
            ctx_v[:, at : at + PAIR] = (total[:, 0:PAIR] * inverse).astype(BF16)
        for group in range(2):
            view, target, sem = prob_part(group, step)
            pltpu.make_async_copy(view, target, sem).start()
        resid = hidden.astype(F32) + (dot_nn(ctx_v[...], wo_v[...]) + out_biases[0, 0:1, :])
        scaled, inverse = normalize(resid)
        buffers["xh1"][...] = scaled.astype(BF16)
        buffers["inv1"][...] = jnp.broadcast_to(inverse, (ROWS, 128))
        normed = scaled * gains[0, 0:1, :] + shifts[0, 0:1, :]
        buffers["low"][...] = normed.astype(BF16)
        acc_v[...] = normed + out_biases[0, 1:2, :]
        for name in ("q", "linv", "ctx", "xh1", "inv1", "low"):
            save(name, step)
        width = 1536
        for half in range(2):
            rows = slice(half * ROWS // 2, (half + 1) * ROWS // 2)
            for chunk in range(FF // width):
                cols = slice(chunk * width, (chunk + 1) * width)
                up = dot_nn(buffers["low"][rows, :], wu_v[:, cols]) + up_bias[0:1, cols]
                gelu, slope = gelu_and_slope(up)
                gelu = gelu.astype(BF16)
                buffers["gelu"][rows, cols] = gelu
                buffers["slope"][rows, cols] = slope.astype(BF16)
                acc_v[rows, :] += dot_nn(gelu, wd_v[cols, :])
            scaled, inverse = normalize(acc_v[rows, :])
            act_v[step, rows, :] = (scaled * gains[0, 1:2, :] + shifts[0, 1:2, :]).astype(BF16)
            buffers["xh2"][rows, :] = scaled.astype(BF16)
            buffers["inv2"][rows, :] = jnp.broadcast_to(inverse, (ROWS // 2, 128))

            @pl.when(section == 0)
            def _():
                source, target = [array.at[step, pl.ds(half * (ROWS // 2), ROWS // 2)] for array in (act_v, h_v)]
                remote(source, target, hop_sent.at[step], in_arrived.at[step], place.other_layer).start()

        outputs.collect(step)
        for name in ("gelu", "slope", "xh2", "inv2"):
            save(name, step)
        return carry

    lax.fori_loop(0, steps, forward_step, 0)

    def backward_step(turn, carry):
        step = steps - 1 - turn

        early = ("xh2", "inv2", "slope", "xh1", "inv1")
        late = ("q", "linv", "ctx")

        def part_copy(group):
            first, last = BACK_GROUPS[group]
            pairs = pl.ds(first, last - first)
            return remote(
                part_v.at[pairs, place.theirs], their_v.at[step, pairs], part_sent.at[group],
                part_arrived.at[step, group], place.sibling,
            )

        def keep(name):
            pltpu.make_async_copy(
                grad_buffers[name], at_step(grads[name], step), grad_sem.at[grad_names.index(name)]
            ).start()

        def free(name):
            buffer = grad_buffers[name]
            pltpu.make_async_copy(buffer, buffer, grad_sem.at[grad_names.index(name)]).wait()

        upstream.await_step(step, section == 1)

        @pl.when(turn > 0)
        def _():
            for name in early:
                settle(name)
            for name in ("d_down", "d_up", "d_attn"):
                free(name)

        grad = g_v[step].astype(F32)
        scaled = buffers["xh2"][...].astype(F32)
        small_out[5:6, :] += column_sum(grad * scaled)
        small_out[7:8, :] += column_sum(grad)
        d_r2 = norm_back(grad, scaled, buffers["inv2"][:, 0:1], gains[0, 1:2, :])
        d_down = d_r2.astype(BF16)
        d_down_v, d_up_v, d_attn_v, d_qkv_v = [grad_buffers[name] for name in grad_names]
        d_down_v[...] = d_down
        small_out[3:4, :] += column_sum(d_down.astype(F32))
        acc_v[...] = d_r2
        for chunk in range(FF // D):
            cols = slice(chunk * D, (chunk + 1) * D)
            d_up = (dot_nt(d_down_v[...], wd_v[cols, :]) * buffers["slope"][:, cols].astype(F32)).astype(BF16)
            d_up_v[:, cols] = d_up
            small_out[8 + chunk : 9 + chunk, :] += column_sum(d_up.astype(F32))
            acc_v[...] += dot_nt(d_up, wu_v[:, cols])
        d_normed = acc_v[...]
        scaled = buffers["xh1"][...].astype(F32)
        small_out[4:5, :] += column_sum(d_normed * scaled)
        small_out[6:7, :] += column_sum(d_normed)
        d_r1 = norm_back(d_normed, scaled, buffers["inv1"][:, 0:1], gains[0, 0:1, :])
        d_attn = d_r1.astype(BF16)
        d_attn_v[...] = d_attn
        small_out[2:3, :] += column_sum(d_attn.astype(F32))
        acc_v[...] = d_r1

        @pl.when(turn == 0)
        def _():
            for name in early:
                settle(name)

        @pl.when(turn > 0)
        def _():
            for name in late:
                settle(name)
            settle_prob()
            free("d_qkv")
            for group in range(len(BACK_GROUPS)):
                part_copy(group).wait_send()

        @pl.when(turn + 1 < steps)
        def _():
            for name in early:
                fetch(name, step - 1)

        for name in ("d_down", "d_up", "d_attn"):
            keep(name)
        d_ctx_v[...] = (dot_nt(d_attn_v[...], wo_v[...]) * buffers["linv"][...]).astype(BF16)
        q_v, ctx_v = buffers["q"], buffers["ctx"]
        for group, (first, last) in enumerate(BACK_GROUPS):
            for pair in range(first, last):
                at = pair * PAIR
                q2 = q_v[:, at : at + PAIR] * SCORE_SCALE
                k2 = kv_v[step, :, at : at + PAIR]
                v2 = kv_v[step, :, D + at : D + at + PAIR]
                dc2 = d_ctx_v[:, at : at + PAIR]
                inner = dc2.astype(F32) * ctx_v[:, at : at + PAIR].astype(F32)
                d_q, d_k, d_v = None, None, None
                for head in range(2):
                    mask = half_mask(head)
                    dc_own = dc2 * mask
                    weight = p_v[pair * 2 + head]
                    row_inner = jnp.sum(inner * mask.astype(F32), axis=-1, keepdims=True)
                    d_prob = dot_nt(dc_own, v2)
                    d_score = (weight.astype(F32) * (d_prob - row_inner)).astype(BF16)
                    one_v = dot_tn(dc_own, weight)
                    one_k = dot_tn(q2 * mask, d_score)
                    one_q = dot_nn(d_score, k2 * mask)
                    d_v = one_v if d_v is None else d_v + one_v
                    d_k = one_k if d_k is None else d_k + one_k
                    d_q = one_q if d_q is None else d_q + one_q
                d_qkv_v[:, at : at + PAIR] = (d_q * SCORE_SCALE).astype(BF16)
                part_v[pair, :, 0:PAIR] = jnp.transpose(d_k).astype(BF16)
                part_v[pair, :, PAIR : 2 * PAIR] = jnp.transpose(d_v).astype(BF16)
            part_copy(group).start()

        @pl.when(turn == 0)
        def _():
            for name in late:
                settle(name)
            settle_prob()

        @pl.when(turn + 1 < steps)
        def _():
            for name in late:
                fetch(name, step - 1)
            for group in range(2):
                view, source, sem = prob_part(group, step - 1)
                pltpu.make_async_copy(source, view, sem).start()

        d_query = d_qkv_v[:, 0:D]
        acc_v[...] += dot_nt(d_query, wqkv_v[:, 0:D])
        small_out[0:1, :] += column_sum(d_query.astype(F32))
        for group, (first, last) in enumerate(BACK_GROUPS):
            part_copy(group).wait_recv()
            for pair in range(first, last):
                total = part_v[pair, place.own, :].astype(F32) + their_v[step, pair].astype(F32)
                at = pair * PAIR
                d_qkv_v[:, D + at : D + at + PAIR] = total[:, 0:PAIR].astype(BF16)
                d_qkv_v[:, 2 * D + at : 2 * D + at + PAIR] = total[:, PAIR : 2 * PAIR].astype(BF16)
            keys = slice(D + first * PAIR, D + last * PAIR)
            values = slice(2 * D + first * PAIR, 2 * D + last * PAIR)
            d_hid = acc_v[...] + dot_nt(d_qkv_v[:, keys], wqkv_v[:, keys]) + dot_nt(d_qkv_v[:, values], wqkv_v[:, values])
            if last < PAIRS:
                acc_v[...] = d_hid
            else:
                d_hid_v[step] = d_hid.astype(BF16)

        @pl.when(section == 1)
        def _():
            remote(d_hid_v.at[step], g_v.at[step], back_sent.at[step], up_arrived.at[step], place.other_layer).start()

        downstream.collect(step)
        small_out[1:2, :] += column_sum(d_qkv_v[:, 2 * D : 3 * D].astype(F32))
        keep("d_qkv")
        return carry

    lax.fori_loop(0, steps, backward_step, 0)

    for name in ("low", "gelu"):
        settle(name)
    for name in grad_names:
        buffer = grad_buffers[name]
        pltpu.make_async_copy(buffer, buffer, grad_sem.at[grad_names.index(name)]).wait()
    for group, (first, last) in enumerate(BACK_GROUPS):
        view = part_v.at[pl.ds(first, last - first), place.theirs]
        remote(view, view, part_sent.at[group], part_arrived.at[0, group], place.sibling).wait_send()
    for step in range(steps):
        pltpu.make_async_copy(h_v.at[step], h_v.at[step], hid_sem.at[step]).wait()
        for block in range(2):
            view = kv_v.at[step, place.own, pl.ds(block * D, D)]
            remote(view, view, kv_sent.at[step, block], kv_arrived.at[step, block], place.sibling).wait_send()

    @pl.when(section == 0)
    def _():
        inputs.spread_done()
        for step in range(steps):
            remote(act_v.at[step], h_v.at[step], hop_sent.at[step], in_arrived.at[step], place.other_layer).wait_send()

    @pl.when(section == 1)
    def _():
        upstream.spread_done()
        for step in range(steps):
            remote(d_hid_v.at[step], g_v.at[step], back_sent.at[step], up_arrived.at[step], place.other_layer).wait_send()

    outputs.collect_done()
    downstream.collect_done()


def layers(tokens, cotangent, weights, segments, lengths, params):
    total = tokens.shape[0]
    sequences = total // SEQ
    steps = 2 * sequences
    shapes = [
        jax.ShapeDtypeStruct((total, D), BF16),
        jax.ShapeDtypeStruct((total, D), BF16),
        jax.ShapeDtypeStruct((SMALL_ROWS, D), F32),
        jax.ShapeDtypeStruct((steps, H, ROWS, SEQ), BF16),
    ] + [jax.ShapeDtypeStruct((total, width), dtype) for _, width, dtype in SAVED + GRADS]
    dma = pltpu.SemaphoreType.DMA
    act, d_hid, small, _, *rest = pl.pallas_call(
        functools.partial(layers_kernel, sequences),
        out_shape=shapes,
        in_specs=[ANY] * 6 + [VMEM, SMEM] + [VMEM] * 5,
        out_specs=[ANY, ANY, VMEM] + [ANY] * (len(shapes) - 3),
        scratch_shapes=[pltpu.VMEM((steps, ROWS, D), BF16)] * 4
        + [
            pltpu.VMEM((steps, SEQ, 2 * D), BF16),
            pltpu.VMEM((H, ROWS, SEQ), BF16),
            pltpu.VMEM((D, 3 * D), BF16),
            pltpu.VMEM((D, D), BF16),
            pltpu.VMEM((D, FF), BF16),
            pltpu.VMEM((FF, D), BF16),
            pltpu.VMEM((ROWS, SEQ), F32),
            pltpu.VMEM((ROWS, D), F32),
            pltpu.VMEM((sequences, 8, SEQ), F32),
            pltpu.VMEM((sequences, 8, SEQ), F32),
            pltpu.VMEM((ROWS, D), BF16),
            pltpu.VMEM((PAIRS, SEQ, 2 * PAIR), BF16),
            pltpu.VMEM((steps, PAIRS, ROWS, 2 * PAIR), BF16),
        ]
        + [pltpu.VMEM((ROWS, width), dtype) for name, width, dtype in SAVED + GRADS if name != "hid"]
        + [
            dma((6,)), dma((len(SAVED),)), dma((steps,)), dma((len(GRADS),)), dma((2,)), dma((2,)),
            dma((steps, 2)), dma((steps, 2)), dma((len(BACK_GROUPS),)), dma((steps, len(BACK_GROUPS))),
        ]
        + [dma((sequences,)), dma((sequences,)), dma((steps,))]
        + [dma((sequences,)), dma((sequences,)), dma((sequences,)), dma((steps,))]
        + [dma((sequences,)), dma((sequences,)), dma((steps,))]
        + [dma((sequences,)), dma((sequences,)), dma((sequences,)), dma((steps,))],
        compiler_params=pltpu.CompilerParams(
            collective_id=1, has_side_effects=True, vmem_limit_bytes=VMEM_LIMIT
        ),
        name="layers",
    )(tokens, cotangent, *weights, segments, lengths, *params)
    return act, d_hid, small, dict(zip([name for name, _, _ in SAVED + GRADS], rest))


UNIT = 16
SLAB = D
WIDTH = D // 2
HALF = SLAB // 2
RAIL = 7 * UNIT
LINES = (3 * UNIT, 2 * UNIT, 2 * UNIT, 3 * UNIT)
SLABS = 2 * FF // D + FF // WIDTH + D // WIDTH + 3 * D // WIDTH


def reduce_kernel(depth, *refs):
    (gelu, d_down, low, d_up, ctx, d_attn, hid, d_qkv, small) = refs[:9]
    (o_v, o_small) = refs[9:11]
    (
        left_v, right_v, p_v, s_v, y_v, rl_v, rr_v, sm_v, sm_in_v, sm_o_v,
        load_sem, send_sem, recv_sem, sm_send, sm_recv,
    ) = refs[11:]
    plan = (
        (2 * FF // D, gelu, d_down),
        (FF // WIDTH, low, d_up),
        (D // WIDTH, ctx, d_attn),
        (3 * D // WIDTH, hid, d_qkv),
    )
    count = SLABS
    section = lax.axis_index("section")
    me = lax.axis_index("dp")
    core = lax.rem(me, 2)
    y = lax.rem(lax.div(me, 2), 2)
    z = lax.div(me, 4)
    sibling = (section, me + 1 - 2 * core)
    partner = (section, me + 2 - 4 * y)
    left = (section, me - 4)
    right = (section, me + 4)

    barrier = pltpu.get_barrier_semaphore()
    pl.semaphore_signal(barrier, inc=1, device_id=sibling, device_id_type=MESH)
    pl.semaphore_signal(barrier, inc=1, device_id=partner, device_id_type=MESH)

    @pl.when(z > 0)
    def _():
        pl.semaphore_signal(barrier, inc=1, device_id=left, device_id_type=MESH)

    @pl.when(z < depth - 1)
    def _():
        pl.semaphore_signal(barrier, inc=1, device_id=right, device_id_type=MESH)

    def at(value, size):
        return pl.ds(pl.multiple_of(value, UNIT), size)

    def load(step, start):
        slot = lax.rem(step, 2)
        if not start:
            pltpu.make_async_copy(low, left_v.at[slot], load_sem.at[0, slot]).wait()
            pltpu.make_async_copy(d_down.at[:, pl.ds(0, WIDTH)], right_v.at[slot], load_sem.at[1, slot]).wait()
            return
        first = 0
        for steps, factor, grad in plan:

            def issue(first=first, factor=factor, grad=grad):
                index = step - first
                halves = grad.shape[1] // WIDTH
                rows = pl.ds(pl.multiple_of(lax.div(index, halves) * SLAB, 128), SLAB)
                cols = pl.ds(pl.multiple_of(lax.rem(index, halves) * WIDTH, 128), WIDTH)
                pltpu.make_async_copy(factor.at[:, rows], left_v.at[slot], load_sem.at[0, slot]).start()
                pltpu.make_async_copy(grad.at[:, cols], right_v.at[slot], load_sem.at[1, slot]).start()

            pl.when((step >= first) & (step < first + steps))(issue)
            first += steps

    def send(kind, step, source, target, arrival, device, compute=None):
        parity = lax.rem(step, 2)
        copy = pltpu.make_async_remote_copy(
            source, target, send_sem.at[kind, parity], arrival, device_id=device, device_id_type=MESH
        )

        @pl.when(step >= 2)
        def _():
            copy.wait_send()

        if compute is not None:
            compute()
        copy.start()

    def finish_send(kind, view):
        for parity in range(2):
            pltpu.make_async_remote_copy(
                view, view, send_sem.at[kind, parity], recv_sem.at[kind, 0], device_id=sibling, device_id_type=MESH
            ).wait_send()

    def arrived(kind, step, view):
        pltpu.make_async_remote_copy(
            view, view, send_sem.at[kind, 0], recv_sem.at[kind, step], device_id=sibling, device_id_type=MESH
        ).wait_recv()

    own = core * HALF
    theirs = HALF - own
    CX, UP, DOWN, SIB_OTHER, YX = range(5)

    def add_into(target, term):
        target[...] = (target[...].astype(F32) + term[...].astype(F32)).astype(target.dtype)

    class Tree:
        def __init__(self, kinds, base, root, reach, size, offset, land, rail):
            self.kinds, self.base, self.root, self.reach = kinds, base, root, reach
            self.size, self.offset, self.land, self.rail = size, offset, land, rail
            self.distance = jnp.abs(z - root)
            self.from_left = (z > 0) & (z <= root)
            self.from_right = (z < depth - 1) & (z >= root)

        def part(self, step):
            return s_v.at[step, at(self.offset, self.size)]

        def total(self, step):
            return o_v.at[step, at(own + self.offset, self.size)]

        def landing(self, buffer, step):
            return buffer.at[step, pl.ds(self.land, self.size)]

        def towards(self, now):
            inward, out_left, out_right, sib = self.kinds
            step = now - self.base - self.reach + self.distance

            @pl.when((step >= 0) & (step < count))
            def _():
                @pl.when(self.from_left)
                def _():
                    arrived(out_left, step, self.landing(rl_v, step))
                    add_into(self.part(step), self.landing(rl_v, step))

                @pl.when(self.from_right)
                def _():
                    arrived(out_right, step, self.landing(rr_v, step))
                    add_into(self.part(step), self.landing(rr_v, step))

                @pl.when(z < self.root)
                def _():
                    send(inward, step, self.part(step), self.landing(rl_v, step), recv_sem.at[out_left, step], right)

                @pl.when(z > self.root)
                def _():
                    send(inward, step, self.part(step), self.landing(rr_v, step), recv_sem.at[out_right, step], left)

                @pl.when(z == self.root)
                def _():
                    if self.rail:
                        self.total(step)[...] = self.part(step)[...]
                    else:
                        view = y_v.at[step, pl.ds(RAIL, self.size)]
                        send(YX, step, self.part(step), view, recv_sem.at[YX, step], partner)

            if not self.rail:
                late = now - self.base - self.reach - 1

                @pl.when((z == self.root) & (late >= 0) & (late < count))
                def _():
                    view = y_v.at[late, pl.ds(RAIL, self.size)]
                    arrived(YX, late, view)
                    self.total(late)[...] = (self.part(late)[...].astype(F32) + view[...].astype(F32)).astype(BF16)

        def away(self, now):
            inward, out_left, out_right, sib = self.kinds
            lag = self.base + self.reach + (0 if self.rail else 1)
            step = now - lag - self.distance

            @pl.when((step >= 0) & (step < count))
            def _():
                view = self.total(step)

                @pl.when(z != self.root)
                def _():
                    arrived(inward, step, view)

                @pl.when(self.from_left)
                def _():
                    send(out_left, step, view, view, recv_sem.at[inward, step], left)

                @pl.when(self.from_right)
                def _():
                    send(out_right, step, view, view, recv_sem.at[inward, step], right)

                if self.rail:
                    send(DOWN, step, view, view, recv_sem.at[DOWN, step], partner)
                send(sib, step, view, view, recv_sem.at[sib, step], sibling)

            done = step - 1

            @pl.when((done >= 0) & (done < count))
            def _():
                arrived(sib, done, o_v.at[done, at(theirs + self.offset, self.size)])

        def finish(self):
            inward, out_left, out_right, sib = self.kinds
            view = self.part(0)

            @pl.when(z != self.root)
            def _():
                finish_send(inward, view)

            @pl.when(self.from_left)
            def _():
                finish_send(out_left, view)

            @pl.when(self.from_right)
            def _():
                finish_send(out_right, view)

            finish_send(sib, view)
            if not self.rail:

                @pl.when(z == self.root)
                def _():
                    finish_send(YX, view)

    half_depth = depth // 2
    rail_root = half_depth - 1 + y
    rail = Tree((5, 6, 7, 8), 2, rail_root, half_depth, RAIL, y * RAIL, 0, True)
    line = []
    offset = 0
    for index, size in enumerate(LINES):
        root = (2 * index + 1) * depth // (2 * len(LINES))
        kinds = tuple(9 + 4 * index + kind for kind in range(4))
        reach = max(root, depth - 1 - root)
        line.append(Tree(kinds, 1, root, reach, size, 2 * RAIL + offset, RAIL + offset, False))
        offset += size
    other_distance = jnp.abs(z - (half_depth - y))
    other = (1 - y) * RAIL

    sm_root = half_depth
    sm_reach = max(sm_root, depth - 1 - sm_root)
    sm_distance = jnp.abs(z - sm_root)

    def sm_copy(kind, source, target, arrival, device):
        return pltpu.make_async_remote_copy(
            source, target, sm_send.at[kind], sm_recv.at[arrival], device_id=device, device_id_type=MESH
        )

    def small_round(now):
        @pl.when(now == 0)
        def _():
            sm_v[...] = small[...]
            sm_copy(0, sm_v, sm_in_v.at[0], 0, sibling).start()

        @pl.when(now == 1)
        def _():
            sm_copy(0, sm_v, sm_in_v.at[0], 0, sibling).wait()
            sm_v[...] = sm_v[...] + sm_in_v[0]

        @pl.when(now == 1 + sm_reach - sm_distance)
        def _():
            @pl.when((z > 0) & (z <= sm_root))
            def _():
                sm_copy(1, sm_v, sm_in_v.at[1], 1, sibling).wait_recv()
                sm_v[...] = sm_v[...] + sm_in_v[1]

            @pl.when((z < depth - 1) & (z >= sm_root))
            def _():
                sm_copy(1, sm_v, sm_in_v.at[2], 2, sibling).wait_recv()
                sm_v[...] = sm_v[...] + sm_in_v[2]

            @pl.when(z < sm_root)
            def _():
                sm_copy(1, sm_v, sm_in_v.at[1], 1, right).start()

            @pl.when(z > sm_root)
            def _():
                sm_copy(1, sm_v, sm_in_v.at[2], 2, left).start()

            @pl.when(z == sm_root)
            def _():
                sm_copy(1, sm_v, sm_in_v.at[3], 3, partner).start()

        @pl.when((now == 2 + sm_reach) & (z == sm_root))
        def _():
            sm_copy(1, sm_v, sm_in_v.at[3], 3, partner).wait_recv()
            sm_o_v[...] = sm_v[...] + sm_in_v[3]

        @pl.when(now == 2 + sm_reach + sm_distance)
        def _():
            @pl.when(z != sm_root)
            def _():
                sm_copy(2, sm_o_v, sm_o_v, 4, sibling).wait_recv()

            @pl.when((z > 0) & (z <= sm_root))
            def _():
                sm_copy(2, sm_o_v, sm_o_v, 4, left).start()

            @pl.when((z < depth - 1) & (z >= sm_root))
            def _():
                sm_copy(3, sm_o_v, sm_o_v, 4, right).start()

    def small_finish():
        sm_copy(1, sm_v, sm_in_v.at[1], 1, sibling).wait_send()

        @pl.when((z > 0) & (z <= sm_root))
        def _():
            sm_copy(2, sm_o_v, sm_o_v, 4, left).wait_send()

        @pl.when((z < depth - 1) & (z >= sm_root))
        def _():
            sm_copy(3, sm_o_v, sm_o_v, 4, right).wait_send()

        o_small[...] = sm_o_v[...]

    load(jnp.int32(0), True)
    neighbours = 2 + (z > 0).astype(jnp.int32) + (z < depth - 1).astype(jnp.int32)

    last = max(
        [2 + half_depth + half_depth + 2] + [2 + tree.reach + max(tree.root, depth - 1 - tree.root) + 1 for tree in line]
    )

    def one_round(now, carry):
        slot = lax.rem(now, 2)

        @pl.when(now < count)
        def _():
            load(now, False)

            @pl.when(now + 1 < count)
            def _():
                load(now + 1, True)

            def form():
                p_v[slot] = dot_tn(left_v[slot], right_v[slot]).astype(BF16)

                @pl.when(now == 0)
                def _():
                    pl.semaphore_wait(barrier, neighbours)

            view = p_v.at[slot, at(theirs, HALF)]
            send(CX, now, view, s_v.at[now], recv_sem.at[CX, now], sibling, form)

        step = now - 1

        @pl.when((step >= 0) & (step < count))
        def _():
            arrived(CX, step, s_v.at[step])
            add_into(s_v.at[step], p_v.at[1 - slot, at(own, HALF)])
            view = s_v.at[step, at(other, RAIL)]
            send(UP, step, view, y_v.at[step, pl.ds(0, RAIL)], recv_sem.at[UP, step], partner)

        for tree in line[::-1]:
            tree.towards(now)

        step_up = now - 2

        @pl.when((step_up >= 0) & (step_up < count))
        def _():
            view = y_v.at[step_up, pl.ds(0, RAIL)]
            arrived(UP, step_up, view)
            add_into(rail.part(step_up), view)

        rail.towards(now)
        rail.away(now)
        for tree in line[::-1]:
            tree.away(now)

        step_down = now - 2 - half_depth - other_distance - 1

        @pl.when((step_down >= 0) & (step_down < count))
        def _():
            view = o_v.at[step_down, at(own + other, RAIL)]
            arrived(DOWN, step_down, view)
            send(SIB_OTHER, step_down, view, view, recv_sem.at[SIB_OTHER, step_down], sibling)

        step_sib = step_down - 1

        @pl.when((step_sib >= 0) & (step_sib < count))
        def _():
            arrived(SIB_OTHER, step_sib, o_v.at[step_sib, at(theirs + other, RAIL)])

        small_round(now)

        return carry

    lax.fori_loop(0, count + last, one_round, 0)
    finish_send(CX, s_v.at[0])
    finish_send(UP, rail.part(0))
    finish_send(DOWN, rail.part(0))
    finish_send(SIB_OTHER, rail.part(0))
    rail.finish()
    for tree in line:
        tree.finish()
    small_finish()


def reduce_gradients(depth, gelu, d_down, low, d_up, ctx, d_attn, hid, d_qkv, small):
    rows = d_down.shape[0]
    columns = WIDTH
    count = SLABS
    kinds = 9 + 4 * len(LINES)
    return pl.pallas_call(
        functools.partial(reduce_kernel, depth),
        out_shape=[
            pltpu.VMEM((count, SLAB, columns), BF16),
            pltpu.VMEM((SMALL_ROWS, small.shape[-1]), F32),
        ],
        in_specs=[ANY] * 8 + [VMEM],
        out_specs=[VMEM] * 2,
        scratch_shapes=[
            pltpu.VMEM((2, rows, SLAB), BF16),
            pltpu.VMEM((2, rows, columns), BF16),
            pltpu.VMEM((2, SLAB, columns), BF16),
            pltpu.VMEM((count, HALF, columns), BF16),
            pltpu.VMEM((count, RAIL + max(LINES), columns), BF16),
            pltpu.VMEM((count, RAIL + sum(LINES), columns), BF16),
            pltpu.VMEM((count, RAIL + sum(LINES), columns), BF16),
            pltpu.VMEM((SMALL_ROWS, small.shape[-1]), F32),
            pltpu.VMEM((4, SMALL_ROWS, small.shape[-1]), F32),
            pltpu.VMEM((SMALL_ROWS, small.shape[-1]), F32),
            pltpu.SemaphoreType.DMA((2, 2)),
            pltpu.SemaphoreType.DMA((kinds, 2)),
            pltpu.SemaphoreType.DMA((kinds, count)),
            pltpu.SemaphoreType.DMA((4,)),
            pltpu.SemaphoreType.DMA((5,)),
        ],
        compiler_params=pltpu.CompilerParams(
            collective_id=0, has_side_effects=True, vmem_limit_bytes=REDUCE_LIMIT
        ),
        name="reduce_gradients",
    )(gelu, d_down, low, d_up, ctx, d_attn, hid, d_qkv, small)


def finish_kernel(*refs):
    (totals, small, act, d_hid) = refs[:4]
    (o_act, o_hid, o_down, o_up, o_out, o_qkv, o_qv, o_bias, o_gain, o_shift, o_up_bias) = refs[4:15]
    stage_v, stage_sem, move_sem = refs[15:]
    moves = [begin(act, o_act.at[0], move_sem.at[0]), begin(d_hid, o_hid.at[0], move_sem.at[1])]
    o_qv[0] = small[0:2, :]
    o_bias[0] = small[2:4, :]
    o_gain[0] = small[4:6, :]
    o_shift[0] = small[6:8, :]
    for part in range(FF // D):
        o_up_bias[0:1, part * D : (part + 1) * D] = small[8 + part : 9 + part, :]
    places = []
    for array in (o_down, o_up, o_out, o_qkv):
        _, rows, columns = array.shape
        places += [(array, row, column) for row in range(rows // SLAB) for column in range(columns // WIDTH)]
    slots = stage_v.shape[0]
    copies = []
    for index, (array, row, column) in enumerate(places):
        slot = index % slots
        if index >= slots:
            copies[index - slots].wait()
        stage_v[slot] = totals[index].astype(F32)
        target = array.at[0, pl.ds(row * SLAB, SLAB), pl.ds(column * WIDTH, WIDTH)]
        copies.append(begin(stage_v.at[slot], target, stage_sem.at[slot]))
    for copy in copies[-slots:] + moves:
        copy.wait()


def finish(totals, small, act, d_hid):
    slots = 6
    shapes = [
        jax.ShapeDtypeStruct((1, *act.shape), BF16),
        jax.ShapeDtypeStruct((1, *act.shape), BF16),
        jax.ShapeDtypeStruct((1, FF, D), F32),
        jax.ShapeDtypeStruct((1, D, FF), F32),
        jax.ShapeDtypeStruct((1, D, D), F32),
        jax.ShapeDtypeStruct((1, D, 3 * D), F32),
        jax.ShapeDtypeStruct((1, 2, D), F32),
        jax.ShapeDtypeStruct((1, 2, D), F32),
        jax.ShapeDtypeStruct((1, 2, D), F32),
        jax.ShapeDtypeStruct((1, 2, D), F32),
        jax.ShapeDtypeStruct((1, FF), F32),
    ]
    return pl.pallas_call(
        finish_kernel,
        out_shape=shapes,
        in_specs=[VMEM, VMEM, ANY, ANY],
        out_specs=[ANY] * 6 + [VMEM] * 5,
        scratch_shapes=[
            pltpu.VMEM((slots, SLAB, WIDTH), F32),
            pltpu.SemaphoreType.DMA((slots,)),
            pltpu.SemaphoreType.DMA((2,)),
        ],
        compiler_params=pltpu.CompilerParams(vmem_limit_bytes=16 << 20),
        name="finish",
    )(*[pltpu.with_memory_space_constraint(array, pltpu.VMEM) for array in (totals, small)], act, d_hid)


def shards(
    tokens, segments, lengths, cotangent, qkv_weight, qv_bias, out_weight, out_biases,
    norm_gains, norm_shifts, up_weight, up_bias, down_weight,
):
    weights = (qkv_weight, out_weight, up_weight, down_weight)
    params = (qv_bias, out_biases, norm_gains, norm_shifts, up_bias)
    act, d_hid, small, kept = layers(tokens, cotangent, weights, segments, lengths, params)
    totals, small = reduce_gradients(
        lax.axis_size("dp") // 4, kept["gelu"], kept["d_down"], kept["low"], kept["d_up"],
        kept["ctx"], kept["d_attn"], kept["hid"], kept["d_qkv"], small,
    )
    (
        o_act, o_hid, g_down, g_up, g_out, g_qkv, g_qv, g_bias, g_gain, g_shift, g_up_bias
    ) = finish(totals, small, act, d_hid)
    return (o_act, o_hid, g_qkv, g_qv, g_out, g_bias, g_gain, g_shift, g_up, g_up_bias, g_down)


def solution(mesh):
    return jax.shard_map(
        shards,
        mesh=mesh,
        in_specs=(
            P("dp", None), P("dp", None), P("dp"), P("dp", None),
            P("section", None, None), P("section", None, None), P("section", None, None), P("section", None, None),
            P("section", None, None), P("section", None, None), P("section", None, None), P("section", None),
            P("section", None, None),
        ),
        out_specs=(
            P("section", "dp", None), P("section", "dp", None),
            P("section", None, None), P("section", None, None), P("section", None, None), P("section", None, None),
            P("section", None, None), P("section", None, None), P("section", None, None), P("section", None),
            P("section", None, None),
        ),
        check_vma=False,
    )
```
